32 devices in a mesh: seq: 8 (over z, x), mlp: 4 (over y, core).
Axes of the slice: x: 2, y: 2, z: 4, core: 2. Of those that a mesh axis runs over, the one named last changes fastest.
Arguments:
- inputs: bfloat16 [4096, 512], P('seq', 'mlp'), may hold values from -6 to 6
- lengths: int32 [9], replicated, may hold values from 16 to 3584, as said below
- valid: int32 [4096], P('seq'), may hold values 0 or 1
- norm_attn: float32 [2, 512], P(None, 'mlp'), may hold values from 0.4 to 1.6
- w_qkv: bfloat16 [2, 3, 512, 512], P(None, None, None, 'mlp'), may hold values from -0.25 to 0.25
- blend: float32 [2, 3, 8], P(None, None, 'mlp'), may hold values from 0.5 to 1.5
- w_out: bfloat16 [2, 512, 512], P(None, 'mlp'), may hold values from -0.25 to 0.25
- norm_ffn: float32 [2, 512], P(None, 'mlp'), may hold values from 0.4 to 1.6
- w_up: bfloat16 [2, 512, 2048], P(None, None, 'mlp'), may hold values from -0.25 to 0.25
- w_down: bfloat16 [2, 2048, 512], P(None, 'mlp'), may hold values from -0.125 to 0.125
- grad_out: bfloat16 [4096, 512], P('seq', 'mlp'), may hold values from -6 to 6
Outputs:
- output: bfloat16 [4096, 512], P('seq', 'mlp')
- d_inputs: bfloat16 [4096, 512], P('seq', 'mlp')
- d_norm_attn: float32 [2, 512], P(None, 'mlp')
- d_w_qkv: float32 [2, 3, 512, 512], P(None, None, None, 'mlp')
- d_blend: float32 [2, 3, 8], P(None, None, 'mlp')
- d_w_out: float32 [2, 512, 512], P(None, 'mlp')
- d_norm_ffn: float32 [2, 512], P(None, 'mlp')
- d_w_up: float32 [2, 512, 2048], P(None, None, 'mlp')
- d_w_down: float32 [2, 2048, 512], P(None, 'mlp')
The draws below stay inside these ranges and needn't reach their ends.
Inputs may be any that keep to these rules, and one draw needn't show every extreme that they name: The item lengths sum to 4096. Item number 4 (counting from 0) has 3584 tokens and begins within the first 512 tokens; the other items together hold 512 tokens.
All inputs are finite; a program needn't handle non-finite values. No bound on the sum of `valid` on one device may be relied on, other than what follows from the above.
Results may differ from the reference program's by a relative error of at most 0.018.
Values may be sent and summed in bfloat16 or wider, within the bound.
No kernel may reach another device: no remote copies, remote signals or barrier semaphores. Data moves between devices by JAX's collectives and lax.ppermute only.
A program may use at most 128 MiB of HBM per device.

```python
import math
import jax
import jax.numpy as jnp
from jax import lax

H = 8
HD = 64
D = 512
FF = 2048
BAND = 30
LAYERS = 2
SHORTS = 4
TOK_DEV = 512
TOKENS = 4096


def draw_lengths(key, part):
    key = jax.random.fold_in(key, 7)
    shortest = max(TOK_DEV // 32, 1)
    longest = TOK_DEV // 8
    leading = jax.random.randint(jax.random.fold_in(key, 1), (SHORTS,), shortest, longest + 1, dtype=jnp.int32)
    trailing = jax.random.randint(jax.random.fold_in(key, 2), (SHORTS - 1,), shortest, longest + 1, dtype=jnp.int32)
    closing = TOK_DEV - jnp.sum(leading) - jnp.sum(trailing)
    spanning = jnp.full((1,), TOKENS - TOK_DEV, jnp.int32)
    return jnp.concatenate([leading, spanning, trailing, closing.reshape(1)]).astype(jnp.int32)


def place_ends(drawn, own_key, low, high):
    place = [jax.random.randint(jax.random.fold_in(own_key, axis), (), 0, length) for axis, length in enumerate(drawn.shape)]
    widest = drawn.shape.index(max(drawn.shape))
    neighbour = place[:widest] + [(place[widest] + 1) % drawn.shape[widest]] + place[widest + 1:]
    return drawn.at[tuple(place)].set(low).at[tuple(neighbour)].set(high)


def shard_levels(key, dims, split, low, largest):
    def one(position, parts):
        heights = jax.random.uniform(jax.random.fold_in(jax.random.fold_in(key, 6), position), (parts,), jnp.float32, low / len(split), largest / len(split))
        return jnp.repeat(jnp.exp(heights), dims[position] // parts).reshape((-1,) + (1,) * (len(dims) - position - 1))

    loudness = one(*split[0])
    for cut in split[1:]:
        loudness = loudness * one(*cut)
    return loudness


def noise(stream_key, dims, deviation, limit, shards=(), kind=jnp.bfloat16):
    array = jax.random.normal(stream_key, dims, jnp.float32) * deviation
    if len(shards) > 0:
        array = shard_levels(stream_key, dims, shards, -0.22, 0.18) * array
    return jnp.clip(array, min=-limit, max=limit).astype(kind)


def setup_inputs(seed: int = 0) -> dict:
    splits = jax.random.split(jax.random.key(seed), 12)
    return {
        "inputs": noise(splits[0], (TOKENS, D), 1.0, 6.0, ((0, 8), (1, 4))),
        "lengths": draw_lengths(jax.random.fold_in(splits[11], 71), 0),
        "valid": place_ends((jax.random.randint(splits[2], (TOKENS,), 0, 8) < 7).astype(jnp.int32), jax.random.fold_in(splits[2], 1), 0, 1),
        "norm_attn": jnp.clip(1.0 + 0.12 * jax.random.normal(splits[3], (LAYERS, D), jnp.float32), 0.4, 1.6),
        "w_qkv": noise(splits[4], (LAYERS, 3, D, D), D ** -0.5, 0.25, ((3, 4),)),
        "blend": jnp.clip(0.5 + 1.0 * jax.random.uniform(splits[5], (LAYERS, 3, H), jnp.float32) ** shard_levels(splits[5], (LAYERS, 3, H), ((2, 4),), -0.2, 0.2), 0.5, 1.5),
        "w_out": noise(splits[6], (LAYERS, D, D), D ** -0.5, 0.25, ((1, 4),)),
        "norm_ffn": jnp.clip(1.0 + 0.12 * jax.random.normal(splits[7], (LAYERS, D), jnp.float32), 0.4, 1.6),
        "w_up": noise(splits[8], (LAYERS, D, FF), D ** -0.5, 0.25, ((2, 4),)),
        "w_down": noise(splits[9], (LAYERS, FF, D), FF ** -0.5, 0.125, ((1, 4),)),
        "grad_out": noise(splits[10], (TOKENS, D), 1.0, 6.0, ((0, 8), (1, 4))),
    }


epsilon = 1e-05
masked_score = -1e+30

@jax.custom_vjp
def low(v):
    return lax.optimization_barrier(v.astype(jnp.bfloat16)).astype(jnp.float32)

@jax.custom_vjp
def low_back(v):
    return v

def low_keep(v):
    return (low(v), None)

def low_pass(kept, grad):
    return (grad,)

def back_keep(v):
    return (v, None)

def back_low(kept, grad):
    return (low(grad),)
low.defvjp(low_keep, low_pass)
low_back.defvjp(back_keep, back_low)

def normalize(hidden, gain_row):
    return hidden * lax.rsqrt(lax.optimization_barrier(jnp.mean(hidden * hidden, axis=-1, keepdims=True)) + epsilon) * gain_row

def item_start(lengths, positions):
    ends_cum = jnp.cumsum(lengths).astype(jnp.int32)
    picked = jnp.where(ends_cum[None, :] <= positions[:, None], lengths[None, :], 0)
    return lax.optimization_barrier(jnp.sum(picked, axis=1)).astype(jnp.int32)

def kernel_maps(values):
    return (jax.nn.elu(values) + 1.0, jnp.tanh(values))

def layer_pass(hidden, starts, valid, params):
    gain_attn, weight_qkv, blend_layer, weight_out, gain_ffn, weight_up, weight_down = params
    precise = lax.Precision.HIGHEST
    total_rows = hidden.shape[0]
    block_rows = min(512, total_rows)
    block_count = total_rows // block_rows
    score_scale = 1.0 / math.sqrt(HD)

    def step(carry, block_inputs):
        state_one, state_two, key_total, key_tail, value_tail, start_tail, valid_tail = carry
        hidden_block, start_block, valid_block, first_row = block_inputs
        normed = low(normalize(hidden_block, gain_attn))
        qkv = low_back(low(jnp.einsum('nd,cde->cne', normed, weight_qkv, precision=precise)))
        queries = qkv[0].reshape(block_rows, H, HD)
        keys_block = qkv[1].reshape(block_rows, H, HD)
        values_block = qkv[2].reshape(block_rows, H, HD)
        keys_all = jnp.concatenate([key_tail, keys_block])
        values_all = jnp.concatenate([value_tail, values_block])
        starts_all = jnp.concatenate([start_tail, start_block])
        valid_all = jnp.concatenate([valid_tail, valid_block])
        query_pos = first_row + jnp.arange(block_rows, dtype=jnp.int32)
        key_pos = first_row - BAND + jnp.arange(block_rows + BAND, dtype=jnp.int32)
        gap_rows = query_pos[:, None] - key_pos[None, :]
        allowed = (gap_rows >= 0) & (gap_rows <= BAND) & (start_block[:, None] == starts_all[None, :]) & ((valid_all[None, :] == 1) | (gap_rows == 0))
        scores = low_back(jnp.einsum('qhe,khe->hqk', queries, keys_all, precision=precise) * score_scale)
        band_weights = low(jax.nn.softmax(jnp.where(allowed[None], scores, masked_score), axis=-1))
        near_field = jnp.einsum('hqk,khe->qhe', band_weights, values_all, precision=precise)
        query_one, query_two = kernel_maps(queries)
        key_one, key_two = kernel_maps(keys_block)
        query_one = low(query_one)
        query_two = low(query_two)
        key_one = low(key_one)
        key_two = low(key_two)
        order = jnp.arange(block_rows, dtype=jnp.int32)
        causal = ((order[None, :] <= order[:, None]) & (start_block[None, :] == start_block[:, None]) & (valid_block[None, :] == 1)).astype(jnp.float32)
        carried = (start_block < first_row).astype(jnp.float32)
        attn_one = jnp.einsum('qhd,khd->hqk', query_one, key_one, precision=precise) * causal[None]
        attn_two = jnp.einsum('qhd,khd->hqk', query_two, key_two, precision=precise) * causal[None]
        num_one = carried[:, None, None] * jnp.einsum('qhd,hde->qhe', query_one, state_one, precision=precise) + jnp.einsum('hqk,khe->qhe', attn_one, values_block, precision=precise)
        num_two = carried[:, None, None] * jnp.einsum('qhd,hde->qhe', query_two, state_two, precision=precise) + jnp.einsum('hqk,khe->qhe', attn_two, values_block, precision=precise)
        zeta_sum = carried[:, None] * jnp.einsum('qhd,hd->qh', query_one, key_total, precision=precise) + lax.optimization_barrier(jnp.sum(attn_one, axis=2)).T
        root_norm = jnp.sqrt(zeta_sum + 1.0)[:, :, None]
        mixed = blend_layer[0][None, :, None] * near_field + blend_layer[1][None, :, None] * num_one / (math.sqrt(HD) * root_norm) + blend_layer[2][None, :, None] * num_two / root_norm
        mixed = low_back(low(mixed.reshape(block_rows, H * HD)))
        middle = hidden_block + low_back(jnp.dot(mixed, weight_out, precision=precise))
        normed_ffn = low(normalize(middle, gain_ffn))
        up_proj = low_back(jnp.dot(normed_ffn, weight_up, precision=precise))
        activated = low(jax.nn.gelu(up_proj))
        result = middle + low_back(jnp.dot(activated, weight_down, precision=precise))
        tail_rows = ((start_block == start_block[block_rows - 1]) & (valid_block == 1)).astype(jnp.float32)[:, None, None]
        keep_flag = (start_block[block_rows - 1] < first_row).astype(jnp.float32)
        state_one = keep_flag * state_one + jnp.einsum('khd,khe->hde', key_one * tail_rows, values_block, precision=precise)
        state_two = keep_flag * state_two + jnp.einsum('khd,khe->hde', key_two * tail_rows, values_block, precision=precise)
        key_total = keep_flag * key_total + lax.optimization_barrier(jnp.sum(key_one * tail_rows, axis=0))
        edge_row = block_rows - BAND
        carry = (state_one, state_two, key_total, keys_block[edge_row:], values_block[edge_row:], start_block[edge_row:], valid_block[edge_row:])
        return (carry, result)
    square = jnp.zeros((H, HD, HD), jnp.float32)
    initial = (square, square, jnp.zeros((H, HD), jnp.float32), jnp.zeros((BAND, H, HD), jnp.float32), jnp.zeros((BAND, H, HD), jnp.float32), jnp.full((BAND,), -1, jnp.int32), jnp.zeros((BAND,), jnp.int32))
    block_firsts = jnp.arange(block_count, dtype=jnp.int32) * block_rows
    block_inputs = (hidden.reshape(block_count, block_rows, D), starts.reshape(block_count, block_rows), valid.reshape(block_count, block_rows), block_firsts)
    unused_carry, blocks_out = lax.scan(jax.checkpoint(step), initial, block_inputs)
    return blocks_out.reshape(total_rows, D)

def reference(inputs, lengths, valid, norm_attn, w_qkv, blend, w_out, norm_ffn, w_up, w_down, grad_out):
    positions = jnp.arange(TOKENS, dtype=jnp.int32)
    starts = item_start(lengths, positions)

    def forward(hidden, gains_attn, weights_qkv, blends, weights_out, gains_ffn, weights_up, weights_down):
        for layer_index in range(LAYERS):
            params = (gains_attn[layer_index], weights_qkv[layer_index], blends[layer_index], weights_out[layer_index], gains_ffn[layer_index], weights_up[layer_index], weights_down[layer_index])
            hidden = layer_pass(hidden, starts, valid, params)
        return hidden
    result, pullback = jax.vjp(forward, inputs.astype(jnp.float32), norm_attn, w_qkv.astype(jnp.float32), blend, w_out.astype(jnp.float32), norm_ffn, w_up.astype(jnp.float32), w_down.astype(jnp.float32))
    gradients = pullback(grad_out.astype(jnp.float32))
    return (result.astype(jnp.bfloat16), gradients[0].astype(jnp.bfloat16), gradients[1], gradients[2], gradients[3], gradients[4], gradients[5], gradients[6], gradients[7])
```

```python
import functools
import math

import jax
import jax.numpy as jnp
from jax import lax
from jax.experimental import pallas as pl
from jax.experimental.pallas import tpu as pltpu
from jax.sharding import PartitionSpec as P

HD = 64
D = 512
BAND = 30
LAYERS = 2
HALO = 32
TILE = 64
LANES = 128
STATE = 144
AXES = ("seq", "mlp")

epsilon = 1e-05
masked_score = -1e30
score_scale = 1.0 / math.sqrt(HD)
far_scale = 1.0 / math.sqrt(HD)
f32 = jnp.float32
bf16 = jnp.bfloat16

VM = pl.BlockSpec(memory_space=pltpu.VMEM)
SM = pl.BlockSpec(memory_space=pltpu.SMEM)


def dot(x, y):
    return jnp.dot(x, y, preferred_element_type=f32)


def dot_nt(x, y):
    return lax.dot_general(x, y, (((1,), (1,)), ((), ())), preferred_element_type=f32)


def dot_tn(x, y):
    return lax.dot_general(x, y, (((0,), (0,)), ((), ())), preferred_element_type=f32)


def low_lanes(rows):
    return lax.broadcasted_iota(jnp.int32, (rows, LANES), 1) < HD


def split_heads(x):
    low = low_lanes(x.shape[0])
    zero = jnp.zeros_like(x)
    return jnp.concatenate([jnp.where(low, x, zero), jnp.where(low, zero, x)], axis=0)


def merge_heads(y):
    rows = y.shape[0] // 2
    return jnp.where(low_lanes(rows), y[:rows], y[rows:])


def head_sum(x):
    row = lax.broadcasted_iota(jnp.int32, (LANES, LANES), 0) < HD
    ones = jnp.where(row == low_lanes(LANES), 1.0, 0.0).astype(bf16)
    high = x.astype(bf16)
    rest = (x - high.astype(f32)).astype(bf16)
    return dot(high, ones) + dot(rest, ones)


def kernel_maps(x):
    return (
        jnp.where(x > 0, x + 1.0, jnp.exp(jnp.minimum(x, 0.0))).astype(bf16),
        jnp.tanh(x).astype(bf16),
    )


def maps_back(x, d_one, d_two):
    tanh = jnp.tanh(x)
    return jnp.where(x > 0, 1.0, jnp.exp(jnp.minimum(x, 0.0))) * d_one + (1.0 - tanh * tanh) * d_two


def put_state(ref, quarter, one, two, total):
    row = lax.broadcasted_iota(jnp.int32, (STATE - 2 * HD, LANES), 0)
    low = low_lanes(HD)
    ref[quarter, 0:HD, :] = jnp.where(low, one[:HD], one[HD:]).astype(bf16)
    ref[quarter, HD : 2 * HD, :] = jnp.where(low, two[:HD], two[HD:]).astype(bf16)
    ref[quarter, 2 * HD : STATE, :] = jnp.where(row == 0, total, 0.0).astype(bf16)


def get_state(ref, quarter):
    one = split_heads(ref[quarter, 0:HD, :])
    two = split_heads(ref[quarter, HD : 2 * HD, :])
    total = ref[quarter, 2 * HD : STATE, :].astype(f32)[0:1]
    return one, two, total


def norm_scale(hidden):
    return lax.rsqrt(jnp.sum(hidden * hidden, axis=1, keepdims=True) * (1.0 / D) + epsilon)


def norm_back(hidden, gain, grad):
    scale = norm_scale(hidden)
    gained = grad * gain
    inner = jnp.sum(gained * hidden, axis=1, keepdims=True) * (1.0 / D)
    back = scale * gained - hidden * (scale * scale * scale * inner)
    return back, jnp.sum(grad * hidden * scale, axis=0, keepdims=True)


def extend(halo, rows):
    return jnp.concatenate([halo, rows, jnp.zeros((HALO, LANES), bf16)], axis=0)


def qkv_kernel(first, place, *refs):
    if first:
        inputs, gain, own, other, tail, hidden_out, normed_out, qkv_out, state_out, halo_out = refs
        hidden = inputs[...].astype(f32)
    else:
        base, part_a, part_b, gain, own, other, tail, hidden_out, normed_out, qkv_out, state_out, halo_out = refs
        hidden = base[...] + (part_a[...].astype(f32) + part_b[...].astype(f32))
    hidden_out[...] = hidden
    normed = (hidden * norm_scale(hidden) * gain[...]).astype(bf16)
    normed_out[...] = normed
    rows = hidden.shape[0]
    found = []
    for kind in range(3):
        weight = jnp.concatenate([own[kind], other[kind]], axis=1)
        found.append(dot(normed, weight).astype(bf16))
        qkv_out[kind] = found[kind]
    for pair in range(2):
        quarter = place[0] if pair == 0 else 1 - place[0]
        lanes = slice(pair * LANES, (pair + 1) * LANES)
        keys, values = found[1][:, lanes], found[2][:, lanes]
        one, two = kernel_maps(keys.astype(f32))
        one, two = one * tail[...], two * tail[...]
        put_state(
            state_out,
            quarter,
            dot_tn(one, values),
            dot_tn(two, values),
            jnp.sum(one.astype(f32), axis=0, keepdims=True),
        )
        halo_out[quarter, 0] = keys[rows - HALO :]
        halo_out[quarter, 1] = values[rows - HALO :]


def local_kernel(place, qkv, halo, causal, band, near_out, one_out, two_out, sums_out):
    rows = qkv.shape[1]
    masks = jnp.concatenate([causal[...], causal[...]], axis=0)
    for pair in range(2):
        quarter = place[0] if pair == 0 else 1 - place[0]
        lanes = slice(pair * LANES, (pair + 1) * LANES)
        queries, keys, values = qkv[0, :, lanes], qkv[1, :, lanes], qkv[2, :, lanes]
        maps_q, maps_k = kernel_maps(queries.astype(f32)), kernel_maps(keys.astype(f32))
        for query, key, out in ((maps_q[0], maps_k[0], one_out), (maps_q[1], maps_k[1], two_out)):
            attn = dot_nt(split_heads(query), key).astype(bf16) * masks
            out[:, lanes] = merge_heads(dot(attn, values))
        sums_out[:, lanes] = dot(causal[...], maps_k[0])
        ext_keys = extend(halo[quarter, 0], keys)
        ext_values = extend(halo[quarter, 1], values)
        for tile in range(rows // TILE):
            at = slice(tile * TILE, (tile + 1) * TILE)
            window = slice(tile * TILE, tile * TILE + LANES)
            allowed = jnp.concatenate([band[at], band[at]], axis=0)
            scores = dot_nt(split_heads(queries[at]), ext_keys[window]) * score_scale + allowed
            weights = jnp.exp(scores - jnp.max(scores, axis=1, keepdims=True))
            weights = weights / jnp.sum(weights, axis=1, keepdims=True)
            near_out[at, lanes] = merge_heads(dot(weights.astype(bf16), ext_values[window]))


def mix_kernel(
    place, qkv, near, one, two, sums, carried, state, blend, own, other,
    mixed_out, far_one_out, far_two_out, root_out, prefix_out, part_out,
):
    mixed = []
    for pair in range(2):
        quarter = place[0] if pair == 0 else 1 - place[0]
        lanes = slice(pair * LANES, (pair + 1) * LANES)
        query_one, query_two = kernel_maps(qkv[0, :, lanes].astype(f32))
        state_one, state_two, total = get_state(state, quarter)
        num_one = one[:, lanes] + carried[...] * dot(query_one, state_one)
        num_two = two[:, lanes] + carried[...] * dot(query_two, state_two)
        prefix = sums[:, lanes] + carried[...] * total
        zeta = head_sum(query_one.astype(f32) * prefix)
        root = lax.rsqrt(zeta + 1.0)
        far_one = num_one * root * far_scale
        far_two = num_two * root
        far_one_out[:, lanes] = far_one
        far_two_out[:, lanes] = far_two
        root_out[:, lanes] = root
        prefix_out[:, lanes] = prefix
        mixed.append(
            (
                blend[0:1, lanes] * near[:, lanes]
                + blend[1:2, lanes] * far_one
                + blend[2:3, lanes] * far_two
            ).astype(bf16)
        )
        mixed_out[:, lanes] = mixed[pair]
    weight = jnp.concatenate([own[...], other[...]], axis=0)
    part_out[...] = dot(jnp.concatenate(mixed, axis=1), weight).astype(bf16)


def ffn_kernel(
    base, part_a, part_b, gain, up_own, up_other, down_own, down_other,
    middle_out, normed_out, pre_own_out, pre_other_out, act_own_out, act_other_out, part_out,
):
    middle = base[...] + (part_a[...].astype(f32) + part_b[...].astype(f32))
    middle_out[...] = middle
    normed = (middle * norm_scale(middle) * gain[...]).astype(bf16)
    normed_out[...] = normed
    total = None
    for up, down, pre_out, act_out in (
        (up_own, down_own, pre_own_out, act_own_out),
        (up_other, down_other, pre_other_out, act_other_out),
    ):
        pre = dot(normed, up[...])
        pre_out[...] = pre
        inner = jnp.tanh(math.sqrt(2.0 / math.pi) * (pre + 0.044715 * pre * pre * pre))
        act = (0.5 * pre * (1.0 + inner)).astype(bf16)
        act_out[...] = act
        product = dot(act, down[...])
        total = product if total is None else total + product
    part_out[...] = total.astype(bf16)


def gelu_slope(pre):
    c = math.sqrt(2.0 / math.pi)
    inner = jnp.tanh(c * (pre + 0.044715 * pre * pre * pre))
    return 0.5 * (1.0 + inner) + 0.5 * pre * (1.0 - inner * inner) * (c * (1.0 + 3 * 0.044715 * pre * pre))


def ffn_back_kernel(first, *refs):
    if first:
        grad_in, up_own, up_other, down_own, down_other, pre_own, pre_other = refs[:7]
        resid_out, rows_out, d_up_own_out, d_up_other_out, part_out = refs[7:]
        resid = grad_in[...].astype(f32)
    else:
        (base, part_a, part_b, hidden, gain, up_own, up_other, down_own, down_other, pre_own, pre_other) = refs[:11]
        resid_out, rows_out, d_up_own_out, d_up_other_out, part_out, gain_out = refs[11:]
        back, gain_out[...] = norm_back(
            hidden[...], gain[...], part_a[...].astype(f32) + part_b[...].astype(f32)
        )
        resid = base[...] + back
    resid_out[...] = resid
    rows = resid.astype(bf16)
    rows_out[...] = rows
    total = None
    for up, down, pre, out in (
        (up_own, down_own, pre_own, d_up_own_out),
        (up_other, down_other, pre_other, d_up_other_out),
    ):
        d_up = (gelu_slope(pre[...]) * dot_nt(rows, down[...])).astype(bf16)
        out[...] = d_up
        product = dot_nt(d_up, up[...])
        total = product if total is None else total + product
    part_out[...] = total.astype(bf16)


def mix_back_kernel(
    place, base, part_a, part_b, middle, gain, own, other, qkv, far_one, far_two, root, carried, blend,
    resid_out, rows_out, mixed_out, gain_out, num_one_out, num_two_out, zeta_out, state_out, blend_out,
):
    back, gain_out[...] = norm_back(
        middle[...], gain[...], part_a[...].astype(f32) + part_b[...].astype(f32)
    )
    resid = base[...] + back
    resid_out[...] = resid
    rows = resid.astype(bf16)
    rows_out[...] = rows
    weight = jnp.concatenate([own[...], other[...]], axis=0)
    d_mixed = dot_nt(rows, weight).astype(bf16)
    mixed_out[...] = d_mixed
    for pair in range(2):
        quarter = place[0] if pair == 0 else 1 - place[0]
        lanes = slice(pair * LANES, (pair + 1) * LANES)
        grad = d_mixed[:, lanes].astype(f32)
        scale = root[:, lanes]
        dot_one = grad * far_one[:, lanes]
        dot_two = grad * far_two[:, lanes]
        blend_one, blend_two = blend[1:2, lanes], blend[2:3, lanes]
        blend_out[0:1, lanes] = jnp.sum(dot_one, axis=0, keepdims=True)
        blend_out[1:2, lanes] = jnp.sum(dot_two, axis=0, keepdims=True)
        num_one = (grad * (blend_one * far_scale) * scale).astype(bf16)
        num_two = (grad * blend_two * scale).astype(bf16)
        d_zeta = head_sum(blend_one * dot_one + blend_two * dot_two) * (-0.5 * scale * scale)
        num_one_out[:, lanes] = num_one
        num_two_out[:, lanes] = num_two
        zeta_out[:, lanes] = d_zeta
        query_one, query_two = kernel_maps(qkv[0, :, lanes].astype(f32))
        reach = carried[...].astype(bf16)
        put_state(
            state_out,
            quarter,
            dot_tn(query_one * reach, num_one),
            dot_tn(query_two * reach, num_two),
            jnp.sum(carried[...] * d_zeta * query_one.astype(f32), axis=0, keepdims=True),
        )


def local_back_kernel(
    place, qkv, halo, causal, causal_t, band, carried, state, prefix, d_mixed, num_one, num_two, d_zeta, blend,
    dq_out, dk_one_out, dk_two_out, dk_near_out, dv_out, halo_out, blend_out, near_k, near_v,
):
    rows = qkv.shape[1]
    masks = jnp.concatenate([causal[...], causal[...]], axis=0)
    masks_t = jnp.concatenate([causal_t[...], causal_t[...]], axis=1)
    row_low = lax.broadcasted_iota(jnp.int32, (2 * TILE, 1), 0) < TILE
    for pair in range(2):
        quarter = place[0] if pair == 0 else 1 - place[0]
        lanes = slice(pair * LANES, (pair + 1) * LANES)
        queries, keys, values = qkv[0, :, lanes], qkv[1, :, lanes], qkv[2, :, lanes]
        grads = d_mixed[:, lanes]
        state_one, state_two, unused_total = get_state(state, quarter)
        query_one, query_two = kernel_maps(queries.astype(f32))
        key_one, key_two = kernel_maps(keys.astype(f32))
        d_values = None
        d_queries = []
        for query, key, num, square, out in (
            (query_one, key_one, num_one[:, lanes], state_one, dk_one_out),
            (query_two, key_two, num_two[:, lanes], state_two, dk_two_out),
        ):
            query_split, num_split = split_heads(query), split_heads(num)
            attn_t = dot_nt(key, query_split).astype(bf16) * masks_t
            grad = dot_nt(num_split, values).astype(bf16) * masks
            grad_t = dot_nt(values, num_split).astype(bf16) * masks_t
            product = dot(attn_t, num_split)
            d_values = product if d_values is None else d_values + product
            d_queries.append(merge_heads(dot(grad, key)) + carried[...] * dot_nt(num, square))
            out[:, lanes] = dot(grad_t, query_split)
        zeta = d_zeta[:, lanes]
        d_queries[0] += zeta * prefix[:, lanes]
        dk_one_out[:, lanes] += dot(causal_t[...], (zeta * query_one.astype(f32)).astype(bf16))

        ext_keys = extend(halo[quarter, 0], keys)
        ext_values = extend(halo[quarter, 1], values)
        near_k[...] = jnp.zeros_like(near_k)
        near_v[...] = jnp.zeros_like(near_v)
        blend_low, blend_high = blend[0:1, pair * LANES : pair * LANES + 1], blend[0:1, pair * LANES + HD : pair * LANES + HD + 1]
        blend_rows = jnp.where(row_low, blend_low, blend_high)
        sums = None
        dq_near = []
        for tile in range(rows // TILE):
            at = slice(tile * TILE, (tile + 1) * TILE)
            window = slice(tile * TILE, tile * TILE + LANES)
            allowed = jnp.concatenate([band[at], band[at]], axis=0)
            query_split, grad_split = split_heads(queries[at]), split_heads(grads[at])
            scores = dot_nt(query_split, ext_keys[window]) * score_scale + allowed
            probs = jnp.exp(scores - jnp.max(scores, axis=1, keepdims=True))
            probs = probs / jnp.sum(probs, axis=1, keepdims=True)
            d_probs = dot_nt(grad_split, ext_values[window])
            inner = jnp.sum(probs * d_probs, axis=1, keepdims=True)
            sums = inner if sums is None else sums + inner
            d_scores = (probs * (d_probs - inner) * blend_rows).astype(bf16)
            dq_near.append(merge_heads(dot(d_scores, ext_keys[window])))
            near_k[window] += dot_tn(d_scores, query_split)
            near_v[window] += dot_tn(probs.astype(bf16), grad_split)
        sum_low = jnp.sum(sums[:TILE], axis=0, keepdims=True)
        sum_high = jnp.sum(sums[TILE:], axis=0, keepdims=True)
        blend_out[0:1, lanes] = jnp.where(low_lanes(1), sum_low, sum_high) * (1.0 / HD)
        back = maps_back(queries.astype(f32), d_queries[0], d_queries[1])
        dq_out[:, lanes] = (back + score_scale * jnp.concatenate(dq_near, axis=0)).astype(bf16)
        dk_near_out[:, lanes] = score_scale * near_k[HALO : HALO + rows]
        dv_out[:, lanes] = d_values + blend[0:1, lanes] * near_v[HALO : HALO + rows]
        halo_out[quarter, 0] = (score_scale * near_k[0:HALO]).astype(bf16)
        halo_out[quarter, 1] = (blend[0:1, lanes] * near_v[0:HALO]).astype(bf16)


def qkv_back_kernel(
    place, qkv, dq, dk_one, dk_two, dk_near, dv, tail, state, halo, own, other, d_qkv_out, part_out
):
    rows = qkv.shape[1]
    empty = jnp.zeros((rows - HALO, LANES), f32)
    for pair in range(2):
        quarter = place[0] if pair == 0 else 1 - place[0]
        lanes = slice(pair * LANES, (pair + 1) * LANES)
        keys, values = qkv[1, :, lanes], qkv[2, :, lanes]
        key_one, key_two = kernel_maps(keys.astype(f32))
        state_one, state_two, total = get_state(state, quarter)
        weight = tail[...].astype(f32)
        d_one = dk_one[:, lanes] + weight * (dot_nt(values, state_one) + total)
        d_two = dk_two[:, lanes] + weight * dot_nt(values, state_two)
        halo_k = jnp.concatenate([empty, halo[quarter, 0].astype(f32)], axis=0)
        halo_v = jnp.concatenate([empty, halo[quarter, 1].astype(f32)], axis=0)
        d_qkv_out[1, :, lanes] = (
            maps_back(keys.astype(f32), d_one, d_two) + dk_near[:, lanes] + halo_k
        ).astype(bf16)
        d_qkv_out[2, :, lanes] = (
            dv[:, lanes] + weight * (dot(key_one, state_one) + dot(key_two, state_two)) + halo_v
        ).astype(bf16)
    d_qkv_out[0] = dq[...]
    total = None
    for kind in range(3):
        weight = jnp.concatenate([own[kind], other[kind]], axis=1)
        product = dot_nt(d_qkv_out[kind], weight)
        total = product if total is None else total + product
    part_out[...] = total.astype(bf16)


def end_kernel(base, part_a, part_b, hidden, gain, out, gain_out):
    back, gain_out[...] = norm_back(
        hidden[...], gain[...], part_a[...].astype(f32) + part_b[...].astype(f32)
    )
    out[...] = (base[...] + back).astype(bf16)


def call(body, outs, operands, scalars=0, scratch=(), flops=0):
    return pl.pallas_call(
        body,
        out_shape=tuple(jax.ShapeDtypeStruct(shape, kind) for shape, kind in outs),
        in_specs=[SM] * scalars + [VM] * (len(operands) - scalars),
        out_specs=tuple(VM for _ in outs),
        scratch_shapes=scratch,
        compiler_params=pltpu.CompilerParams(vmem_limit_bytes=24 * 2**20),
    )(*operands)


def core_swap(value):
    count = lax.axis_size("mlp")
    return lax.ppermute(value, "mlp", [(i, i ^ 1) for i in range(count)])


def far_swap(value):
    count = lax.axis_size("mlp")
    return lax.ppermute(value, "mlp", [(i, i ^ 2) for i in range(count)])


def chunk_move(value, target):
    shards, parts = lax.axis_size("seq"), lax.axis_size("mlp")
    pairs = []
    for chunk in range(2 * shards):
        goal = target(chunk)
        if goal is None or not 0 <= goal < 2 * shards:
            continue
        for core in range(2):
            pairs.append(
                ((chunk // 2) * parts + (chunk % 2) * 2 + core, (goal // 2) * parts + (goal % 2) * 2 + core)
            )
    return lax.ppermute(value, AXES, pairs)


def item_start(lengths, positions):
    count = lengths.shape[0]
    order = jnp.arange(count)
    ends = jnp.sum(jnp.where(order[None, :] <= order[:, None], lengths[None, :], 0), axis=1)
    picked = jnp.where(ends[None, :] <= positions[:, None], lengths[None, :], 0)
    return jnp.sum(picked, axis=1)


def scan_plan(chunks):
    stages, size = [], 1
    while size < chunks:
        ways = min(4, chunks // size)
        stages.append((size, ways, size * ways >= chunks))
        size *= ways
    return stages


def scan_weights(lengths, chunk, chunks, rows, reverse):
    def inner(index):
        return index * rows + (0 if reverse else rows - 1)

    first, second = [], []
    for size, ways, last in scan_plan(chunks):
        member = (chunk // size) % ways
        base = chunk - member * size - chunk % size
        end = base + (0 if reverse else ways * size - 1)
        for step in range(ways):
            if last:
                other = member + step if reverse else member - step
            else:
                other = member ^ step
            block = base + other * size + (0 if reverse else size - 1)
            before = (other > member) if reverse else (other < member)
            before = before & (other >= 0) & (other < ways)
            edge = chunk * rows + (rows - 1 if reverse else 0)
            first.append((jnp.where(before, inner(block), -1), edge, before))
            second.append((inner(block), inner(end), jnp.bool_(True)))
    wanted = first + second
    left = item_start(lengths, jnp.stack([jnp.int32(w[0]) for w in wanted]))
    right = item_start(lengths, jnp.stack([jnp.int32(w[1]) for w in wanted]))
    flags = (left == right) & jnp.stack([w[2] for w in wanted])
    flags = flags.astype(f32)
    return flags[: len(first)], flags[len(first) :]


def scan(value, weights, chunks, reverse):
    to_mine, to_total = weights
    found, at = 0.0, 0
    for size, ways, last in scan_plan(chunks):
        got = [value]
        for step in range(1, ways):
            if last:

                def target(chunk, step=step):
                    member = (chunk // size) % ways + (-step if reverse else step)
                    return chunk + (-step if reverse else step) * size if 0 <= member < ways else None

            else:

                def target(chunk, step=step):
                    member = (chunk // size) % ways
                    return chunk + ((member ^ step) - member) * size

            got.append(chunk_move(value, target))
        for step in range(1, ways):
            found = found + to_mine[at + step] * got[step].astype(f32)
        if not last:
            value = sum(to_total[at + step] * got[step].astype(f32) for step in range(ways)).astype(bf16)
        at += ways
    return found.astype(bf16)


def three_parts(value):
    high = value.astype(bf16)
    rest = value - high.astype(f32)
    middle = rest.astype(bf16)
    return jnp.concatenate([high, middle, (rest - middle.astype(f32)).astype(bf16)], axis=0)


def by_place(flag, mine, other):
    return jnp.where(flag == 0, mine, other), jnp.where(flag == 0, other, mine)


def take_rows(value, half, core, more):
    rows = value.shape[0] // 2
    mine = lax.dynamic_slice_in_dim(value, half * rows, rows, 0)
    theirs = lax.dynamic_slice_in_dim(value, (1 - half) * rows, rows, 0)
    if more is not None:
        mine, theirs = jnp.concatenate([mine, more]), jnp.concatenate([theirs, more])
    got = far_swap(theirs)
    pair = jnp.stack(by_place(half, mine, got))
    even, odd = by_place(core, pair, core_swap(pair))
    whole = jnp.concatenate([even[0], odd[0], even[1], odd[1]], axis=1)
    return whole[:rows], whole[rows:], got[rows:]


def give_rows(whole, half, core):
    mine = lax.dynamic_slice_in_dim(whole, (2 * half + core) * LANES, LANES, 1)
    theirs = lax.dynamic_slice_in_dim(whole, (2 * (1 - half) + core) * LANES, LANES, 1)
    return jnp.concatenate(by_place(half, mine, far_swap(theirs)))


def per_device(inputs, lengths, valid, norm_attn, w_qkv, blend, w_out, norm_ffn, w_up, w_down, grad_out):
    shards, parts = lax.axis_size("seq"), lax.axis_size("mlp")
    shard, part = lax.axis_index("seq"), lax.axis_index("mlp")
    half, core = part // 2, part % 2
    rows = inputs.shape[0] // 2
    chunks = 2 * shards
    chunk = shard * 2 + half
    first_row = chunk * rows
    width = inputs.shape[1]
    place = jnp.reshape(half, (1,)).astype(jnp.int32)

    blend_lanes = jnp.repeat(blend, HD, axis=2).reshape(LAYERS * 3, width)
    small = jnp.concatenate([norm_attn, norm_ffn, blend_lanes], axis=0)
    small = jnp.concatenate([small, jnp.zeros((16 - small.shape[0], width), f32)], axis=0)
    whole, gains, far_small = take_rows(inputs, half, core, three_parts(small))

    def joined(value):
        count = value.shape[0] // 3
        value = value.astype(f32)
        return value[:count] + value[count : 2 * count] + value[2 * count :]

    gains, far_small = joined(gains), joined(far_small)
    others = []
    for layer in range(LAYERS):
        others.append(tuple(far_swap(w[layer]) for w in (w_qkv, w_out, w_up, w_down)))
    grad_whole, unused_a, unused_b = take_rows(grad_out, half, core, None)
    gain_attn = [gains[layer : layer + 1] for layer in range(LAYERS)]
    gain_ffn = [gains[LAYERS + layer : LAYERS + layer + 1] for layer in range(LAYERS)]
    blends = [
        jnp.concatenate(
            [blend_lanes[3 * layer : 3 * layer + 3], far_small[2 * LAYERS + 3 * layer : 2 * LAYERS + 3 * layer + 3]],
            axis=1,
        )
        for layer in range(LAYERS)
    ]

    halo_words = lax.ppermute(
        valid[2 * rows - HALO :], "seq", [(source, source + 1) for source in range(shards - 1)]
    )
    halo_words = jnp.where(half == 0, halo_words, valid[rows - HALO : rows])
    own_words = lax.dynamic_slice_in_dim(valid, half * rows, rows, 0)
    starts = item_start(lengths, first_row + jnp.arange(rows, dtype=jnp.int32))
    halo_starts = item_start(lengths, first_row - HALO + jnp.arange(HALO, dtype=jnp.int32))
    ext_starts = jnp.concatenate([halo_starts, starts, jnp.full((HALO,), -1, jnp.int32)])
    ext_valid = jnp.concatenate([halo_words, own_words, jnp.zeros((HALO,), jnp.int32)])
    order = jnp.arange(rows, dtype=jnp.int32)
    same = starts[:, None] == starts[None, :]
    causal = ((order[None, :] <= order[:, None]) & same & (own_words[None, :] == 1)).astype(bf16)
    causal_t = ((order[:, None] <= order[None, :]) & same & (own_words[:, None] == 1)).astype(bf16)
    tiles = rows // TILE
    window_starts = jnp.stack([ext_starts[t * TILE : t * TILE + LANES] for t in range(tiles)])
    window_valid = jnp.stack([ext_valid[t * TILE : t * TILE + LANES] for t in range(tiles)])
    gap = jnp.arange(TILE)[:, None] + HALO - jnp.arange(LANES)[None, :]
    allowed = (
        ((gap >= 0) & (gap <= BAND))[None]
        & (starts.reshape(tiles, TILE, 1) == window_starts[:, None, :])
        & ((window_valid[:, None, :] == 1) | (gap == 0)[None])
    )
    band = jnp.where(allowed, 0.0, masked_score).astype(f32).reshape(rows, LANES)
    carried = jnp.broadcast_to((starts < first_row).astype(f32)[:, None], (rows, LANES))
    tail = jnp.broadcast_to(
        ((starts == starts[rows - 1]) & (own_words == 1)).astype(bf16)[:, None], (rows, LANES)
    )
    ahead = scan_weights(lengths, chunk, chunks, rows, False)
    behind = scan_weights(lengths, chunk, chunks, rows, True)

    wide = 2 * LANES
    hidden_like = ((rows, D), f32)
    low_like = ((rows, D), bf16)
    heads_like = ((rows, wide), f32)
    heads_low = ((rows, wide), bf16)
    qkv_like = ((3, rows, wide), bf16)
    state_like = ((2, STATE, LANES), bf16)
    halo_like = ((2, 2, HALO, LANES), bf16)
    units = w_up.shape[2]
    ffn_like = ((rows, units), f32)
    ffn_low = ((rows, units), bf16)

    saved = []
    base, pieces = whole, ()
    for layer in range(LAYERS):
        far_qkv, far_out, far_up, far_down = others[layer]
        hidden, normed, qkv, state, halo = call(
            functools.partial(qkv_kernel, layer == 0),
            (hidden_like, low_like, qkv_like, state_like, halo_like),
            (place, base, *pieces, gain_attn[layer], w_qkv[layer], far_qkv, tail),
            1,
        )
        halo = chunk_move(halo, lambda c: c + 1)
        near, one, two, sums = call(
            local_kernel, (heads_like,) * 4, (place, qkv, halo, causal, band), 1
        )
        state = scan(state, ahead, chunks, False)
        mixed, far_one, far_two, root, prefix, piece = call(
            mix_kernel,
            (heads_low, heads_like, heads_like, heads_like, heads_like, low_like),
            (place, qkv, near, one, two, sums, carried, state, blends[layer], w_out[layer], far_out),
            1,
        )
        middle, normed_ffn, pre_own, pre_far, act_own, act_far, piece_ffn = call(
            ffn_kernel,
            (hidden_like, low_like, ffn_like, ffn_like, ffn_low, ffn_low, low_like),
            (hidden, piece, core_swap(piece), gain_ffn[layer], w_up[layer], far_up, w_down[layer], far_down),
        )
        saved.append(
            (hidden, normed, qkv, state, halo, mixed, far_one, far_two, root, prefix, middle, normed_ffn,
             pre_own, pre_far, act_own, act_far)
        )
        base, pieces = middle, (piece_ffn, core_swap(piece_ffn))
    result = (base + (pieces[0].astype(f32) + pieces[1].astype(f32))).astype(bf16)
    output = give_rows(result, half, core)

    def weight_grads(left, rights):
        return [
            lax.dot_general(left, right, (((0,), (0,)), ((), ())), preferred_element_type=f32)
            for right in rights
        ]

    def over_chips(own, other):
        got = far_swap(other.astype(bf16))
        return (own + got.astype(f32)).astype(bf16)

    base, pieces = None, None
    d_gain_attn, d_gain_ffn, d_blends = [None] * LAYERS, [None] * LAYERS, [None] * LAYERS
    grads = [None] * LAYERS
    for layer in reversed(range(LAYERS)):
        far_qkv, far_out, far_up, far_down = others[layer]
        (hidden, normed, qkv, state, halo, mixed, far_one, far_two, root, prefix, middle, normed_ffn,
         pre_own, pre_far, act_own, act_far) = saved[layer]
        weights = (w_up[layer], far_up, w_down[layer], far_down, pre_own, pre_far)
        outs = (hidden_like, low_like, ffn_low, ffn_low, low_like)
        if base is None:
            resid, grad_rows, d_up_own, d_up_far, piece = call(
                functools.partial(ffn_back_kernel, True), outs, (grad_whole, *weights)
            )
        else:
            resid, grad_rows, d_up_own, d_up_far, piece, d_gain_attn[layer + 1] = call(
                functools.partial(ffn_back_kernel, False),
                outs + (((1, D), f32),),
                (base, *pieces, saved[layer + 1][0], gain_attn[layer + 1], *weights),
            )
        swapped = core_swap(piece)
        d_down_own, d_down_far = [weight_grads(x, [grad_rows])[0] for x in (act_own, act_far)]
        d_up_own_w, d_up_far_w = weight_grads(normed_ffn, [d_up_own, d_up_far])
        (resid, grad_rows, d_mixed, d_gain_ffn[layer], num_one, num_two, d_zeta, state_back, blend_far) = call(
            mix_back_kernel,
            (hidden_like, low_like, heads_low, ((1, D), f32), heads_low, heads_low, heads_like, state_like,
             ((2, wide), f32)),
            (place, resid, piece, swapped, middle, gain_ffn[layer], w_out[layer], far_out, qkv, far_one, far_two,
             root, carried, blends[layer]),
            1,
        )
        d_out_own, d_out_far = [
            weight_grads(x, [grad_rows])[0] for x in (mixed[:, :LANES], mixed[:, LANES:])
        ]
        ext = HALO + rows + HALO
        dq, dk_one, dk_two, dk_near, dv, halo_back, blend_near = call(
            local_back_kernel,
            (heads_low, heads_like, heads_like, heads_like, heads_like, halo_like, ((1, wide), f32)),
            (place, qkv, halo, causal, causal_t, band, carried, state, prefix, d_mixed, num_one, num_two, d_zeta,
             blends[layer]),
            1,
            scratch=(pltpu.VMEM((ext, LANES), f32), pltpu.VMEM((ext, LANES), f32)),
        )
        state_back = scan(state_back, behind, chunks, True)
        halo_back = chunk_move(halo_back, lambda c: c - 1)
        d_qkv, piece = call(
            qkv_back_kernel,
            (qkv_like, low_like),
            (place, qkv, dq, dk_one, dk_two, dk_near, dv, tail, state_back, halo_back, w_qkv[layer], far_qkv),
            1,
        )
        base, pieces = resid, (piece, core_swap(piece))
        d_qkv_w = lax.dot_general(normed, d_qkv, (((0,), (1,)), ((), ())), preferred_element_type=f32)
        d_qkv_w = jnp.transpose(d_qkv_w, (1, 0, 2))
        d_blends[layer] = jnp.concatenate([blend_near, blend_far], axis=0)
        ready = [over_chips(d_up_own_w, d_up_far_w), over_chips(d_down_own, d_down_far), over_chips(d_out_own, d_out_far)]
        if layer > 0:
            ready.append(over_chips(d_qkv_w[:, :, :LANES], d_qkv_w[:, :, LANES:]))
        grads[layer] = lax.psum(tuple(ready), "seq")
    d_inputs, d_gain_attn[0] = call(
        end_kernel, (low_like, ((1, D), f32)), (base, *pieces, saved[0][0], gain_attn[0])
    )
    d_inputs = give_rows(d_inputs, half, core)

    gains_back = jnp.concatenate(d_gain_attn + d_gain_ffn, axis=0)
    blends_back = jnp.concatenate(d_blends, axis=0)
    blends_back = by_place(half, blends_back[:, :LANES], blends_back[:, LANES:])
    count = 2 * LAYERS + 3 * LAYERS
    extra = []
    for to in range(2):
        features = lax.dynamic_slice_in_dim(gains_back, (2 * to + core) * LANES, LANES, 1)
        extra.append(
            jnp.concatenate([features, blends_back[to], jnp.zeros((16 - count, LANES), f32)], axis=0)
        )
    flat = by_place(
        half,
        d_qkv_w[:, :, :LANES].reshape(shards, -1, LANES),
        d_qkv_w[:, :, LANES:].reshape(shards, -1, LANES),
    )
    block = flat[0].shape[1]
    send = jnp.stack(
        [
            jnp.concatenate([flat[to], jnp.broadcast_to(extra[to][None], (shards, 16, LANES))], axis=1)
            for to in range(2)
        ],
        axis=1,
    ).astype(bf16)
    groups = [
        [s * parts + h * 2 + c for s in range(shards) for h in range(2)] for c in range(2)
    ]
    got = lax.all_to_all(
        send.reshape(2 * shards, block + 16, LANES), AXES, 0, 0, axis_index_groups=groups, tiled=True
    )
    got = jnp.sum(got.astype(f32), axis=0)
    mine = jnp.broadcast_to(got[:block].astype(bf16)[None], (shards, block, LANES))
    qkv_last = lax.all_to_all(mine, "seq", 0, 0, tiled=True).reshape(3, D, LANES)
    rest = got[block:]

    d_norm_attn = rest[:LAYERS]
    d_norm_ffn = rest[LAYERS : 2 * LAYERS]
    d_blend = jnp.sum(rest[2 * LAYERS : count].reshape(LAYERS, 3, 2, HD), axis=3)
    up, down, out, qkv = [
        jnp.stack(pair).astype(f32)
        for pair in (
            (grads[0][0], grads[1][0]),
            (grads[0][1], grads[1][1]),
            (grads[0][2], grads[1][2]),
            (qkv_last, grads[1][3]),
        )
    ]
    return (output, d_inputs, d_norm_attn, qkv, d_blend, out, d_norm_ffn, up, down)


def solution(mesh):
    placed = (
        P("seq", "mlp"),
        P(),
        P("seq"),
        P(None, "mlp"),
        P(None, None, None, "mlp"),
        P(None, None, "mlp"),
        P(None, "mlp", None),
        P(None, "mlp"),
        P(None, None, "mlp"),
        P(None, "mlp", None),
        P("seq", "mlp"),
    )
    return jax.shard_map(
        per_device,
        mesh=mesh,
        in_specs=placed,
        out_specs=(
            P("seq", "mlp"),
            P("seq", "mlp"),
            P(None, "mlp"),
            P(None, None, None, "mlp"),
            P(None, None, "mlp"),
            P(None, "mlp", None),
            P(None, "mlp"),
            P(None, None, "mlp"),
            P(None, "mlp", None),
        ),
        check_vma=False,
    )
```

```python
import functools
import math

import jax
import jax.numpy as jnp
from jax import lax
from jax.experimental import pallas as pl
from jax.experimental.pallas import tpu as pltpu
from jax.sharding import PartitionSpec as P

HD = 64
D = 512
BAND = 30
LAYERS = 2
HALO = 32
TILE = 64
LANES = 128
STATE = 144
SMALL = 16
AXES = ("seq", "mlp")

epsilon = 1e-05
masked_score = -1e30
score_scale = 1.0 / math.sqrt(HD)
far_scale = 1.0 / math.sqrt(HD)
f32 = jnp.float32
bf16 = jnp.bfloat16

VM = pl.BlockSpec(memory_space=pltpu.VMEM)
SM = pl.BlockSpec(memory_space=pltpu.SMEM)


def dot(x, y):
    return jnp.dot(x, y, preferred_element_type=f32)


def dot_nt(x, y):
    return lax.dot_general(x, y, (((1,), (1,)), ((), ())), preferred_element_type=f32)


def dot_tn(x, y):
    return lax.dot_general(x, y, (((0,), (0,)), ((), ())), preferred_element_type=f32)


def low_lanes(rows):
    return lax.broadcasted_iota(jnp.int32, (rows, LANES), 1) < HD


def split_heads(x):
    low = low_lanes(x.shape[0])
    zero = jnp.zeros_like(x)
    return jnp.concatenate([jnp.where(low, x, zero), jnp.where(low, zero, x)], axis=0)


def merge_heads(y):
    rows = y.shape[0] // 2
    return jnp.where(low_lanes(rows), y[:rows], y[rows:])


def head_sum(x):
    row = lax.broadcasted_iota(jnp.int32, (LANES, LANES), 0) < HD
    ones = jnp.where(row == low_lanes(LANES), 1.0, 0.0).astype(bf16)
    high = x.astype(bf16)
    rest = (x - high.astype(f32)).astype(bf16)
    return dot(high, ones) + dot(rest, ones)


def kernel_maps(x):
    return (
        jnp.where(x > 0, x + 1.0, jnp.exp(jnp.minimum(x, 0.0))).astype(bf16),
        jnp.tanh(x).astype(bf16),
    )


def maps_back(x, d_one, d_two):
    tanh = jnp.tanh(x)
    return jnp.where(x > 0, 1.0, jnp.exp(jnp.minimum(x, 0.0))) * d_one + (1.0 - tanh * tanh) * d_two


def put_state(ref, quarter, one, two, total):
    row = lax.broadcasted_iota(jnp.int32, (STATE - 2 * HD, LANES), 0)
    low = low_lanes(HD)
    ref[quarter, 0:HD, :] = jnp.where(low, one[:HD], one[HD:]).astype(bf16)
    ref[quarter, HD : 2 * HD, :] = jnp.where(low, two[:HD], two[HD:]).astype(bf16)
    ref[quarter, 2 * HD : STATE, :] = jnp.where(row == 0, total, 0.0).astype(bf16)


def get_state(ref, quarter):
    one = split_heads(ref[quarter, 0:HD, :])
    two = split_heads(ref[quarter, HD : 2 * HD, :])
    total = ref[quarter, 2 * HD : STATE, :].astype(f32)[0:1]
    return one, two, total


def norm_scale(hidden):
    return lax.rsqrt(jnp.sum(hidden * hidden, axis=1, keepdims=True) * (1.0 / D) + epsilon)


def norm_back(hidden, gain, grad):
    scale = norm_scale(hidden)
    gained = grad * gain
    inner = jnp.sum(gained * hidden, axis=1, keepdims=True) * (1.0 / D)
    back = scale * gained - hidden * (scale * scale * scale * inner)
    return back, jnp.sum(grad * hidden * scale, axis=0, keepdims=True)


def extend(halo, rows):
    return jnp.concatenate([halo, rows, jnp.zeros((HALO, LANES), bf16)], axis=0)


def three_parts(value):
    high = value.astype(bf16)
    rest = value - high.astype(f32)
    middle = rest.astype(bf16)
    low = (rest - middle.astype(f32)).astype(bf16)
    return jnp.concatenate([high, middle, low], axis=0)


def pack_kernel(place, blend, inputs, norm_attn, norm_ffn, mine_out, theirs_out):
    rows = inputs.shape[0] // 2
    low = low_lanes(1)
    small = [norm_attn[...], norm_ffn[...]]
    for layer in range(LAYERS):
        for kind in range(3):
            small.append(jnp.where(low, blend[layer, kind, 0], blend[layer, kind, 1]))
    small.append(jnp.zeros((SMALL - 5 * LAYERS, LANES), f32))
    small = three_parts(jnp.concatenate(small, axis=0))
    first, second = inputs[:rows], inputs[rows:]
    mine_out[:rows] = jnp.where(place[0] == 0, first, second)
    theirs_out[:rows] = jnp.where(place[0] == 0, second, first)
    mine_out[rows:] = small
    theirs_out[rows:] = small


def pack_grad_kernel(place, grads, mine_out, theirs_out):
    rows = grads.shape[0] // 2
    first, second = grads[:rows], grads[rows:]
    mine_out[...] = jnp.where(place[0] == 0, first, second)
    theirs_out[...] = jnp.where(place[0] == 0, second, first)


def quarters(place):
    half, core = place[0], place[1]
    return 2 * half + core, 2 * (1 - half) + core, 2 * half + 1 - core, 2 * (1 - half) + 1 - core


def quarter_lanes(quarter):
    return pl.ds(pl.multiple_of(quarter * LANES, LANES), LANES)


def item_ends(lengths):
    ends = []
    for k in range(lengths.shape[0]):
        ends.append(lengths[k] if k == 0 else ends[-1] + lengths[k])
    return ends


def item_start(lengths, ends, positions):
    start = jnp.zeros_like(positions)
    for k, end in enumerate(ends):
        start = start + jnp.where(end <= positions, lengths[k], 0)
    return start


def scan_plan(chunks):
    stages, size = [], 1
    while size < chunks:
        ways = min(4, chunks // size)
        stages.append((size, ways, size * ways >= chunks))
        size *= ways
    return stages


def flag_places(chunks):
    at, places = 0, {}
    for reverse in (False, True):
        for stage, (_, ways, _) in enumerate(scan_plan(chunks)):
            places[reverse, stage] = at
            at += 2 * ways
    return places, at


def setup_kernel(chunks, place, lengths, valid, before, causal_out, causal_t_out, band_out, carried_out, tail_out, flags_out):
    rows = causal_out.shape[0]
    chunk = place[2] * 2 + place[0]
    first_row = chunk * rows
    ends = item_ends(lengths)

    def start_of(positions):
        return item_start(lengths, ends, positions)

    lane = lax.broadcasted_iota(jnp.int32, (1, rows), 1)
    starts_row = start_of(first_row + lane)
    starts = start_of(first_row + lax.broadcasted_iota(jnp.int32, (rows, LANES), 0))
    both = jnp.concatenate([starts, starts], axis=1)
    words = valid[...]
    own_words = jnp.where(place[0] == 0, words[:, :rows], words[:, rows:])
    last_words = jnp.where(place[0] == 0, before[...], words[:, rows - LANES : rows])
    row_at = lax.broadcasted_iota(jnp.int32, (rows, rows), 0)
    lane_at = lax.broadcasted_iota(jnp.int32, (rows, rows), 1)
    own_column = jnp.sum(jnp.where(row_at == lane_at, own_words, 0), axis=1, keepdims=True)
    same = both == starts_row
    causal_out[...] = jnp.where((lane_at <= row_at) & same & (own_words == 1), 1.0, 0.0).astype(bf16)
    causal_t_out[...] = jnp.where((row_at <= lane_at) & same & (own_column == 1), 1.0, 0.0).astype(bf16)
    carried_out[...] = jnp.where(starts < first_row, 1.0, 0.0)
    last_start = start_of(first_row + rows - 1)
    tail_out[...] = jnp.where((starts == last_start) & (own_column == 1), 1.0, 0.0).astype(bf16)
    all_words = jnp.concatenate([last_words, own_words, jnp.zeros((1, LANES), jnp.int32)], axis=1)
    tile_row = lax.broadcasted_iota(jnp.int32, (TILE, LANES), 0)
    tile_lane = lax.broadcasted_iota(jnp.int32, (TILE, LANES), 1)
    gap = tile_row + HALO - tile_lane
    for tile in range(rows // TILE):
        key_starts = start_of(first_row + tile * TILE - HALO + lax.broadcasted_iota(jnp.int32, (1, LANES), 1))
        offset = LANES - HALO + tile * TILE
        key_words = all_words[:, offset : offset + LANES]
        at = slice(tile * TILE, (tile + 1) * TILE)
        allowed = (gap >= 0) & (gap <= BAND) & (starts[at] == key_starts) & ((key_words == 1) | (gap == 0))
        band_out[at] = jnp.where(allowed, 0.0, masked_score)

    places, _ = flag_places(chunks)
    for reverse in (False, True):
        edge = start_of(first_row + (rows - 1 if reverse else 0))
        for stage, (size, ways, last) in enumerate(scan_plan(chunks)):
            member = lax.rem(lax.div(chunk, size), ways)
            base = chunk - member * size - lax.rem(chunk, size)
            group = base if reverse else base + ways * size - 1
            group = start_of(group * rows + (0 if reverse else rows - 1))
            for step in range(ways):
                if last:
                    other = member + step if reverse else member - step
                else:
                    other = jnp.bitwise_xor(member, step)
                block = base + other * size + (0 if reverse else size - 1)
                start = start_of(block * rows + (0 if reverse else rows - 1))
                ahead = (other > member) if reverse else (other < member)
                ahead = ahead & (other >= 0) & (other < ways)
                at = places[reverse, stage] + 2 * step
                flags_out[at] = jnp.where(ahead & (start == edge), 1.0, 0.0)
                flags_out[at + 1] = jnp.where(start == group, 1.0, 0.0)


def combine_kernel(at, ways, has_found, flags, *refs):
    got, refs = refs[:ways], refs[ways:]
    total = sum(flags[at + 2 * step + 1] * got[step][...].astype(f32) for step in range(ways))
    refs[-2][...] = total.astype(bf16)
    found = sum(flags[at + 2 * step] * got[step][...].astype(f32) for step in range(1, ways))
    refs[-1][...] = found + refs[0][...] if has_found else found


def last_combine(at, flags, found, got, out):
    value = found[...]
    for step, part in enumerate(got):
        value = value + flags[at + 2 * (step + 1)] * part[...].astype(f32)
    out[...] = value.astype(bf16)


def qkv_kernel(first, layer, place, *refs):
    if first:
        refs, outs = refs[:7], refs[7:]
        pieces, (own, other, tail) = refs[:4], refs[4:]
        hidden_out, normed_out, qkv_out, state_out, halo_out, gains, blends_out = outs
        rows = hidden_out.shape[0]
        for index, (piece, quarter) in enumerate(zip(pieces, quarters(place))):
            hidden_out[:, quarter_lanes(quarter)] = piece[:rows].astype(f32)
            parts = piece[rows:].astype(f32)
            small = parts[:SMALL] + parts[SMALL : 2 * SMALL] + parts[2 * SMALL :]
            gains[:, quarter_lanes(quarter)] = small
            if index < 2:
                blends_out[:, index * LANES : (index + 1) * LANES] = small
        hidden = hidden_out[...]
    else:
        base, part_a, part_b, gains, own, other, tail, hidden_out, normed_out, qkv_out, state_out, halo_out = refs
        hidden = base[...] + (part_a[...].astype(f32) + part_b[...].astype(f32))
        hidden_out[...] = hidden
    rows = hidden.shape[0]
    normed = (hidden * norm_scale(hidden) * gains[layer : layer + 1]).astype(bf16)
    normed_out[...] = normed
    found = []
    for kind in range(3):
        weight = jnp.concatenate([own[layer, kind], other[kind]], axis=1)
        found.append(dot(normed, weight).astype(bf16))
        qkv_out[kind] = found[kind]
    for pair in range(2):
        quarter = place[0] if pair == 0 else 1 - place[0]
        lanes = slice(pair * LANES, (pair + 1) * LANES)
        keys, values = found[1][:, lanes], found[2][:, lanes]
        one, two = kernel_maps(keys.astype(f32))
        one, two = one * tail[...], two * tail[...]
        put_state(
            state_out,
            quarter,
            dot_tn(one, values),
            dot_tn(two, values),
            jnp.sum(one.astype(f32), axis=0, keepdims=True),
        )
        halo_out[quarter, 0] = keys[rows - HALO :]
        halo_out[quarter, 1] = values[rows - HALO :]


def local_kernel(place, qkv, halo, causal, band, near_out, one_out, two_out, sums_out):
    rows = qkv.shape[1]
    masks = jnp.concatenate([causal[...], causal[...]], axis=0)
    for pair in range(2):
        quarter = place[0] if pair == 0 else 1 - place[0]
        lanes = slice(pair * LANES, (pair + 1) * LANES)
        queries, keys, values = qkv[0, :, lanes], qkv[1, :, lanes], qkv[2, :, lanes]
        maps_q, maps_k = kernel_maps(queries.astype(f32)), kernel_maps(keys.astype(f32))
        for query, key, out in ((maps_q[0], maps_k[0], one_out), (maps_q[1], maps_k[1], two_out)):
            attn = dot_nt(split_heads(query), key).astype(bf16) * masks
            out[:, lanes] = merge_heads(dot(attn, values))
        sums_out[:, lanes] = dot(causal[...], maps_k[0])
        ext_keys = extend(halo[quarter, 0], keys)
        ext_values = extend(halo[quarter, 1], values)
        for tile in range(rows // TILE):
            at = slice(tile * TILE, (tile + 1) * TILE)
            window = slice(tile * TILE, tile * TILE + LANES)
            allowed = jnp.concatenate([band[at], band[at]], axis=0)
            scores = dot_nt(split_heads(queries[at]), ext_keys[window]) * score_scale + allowed
            weights = jnp.exp(scores - jnp.max(scores, axis=1, keepdims=True))
            weights = weights / jnp.sum(weights, axis=1, keepdims=True)
            near_out[at, lanes] = merge_heads(dot(weights.astype(bf16), ext_values[window]))


def mix_kernel(layer, at, count, place, flags, qkv, near, one, two, sums, carried, blends, own, other, found, *refs):
    got = refs[:count]
    mixed_out, far_one_out, far_two_out, root_out, prefix_out, state, part_out = refs[count:]
    last_combine(at, flags, found, got, state)
    mixed = []
    row = 2 * LAYERS + 3 * layer
    for pair in range(2):
        quarter = place[0] if pair == 0 else 1 - place[0]
        lanes = slice(pair * LANES, (pair + 1) * LANES)
        query_one, query_two = kernel_maps(qkv[0, :, lanes].astype(f32))
        state_one, state_two, total = get_state(state, quarter)
        num_one = one[:, lanes] + carried[...] * dot(query_one, state_one)
        num_two = two[:, lanes] + carried[...] * dot(query_two, state_two)
        prefix = sums[:, lanes] + carried[...] * total
        zeta = head_sum(query_one.astype(f32) * prefix)
        root = lax.rsqrt(zeta + 1.0)
        far_one = num_one * root * far_scale
        far_two = num_two * root
        far_one_out[:, lanes] = far_one
        far_two_out[:, lanes] = far_two
        root_out[:, lanes] = root
        prefix_out[:, lanes] = prefix
        mixed.append(
            (
                blends[row : row + 1, lanes] * near[:, lanes]
                + blends[row + 1 : row + 2, lanes] * far_one
                + blends[row + 2 : row + 3, lanes] * far_two
            ).astype(bf16)
        )
        mixed_out[:, lanes] = mixed[pair]
    weight = jnp.concatenate([own[layer], other[...]], axis=0)
    part_out[...] = dot(jnp.concatenate(mixed, axis=1), weight).astype(bf16)


def ffn_kernel(
    layer, base, part_a, part_b, gains, up_own, down_own, up_a, down_a, up_b, down_b,
    middle_out, normed_out, pre_own_out, pre_far_out, act_own_out, act_far_out, part_out,
):
    middle = base[...] + (part_a[...].astype(f32) + part_b[...].astype(f32))
    middle_out[...] = middle
    gain = gains[LAYERS + layer : LAYERS + layer + 1]
    normed = (middle * norm_scale(middle) * gain).astype(bf16)
    normed_out[...] = normed
    weights = (
        (up_own[layer], down_own[layer], pre_own_out, act_own_out),
        (
            jnp.concatenate([up_a[...], up_b[...]], axis=1),
            jnp.concatenate([down_a[...], down_b[...]], axis=0),
            pre_far_out,
            act_far_out,
        ),
    )
    total = None
    for up, down, pre_out, act_out in weights:
        pre = dot(normed, up)
        pre_out[...] = pre
        inner = jnp.tanh(math.sqrt(2.0 / math.pi) * (pre + 0.044715 * pre * pre * pre))
        act = (0.5 * pre * (1.0 + inner)).astype(bf16)
        act_out[...] = act
        product = dot(act, down)
        total = product if total is None else total + product
    part_out[...] = total.astype(bf16)


def shard_rows(whole, place, mine_out, theirs_out):
    first = [whole[:, m * LANES : (m + 1) * LANES] for m in range(4)]
    even, odd = [jnp.where(place[1] == 0, first[2 * h], first[2 * h + 1]) for h in range(2)]
    mine_out[...] = jnp.where(place[0] == 0, even, odd)
    theirs_out[...] = jnp.where(place[0] == 0, odd, even)


def output_kernel(place, base, part_a, part_b, mine_out, theirs_out):
    whole = base[...] + (part_a[...].astype(f32) + part_b[...].astype(f32))
    shard_rows(whole.astype(bf16), place, mine_out, theirs_out)


def gelu_slope(pre):
    c = math.sqrt(2.0 / math.pi)
    inner = jnp.tanh(c * (pre + 0.044715 * pre * pre * pre))
    return 0.5 * (1.0 + inner) + 0.5 * pre * (1.0 - inner * inner) * (c * (1.0 + 3 * 0.044715 * pre * pre))


def ffn_back_kernel(first, layer, *refs):
    if first:
        place, *refs = refs
        pieces, refs = refs[:4], refs[4:]
        weights, outs = refs[:8], refs[8:]
        resid_out, rows_out, d_up_own_out, d_up_far_out, part_out = outs
        for piece, quarter in zip(pieces, quarters(place)):
            resid_out[:, quarter_lanes(quarter)] = piece[...].astype(f32)
        resid = resid_out[...]
    else:
        base, part_a, part_b, hidden, gains, *refs = refs
        weights, outs = refs[:8], refs[8:]
        resid_out, rows_out, d_up_own_out, d_up_far_out, part_out, gain_out = outs
        back, gain_out[...] = norm_back(
            hidden[...], gains[layer + 1 : layer + 2], part_a[...].astype(f32) + part_b[...].astype(f32)
        )
        resid = base[...] + back
        resid_out[...] = resid
    up_own, down_own, up_a, down_a, up_b, down_b, pre_own, pre_far = weights
    rows = resid.astype(bf16)
    rows_out[...] = rows
    total = None
    for up, down, pre, out in (
        (up_own[layer], down_own[layer], pre_own, d_up_own_out),
        (
            jnp.concatenate([up_a[...], up_b[...]], axis=1),
            jnp.concatenate([down_a[...], down_b[...]], axis=0),
            pre_far,
            d_up_far_out,
        ),
    ):
        d_up = (gelu_slope(pre[...]) * dot_nt(rows, down)).astype(bf16)
        out[...] = d_up
        product = dot_nt(d_up, up)
        total = product if total is None else total + product
    part_out[...] = total.astype(bf16)


def mix_back_kernel(
    layer, place, base, part_a, part_b, middle, gains, own, other, qkv, far_one, far_two, root, carried, blends,
    resid_out, rows_out, mixed_out, gain_out, num_one_out, num_two_out, zeta_out, state_out, blend_out,
):
    back, gain_out[...] = norm_back(
        middle[...],
        gains[LAYERS + layer : LAYERS + layer + 1],
        part_a[...].astype(f32) + part_b[...].astype(f32),
    )
    resid = base[...] + back
    resid_out[...] = resid
    blend = blends[2 * LAYERS + 3 * layer : 2 * LAYERS + 3 * layer + 3]
    rows = resid.astype(bf16)
    rows_out[...] = rows
    weight = jnp.concatenate([own[layer], other[...]], axis=0)
    d_mixed = dot_nt(rows, weight).astype(bf16)
    mixed_out[...] = d_mixed
    for pair in range(2):
        quarter = place[0] if pair == 0 else 1 - place[0]
        lanes = slice(pair * LANES, (pair + 1) * LANES)
        grad = d_mixed[:, lanes].astype(f32)
        scale = root[:, lanes]
        dot_one = grad * far_one[:, lanes]
        dot_two = grad * far_two[:, lanes]
        blend_one, blend_two = blend[1:2, lanes], blend[2:3, lanes]
        blend_out[0:1, lanes] = jnp.sum(dot_one, axis=0, keepdims=True)
        blend_out[1:2, lanes] = jnp.sum(dot_two, axis=0, keepdims=True)
        num_one = (grad * (blend_one * far_scale) * scale).astype(bf16)
        num_two = (grad * blend_two * scale).astype(bf16)
        d_zeta = head_sum(blend_one * dot_one + blend_two * dot_two) * (-0.5 * scale * scale)
        num_one_out[:, lanes] = num_one
        num_two_out[:, lanes] = num_two
        zeta_out[:, lanes] = d_zeta
        query_one, query_two = kernel_maps(qkv[0, :, lanes].astype(f32))
        reach = carried[...].astype(bf16)
        put_state(
            state_out,
            quarter,
            dot_tn(query_one * reach, num_one),
            dot_tn(query_two * reach, num_two),
            jnp.sum(carried[...] * d_zeta * query_one.astype(f32), axis=0, keepdims=True),
        )


def local_back_kernel(
    layer, place, qkv, halo, causal, causal_t, band, carried, state, prefix, d_mixed, num_one, num_two, d_zeta, blends,
    dq_out, dk_one_out, dk_two_out, dk_near_out, dv_out, halo_out, blend_out, near_k, near_v,
):
    rows = qkv.shape[1]
    masks = jnp.concatenate([causal[...], causal[...]], axis=0)
    masks_t = jnp.concatenate([causal_t[...], causal_t[...]], axis=1)
    row_low = lax.broadcasted_iota(jnp.int32, (2 * TILE, 1), 0) < TILE
    blend = blends[2 * LAYERS + 3 * layer : 2 * LAYERS + 3 * layer + 3]
    for pair in range(2):
        quarter = place[0] if pair == 0 else 1 - place[0]
        lanes = slice(pair * LANES, (pair + 1) * LANES)
        queries, keys, values = qkv[0, :, lanes], qkv[1, :, lanes], qkv[2, :, lanes]
        grads = d_mixed[:, lanes]
        state_one, state_two, unused_total = get_state(state, quarter)
        query_one, query_two = kernel_maps(queries.astype(f32))
        key_one, key_two = kernel_maps(keys.astype(f32))
        d_values = None
        d_queries = []
        for query, key, num, square, out in (
            (query_one, key_one, num_one[:, lanes], state_one, dk_one_out),
            (query_two, key_two, num_two[:, lanes], state_two, dk_two_out),
        ):
            query_split, num_split = split_heads(query), split_heads(num)
            attn_t = dot_nt(key, query_split).astype(bf16) * masks_t
            grad = dot_nt(num_split, values).astype(bf16) * masks
            grad_t = dot_nt(values, num_split).astype(bf16) * masks_t
            product = dot(attn_t, num_split)
            d_values = product if d_values is None else d_values + product
            d_queries.append(merge_heads(dot(grad, key)) + carried[...] * dot_nt(num, square))
            out[:, lanes] = dot(grad_t, query_split)
        zeta = d_zeta[:, lanes]
        d_queries[0] += zeta * prefix[:, lanes]
        dk_one_out[:, lanes] += dot(causal_t[...], (zeta * query_one.astype(f32)).astype(bf16))

        ext_keys = extend(halo[quarter, 0], keys)
        ext_values = extend(halo[quarter, 1], values)
        near_k[...] = jnp.zeros_like(near_k)
        near_v[...] = jnp.zeros_like(near_v)
        blend_low, blend_high = blend[0:1, pair * LANES : pair * LANES + 1], blend[0:1, pair * LANES + HD : pair * LANES + HD + 1]
        blend_rows = jnp.where(row_low, blend_low, blend_high)
        sums = None
        dq_near = []
        for tile in range(rows // TILE):
            at = slice(tile * TILE, (tile + 1) * TILE)
            window = slice(tile * TILE, tile * TILE + LANES)
            allowed = jnp.concatenate([band[at], band[at]], axis=0)
            query_split, grad_split = split_heads(queries[at]), split_heads(grads[at])
            scores = dot_nt(query_split, ext_keys[window]) * score_scale + allowed
            probs = jnp.exp(scores - jnp.max(scores, axis=1, keepdims=True))
            probs = probs / jnp.sum(probs, axis=1, keepdims=True)
            d_probs = dot_nt(grad_split, ext_values[window])
            inner = jnp.sum(probs * d_probs, axis=1, keepdims=True)
            sums = inner if sums is None else sums + inner
            d_scores = (probs * (d_probs - inner) * blend_rows).astype(bf16)
            dq_near.append(merge_heads(dot(d_scores, ext_keys[window])))
            near_k[window] += dot_tn(d_scores, query_split)
            near_v[window] += dot_tn(probs.astype(bf16), grad_split)
        sum_low = jnp.sum(sums[:TILE], axis=0, keepdims=True)
        sum_high = jnp.sum(sums[TILE:], axis=0, keepdims=True)
        blend_out[0:1, lanes] = jnp.where(low_lanes(1), sum_low, sum_high) * (1.0 / HD)
        back = maps_back(queries.astype(f32), d_queries[0], d_queries[1])
        dq_out[:, lanes] = (back + score_scale * jnp.concatenate(dq_near, axis=0)).astype(bf16)
        dk_near_out[:, lanes] = score_scale * near_k[HALO : HALO + rows]
        dv_out[:, lanes] = d_values + blend[0:1, lanes] * near_v[HALO : HALO + rows]
        halo_out[quarter, 0] = (score_scale * near_k[0:HALO]).astype(bf16)
        halo_out[quarter, 1] = (blend[0:1, lanes] * near_v[0:HALO]).astype(bf16)


def qkv_back_kernel(
    layer, at, count, place, flags, qkv, dq, dk_one, dk_two, dk_near, dv, tail, halo, own, other, found, *refs
):
    got = refs[:count]
    d_qkv_out, part_out, state = refs[count:]
    last_combine(at, flags, found, got, state)
    rows = qkv.shape[1]
    empty = jnp.zeros((rows - HALO, LANES), f32)
    for pair in range(2):
        quarter = place[0] if pair == 0 else 1 - place[0]
        lanes = slice(pair * LANES, (pair + 1) * LANES)
        keys, values = qkv[1, :, lanes], qkv[2, :, lanes]
        key_one, key_two = kernel_maps(keys.astype(f32))
        state_one, state_two, total = get_state(state, quarter)
        weight = tail[...].astype(f32)
        d_one = dk_one[:, lanes] + weight * (dot_nt(values, state_one) + total)
        d_two = dk_two[:, lanes] + weight * dot_nt(values, state_two)
        halo_k = jnp.concatenate([empty, halo[quarter, 0].astype(f32)], axis=0)
        halo_v = jnp.concatenate([empty, halo[quarter, 1].astype(f32)], axis=0)
        d_qkv_out[1, :, lanes] = (
            maps_back(keys.astype(f32), d_one, d_two) + dk_near[:, lanes] + halo_k
        ).astype(bf16)
        d_qkv_out[2, :, lanes] = (
            dv[:, lanes] + weight * (dot(key_one, state_one) + dot(key_two, state_two)) + halo_v
        ).astype(bf16)
    d_qkv_out[0] = dq[...]
    total = None
    for kind in range(3):
        weight = jnp.concatenate([own[layer, kind], other[kind]], axis=1)
        product = dot_nt(d_qkv_out[kind], weight)
        total = product if total is None else total + product
    part_out[...] = total.astype(bf16)


def wide_grads_kernel(with_qkv, place, normed, act_own, act_far, d_up_own, d_up_far, grad_rows, mixed, out_rows, *refs):
    if with_qkv:
        above, d_qkv, own, far = refs
    else:
        own, far = refs
    units = act_own.shape[1]
    piece = units // 2
    side = lax.rem(place[2], 2)
    own[:D] = dot_tn(normed[...], d_up_own[...]).astype(bf16)
    own[D : D + units] = dot_tn(act_own[...], grad_rows[...]).astype(bf16)
    d_up = dot_tn(normed[...], d_up_far[...]).astype(bf16)
    d_down = dot_tn(act_far[...], grad_rows[...]).astype(bf16)
    far[:D] = jnp.where(side == 0, d_up, jnp.concatenate([d_up[:, piece:], d_up[:, :piece]], axis=1))
    far[D : D + units] = jnp.where(side == 0, d_down, jnp.concatenate([d_down[piece:], d_down[:piece]], axis=0))
    d_out = dot_tn(mixed[...], out_rows[...]).astype(bf16)
    at = D + units
    own[at : at + LANES] = d_out[:LANES]
    far[at : at + LANES] = d_out[LANES:]
    if with_qkv:
        at += LANES
        for kind in range(3):
            found = dot_tn(above[...], d_qkv[kind]).astype(bf16)
            for block in range(D // LANES):
                rows = slice(at + kind * LANES, at + (kind + 1) * LANES)
                lanes = slice(block * LANES, (block + 1) * LANES)
                own[rows, lanes] = found[lanes, :LANES]
                far[rows, lanes] = found[lanes, LANES:]


def halve_kernel(place, own, got, keep_out, send_out):
    rows = own.shape[0] // 2
    total = own[...].astype(f32) + got[...].astype(f32)
    side = lax.rem(place[2], 2)
    keep_out[...] = jnp.where(side == 0, total[:rows], total[rows:])
    send_out[...] = jnp.where(side == 0, total[rows:], total[:rows]).astype(bf16)


def add_kernel(keep, got, out):
    out[...] = (keep[...] + got[...].astype(f32)).astype(bf16)


def fold_kernel(ways, got, out):
    rows = got.shape[0] // ways
    whole = got[...].astype(f32)
    total = sum(whole[k * rows : (k + 1) * rows] for k in range(ways)).astype(bf16)
    for k in range(ways):
        out[k * rows : (k + 1) * rows] = total


def last_qkv_kernel(normed, d_qkv, own_out, far_out):
    for kind in range(3):
        found = dot_tn(normed[...], d_qkv[kind])
        own_out[kind * D : (kind + 1) * D] = found[:, :LANES]
        far_out[kind * D : (kind + 1) * D] = found[:, LANES:]


def end_kernel(
    shards, place, base, part_a, part_b, hidden, gains, own, far, *refs
):
    smalls, (mine_out, theirs_out, send_out) = refs[: 4 * LAYERS - 1], refs[4 * LAYERS - 1 :]
    gain_refs, blend_refs = smalls[: 2 * LAYERS - 1], smalls[2 * LAYERS - 1 :]
    back, gain = norm_back(hidden[...], gains[0:1], part_a[...].astype(f32) + part_b[...].astype(f32))
    shard_rows((base[...] + back).astype(bf16), place, mine_out, theirs_out)
    block = own.shape[0] // shards
    gain_rows = jnp.concatenate([gain] + [ref[...] for ref in gain_refs], axis=0)
    blend_rows = jnp.concatenate([ref[...] for ref in blend_refs], axis=0)
    for to in range(2):
        features = jnp.where(
            place[1] == 0,
            gain_rows[:, 2 * to * LANES : (2 * to + 1) * LANES],
            gain_rows[:, (2 * to + 1) * LANES : (2 * to + 2) * LANES],
        )
        blends = jnp.where(place[0] == to, blend_rows[:, :LANES], blend_rows[:, LANES:])
        empty = jnp.zeros((SMALL - 5 * LAYERS, LANES), f32)
        extra = jnp.concatenate([features, blends, empty], axis=0).astype(bf16)
        rows = jnp.where(place[0] == to, own[...], far[...])
        for shard in range(shards):
            send_out[2 * shard + to, :SMALL] = extra
            send_out[2 * shard + to, SMALL:] = rows[shard * block : (shard + 1) * block].astype(bf16)


def collect_kernel(shards, got, out, rest_out):
    total = jnp.sum(got[...].astype(f32), axis=0)
    rest_out[...] = total[:SMALL]
    mine = total[SMALL:].astype(bf16)
    for shard in range(shards):
        out[shard] = mine


def in_order(place, mine, other):
    side = lax.rem(place[2], 2)
    return jnp.where(side == 0, mine[...], other[...]), jnp.where(side == 0, other[...], mine[...])


def finish_wide_kernel(place, low_mine, low_other, high_mine, high_other, up_out, down_out, out_out, above_out):
    units = up_out.shape[2]
    for layer, pair in ((0, (low_mine, low_other)), (1, (high_mine, high_other))):
        whole = jnp.concatenate(in_order(place, *pair), axis=0)
        up_out[layer] = whole[:D].astype(f32)
        down_out[layer] = whole[D : D + units].astype(f32)
        out_out[layer] = whole[D + units : D + units + LANES].astype(f32)
        if layer == 0:
            above_out[...] = whole[D + units + LANES :]


def finish_qkv_kernel(last, above, out):
    for kind in range(3):
        out[0, kind] = last[kind * D : (kind + 1) * D].astype(f32)
        for block in range(D // LANES):
            lanes = slice(block * LANES, (block + 1) * LANES)
            out[1, kind, lanes] = above[kind * LANES : (kind + 1) * LANES, lanes].astype(f32)


def call(body, outs, operands, scalars=0, scratch=(), scalar_outs=0):
    return pl.pallas_call(
        body,
        out_shape=tuple(jax.ShapeDtypeStruct(shape, kind) for shape, kind in outs),
        in_specs=[SM] * scalars + [VM] * (len(operands) - scalars),
        out_specs=tuple([VM] * (len(outs) - scalar_outs) + [SM] * scalar_outs),
        scratch_shapes=scratch,
        compiler_params=pltpu.CompilerParams(vmem_limit_bytes=24 * 2**20),
    )(*operands)


def after(value, *others):
    return lax.optimization_barrier((value, *others))[0]


def core_swap(value):
    count = lax.axis_size("mlp")
    return lax.ppermute(value, "mlp", [(i, i ^ 1) for i in range(count)])


def far_swap(value):
    count = lax.axis_size("mlp")
    return lax.ppermute(value, "mlp", [(i, i ^ 2) for i in range(count)])


def side_swap(value):
    count = lax.axis_size("seq")
    return lax.ppermute(value, "seq", [(i, i ^ 1) for i in range(count)])


def chunk_move(value, target):
    shards, parts = lax.axis_size("seq"), lax.axis_size("mlp")
    pairs = []
    for chunk in range(2 * shards):
        goal = target(chunk)
        if goal is None or not 0 <= goal < 2 * shards:
            continue
        for core in range(2):
            pairs.append(
                ((chunk // 2) * parts + (chunk % 2) * 2 + core, (goal // 2) * parts + (goal % 2) * 2 + core)
            )
    return lax.ppermute(value, AXES, pairs)


def scan(value, flags, chunks, reverse):
    places, _ = flag_places(chunks)
    found, arrived = None, None
    for stage, (size, ways, last) in enumerate(scan_plan(chunks)):
        got = []
        for step in range(1, ways):
            if last:

                def target(chunk, step=step):
                    move = -step if reverse else step
                    return chunk + move * size if 0 <= (chunk // size) % ways + move < ways else None

            else:

                def target(chunk, step=step):
                    member = (chunk // size) % ways
                    return chunk + ((member ^ step) - member) * size

            got.append(chunk_move(value, target))
        at = places[reverse, stage]
        if last:
            return (found, tuple(got), at), arrived
        arrived = arrived or tuple(got)
        operands = (flags, value, *got) + (() if found is None else (found,))
        value, found = call(
            functools.partial(combine_kernel, at, ways, found is not None),
            ((value.shape, bf16), (value.shape, f32)),
            operands,
            1,
        )


def line_exchange(value):
    shards, parts = lax.axis_size("seq"), lax.axis_size("mlp")
    groups = [
        [shard * parts + part for shard in range(side, shards, 2)] for side in range(2) for part in range(parts)
    ]
    return lax.all_to_all(value, AXES, 0, 0, axis_index_groups=groups, tiled=True)


def by_place(flag, mine, other):
    return jnp.where(flag == 0, mine, other), jnp.where(flag == 0, other, mine)


def per_device(inputs, lengths, valid, norm_attn, w_qkv, blend, w_out, norm_ffn, w_up, w_down, grad_out):
    shards, parts = lax.axis_size("seq"), lax.axis_size("mlp")
    shard, part = lax.axis_index("seq"), lax.axis_index("mlp")
    half, core = part // 2, part % 2
    side = shard % 2
    rows = inputs.shape[0] // 2
    chunks = 2 * shards
    units = w_up.shape[2]
    place = jnp.stack([half, core, shard]).astype(jnp.int32)

    wide = 2 * LANES
    hidden_like = ((rows, D), f32)
    low_like = ((rows, D), bf16)
    heads_like = ((rows, wide), f32)
    heads_low = ((rows, wide), bf16)
    qkv_like = ((3, rows, wide), bf16)
    state_like = ((2, STATE, LANES), bf16)
    halo_like = ((2, 2, HALO, LANES), bf16)
    ffn_like = ((rows, units), f32)
    ffn_low = ((rows, units), bf16)
    shard_like = ((rows, LANES), bf16)
    gain_like = ((1, D), f32)

    piece_like = ((rows + 3 * SMALL, LANES), bf16)
    mine, theirs = call(pack_kernel, (piece_like, piece_like), (place, blend, inputs, norm_attn, norm_ffn), 2)
    got = far_swap(theirs)
    pieces = (mine, got, core_swap(mine), core_swap(got))
    far_qkv = [far_swap(after(w_qkv[0], theirs)), None]
    far_out = [far_swap(after(w_out[0], theirs)), None]

    def up_piece(layer):
        return lax.dynamic_slice_in_dim(w_up[layer], side * (units // 2), units // 2, 1)

    def down_piece(layer):
        return lax.dynamic_slice_in_dim(w_down[layer], side * (units // 2), units // 2, 0)

    up_a, up_b, down_a, down_b = ([None] * LAYERS for _ in range(4))
    up_a[0] = far_swap(after(up_piece(0), theirs))

    before = lax.ppermute(
        valid[2 * rows - LANES :].reshape(1, LANES), "seq", [(source, source + 1) for source in range(shards - 1)]
    )
    _, flag_count = flag_places(chunks)
    causal, causal_t, band, carried, tail, flags = call(
        functools.partial(setup_kernel, chunks),
        (
            ((rows, rows), bf16),
            ((rows, rows), bf16),
            ((rows, LANES), f32),
            ((rows, LANES), f32),
            ((rows, LANES), bf16),
            ((flag_count,), f32),
        ),
        (place, lengths, valid.reshape(1, 2 * rows), before),
        2,
        scalar_outs=1,
    )

    saved = []
    base, adds = None, None
    for layer in range(LAYERS):
        outs = (hidden_like, low_like, qkv_like, state_like, halo_like)
        if layer == 0:
            hidden, normed, qkv, state, halo, gains, blends = call(
                functools.partial(qkv_kernel, True, layer),
                outs + (((SMALL, D), f32), ((SMALL, wide), f32)),
                (place, *pieces, w_qkv, far_qkv[layer], tail),
                1,
            )
        else:
            hidden, normed, qkv, state, halo = call(
                functools.partial(qkv_kernel, False, layer),
                outs,
                (place, base, *adds, gains, w_qkv, far_qkv[layer], tail),
                1,
            )
        halo = chunk_move(halo, lambda c: c + 1)
        (found, parts_got, at), arrived = scan(state, flags, chunks, False)
        if layer == 0:
            down_a[0] = far_swap(after(down_piece(0), *arrived))
            up_b[0] = side_swap(after(up_a[0], *arrived))
            far_qkv[1] = far_swap(after(w_qkv[1], *arrived))
            down_b[0] = side_swap(down_a[0])
            far_out[1] = far_swap(after(w_out[1], *arrived))
            up_a[1] = far_swap(after(up_piece(1), *arrived))
            down_a[1] = far_swap(after(down_piece(1), *arrived))
            up_b[1] = side_swap(after(up_a[1], *arrived))
            down_b[1] = side_swap(after(down_a[1], *arrived))
        near, one, two, sums = call(
            local_kernel, (heads_like,) * 4, (place, qkv, halo, causal, band), 1
        )
        mixed, far_one, far_two, root, prefix, state, piece = call(
            functools.partial(mix_kernel, layer, at, len(parts_got)),
            (heads_low, heads_like, heads_like, heads_like, heads_like, state_like, low_like),
            (place, flags, qkv, near, one, two, sums, carried, blends, w_out, far_out[layer], found, *parts_got),
            2,
        )
        weights = (w_up, w_down, up_a[layer], down_a[layer], up_b[layer], down_b[layer])
        middle, normed_ffn, pre_own, pre_far, act_own, act_far, piece_ffn = call(
            functools.partial(ffn_kernel, layer),
            (hidden_like, low_like, ffn_like, ffn_like, ffn_low, ffn_low, low_like),
            (hidden, piece, core_swap(piece), gains, *weights),
        )
        saved.append(
            (hidden, normed, qkv, state, halo, mixed, far_one, far_two, root, prefix, middle, normed_ffn,
             weights, pre_own, pre_far, act_own, act_far)
        )
        base, adds = middle, (piece_ffn, core_swap(piece_ffn))
    out_mine, out_theirs = call(output_kernel, (shard_like, shard_like), (place, base, *adds), 1)
    output = jnp.concatenate(by_place(half, out_mine, far_swap(out_theirs)))

    mine, theirs = call(pack_grad_kernel, (shard_like, shard_like), (place, after(grad_out, saved[0][2])), 1)
    got = far_swap(theirs)
    grad_pieces = (mine, got, core_swap(mine), core_swap(got))

    base, adds = None, None
    d_gain_attn, d_gain_ffn, d_blends = [None] * LAYERS, [None] * LAYERS, [None] * LAYERS
    wide_sums = [None] * LAYERS
    d_qkvs = [None] * LAYERS
    arrived = None
    for layer in reversed(range(LAYERS)):
        (hidden, normed, qkv, state, halo, mixed, far_one, far_two, root, prefix, middle, normed_ffn,
         weights, pre_own, pre_far, act_own, act_far) = saved[layer]
        outs = (hidden_like, low_like, ffn_low, ffn_low, low_like)
        if base is None:
            resid, grad_rows, d_up_own, d_up_far, piece = call(
                functools.partial(ffn_back_kernel, True, layer),
                outs,
                (place, *grad_pieces, *weights, pre_own, pre_far),
                1,
            )
        else:
            resid, grad_rows, d_up_own, d_up_far, piece, d_gain_attn[layer + 1] = call(
                functools.partial(ffn_back_kernel, False, layer),
                outs + (gain_like,),
                (base, *adds, saved[layer + 1][0], gains, *weights, pre_own, pre_far),
            )
        (resid, out_rows, d_mixed, d_gain_ffn[layer], num_one, num_two, d_zeta, state_back, blend_far) = call(
            functools.partial(mix_back_kernel, layer),
            (hidden_like, low_like, heads_low, gain_like, heads_low, heads_low, heads_like, state_like,
             ((2, wide), f32)),
            (place, resid, piece, core_swap(piece), middle, gains, w_out, far_out[layer], qkv, far_one, far_two,
             root, carried, blends),
            1,
        )
        (found, parts_got, at), arrived = scan(state_back, flags, chunks, True)
        ext = HALO + rows + HALO
        dq, dk_one, dk_two, dk_near, dv, halo_back, blend_near = call(
            functools.partial(local_back_kernel, layer),
            (heads_low, heads_like, heads_like, heads_like, heads_like, halo_like, ((1, wide), f32)),
            (place, qkv, halo, causal, causal_t, band, carried, state, prefix, d_mixed, num_one, num_two, d_zeta,
             blends),
            1,
            scratch=(pltpu.VMEM((ext, LANES), f32), pltpu.VMEM((ext, LANES), f32)),
        )
        halo_back = chunk_move(halo_back, lambda c: c - 1)
        with_qkv = layer + 1 < LAYERS
        height = D + units + LANES + (3 * LANES if with_qkv else 0)
        own, far = call(
            functools.partial(wide_grads_kernel, with_qkv),
            (((height, D), bf16), ((height, D), bf16)),
            (place, normed_ffn, act_own, act_far, d_up_own, d_up_far, grad_rows, mixed, out_rows)
            + ((saved[layer + 1][1], d_qkvs[layer + 1]) if with_qkv else ()),
            1,
        )
        keep, send = call(
            halve_kernel,
            (((height // 2, D), f32), ((height // 2, D), bf16)),
            (place, own, far_swap(after(far, *arrived))),
            1,
        )
        (folded,) = call(add_kernel, (((height // 2, D), bf16),), (keep, side_swap(send)))
        (folded,) = call(
            functools.partial(fold_kernel, shards // 2), (((height // 2, D), bf16),), (line_exchange(folded),)
        )
        folded = line_exchange(folded)
        wide_sums[layer] = (folded, side_swap(folded))
        d_qkvs[layer], piece = call(
            functools.partial(qkv_back_kernel, layer, at, len(parts_got)),
            (qkv_like, low_like),
            (place, flags, qkv, dq, dk_one, dk_two, dk_near, dv, tail, halo_back, w_qkv, far_qkv[layer], found,
             *parts_got),
            2,
            scratch=(pltpu.VMEM((2, STATE, LANES), bf16),),
        )
        base, adds = resid, (piece, core_swap(piece))
        d_blends[layer] = (blend_near, blend_far)

    last_like = ((3 * D, LANES), f32)
    own, far = call(last_qkv_kernel, (last_like, last_like), (saved[0][1], d_qkvs[0]))
    block = 3 * D // shards
    smalls = d_gain_attn[1:] + d_gain_ffn + [ref for pair in d_blends for ref in pair]
    mine, theirs, send = call(
        functools.partial(end_kernel, shards),
        (shard_like, shard_like, ((chunks, SMALL + block, LANES), bf16)),
        (place, base, *adds, saved[0][0], gains, own, far, *smalls),
        1,
    )
    groups = [[s * parts + h * 2 + c for s in range(shards) for h in range(2)] for c in range(2)]
    got = lax.all_to_all(send, AXES, 0, 0, axis_index_groups=groups, tiled=True)
    spread, rest = call(
        functools.partial(collect_kernel, shards),
        (((shards, block, LANES), bf16), ((SMALL, LANES), f32)),
        (got,),
    )
    last = lax.all_to_all(spread, "seq", 0, 0, tiled=True).reshape(3 * D, LANES)
    d_inputs = jnp.concatenate(by_place(half, mine, far_swap(theirs)))

    count = 2 * LAYERS + 3 * LAYERS
    d_norm_attn = rest[:LAYERS]
    d_norm_ffn = rest[LAYERS : 2 * LAYERS]
    d_blend = jnp.sum(rest[2 * LAYERS : count].reshape(LAYERS, 3, 2, HD), axis=3)
    d_up, d_down, d_out, above = call(
        finish_wide_kernel,
        (((LAYERS, D, units), f32), ((LAYERS, units, D), f32), ((LAYERS, LANES, D), f32), ((3 * LANES, D), bf16)),
        (place, *wide_sums[0], *wide_sums[1]),
        1,
    )
    (d_qkv,) = call(finish_qkv_kernel, (((LAYERS, 3, D, LANES), f32),), (last, above))
    return (output, d_inputs, d_norm_attn, d_qkv, d_blend, d_out, d_norm_ffn, d_up, d_down)


def solution(mesh):
    placed = (
        P("seq", "mlp"),
        P(),
        P("seq"),
        P(None, "mlp"),
        P(None, None, None, "mlp"),
        P(None, None, "mlp"),
        P(None, "mlp", None),
        P(None, "mlp"),
        P(None, None, "mlp"),
        P(None, "mlp", None),
        P("seq", "mlp"),
    )
    return jax.shard_map(
        per_device,
        mesh=mesh,
        in_specs=placed,
        out_specs=(
            P("seq", "mlp"),
            P("seq", "mlp"),
            P(None, "mlp"),
            P(None, None, None, "mlp"),
            P(None, None, "mlp"),
            P(None, "mlp", None),
            P(None, "mlp"),
            P(None, None, "mlp"),
            P(None, "mlp", None),
        ),
        check_vma=False,
    )
```

```python
import functools
import math

import jax
import jax.numpy as jnp
from jax import lax
from jax.experimental import pallas as pl
from jax.experimental.pallas import tpu as pltpu
from jax.sharding import PartitionSpec as P

HD = 64
D = 512
BAND = 30
LAYERS = 2
HALO = 32
TILE = 64
LANES = 128
STATE = 144
SMALL = 16
AXES = ("seq", "mlp")

epsilon = 1e-05
masked_score = -1e30
score_scale = 1.0 / math.sqrt(HD)
far_scale = 1.0 / math.sqrt(HD)
f32 = jnp.float32
bf16 = jnp.bfloat16

VM = pl.BlockSpec(memory_space=pltpu.VMEM)
SM = pl.BlockSpec(memory_space=pltpu.SMEM)


def dot(x, y):
    return jnp.dot(x, y, preferred_element_type=f32)


def dot_nt(x, y):
    return lax.dot_general(x, y, (((1,), (1,)), ((), ())), preferred_element_type=f32)


def dot_tn(x, y):
    return lax.dot_general(x, y, (((0,), (0,)), ((), ())), preferred_element_type=f32)


def low_lanes(rows):
    return lax.broadcasted_iota(jnp.int32, (rows, LANES), 1) < HD


def split_heads(x):
    low = low_lanes(x.shape[0])
    zero = jnp.zeros_like(x)
    return jnp.concatenate([jnp.where(low, x, zero), jnp.where(low, zero, x)], axis=0)


def merge_heads(y):
    rows = y.shape[0] // 2
    return jnp.where(low_lanes(rows), y[:rows], y[rows:])


def head_sum(x):
    row = lax.broadcasted_iota(jnp.int32, (LANES, LANES), 0) < HD
    ones = jnp.where(row == low_lanes(LANES), 1.0, 0.0).astype(bf16)
    high = x.astype(bf16)
    rest = (x - high.astype(f32)).astype(bf16)
    return dot(high, ones) + dot(rest, ones)


def kernel_maps(x):
    return (
        jnp.where(x > 0, x + 1.0, jnp.exp(jnp.minimum(x, 0.0))).astype(bf16),
        jnp.tanh(x).astype(bf16),
    )


def maps_back(x, d_one, d_two):
    tanh = jnp.tanh(x)
    return jnp.where(x > 0, 1.0, jnp.exp(jnp.minimum(x, 0.0))) * d_one + (1.0 - tanh * tanh) * d_two


def put_state(ref, quarter, one, two, total):
    row = lax.broadcasted_iota(jnp.int32, (STATE - 2 * HD, LANES), 0)
    low = low_lanes(HD)
    ref[quarter, 0:HD, :] = jnp.where(low, one[:HD], one[HD:]).astype(bf16)
    ref[quarter, HD : 2 * HD, :] = jnp.where(low, two[:HD], two[HD:]).astype(bf16)
    ref[quarter, 2 * HD : STATE, :] = jnp.where(row == 0, total, 0.0).astype(bf16)


def get_state(ref, quarter):
    one = split_heads(ref[quarter, 0:HD, :])
    two = split_heads(ref[quarter, HD : 2 * HD, :])
    total = ref[quarter, 2 * HD : STATE, :].astype(f32)[0:1]
    return one, two, total


def norm_scale(hidden):
    return lax.rsqrt(jnp.sum(hidden * hidden, axis=1, keepdims=True) * (1.0 / D) + epsilon)


def norm_back(hidden, gain, grad):
    scale = norm_scale(hidden)
    gained = grad * gain
    inner = jnp.sum(gained * hidden, axis=1, keepdims=True) * (1.0 / D)
    back = scale * gained - hidden * (scale * scale * scale * inner)
    return back, jnp.sum(grad * hidden * scale, axis=0, keepdims=True)


def extend(halo, rows):
    return jnp.concatenate([halo, rows, jnp.zeros((HALO, LANES), bf16)], axis=0)


def three_parts(value):
    high = value.astype(bf16)
    rest = value - high.astype(f32)
    middle = rest.astype(bf16)
    low = (rest - middle.astype(f32)).astype(bf16)
    return jnp.concatenate([high, middle, low], axis=0)


def pack_kernel(place, blend, inputs, norm_attn, norm_ffn, mine_out, theirs_out):
    rows = inputs.shape[0] // 2
    low = low_lanes(1)
    small = [norm_attn[...], norm_ffn[...]]
    for layer in range(LAYERS):
        for kind in range(3):
            small.append(jnp.where(low, blend[layer, kind, 0], blend[layer, kind, 1]))
    small.append(jnp.zeros((SMALL - 5 * LAYERS, LANES), f32))
    small = three_parts(jnp.concatenate(small, axis=0))
    first, second = inputs[:rows], inputs[rows:]
    mine_out[:rows] = jnp.where(place[0] == 0, first, second)
    theirs_out[:rows] = jnp.where(place[0] == 0, second, first)
    mine_out[rows:] = small
    theirs_out[rows:] = small


def pack_grad_kernel(place, grads, mine_out, theirs_out):
    rows = grads.shape[0] // 2
    first, second = grads[:rows], grads[rows:]
    mine_out[...] = jnp.where(place[0] == 0, first, second)
    theirs_out[...] = jnp.where(place[0] == 0, second, first)


def quarters(place):
    half, core = place[0], place[1]
    return 2 * half + core, 2 * (1 - half) + core, 2 * half + 1 - core, 2 * (1 - half) + 1 - core


def quarter_lanes(quarter):
    return pl.ds(pl.multiple_of(quarter * LANES, LANES), LANES)


def item_ends(lengths):
    ends = []
    for k in range(lengths.shape[0]):
        ends.append(lengths[k] if k == 0 else ends[-1] + lengths[k])
    return ends


def item_start(lengths, ends, positions):
    start = jnp.zeros_like(positions)
    for k, end in enumerate(ends):
        start = start + jnp.where(end <= positions, lengths[k], 0)
    return start


def scan_plan(chunks):
    stages, size = [], 1
    while size < chunks:
        ways = min(4, chunks // size)
        stages.append((size, ways, size * ways >= chunks))
        size *= ways
    return stages


def flag_places(chunks):
    at, places = 0, {}
    for reverse in (False, True):
        for stage, (_, ways, _) in enumerate(scan_plan(chunks)):
            places[reverse, stage] = at
            at += 2 * ways
    return places, at


def setup_kernel(chunks, place, lengths, valid, before, causal_out, causal_t_out, band_out, carried_out, tail_out, flags_out):
    rows = causal_out.shape[0]
    chunk = place[2] * 2 + place[0]
    first_row = chunk * rows
    ends = item_ends(lengths)

    def start_of(positions):
        return item_start(lengths, ends, positions)

    lane = lax.broadcasted_iota(jnp.int32, (1, rows), 1)
    starts_row = start_of(first_row + lane)
    starts = start_of(first_row + lax.broadcasted_iota(jnp.int32, (rows, LANES), 0))
    both = jnp.concatenate([starts, starts], axis=1)
    words = valid[...]
    own_words = jnp.where(place[0] == 0, words[:, :rows], words[:, rows:])
    last_words = jnp.where(place[0] == 0, before[...], words[:, rows - LANES : rows])
    row_at = lax.broadcasted_iota(jnp.int32, (rows, rows), 0)
    lane_at = lax.broadcasted_iota(jnp.int32, (rows, rows), 1)
    own_column = jnp.sum(jnp.where(row_at == lane_at, own_words, 0), axis=1, keepdims=True)
    same = both == starts_row
    causal_out[...] = jnp.where((lane_at <= row_at) & same & (own_words == 1), 1.0, 0.0).astype(bf16)
    causal_t_out[...] = jnp.where((row_at <= lane_at) & same & (own_column == 1), 1.0, 0.0).astype(bf16)
    carried_out[...] = jnp.where(starts < first_row, 1.0, 0.0)
    last_start = start_of(first_row + rows - 1)
    tail_out[...] = jnp.where((starts == last_start) & (own_column == 1), 1.0, 0.0).astype(bf16)
    all_words = jnp.concatenate([last_words, own_words, jnp.zeros((1, LANES), jnp.int32)], axis=1)
    tile_row = lax.broadcasted_iota(jnp.int32, (TILE, LANES), 0)
    tile_lane = lax.broadcasted_iota(jnp.int32, (TILE, LANES), 1)
    gap = tile_row + HALO - tile_lane
    for tile in range(rows // TILE):
        key_starts = start_of(first_row + tile * TILE - HALO + lax.broadcasted_iota(jnp.int32, (1, LANES), 1))
        offset = LANES - HALO + tile * TILE
        key_words = all_words[:, offset : offset + LANES]
        at = slice(tile * TILE, (tile + 1) * TILE)
        allowed = (gap >= 0) & (gap <= BAND) & (starts[at] == key_starts) & ((key_words == 1) | (gap == 0))
        band_out[at] = jnp.where(allowed, 0.0, masked_score)

    places, _ = flag_places(chunks)
    for reverse in (False, True):
        edge = start_of(first_row + (rows - 1 if reverse else 0))
        for stage, (size, ways, last) in enumerate(scan_plan(chunks)):
            member = lax.rem(lax.div(chunk, size), ways)
            base = chunk - member * size - lax.rem(chunk, size)
            group = base if reverse else base + ways * size - 1
            group = start_of(group * rows + (0 if reverse else rows - 1))
            for step in range(ways):
                if last:
                    other = member + step if reverse else member - step
                else:
                    other = jnp.bitwise_xor(member, step)
                block = base + other * size + (0 if reverse else size - 1)
                start = start_of(block * rows + (0 if reverse else rows - 1))
                ahead = (other > member) if reverse else (other < member)
                ahead = ahead & (other >= 0) & (other < ways)
                at = places[reverse, stage] + 2 * step
                flags_out[at] = jnp.where(ahead & (start == edge), 1.0, 0.0)
                flags_out[at + 1] = jnp.where(start == group, 1.0, 0.0)


def combine_kernel(at, ways, has_found, flags, *refs):
    got, refs = refs[:ways], refs[ways:]
    total = sum(flags[at + 2 * step + 1] * got[step][...].astype(f32) for step in range(ways))
    refs[-2][...] = total.astype(bf16)
    found = sum(flags[at + 2 * step] * got[step][...].astype(f32) for step in range(1, ways))
    refs[-1][...] = found + refs[0][...] if has_found else found


def last_combine(at, flags, found, got, out):
    value = found[...]
    for step, part in enumerate(got):
        value = value + flags[at + 2 * (step + 1)] * part[...].astype(f32)
    out[...] = value.astype(bf16)


def qkv_kernel(first, layer, place, *refs):
    if first:
        refs, outs = refs[:7], refs[7:]
        pieces, (own, other, tail) = refs[:4], refs[4:]
        hidden_out, normed_out, qkv_out, state_out, halo_out, gains, blends_out = outs
        rows = hidden_out.shape[0]
        for index, (piece, quarter) in enumerate(zip(pieces, quarters(place))):
            hidden_out[:, quarter_lanes(quarter)] = piece[:rows].astype(f32)
            parts = piece[rows:].astype(f32)
            small = parts[:SMALL] + parts[SMALL : 2 * SMALL] + parts[2 * SMALL :]
            gains[:, quarter_lanes(quarter)] = small
            if index < 2:
                blends_out[:, index * LANES : (index + 1) * LANES] = small
        hidden = hidden_out[...]
    else:
        base, part_a, part_b, gains, own, other, tail, hidden_out, normed_out, qkv_out, state_out, halo_out = refs
        hidden = base[...] + (part_a[...].astype(f32) + part_b[...].astype(f32))
        hidden_out[...] = hidden
    rows = hidden.shape[0]
    normed = (hidden * norm_scale(hidden) * gains[layer : layer + 1]).astype(bf16)
    normed_out[...] = normed
    found = []
    for kind in range(3):
        weight = jnp.concatenate([own[layer, kind], other[kind]], axis=1)
        found.append(dot(normed, weight).astype(bf16))
        qkv_out[kind] = found[kind]
    for pair in range(2):
        quarter = place[0] if pair == 0 else 1 - place[0]
        lanes = slice(pair * LANES, (pair + 1) * LANES)
        keys, values = found[1][:, lanes], found[2][:, lanes]
        one, two = kernel_maps(keys.astype(f32))
        one, two = one * tail[...], two * tail[...]
        put_state(
            state_out,
            quarter,
            dot_tn(one, values),
            dot_tn(two, values),
            jnp.sum(one.astype(f32), axis=0, keepdims=True),
        )
        halo_out[quarter, 0] = keys[rows - HALO :]
        halo_out[quarter, 1] = values[rows - HALO :]


def far_kernel(qkv, causal, one_out, two_out, sums_out):
    masks = jnp.concatenate([causal[...], causal[...]], axis=0)
    for pair in range(2):
        lanes = slice(pair * LANES, (pair + 1) * LANES)
        queries, keys, values = qkv[0, :, lanes], qkv[1, :, lanes], qkv[2, :, lanes]
        maps_q, maps_k = kernel_maps(queries.astype(f32)), kernel_maps(keys.astype(f32))
        for query, key, out in ((maps_q[0], maps_k[0], one_out), (maps_q[1], maps_k[1], two_out)):
            attn = dot_nt(split_heads(query), key).astype(bf16) * masks
            out[:, lanes] = merge_heads(dot(attn, values))
        sums_out[:, lanes] = dot(causal[...], maps_k[0])


def near_kernel(place, qkv, halo, band, near_out):
    rows = qkv.shape[1]
    for pair in range(2):
        quarter = place[0] if pair == 0 else 1 - place[0]
        lanes = slice(pair * LANES, (pair + 1) * LANES)
        queries, keys, values = qkv[0, :, lanes], qkv[1, :, lanes], qkv[2, :, lanes]
        ext_keys = extend(halo[quarter, 0], keys)
        ext_values = extend(halo[quarter, 1], values)
        for tile in range(rows // TILE):
            at = slice(tile * TILE, (tile + 1) * TILE)
            window = slice(tile * TILE, tile * TILE + LANES)
            allowed = jnp.concatenate([band[at], band[at]], axis=0)
            scores = dot_nt(split_heads(queries[at]), ext_keys[window]) * score_scale + allowed
            weights = jnp.exp(scores - jnp.max(scores, axis=1, keepdims=True))
            weights = weights / jnp.sum(weights, axis=1, keepdims=True)
            near_out[at, lanes] = merge_heads(dot(weights.astype(bf16), ext_values[window]))


def mix_kernel(layer, at, count, place, flags, qkv, near, one, two, sums, carried, blends, own, other, found, *refs):
    got = refs[:count]
    mixed_out, far_one_out, far_two_out, root_out, prefix_out, state, part_out = refs[count:]
    last_combine(at, flags, found, got, state)
    mixed = []
    row = 2 * LAYERS + 3 * layer
    for pair in range(2):
        quarter = place[0] if pair == 0 else 1 - place[0]
        lanes = slice(pair * LANES, (pair + 1) * LANES)
        query_one, query_two = kernel_maps(qkv[0, :, lanes].astype(f32))
        state_one, state_two, total = get_state(state, quarter)
        num_one = one[:, lanes] + carried[...] * dot(query_one, state_one)
        num_two = two[:, lanes] + carried[...] * dot(query_two, state_two)
        prefix = sums[:, lanes] + carried[...] * total
        zeta = head_sum(query_one.astype(f32) * prefix)
        root = lax.rsqrt(zeta + 1.0)
        far_one = num_one * root * far_scale
        far_two = num_two * root
        far_one_out[:, lanes] = far_one
        far_two_out[:, lanes] = far_two
        root_out[:, lanes] = root
        prefix_out[:, lanes] = prefix
        mixed.append(
            (
                blends[row : row + 1, lanes] * near[:, lanes]
                + blends[row + 1 : row + 2, lanes] * far_one
                + blends[row + 2 : row + 3, lanes] * far_two
            ).astype(bf16)
        )
        mixed_out[:, lanes] = mixed[pair]
    weight = jnp.concatenate([own[layer], other[...]], axis=0)
    part_out[...] = dot(jnp.concatenate(mixed, axis=1), weight).astype(bf16)


def ffn_kernel(
    layer, base, part_a, part_b, gains, up_own, down_own, up_a, down_a, up_b, down_b,
    middle_out, normed_out, pre_own_out, pre_far_out, act_own_out, act_far_out, part_out,
):
    middle = base[...] + (part_a[...].astype(f32) + part_b[...].astype(f32))
    middle_out[...] = middle
    gain = gains[LAYERS + layer : LAYERS + layer + 1]
    normed = (middle * norm_scale(middle) * gain).astype(bf16)
    normed_out[...] = normed
    weights = (
        (up_own[layer], down_own[layer], pre_own_out, act_own_out),
        (
            jnp.concatenate([up_a[...], up_b[...]], axis=1),
            jnp.concatenate([down_a[...], down_b[...]], axis=0),
            pre_far_out,
            act_far_out,
        ),
    )
    total = None
    for up, down, pre_out, act_out in weights:
        pre = dot(normed, up)
        pre_out[...] = pre
        inner = jnp.tanh(math.sqrt(2.0 / math.pi) * (pre + 0.044715 * pre * pre * pre))
        act = (0.5 * pre * (1.0 + inner)).astype(bf16)
        act_out[...] = act
        product = dot(act, down)
        total = product if total is None else total + product
    part_out[...] = total.astype(bf16)


def shard_rows(whole, place, mine_out, theirs_out):
    first = [whole[:, m * LANES : (m + 1) * LANES] for m in range(4)]
    even, odd = [jnp.where(place[1] == 0, first[2 * h], first[2 * h + 1]) for h in range(2)]
    mine_out[...] = jnp.where(place[0] == 0, even, odd)
    theirs_out[...] = jnp.where(place[0] == 0, odd, even)


def output_kernel(place, base, part_a, part_b, mine_out, theirs_out):
    whole = base[...] + (part_a[...].astype(f32) + part_b[...].astype(f32))
    shard_rows(whole.astype(bf16), place, mine_out, theirs_out)


def gelu_slope(pre):
    c = math.sqrt(2.0 / math.pi)
    inner = jnp.tanh(c * (pre + 0.044715 * pre * pre * pre))
    return 0.5 * (1.0 + inner) + 0.5 * pre * (1.0 - inner * inner) * (c * (1.0 + 3 * 0.044715 * pre * pre))


def ffn_back_kernel(first, layer, *refs):
    if first:
        place, *refs = refs
        pieces, refs = refs[:4], refs[4:]
        weights, outs = refs[:8], refs[8:]
        resid_out, rows_out, d_up_own_out, d_up_far_out, part_out = outs
        for piece, quarter in zip(pieces, quarters(place)):
            resid_out[:, quarter_lanes(quarter)] = piece[...].astype(f32)
        resid = resid_out[...]
    else:
        base, part_a, part_b, hidden, gains, *refs = refs
        weights, outs = refs[:8], refs[8:]
        resid_out, rows_out, d_up_own_out, d_up_far_out, part_out, gain_out = outs
        back, gain_out[...] = norm_back(
            hidden[...], gains[layer + 1 : layer + 2], part_a[...].astype(f32) + part_b[...].astype(f32)
        )
        resid = base[...] + back
        resid_out[...] = resid
    up_own, down_own, up_a, down_a, up_b, down_b, pre_own, pre_far = weights
    rows = resid.astype(bf16)
    rows_out[...] = rows
    total = None
    for up, down, pre, out in (
        (up_own[layer], down_own[layer], pre_own, d_up_own_out),
        (
            jnp.concatenate([up_a[...], up_b[...]], axis=1),
            jnp.concatenate([down_a[...], down_b[...]], axis=0),
            pre_far,
            d_up_far_out,
        ),
    ):
        d_up = (gelu_slope(pre[...]) * dot_nt(rows, down)).astype(bf16)
        out[...] = d_up
        product = dot_nt(d_up, up)
        total = product if total is None else total + product
    part_out[...] = total.astype(bf16)


def mix_back_kernel(
    layer, place, base, part_a, part_b, middle, gains, own, other, qkv, far_one, far_two, root, carried, blends,
    resid_out, rows_out, mixed_out, gain_out, num_one_out, num_two_out, zeta_out, state_out, blend_out,
):
    back, gain_out[...] = norm_back(
        middle[...],
        gains[LAYERS + layer : LAYERS + layer + 1],
        part_a[...].astype(f32) + part_b[...].astype(f32),
    )
    resid = base[...] + back
    resid_out[...] = resid
    blend = blends[2 * LAYERS + 3 * layer : 2 * LAYERS + 3 * layer + 3]
    rows = resid.astype(bf16)
    rows_out[...] = rows
    weight = jnp.concatenate([own[layer], other[...]], axis=0)
    d_mixed = dot_nt(rows, weight).astype(bf16)
    mixed_out[...] = d_mixed
    for pair in range(2):
        quarter = place[0] if pair == 0 else 1 - place[0]
        lanes = slice(pair * LANES, (pair + 1) * LANES)
        grad = d_mixed[:, lanes].astype(f32)
        scale = root[:, lanes]
        dot_one = grad * far_one[:, lanes]
        dot_two = grad * far_two[:, lanes]
        blend_one, blend_two = blend[1:2, lanes], blend[2:3, lanes]
        blend_out[0:1, lanes] = jnp.sum(dot_one, axis=0, keepdims=True)
        blend_out[1:2, lanes] = jnp.sum(dot_two, axis=0, keepdims=True)
        num_one = (grad * (blend_one * far_scale) * scale).astype(bf16)
        num_two = (grad * blend_two * scale).astype(bf16)
        d_zeta = head_sum(blend_one * dot_one + blend_two * dot_two) * (-0.5 * scale * scale)
        num_one_out[:, lanes] = num_one
        num_two_out[:, lanes] = num_two
        zeta_out[:, lanes] = d_zeta
        query_one, query_two = kernel_maps(qkv[0, :, lanes].astype(f32))
        reach = carried[...].astype(bf16)
        put_state(
            state_out,
            quarter,
            dot_tn(query_one * reach, num_one),
            dot_tn(query_two * reach, num_two),
            jnp.sum(carried[...] * d_zeta * query_one.astype(f32), axis=0, keepdims=True),
        )


def near_back_kernel(
    layer, place, qkv, halo, band, d_mixed, blends, dq_out, dk_out, dv_out, halo_out, blend_out, near_k, near_v
):
    rows = qkv.shape[1]
    row_low = lax.broadcasted_iota(jnp.int32, (2 * TILE, 1), 0) < TILE
    row = 2 * LAYERS + 3 * layer
    for pair in range(2):
        quarter = place[0] if pair == 0 else 1 - place[0]
        lanes = slice(pair * LANES, (pair + 1) * LANES)
        queries, keys, values = qkv[0, :, lanes], qkv[1, :, lanes], qkv[2, :, lanes]
        grads = d_mixed[:, lanes]
        blend = blends[row : row + 1, lanes]
        ext_keys = extend(halo[quarter, 0], keys)
        ext_values = extend(halo[quarter, 1], values)
        near_k[...] = jnp.zeros_like(near_k)
        near_v[...] = jnp.zeros_like(near_v)
        blend_rows = jnp.where(row_low, blend[:, :1], blend[:, HD : HD + 1])
        sums = None
        for tile in range(rows // TILE):
            at = slice(tile * TILE, (tile + 1) * TILE)
            window = slice(tile * TILE, tile * TILE + LANES)
            allowed = jnp.concatenate([band[at], band[at]], axis=0)
            query_split, grad_split = split_heads(queries[at]), split_heads(grads[at])
            scores = dot_nt(query_split, ext_keys[window]) * score_scale + allowed
            probs = jnp.exp(scores - jnp.max(scores, axis=1, keepdims=True))
            probs = probs / jnp.sum(probs, axis=1, keepdims=True)
            d_probs = dot_nt(grad_split, ext_values[window])
            inner = jnp.sum(probs * d_probs, axis=1, keepdims=True)
            sums = inner if sums is None else sums + inner
            d_scores = (probs * (d_probs - inner) * blend_rows).astype(bf16)
            dq_out[at, lanes] = score_scale * merge_heads(dot(d_scores, ext_keys[window]))
            near_k[window] += dot_tn(d_scores, query_split)
            near_v[window] += dot_tn(probs.astype(bf16), grad_split)
        sum_low = jnp.sum(sums[:TILE], axis=0, keepdims=True)
        sum_high = jnp.sum(sums[TILE:], axis=0, keepdims=True)
        blend_out[0:1, lanes] = jnp.where(low_lanes(1), sum_low, sum_high) * (1.0 / HD)
        dk_out[:, lanes] = score_scale * near_k[HALO : HALO + rows]
        dv_out[:, lanes] = blend * near_v[HALO : HALO + rows]
        halo_out[quarter, 0] = (score_scale * near_k[0:HALO]).astype(bf16)
        halo_out[quarter, 1] = (blend * near_v[0:HALO]).astype(bf16)


def far_back_kernel(
    place, qkv, causal, causal_t, carried, state, prefix, num_one, num_two, d_zeta, dq_near, dv_near,
    dq_out, dk_one_out, dk_two_out, dv_out,
):
    masks = jnp.concatenate([causal[...], causal[...]], axis=0)
    masks_t = jnp.concatenate([causal_t[...], causal_t[...]], axis=1)
    for pair in range(2):
        quarter = place[0] if pair == 0 else 1 - place[0]
        lanes = slice(pair * LANES, (pair + 1) * LANES)
        queries, keys, values = qkv[0, :, lanes], qkv[1, :, lanes], qkv[2, :, lanes]
        state_one, state_two, unused_total = get_state(state, quarter)
        query_one, query_two = kernel_maps(queries.astype(f32))
        key_one, key_two = kernel_maps(keys.astype(f32))
        d_values = dv_near[:, lanes]
        d_queries = []
        for query, key, num, square, out in (
            (query_one, key_one, num_one[:, lanes], state_one, dk_one_out),
            (query_two, key_two, num_two[:, lanes], state_two, dk_two_out),
        ):
            query_split, num_split = split_heads(query), split_heads(num)
            attn_t = dot_nt(key, query_split).astype(bf16) * masks_t
            grad = dot_nt(num_split, values).astype(bf16) * masks
            grad_t = dot_nt(values, num_split).astype(bf16) * masks_t
            d_values = d_values + dot(attn_t, num_split)
            d_queries.append(merge_heads(dot(grad, key)) + carried[...] * dot_nt(num, square))
            out[:, lanes] = dot(grad_t, query_split)
        zeta = d_zeta[:, lanes]
        d_queries[0] += zeta * prefix[:, lanes]
        dk_one_out[:, lanes] += dot(causal_t[...], (zeta * query_one.astype(f32)).astype(bf16))
        back = maps_back(queries.astype(f32), d_queries[0], d_queries[1])
        dq_out[:, lanes] = (back + dq_near[:, lanes]).astype(bf16)
        dv_out[:, lanes] = d_values


def qkv_back_kernel(
    layer, at, count, place, flags, qkv, dq, dk_one, dk_two, dk_near, dv, tail, halo, own, other, found, *refs
):
    got = refs[:count]
    d_qkv_out, part_out, state = refs[count:]
    last_combine(at, flags, found, got, state)
    rows = qkv.shape[1]
    empty = jnp.zeros((rows - HALO, LANES), f32)
    for pair in range(2):
        quarter = place[0] if pair == 0 else 1 - place[0]
        lanes = slice(pair * LANES, (pair + 1) * LANES)
        keys, values = qkv[1, :, lanes], qkv[2, :, lanes]
        key_one, key_two = kernel_maps(keys.astype(f32))
        state_one, state_two, total = get_state(state, quarter)
        weight = tail[...].astype(f32)
        d_one = dk_one[:, lanes] + weight * (dot_nt(values, state_one) + total)
        d_two = dk_two[:, lanes] + weight * dot_nt(values, state_two)
        halo_k = jnp.concatenate([empty, halo[quarter, 0].astype(f32)], axis=0)
        halo_v = jnp.concatenate([empty, halo[quarter, 1].astype(f32)], axis=0)
        d_qkv_out[1, :, lanes] = (
            maps_back(keys.astype(f32), d_one, d_two) + dk_near[:, lanes] + halo_k
        ).astype(bf16)
        d_qkv_out[2, :, lanes] = (
            dv[:, lanes] + weight * (dot(key_one, state_one) + dot(key_two, state_two)) + halo_v
        ).astype(bf16)
    d_qkv_out[0] = dq[...]
    total = None
    for kind in range(3):
        weight = jnp.concatenate([own[layer, kind], other[kind]], axis=1)
        product = dot_nt(d_qkv_out[kind], weight)
        total = product if total is None else total + product
    part_out[...] = total.astype(bf16)


JOB_REFS = {"up": 3, "down": 3, "out": 2, "qkv": 2}


def job_rows(job, units):
    return {"up": D, "down": units, "out": LANES, "qkv": 3 * LANES}[job]


def wide_grads_kernel(jobs, place, *refs):
    refs, (own_a, send_a, keep_b, send_b, own, far) = refs[:-6], refs[-6:]
    side = lax.rem(place[2], 2)
    at = 0
    for job in jobs:
        mine, refs = refs[: JOB_REFS[job]], refs[JOB_REFS[job] :]
        if job == "up":
            normed, grad_own, grad_far = mine
            units = grad_own.shape[1]
            piece = units // 2
            own[at : at + D] = dot_tn(normed[...], grad_own[...]).astype(bf16)
            found = dot_tn(normed[...], grad_far[...]).astype(bf16)
            turned = jnp.concatenate([found[:, piece:], found[:, :piece]], axis=1)
            far[at : at + D] = jnp.where(side == 0, found, turned)
            at += D
        elif job == "down":
            act_own, act_far, grad = mine
            units = act_own.shape[1]
            piece = units // 2
            own[at : at + units] = dot_tn(act_own[...], grad[...]).astype(bf16)
            found = dot_tn(act_far[...], grad[...]).astype(bf16)
            turned = jnp.concatenate([found[piece:], found[:piece]], axis=0)
            far[at : at + units] = jnp.where(side == 0, found, turned)
            at += units
        elif job == "out":
            mixed, grad = mine
            found = dot_tn(mixed[...], grad[...]).astype(bf16)
            own[at : at + LANES] = found[:LANES]
            far[at : at + LANES] = found[LANES:]
            at += LANES
        else:
            normed, d_qkv = mine
            for kind in range(3):
                found = dot_tn(normed[...], d_qkv[kind]).astype(bf16)
                for block in range(D // LANES):
                    lanes = slice(block * LANES, (block + 1) * LANES)
                    own[at : at + LANES, lanes] = found[lanes, :LANES]
                    far[at : at + LANES, lanes] = found[lanes, LANES:]
                at += LANES
    part, piece = at // 2, at // 4
    own_a[...] = own[:part]
    send_a[...] = far[:part]
    for k, ref in enumerate((own, far)):
        first, second = ref[part : part + piece], ref[part + piece :]
        keep_b[k * piece : (k + 1) * piece] = jnp.where(side == 0, first, second)
        send_b[k * piece : (k + 1) * piece] = jnp.where(side == 0, second, first)


def second_kernel(place, own_a, got_a, keep_b, got_b, keep_a_out, send_a_out, keep_b_out, send_b_out):
    piece = keep_a_out.shape[0]
    side = lax.rem(place[2], 2)
    total = own_a[...].astype(f32) + got_a[...].astype(f32)
    keep_a_out[...] = jnp.where(side == 0, total[:piece], total[piece:])
    send_a_out[...] = jnp.where(side == 0, total[piece:], total[:piece]).astype(bf16)
    total = keep_b[...].astype(f32) + got_b[...].astype(f32)
    keep_b_out[...] = total[:piece]
    send_b_out[...] = total[piece:].astype(bf16)


def line_bit(place, step):
    return lax.rem(lax.div(place[2], 2 * step), 2)


def give_half(place, step, total, keep_out, send_out):
    rows = total.shape[0] // 2
    low = line_bit(place, step) == 0
    keep_out[...] = jnp.where(low, total[:rows], total[rows:])
    send_out[...] = jnp.where(low, total[rows:], total[:rows]).astype(bf16)


def third_kernel(step, place, keep_a, got_a, keep_b, got_b, keep_out, send_out):
    total = jnp.concatenate([keep_a[...] + got_a[...].astype(f32), keep_b[...] + got_b[...].astype(f32)], axis=0)
    give_half(place, step, total, keep_out, send_out)


def halve_kernel(step, place, keep, got, keep_out, send_out):
    give_half(place, step, keep[...] + got[...].astype(f32), keep_out, send_out)


def add_kernel(keep, got, out):
    out[...] = (keep[...] + got[...].astype(f32)).astype(bf16)


def join_kernel(step, place, mine, got, out):
    low = line_bit(place, step) == 0
    rows = mine.shape[0]
    out[:rows] = jnp.where(low, mine[...], got[...])
    out[rows:] = jnp.where(low, got[...], mine[...])


def last_qkv_kernel(normed, d_qkv, own_out, far_out):
    for kind in range(3):
        found = dot_tn(normed[...], d_qkv[kind])
        own_out[kind * D : (kind + 1) * D] = found[:, :LANES]
        far_out[kind * D : (kind + 1) * D] = found[:, LANES:]


def end_kernel(
    shards, place, base, part_a, part_b, hidden, gains, own, far, *refs
):
    smalls, (mine_out, theirs_out, send_out) = refs[: 4 * LAYERS - 1], refs[4 * LAYERS - 1 :]
    gain_refs, blend_refs = smalls[: 2 * LAYERS - 1], smalls[2 * LAYERS - 1 :]
    back, gain = norm_back(hidden[...], gains[0:1], part_a[...].astype(f32) + part_b[...].astype(f32))
    shard_rows((base[...] + back).astype(bf16), place, mine_out, theirs_out)
    block = own.shape[0] // shards
    gain_rows = jnp.concatenate([gain] + [ref[...] for ref in gain_refs], axis=0)
    blend_rows = jnp.concatenate([ref[...] for ref in blend_refs], axis=0)
    for to in range(2):
        features = jnp.where(
            place[1] == 0,
            gain_rows[:, 2 * to * LANES : (2 * to + 1) * LANES],
            gain_rows[:, (2 * to + 1) * LANES : (2 * to + 2) * LANES],
        )
        blends = jnp.where(place[0] == to, blend_rows[:, :LANES], blend_rows[:, LANES:])
        empty = jnp.zeros((SMALL - 5 * LAYERS, LANES), f32)
        extra = jnp.concatenate([features, blends, empty], axis=0).astype(bf16)
        rows = jnp.where(place[0] == to, own[...], far[...])
        for shard in range(shards):
            send_out[2 * shard + to, :SMALL] = extra
            send_out[2 * shard + to, SMALL:] = rows[shard * block : (shard + 1) * block].astype(bf16)


def collect_kernel(shards, got, out, rest_out):
    total = jnp.sum(got[...].astype(f32), axis=0)
    rest_out[...] = total[:SMALL]
    mine = total[SMALL:].astype(bf16)
    for shard in range(shards):
        out[shard] = mine


def in_order(place, mine, other):
    side = lax.rem(place[2], 2)
    piece = mine.shape[0] // 2
    first, second = jnp.where(side == 0, mine[...], other[...]), jnp.where(side == 0, other[...], mine[...])
    return jnp.concatenate([first[:piece], second[:piece], first[piece:], second[piece:]], axis=0)


def finish_wide_kernel(groups, place, *refs):
    outs = dict(zip(("up", "down", "out"), refs[-4:-1]))
    for group, (layers, jobs) in enumerate(groups):
        whole = in_order(place, refs[2 * group], refs[2 * group + 1])
        at = 0
        for layer, job in zip(layers, jobs):
            rows = whole[at : at + job_rows(job, outs["up"].shape[2])]
            at += rows.shape[0]
            if job == "qkv":
                refs[-1][...] = rows
            else:
                outs[job][layer] = rows.astype(f32)


def finish_qkv_kernel(last, above, out):
    for kind in range(3):
        out[0, kind] = last[kind * D : (kind + 1) * D].astype(f32)
        for block in range(D // LANES):
            lanes = slice(block * LANES, (block + 1) * LANES)
            out[1, kind, lanes] = above[kind * LANES : (kind + 1) * LANES, lanes].astype(f32)


def call(body, outs, operands, scalars=0, scratch=(), scalar_outs=0, bulk=(), bulk_outs=()):
    specs = [SM] * scalars + [VM] * (len(operands) - scalars)
    out_specs = [VM] * (len(outs) - scalar_outs) + [SM] * scalar_outs
    for index in bulk:
        specs[index] = pl.BlockSpec()
    for index in bulk_outs:
        out_specs[index] = pl.BlockSpec()
    return pl.pallas_call(
        body,
        out_shape=tuple(jax.ShapeDtypeStruct(shape, kind) for shape, kind in outs),
        in_specs=specs,
        out_specs=tuple(out_specs),
        scratch_shapes=scratch,
        compiler_params=pltpu.CompilerParams(vmem_limit_bytes=24 * 2**20),
    )(*operands)


def after(value, *others):
    return lax.optimization_barrier((value, *others))[0] if others else value


def core_swap(value):
    count = lax.axis_size("mlp")
    return lax.ppermute(value, "mlp", [(i, i ^ 1) for i in range(count)])


def far_swap(value):
    count = lax.axis_size("mlp")
    return lax.ppermute(value, "mlp", [(i, i ^ 2) for i in range(count)])


def side_swap(value):
    count = lax.axis_size("seq")
    return lax.ppermute(value, "seq", [(i, i ^ 1) for i in range(count)])


def chunk_move(value, target):
    shards, parts = lax.axis_size("seq"), lax.axis_size("mlp")
    pairs = []
    for chunk in range(2 * shards):
        goal = target(chunk)
        if goal is None or not 0 <= goal < 2 * shards:
            continue
        for core in range(2):
            pairs.append(
                ((chunk // 2) * parts + (chunk % 2) * 2 + core, (goal // 2) * parts + (goal % 2) * 2 + core)
            )
    return lax.ppermute(value, AXES, pairs)


def scan(value, flags, chunks, reverse, others=lambda: ()):
    places, _ = flag_places(chunks)
    found, arrived = None, None
    for stage, (size, ways, last) in enumerate(scan_plan(chunks)):
        got = []
        for step in range(1, ways):
            if last:

                def target(chunk, step=step):
                    move = -step if reverse else step
                    return chunk + move * size if 0 <= (chunk // size) % ways + move < ways else None

            else:

                def target(chunk, step=step):
                    member = (chunk // size) % ways
                    return chunk + ((member ^ step) - member) * size

            got.append(chunk_move(value, target))
        at = places[reverse, stage]
        if last:
            return (found, tuple(got), at), arrived, value
        arrived = arrived or tuple(got)
        operands = (flags, after(value, *others()), *got) + (() if found is None else (found,))
        value, found = call(
            functools.partial(combine_kernel, at, ways, found is not None),
            ((value.shape, bf16), (value.shape, f32)),
            operands,
            1,
        )


def line_swap(value, step):
    count = lax.axis_size("seq")
    return lax.ppermute(value, "seq", [(i, i ^ (2 * step)) for i in range(count)])


def by_place(flag, mine, other):
    return jnp.where(flag == 0, mine, other), jnp.where(flag == 0, other, mine)


def per_device(inputs, lengths, valid, norm_attn, w_qkv, blend, w_out, norm_ffn, w_up, w_down, grad_out):
    shards, parts = lax.axis_size("seq"), lax.axis_size("mlp")
    shard, part = lax.axis_index("seq"), lax.axis_index("mlp")
    half, core = part // 2, part % 2
    side = shard % 2
    rows = inputs.shape[0] // 2
    chunks = 2 * shards
    units = w_up.shape[2]
    place = jnp.stack([half, core, shard]).astype(jnp.int32)

    wide = 2 * LANES
    hidden_like = ((rows, D), f32)
    low_like = ((rows, D), bf16)
    heads_like = ((rows, wide), f32)
    heads_low = ((rows, wide), bf16)
    qkv_like = ((3, rows, wide), bf16)
    state_like = ((2, STATE, LANES), bf16)
    halo_like = ((2, 2, HALO, LANES), bf16)
    ffn_like = ((rows, units), f32)
    ffn_low = ((rows, units), bf16)
    shard_like = ((rows, LANES), bf16)
    gain_like = ((1, D), f32)

    piece_like = ((rows + 3 * SMALL, LANES), bf16)
    mine, theirs = call(pack_kernel, (piece_like, piece_like), (place, blend, inputs, norm_attn, norm_ffn), 2)
    got = far_swap(theirs)
    pieces = (mine, got, core_swap(mine), core_swap(got))
    far_qkv = [far_swap(after(w_qkv[0], theirs)), None]
    far_out = [far_swap(after(w_out[0], theirs)), None]

    def up_piece(layer):
        return lax.dynamic_slice_in_dim(w_up[layer], side * (units // 2), units // 2, 1)

    def down_piece(layer):
        return lax.dynamic_slice_in_dim(w_down[layer], side * (units // 2), units // 2, 0)

    up_a, up_b, down_a, down_b = ([None] * LAYERS for _ in range(4))
    up_a[0] = far_swap(after(up_piece(0), theirs))

    before = lax.ppermute(
        valid[2 * rows - LANES :].reshape(1, LANES), "seq", [(source, source + 1) for source in range(shards - 1)]
    )
    _, flag_count = flag_places(chunks)
    causal, causal_t, band, carried, tail, flags = call(
        functools.partial(setup_kernel, chunks),
        (
            ((rows, rows), bf16),
            ((rows, rows), bf16),
            ((rows, LANES), f32),
            ((rows, LANES), f32),
            ((rows, LANES), bf16),
            ((flag_count,), f32),
        ),
        (place, lengths, valid.reshape(1, 2 * rows), before),
        2,
        scalar_outs=1,
    )

    saved = []
    base, adds = None, None
    for layer in range(LAYERS):
        outs = (hidden_like, low_like, qkv_like, state_like, halo_like)
        if layer == 0:
            hidden, normed, qkv, state, halo, gains, blends = call(
                functools.partial(qkv_kernel, True, layer),
                outs + (((SMALL, D), f32), ((SMALL, wide), f32)),
                (place, *pieces, w_qkv, far_qkv[layer], tail),
                1,
            )
        else:
            hidden, normed, qkv, state, halo = call(
                functools.partial(qkv_kernel, False, layer),
                outs,
                (place, base, *adds, gains, w_qkv, far_qkv[layer], tail),
                1,
            )
        halo = chunk_move(halo, lambda c: c + 1)
        one, two, sums = call(far_kernel, (heads_like,) * 3, (qkv, causal))
        (found, parts_got, at), arrived, _ = scan(state, flags, chunks, False, lambda: (one, halo))
        if layer == 0:
            down_a[0] = far_swap(after(down_piece(0), *arrived))
            up_b[0] = side_swap(after(up_a[0], *arrived))
            far_qkv[1] = far_swap(after(w_qkv[1], *arrived))
            down_b[0] = side_swap(down_a[0])
            far_out[1] = far_swap(after(w_out[1], *arrived))
            up_a[1] = far_swap(after(up_piece(1), *arrived))
            down_a[1] = far_swap(after(down_piece(1), *arrived))
            up_b[1] = side_swap(up_a[1])
            down_b[1] = side_swap(down_a[1])
        (near,) = call(near_kernel, (heads_like,), (place, qkv, halo, band), 1)
        if layer == 0:
            found = after(found, far_qkv[1])
        mixed, far_one, far_two, root, prefix, state, piece = call(
            functools.partial(mix_kernel, layer, at, len(parts_got)),
            (heads_low, heads_like, heads_like, heads_like, heads_like, state_like, low_like),
            (place, flags, qkv, near, one, two, sums, carried, blends, w_out, far_out[layer], found, *parts_got),
            2,
        )
        weights = (w_up, w_down, up_a[layer], down_a[layer], up_b[layer], down_b[layer])
        if layer == 0:
            hidden = after(hidden, far_out[1], up_a[1])
        middle, normed_ffn, pre_own, pre_far, act_own, act_far, piece_ffn = call(
            functools.partial(ffn_kernel, layer),
            (hidden_like, low_like, ffn_like, ffn_like, ffn_low, ffn_low, low_like),
            (hidden, piece, core_swap(piece), gains, *weights),
        )
        saved.append(
            (hidden, normed, qkv, state, halo, mixed, far_one, far_two, root, prefix, middle, normed_ffn,
             weights, pre_own, pre_far, act_own, act_far)
        )
        base, adds = middle, (piece_ffn, core_swap(piece_ffn))
        if layer == 0:
            base = after(base, down_a[1])
    out_mine, out_theirs = call(output_kernel, (shard_like, shard_like), (place, base, *adds), 1)
    output = jnp.concatenate(by_place(half, out_mine, far_swap(out_theirs)))

    mine, theirs = call(pack_grad_kernel, (shard_like, shard_like), (place, after(grad_out, saved[0][2])), 1)
    got = far_swap(theirs)
    grad_pieces = (mine, got, core_swap(mine), core_swap(got))

    base, adds = None, None
    d_gain_attn, d_gain_ffn, d_blends = [None] * LAYERS, [None] * LAYERS, [None] * LAYERS
    d_qkvs = [None] * LAYERS
    first_steps = []

    def first_step(jobs, operands):
        height = sum(job_rows(job, units) for job in jobs)
        outs = tuple(((height // 2, D), bf16) for _ in range(4))
        scratch = (pltpu.VMEM((height, D), bf16), pltpu.VMEM((height, D), bf16))
        return call(
            functools.partial(wide_grads_kernel, jobs), outs, (place, *operands), 1, scratch=scratch, bulk_outs=(0, 2)
        )

    def second_step(layers, jobs, own_a, send_a, keep_b, send_b, *others):
        height = own_a.shape[0] // 2
        got_a, got_b = far_swap(send_a), side_swap(send_b)
        return call(
            second_kernel,
            (((height, D), f32), ((height, D), bf16)) * 2,
            (place, own_a, after(got_a, *others), keep_b, got_b),
            1,
            bulk=(1, 3),
            bulk_outs=(0, 2),
        )

    line = [1 << k for k in range((shards // 2).bit_length() - 1)]

    def third_step(keep_a, send_a, keep_b, send_b, *others):
        height = keep_a.shape[0]
        got_a, got_b = side_swap(send_a), far_swap(send_b)
        keep, send = call(
            functools.partial(third_kernel, line[0]),
            (((height, D), f32), ((height, D), bf16)),
            (place, keep_a, after(got_a, *others), keep_b, got_b),
            1,
            bulk=(1, 3),
        )
        for place_at, step in enumerate(line):
            got = line_swap(send, step)
            if place_at + 1 == len(line):
                (value,) = call(add_kernel, (((height, D), bf16),), (keep, got))
                break
            height //= 2
            keep, send = call(
                functools.partial(halve_kernel, line[place_at + 1]),
                (((height, D), f32), ((height, D), bf16)),
                (place, keep, got),
                1,
            )
        for step in reversed(line):
            height *= 2
            (value,) = call(
                functools.partial(join_kernel, step),
                (((height, D), bf16),),
                (place, value, line_swap(value, step)),
                1,
            )
        return value, side_swap(value)

    for layer in reversed(range(LAYERS)):
        (hidden, normed, qkv, state, halo, mixed, far_one, far_two, root, prefix, middle, normed_ffn,
         weights, pre_own, pre_far, act_own, act_far) = saved[layer]
        outs = (hidden_like, low_like, ffn_low, ffn_low, low_like)
        if base is None:
            resid, grad_rows, d_up_own, d_up_far, piece = call(
                functools.partial(ffn_back_kernel, True, layer),
                outs,
                (place, *grad_pieces, *weights, pre_own, pre_far),
                1,
            )
        else:
            resid, grad_rows, d_up_own, d_up_far, piece, d_gain_attn[layer + 1] = call(
                functools.partial(ffn_back_kernel, False, layer),
                outs + (gain_like,),
                (base, *adds, saved[layer + 1][0], gains, *weights, pre_own, pre_far),
            )
        (resid, out_rows, d_mixed, d_gain_ffn[layer], num_one, num_two, d_zeta, state_back, blend_far) = call(
            functools.partial(mix_back_kernel, layer),
            (hidden_like, low_like, heads_low, gain_like, heads_low, heads_low, heads_like, state_like,
             ((2, wide), f32)),
            (place, resid, piece, core_swap(piece), middle, gains, w_out, far_out[layer], qkv, far_one, far_two,
             root, carried, blends),
            1,
        )
        ext = HALO + rows + HALO
        dq_near, dk_near, dv_near, halo_back, blend_near = call(
            functools.partial(near_back_kernel, layer),
            (heads_like, heads_like, heads_like, halo_like, ((1, wide), f32)),
            (place, qkv, halo, band, d_mixed, blends),
            1,
            scratch=(pltpu.VMEM((ext, LANES), f32), pltpu.VMEM((ext, LANES), f32)),
        )
        halo_back = chunk_move(halo_back, lambda c: c - 1)
        (found, parts_got, at), arrived, value = scan(state_back, flags, chunks, True, lambda: (dq_near,))
        ready = [value]
        if layer + 1 == LAYERS:
            jobs = ("up", "down", "out")
            operands = (after(normed_ffn, value), d_up_own, d_up_far, act_own, act_far, grad_rows, mixed, out_rows)
            groups = [((layer,) * 3, jobs, operands)]
        else:
            second = second_step(*first_steps[0], value)
            above = saved[layer + 1][1]
            groups = [
                (
                    (layer + 1, layer),
                    ("qkv", "up"),
                    (after(above, second[1], value), d_qkvs[layer + 1], normed_ffn, d_up_own, d_up_far),
                ),
                (
                    (layer, layer),
                    ("down", "out"),
                    (after(act_own, second[1], value), act_far, grad_rows, mixed, out_rows),
                ),
            ]
        for layers, jobs, operands in groups:
            first_steps.append((layers, jobs, *first_step(jobs, operands)))
            ready.append(first_steps[-1][3])
        dq, dk_one, dk_two, dv = call(
            far_back_kernel,
            (heads_low, heads_like, heads_like, heads_like),
            (place, qkv, causal, causal_t, carried, state, prefix, after(num_one, *ready), num_two, d_zeta, dq_near,
             dv_near),
            1,
        )
        d_qkvs[layer], piece = call(
            functools.partial(qkv_back_kernel, layer, at, len(parts_got)),
            (qkv_like, low_like),
            (place, flags, qkv, dq, dk_one, dk_two, dk_near, dv, tail, halo_back, w_qkv, far_qkv[layer], found,
             *parts_got),
            2,
            scratch=(pltpu.VMEM((2, STATE, LANES), bf16),),
        )
        base, adds = resid, (piece, core_swap(piece))
        d_blends[layer] = (blend_near, blend_far)

    last_like = ((3 * D, LANES), f32)
    own, far = call(last_qkv_kernel, (last_like, last_like), (saved[0][1], d_qkvs[0]))
    block = 3 * D // shards
    smalls = d_gain_attn[1:] + d_gain_ffn + [ref for pair in d_blends for ref in pair]
    mine, theirs, send = call(
        functools.partial(end_kernel, shards),
        (shard_like, shard_like, ((chunks, SMALL + block, LANES), bf16)),
        (place, base, *adds, saved[0][0], gains, own, far, *smalls),
        1,
    )
    groups = [[s * parts + h * 2 + c for s in range(shards) for h in range(2)] for c in range(2)]
    got = lax.all_to_all(send, AXES, 0, 0, axis_index_groups=groups, tiled=True)
    spread, rest = call(
        functools.partial(collect_kernel, shards),
        (((shards, block, LANES), bf16), ((SMALL, LANES), f32)),
        (got,),
    )
    last = lax.all_to_all(spread, "seq", 0, 0, tiled=True).reshape(3 * D, LANES)
    d_inputs = jnp.concatenate(by_place(half, mine, far_swap(theirs)))

    wide_sums = [third_step(*second, d_qkvs[0])]
    for step in first_steps[1:]:
        wide_sums.append(third_step(*second_step(*step, d_qkvs[0])))
    plan = [(step[0], step[1]) for step in first_steps]
    count = 2 * LAYERS + 3 * LAYERS
    d_norm_attn = rest[:LAYERS]
    d_norm_ffn = rest[LAYERS : 2 * LAYERS]
    d_blend = jnp.sum(rest[2 * LAYERS : count].reshape(LAYERS, 3, 2, HD), axis=3)
    d_up, d_down, d_out, above = call(
        functools.partial(finish_wide_kernel, plan),
        (((LAYERS, D, units), f32), ((LAYERS, units, D), f32), ((LAYERS, LANES, D), f32), ((3 * LANES, D), bf16)),
        (place, *[ref for pair in wide_sums for ref in pair]),
        1,
    )
    (d_qkv,) = call(finish_qkv_kernel, (((LAYERS, 3, D, LANES), f32),), (last, above))
    return (output, d_inputs, d_norm_attn, d_qkv, d_blend, d_out, d_norm_ffn, d_up, d_down)


def solution(mesh):
    placed = (
        P("seq", "mlp"),
        P(),
        P("seq"),
        P(None, "mlp"),
        P(None, None, None, "mlp"),
        P(None, None, "mlp"),
        P(None, "mlp", None),
        P(None, "mlp"),
        P(None, None, "mlp"),
        P(None, "mlp", None),
        P("seq", "mlp"),
    )
    return jax.shard_map(
        per_device,
        mesh=mesh,
        in_specs=placed,
        out_specs=(
            P("seq", "mlp"),
            P("seq", "mlp"),
            P(None, "mlp"),
            P(None, None, None, "mlp"),
            P(None, None, "mlp"),
            P(None, "mlp", None),
            P(None, "mlp"),
            P(None, None, "mlp"),
            P(None, "mlp", None),
        ),
        check_vma=False,
    )
```

```python
import functools
import math

import jax
import jax.numpy as jnp
from jax import lax
from jax.experimental import pallas as pl
from jax.experimental.pallas import tpu as pltpu
from jax.sharding import PartitionSpec as P

HD = 64
D = 512
BAND = 30
LAYERS = 2
HALO = 32
TILE = 64
LANES = 128
STATE = 144
SMALL = 16
AXES = ("seq", "mlp")

epsilon = 1e-05
masked_score = -1e30
score_scale = 1.0 / math.sqrt(HD)
far_scale = 1.0 / math.sqrt(HD)
f32 = jnp.float32
bf16 = jnp.bfloat16

VM = pl.BlockSpec(memory_space=pltpu.VMEM)
SM = pl.BlockSpec(memory_space=pltpu.SMEM)


def dot(x, y):
    return jnp.dot(x, y, preferred_element_type=f32)


def dot_nt(x, y):
    return lax.dot_general(x, y, (((1,), (1,)), ((), ())), preferred_element_type=f32)


def dot_tn(x, y):
    return lax.dot_general(x, y, (((0,), (0,)), ((), ())), preferred_element_type=f32)


def low_lanes(rows):
    return lax.broadcasted_iota(jnp.int32, (rows, LANES), 1) < HD


def split_heads(x):
    low = low_lanes(x.shape[0])
    zero = jnp.zeros_like(x)
    return jnp.concatenate([jnp.where(low, x, zero), jnp.where(low, zero, x)], axis=0)


def merge_heads(y):
    rows = y.shape[0] // 2
    return jnp.where(low_lanes(rows), y[:rows], y[rows:])


def head_sum(x):
    row = lax.broadcasted_iota(jnp.int32, (LANES, LANES), 0) < HD
    ones = jnp.where(row == low_lanes(LANES), 1.0, 0.0).astype(bf16)
    high = x.astype(bf16)
    rest = (x - high.astype(f32)).astype(bf16)
    return dot(high, ones) + dot(rest, ones)


def kernel_maps(x):
    return (
        jnp.where(x > 0, x + 1.0, jnp.exp(jnp.minimum(x, 0.0))).astype(bf16),
        jnp.tanh(x).astype(bf16),
    )


def maps_back(x, d_one, d_two):
    tanh = jnp.tanh(x)
    return jnp.where(x > 0, 1.0, jnp.exp(jnp.minimum(x, 0.0))) * d_one + (1.0 - tanh * tanh) * d_two


def put_state(ref, quarter, one, two, total):
    row = lax.broadcasted_iota(jnp.int32, (STATE - 2 * HD, LANES), 0)
    low = low_lanes(HD)
    ref[quarter, 0:HD, :] = jnp.where(low, one[:HD], one[HD:]).astype(bf16)
    ref[quarter, HD : 2 * HD, :] = jnp.where(low, two[:HD], two[HD:]).astype(bf16)
    ref[quarter, 2 * HD : STATE, :] = jnp.where(row == 0, total, 0.0).astype(bf16)


def get_state(ref, quarter):
    one = split_heads(ref[quarter, 0:HD, :])
    two = split_heads(ref[quarter, HD : 2 * HD, :])
    total = ref[quarter, 2 * HD : STATE, :].astype(f32)[0:1]
    return one, two, total


def norm_scale(hidden):
    return lax.rsqrt(jnp.sum(hidden * hidden, axis=1, keepdims=True) * (1.0 / D) + epsilon)


def norm_back(hidden, gain, grad):
    scale = norm_scale(hidden)
    gained = grad * gain
    inner = jnp.sum(gained * hidden, axis=1, keepdims=True) * (1.0 / D)
    back = scale * gained - hidden * (scale * scale * scale * inner)
    return back, jnp.sum(grad * hidden * scale, axis=0, keepdims=True)


def extend(halo, rows):
    return jnp.concatenate([halo, rows, jnp.zeros((HALO, LANES), bf16)], axis=0)


def three_parts(value):
    high = value.astype(bf16)
    rest = value - high.astype(f32)
    middle = rest.astype(bf16)
    low = (rest - middle.astype(f32)).astype(bf16)
    return jnp.concatenate([high, middle, low], axis=0)


def pack_kernel(place, blend, inputs, norm_attn, norm_ffn, mine_out, theirs_out):
    rows = inputs.shape[0] // 2
    low = low_lanes(1)
    small = [norm_attn[...], norm_ffn[...]]
    for layer in range(LAYERS):
        for kind in range(3):
            small.append(jnp.where(low, blend[layer, kind, 0], blend[layer, kind, 1]))
    small.append(jnp.zeros((SMALL - 5 * LAYERS, LANES), f32))
    small = three_parts(jnp.concatenate(small, axis=0))
    first, second = inputs[:rows], inputs[rows:]
    mine_out[:rows] = jnp.where(place[0] == 0, first, second)
    theirs_out[:rows] = jnp.where(place[0] == 0, second, first)
    mine_out[rows:] = small
    theirs_out[rows:] = small


def pack_grad_kernel(place, grads, mine_out, theirs_out):
    rows = grads.shape[0] // 2
    first, second = grads[:rows], grads[rows:]
    mine_out[...] = jnp.where(place[0] == 0, first, second)
    theirs_out[...] = jnp.where(place[0] == 0, second, first)


def quarters(place):
    half, part = place[0], place[1]
    return 2 * part + half, 2 * part + 1 - half, 2 * (1 - part) + half, 2 * (1 - part) + 1 - half


def quarter_lanes(quarter):
    return pl.ds(pl.multiple_of(quarter * LANES, LANES), LANES)


def item_ends(lengths):
    ends = []
    for k in range(lengths.shape[0]):
        ends.append(lengths[k] if k == 0 else ends[-1] + lengths[k])
    return ends


def item_start(lengths, ends, positions):
    start = jnp.zeros_like(positions)
    for k, end in enumerate(ends):
        start = start + jnp.where(end <= positions, lengths[k], 0)
    return start


def scan_plan(chunks):
    stages, size = [], 1
    while size < chunks:
        ways = min(4, chunks // size)
        stages.append((size, ways, size * ways >= chunks))
        size *= ways
    return stages


def flag_places(chunks):
    at, places = 0, {}
    for reverse in (False, True):
        for stage, (_, ways, _) in enumerate(scan_plan(chunks)):
            places[reverse, stage] = at
            at += 2 * ways
    return places, at


def setup_kernel(chunks, place, lengths, valid, before, causal_out, causal_t_out, band_out, carried_out, tail_out, flags_out):
    rows = causal_out.shape[0]
    chunk = place[2] * 2 + place[0]
    first_row = chunk * rows
    ends = item_ends(lengths)

    def start_of(positions):
        return item_start(lengths, ends, positions)

    lane = lax.broadcasted_iota(jnp.int32, (1, rows), 1)
    starts_row = start_of(first_row + lane)
    starts = start_of(first_row + lax.broadcasted_iota(jnp.int32, (rows, LANES), 0))
    both = jnp.concatenate([starts, starts], axis=1)
    words = valid[...]
    own_words = jnp.where(place[0] == 0, words[:, :rows], words[:, rows:])
    last_words = jnp.where(place[0] == 0, before[...], words[:, rows - LANES : rows])
    row_at = lax.broadcasted_iota(jnp.int32, (rows, rows), 0)
    lane_at = lax.broadcasted_iota(jnp.int32, (rows, rows), 1)
    own_column = jnp.sum(jnp.where(row_at == lane_at, own_words, 0), axis=1, keepdims=True)
    same = both == starts_row
    causal_out[...] = jnp.where((lane_at <= row_at) & same & (own_words == 1), 1.0, 0.0).astype(bf16)
    causal_t_out[...] = jnp.where((row_at <= lane_at) & same & (own_column == 1), 1.0, 0.0).astype(bf16)
    carried_out[...] = jnp.where(starts < first_row, 1.0, 0.0)
    last_start = start_of(first_row + rows - 1)
    tail_out[...] = jnp.where((starts == last_start) & (own_column == 1), 1.0, 0.0).astype(bf16)
    all_words = jnp.concatenate([last_words, own_words, jnp.zeros((1, LANES), jnp.int32)], axis=1)
    tile_row = lax.broadcasted_iota(jnp.int32, (TILE, LANES), 0)
    tile_lane = lax.broadcasted_iota(jnp.int32, (TILE, LANES), 1)
    gap = tile_row + HALO - tile_lane
    for tile in range(rows // TILE):
        key_starts = start_of(first_row + tile * TILE - HALO + lax.broadcasted_iota(jnp.int32, (1, LANES), 1))
        offset = LANES - HALO + tile * TILE
        key_words = all_words[:, offset : offset + LANES]
        at = slice(tile * TILE, (tile + 1) * TILE)
        allowed = (gap >= 0) & (gap <= BAND) & (starts[at] == key_starts) & ((key_words == 1) | (gap == 0))
        band_out[at] = jnp.where(allowed, 0.0, masked_score)

    places, _ = flag_places(chunks)
    for reverse in (False, True):
        edge = start_of(first_row + (rows - 1 if reverse else 0))
        for stage, (size, ways, last) in enumerate(scan_plan(chunks)):
            member = lax.rem(lax.div(chunk, size), ways)
            base = chunk - member * size - lax.rem(chunk, size)
            group = base if reverse else base + ways * size - 1
            group = start_of(group * rows + (0 if reverse else rows - 1))
            for step in range(ways):
                if last:
                    other = member + step if reverse else member - step
                else:
                    other = jnp.bitwise_xor(member, step)
                block = base + other * size + (0 if reverse else size - 1)
                start = start_of(block * rows + (0 if reverse else rows - 1))
                ahead = (other > member) if reverse else (other < member)
                ahead = ahead & (other >= 0) & (other < ways)
                at = places[reverse, stage] + 2 * step
                flags_out[at] = jnp.where(ahead & (start == edge), 1.0, 0.0)
                flags_out[at + 1] = jnp.where(start == group, 1.0, 0.0)


def combine_kernel(at, ways, has_found, flags, *refs):
    got, refs = refs[:ways], refs[ways:]
    total = sum(flags[at + 2 * step + 1] * got[step][...].astype(f32) for step in range(ways))
    refs[-2][...] = total.astype(bf16)
    found = sum(flags[at + 2 * step] * got[step][...].astype(f32) for step in range(1, ways))
    refs[-1][...] = found + refs[0][...] if has_found else found


def last_combine(at, flags, found, got, out):
    value = found[...]
    for step, part in enumerate(got):
        value = value + flags[at + 2 * (step + 1)] * part[...].astype(f32)
    out[...] = value.astype(bf16)


def qkv_kernel(first, layer, place, *refs):
    if first:
        refs, outs = refs[:7], refs[7:]
        pieces, (own, other, tail) = refs[:4], refs[4:]
        hidden_out, normed_out, qkv_out, state_out, halo_out, gains, blends_out = outs
        rows = hidden_out.shape[0]
        for index, (piece, quarter) in enumerate(zip(pieces, quarters(place))):
            hidden_out[:, quarter_lanes(quarter)] = piece[:rows].astype(f32)
            parts = piece[rows:].astype(f32)
            small = parts[:SMALL] + parts[SMALL : 2 * SMALL] + parts[2 * SMALL :]
            gains[:, quarter_lanes(quarter)] = small
            if index < 2:
                blends_out[:, index * LANES : (index + 1) * LANES] = small
        hidden = hidden_out[...]
    else:
        base, part_a, part_b, gains, own, other, tail, hidden_out, normed_out, qkv_out, state_out, halo_out = refs
        hidden = base[...] + (part_a[...].astype(f32) + part_b[...].astype(f32))
        hidden_out[...] = hidden
    rows = hidden.shape[0]
    normed = (hidden * norm_scale(hidden) * gains[layer : layer + 1]).astype(bf16)
    normed_out[...] = normed
    found = []
    for kind in range(3):
        weight = jnp.concatenate([own[layer, kind], other[kind]], axis=1)
        found.append(dot(normed, weight).astype(bf16))
        qkv_out[kind] = found[kind]
    for pair in range(2):
        quarter = place[0] if pair == 0 else 1 - place[0]
        lanes = slice(pair * LANES, (pair + 1) * LANES)
        keys, values = found[1][:, lanes], found[2][:, lanes]
        one, two = kernel_maps(keys.astype(f32))
        one, two = one * tail[...], two * tail[...]
        put_state(
            state_out,
            quarter,
            dot_tn(one, values),
            dot_tn(two, values),
            jnp.sum(one.astype(f32), axis=0, keepdims=True),
        )
        halo_out[quarter, 0] = keys[rows - HALO :]
        halo_out[quarter, 1] = values[rows - HALO :]


def far_kernel(qkv, causal, one_out, two_out, sums_out):
    masks = jnp.concatenate([causal[...], causal[...]], axis=0)
    for pair in range(2):
        lanes = slice(pair * LANES, (pair + 1) * LANES)
        queries, keys, values = qkv[0, :, lanes], qkv[1, :, lanes], qkv[2, :, lanes]
        maps_q, maps_k = kernel_maps(queries.astype(f32)), kernel_maps(keys.astype(f32))
        for query, key, out in ((maps_q[0], maps_k[0], one_out), (maps_q[1], maps_k[1], two_out)):
            attn = dot_nt(split_heads(query), key).astype(bf16) * masks
            out[:, lanes] = merge_heads(dot(attn, values))
        sums_out[:, lanes] = dot(causal[...], maps_k[0])


def near_kernel(place, qkv, halo, band, near_out):
    rows = qkv.shape[1]
    for pair in range(2):
        quarter = place[0] if pair == 0 else 1 - place[0]
        lanes = slice(pair * LANES, (pair + 1) * LANES)
        queries, keys, values = qkv[0, :, lanes], qkv[1, :, lanes], qkv[2, :, lanes]
        ext_keys = extend(halo[quarter, 0], keys)
        ext_values = extend(halo[quarter, 1], values)
        for tile in range(rows // TILE):
            at = slice(tile * TILE, (tile + 1) * TILE)
            window = slice(tile * TILE, tile * TILE + LANES)
            allowed = jnp.concatenate([band[at], band[at]], axis=0)
            scores = dot_nt(split_heads(queries[at]), ext_keys[window]) * score_scale + allowed
            weights = jnp.exp(scores - jnp.max(scores, axis=1, keepdims=True))
            weights = weights / jnp.sum(weights, axis=1, keepdims=True)
            near_out[at, lanes] = merge_heads(dot(weights.astype(bf16), ext_values[window]))


def mix_kernel(layer, at, count, place, flags, qkv, near, one, two, sums, carried, blends, own, other, found, *refs):
    got = refs[:count]
    mixed_out, far_one_out, far_two_out, root_out, prefix_out, state, part_out = refs[count:]
    last_combine(at, flags, found, got, state)
    mixed = []
    row = 2 * LAYERS + 3 * layer
    for pair in range(2):
        quarter = place[0] if pair == 0 else 1 - place[0]
        lanes = slice(pair * LANES, (pair + 1) * LANES)
        query_one, query_two = kernel_maps(qkv[0, :, lanes].astype(f32))
        state_one, state_two, total = get_state(state, quarter)
        num_one = one[:, lanes] + carried[...] * dot(query_one, state_one)
        num_two = two[:, lanes] + carried[...] * dot(query_two, state_two)
        prefix = sums[:, lanes] + carried[...] * total
        zeta = head_sum(query_one.astype(f32) * prefix)
        root = lax.rsqrt(zeta + 1.0)
        far_one = num_one * root * far_scale
        far_two = num_two * root
        far_one_out[:, lanes] = far_one
        far_two_out[:, lanes] = far_two
        root_out[:, lanes] = root
        prefix_out[:, lanes] = prefix
        mixed.append(
            (
                blends[row : row + 1, lanes] * near[:, lanes]
                + blends[row + 1 : row + 2, lanes] * far_one
                + blends[row + 2 : row + 3, lanes] * far_two
            ).astype(bf16)
        )
        mixed_out[:, lanes] = mixed[pair]
    weight = jnp.concatenate([own[layer], other[...]], axis=0)
    part_out[...] = dot(jnp.concatenate(mixed, axis=1), weight).astype(bf16)


def ffn_kernel(
    layer, base, part_a, part_b, gains, up_own, down_own, up_far, down_far,
    middle_out, normed_out, pre_own_out, pre_far_out, act_own_out, act_far_out, part_out,
):
    middle = base[...] + (part_a[...].astype(f32) + part_b[...].astype(f32))
    middle_out[...] = middle
    gain = gains[LAYERS + layer : LAYERS + layer + 1]
    normed = (middle * norm_scale(middle) * gain).astype(bf16)
    normed_out[...] = normed
    weights = (
        (up_own[layer], down_own[layer], pre_own_out, act_own_out),
        (up_far[...], down_far[...], pre_far_out, act_far_out),
    )
    total = None
    for up, down, pre_out, act_out in weights:
        pre = dot(normed, up)
        pre_out[...] = pre
        inner = jnp.tanh(math.sqrt(2.0 / math.pi) * (pre + 0.044715 * pre * pre * pre))
        act = (0.5 * pre * (1.0 + inner)).astype(bf16)
        act_out[...] = act
        product = dot(act, down)
        total = product if total is None else total + product
    part_out[...] = total.astype(bf16)


def shard_rows(whole, place, mine_out, theirs_out):
    first = [whole[:, m * LANES : (m + 1) * LANES] for m in range(4)]
    even, odd = [jnp.where(place[1] == 0, first[h], first[2 + h]) for h in range(2)]
    mine_out[...] = jnp.where(place[0] == 0, even, odd)
    theirs_out[...] = jnp.where(place[0] == 0, odd, even)


def output_kernel(place, base, part_a, part_b, mine_out, theirs_out):
    whole = base[...] + (part_a[...].astype(f32) + part_b[...].astype(f32))
    shard_rows(whole.astype(bf16), place, mine_out, theirs_out)


def gelu_slope(pre):
    c = math.sqrt(2.0 / math.pi)
    inner = jnp.tanh(c * (pre + 0.044715 * pre * pre * pre))
    return 0.5 * (1.0 + inner) + 0.5 * pre * (1.0 - inner * inner) * (c * (1.0 + 3 * 0.044715 * pre * pre))


def ffn_back_kernel(first, layer, *refs):
    if first:
        place, *refs = refs
        pieces, refs = refs[:4], refs[4:]
        weights, outs = refs[:6], refs[6:]
        resid_out, rows_out, d_up_own_out, d_up_far_out, part_out = outs
        for piece, quarter in zip(pieces, quarters(place)):
            resid_out[:, quarter_lanes(quarter)] = piece[...].astype(f32)
        resid = resid_out[...]
    else:
        base, part_a, part_b, hidden, gains, *refs = refs
        weights, outs = refs[:6], refs[6:]
        resid_out, rows_out, d_up_own_out, d_up_far_out, part_out, gain_out = outs
        back, gain_out[...] = norm_back(
            hidden[...], gains[layer + 1 : layer + 2], part_a[...].astype(f32) + part_b[...].astype(f32)
        )
        resid = base[...] + back
        resid_out[...] = resid
    up_own, down_own, up_far, down_far, pre_own, pre_far = weights
    rows = resid.astype(bf16)
    rows_out[...] = rows
    total = None
    for up, down, pre, out in (
        (up_own[layer], down_own[layer], pre_own, d_up_own_out),
        (up_far[...], down_far[...], pre_far, d_up_far_out),
    ):
        d_up = (gelu_slope(pre[...]) * dot_nt(rows, down)).astype(bf16)
        out[...] = d_up
        product = dot_nt(d_up, up)
        total = product if total is None else total + product
    part_out[...] = total.astype(bf16)


def mix_back_kernel(
    layer, place, base, part_a, part_b, middle, gains, own, other, qkv, far_one, far_two, root, carried, blends,
    resid_out, rows_out, mixed_out, gain_out, num_one_out, num_two_out, zeta_out, state_out, blend_out,
):
    back, gain_out[...] = norm_back(
        middle[...],
        gains[LAYERS + layer : LAYERS + layer + 1],
        part_a[...].astype(f32) + part_b[...].astype(f32),
    )
    resid = base[...] + back
    resid_out[...] = resid
    blend = blends[2 * LAYERS + 3 * layer : 2 * LAYERS + 3 * layer + 3]
    rows = resid.astype(bf16)
    rows_out[...] = rows
    weight = jnp.concatenate([own[layer], other[...]], axis=0)
    d_mixed = dot_nt(rows, weight).astype(bf16)
    mixed_out[...] = d_mixed
    for pair in range(2):
        quarter = place[0] if pair == 0 else 1 - place[0]
        lanes = slice(pair * LANES, (pair + 1) * LANES)
        grad = d_mixed[:, lanes].astype(f32)
        scale = root[:, lanes]
        dot_one = grad * far_one[:, lanes]
        dot_two = grad * far_two[:, lanes]
        blend_one, blend_two = blend[1:2, lanes], blend[2:3, lanes]
        blend_out[0:1, lanes] = jnp.sum(dot_one, axis=0, keepdims=True)
        blend_out[1:2, lanes] = jnp.sum(dot_two, axis=0, keepdims=True)
        num_one = (grad * (blend_one * far_scale) * scale).astype(bf16)
        num_two = (grad * blend_two * scale).astype(bf16)
        d_zeta = head_sum(blend_one * dot_one + blend_two * dot_two) * (-0.5 * scale * scale)
        num_one_out[:, lanes] = num_one
        num_two_out[:, lanes] = num_two
        zeta_out[:, lanes] = d_zeta
        query_one, query_two = kernel_maps(qkv[0, :, lanes].astype(f32))
        reach = carried[...].astype(bf16)
        put_state(
            state_out,
            quarter,
            dot_tn(query_one * reach, num_one),
            dot_tn(query_two * reach, num_two),
            jnp.sum(carried[...] * d_zeta * query_one.astype(f32), axis=0, keepdims=True),
        )


def near_back_kernel(
    layer, place, qkv, halo, band, d_mixed, blends, dq_out, dk_out, dv_out, halo_out, blend_out, near_k, near_v
):
    rows = qkv.shape[1]
    row_low = lax.broadcasted_iota(jnp.int32, (2 * TILE, 1), 0) < TILE
    row = 2 * LAYERS + 3 * layer
    for pair in range(2):
        quarter = place[0] if pair == 0 else 1 - place[0]
        lanes = slice(pair * LANES, (pair + 1) * LANES)
        queries, keys, values = qkv[0, :, lanes], qkv[1, :, lanes], qkv[2, :, lanes]
        grads = d_mixed[:, lanes]
        blend = blends[row : row + 1, lanes]
        ext_keys = extend(halo[quarter, 0], keys)
        ext_values = extend(halo[quarter, 1], values)
        near_k[...] = jnp.zeros_like(near_k)
        near_v[...] = jnp.zeros_like(near_v)
        blend_rows = jnp.where(row_low, blend[:, :1], blend[:, HD : HD + 1])
        sums = None
        for tile in range(rows // TILE):
            at = slice(tile * TILE, (tile + 1) * TILE)
            window = slice(tile * TILE, tile * TILE + LANES)
            allowed = jnp.concatenate([band[at], band[at]], axis=0)
            query_split, grad_split = split_heads(queries[at]), split_heads(grads[at])
            scores = dot_nt(query_split, ext_keys[window]) * score_scale + allowed
            probs = jnp.exp(scores - jnp.max(scores, axis=1, keepdims=True))
            probs = probs / jnp.sum(probs, axis=1, keepdims=True)
            d_probs = dot_nt(grad_split, ext_values[window])
            inner = jnp.sum(probs * d_probs, axis=1, keepdims=True)
            sums = inner if sums is None else sums + inner
            d_scores = (probs * (d_probs - inner) * blend_rows).astype(bf16)
            dq_out[at, lanes] = score_scale * merge_heads(dot(d_scores, ext_keys[window]))
            near_k[window] += dot_tn(d_scores, query_split)
            near_v[window] += dot_tn(probs.astype(bf16), grad_split)
        sum_low = jnp.sum(sums[:TILE], axis=0, keepdims=True)
        sum_high = jnp.sum(sums[TILE:], axis=0, keepdims=True)
        blend_out[0:1, lanes] = jnp.where(low_lanes(1), sum_low, sum_high) * (1.0 / HD)
        dk_out[:, lanes] = score_scale * near_k[HALO : HALO + rows]
        dv_out[:, lanes] = blend * near_v[HALO : HALO + rows]
        halo_out[quarter, 0] = (score_scale * near_k[0:HALO]).astype(bf16)
        halo_out[quarter, 1] = (blend * near_v[0:HALO]).astype(bf16)


def far_back_kernel(
    place, qkv, causal, causal_t, carried, state, prefix, num_one, num_two, d_zeta, dq_near, dv_near,
    dq_out, dk_one_out, dk_two_out, dv_out,
):
    masks = jnp.concatenate([causal[...], causal[...]], axis=0)
    masks_t = jnp.concatenate([causal_t[...], causal_t[...]], axis=1)
    for pair in range(2):
        quarter = place[0] if pair == 0 else 1 - place[0]
        lanes = slice(pair * LANES, (pair + 1) * LANES)
        queries, keys, values = qkv[0, :, lanes], qkv[1, :, lanes], qkv[2, :, lanes]
        state_one, state_two, unused_total = get_state(state, quarter)
        query_one, query_two = kernel_maps(queries.astype(f32))
        key_one, key_two = kernel_maps(keys.astype(f32))
        d_values = dv_near[:, lanes]
        d_queries = []
        for query, key, num, square, out in (
            (query_one, key_one, num_one[:, lanes], state_one, dk_one_out),
            (query_two, key_two, num_two[:, lanes], state_two, dk_two_out),
        ):
            query_split, num_split = split_heads(query), split_heads(num)
            attn_t = dot_nt(key, query_split).astype(bf16) * masks_t
            grad = dot_nt(num_split, values).astype(bf16) * masks
            grad_t = dot_nt(values, num_split).astype(bf16) * masks_t
            d_values = d_values + dot(attn_t, num_split)
            d_queries.append(merge_heads(dot(grad, key)) + carried[...] * dot_nt(num, square))
            out[:, lanes] = dot(grad_t, query_split)
        zeta = d_zeta[:, lanes]
        d_queries[0] += zeta * prefix[:, lanes]
        dk_one_out[:, lanes] += dot(causal_t[...], (zeta * query_one.astype(f32)).astype(bf16))
        back = maps_back(queries.astype(f32), d_queries[0], d_queries[1])
        dq_out[:, lanes] = (back + dq_near[:, lanes]).astype(bf16)
        dv_out[:, lanes] = d_values


def qkv_back_kernel(
    layer, at, count, place, flags, qkv, dq, dk_one, dk_two, dk_near, dv, tail, halo, own, other, found, *refs
):
    got = refs[:count]
    d_qkv_out, part_out, state = refs[count:]
    last_combine(at, flags, found, got, state)
    rows = qkv.shape[1]
    empty = jnp.zeros((rows - HALO, LANES), f32)
    for pair in range(2):
        quarter = place[0] if pair == 0 else 1 - place[0]
        lanes = slice(pair * LANES, (pair + 1) * LANES)
        keys, values = qkv[1, :, lanes], qkv[2, :, lanes]
        key_one, key_two = kernel_maps(keys.astype(f32))
        state_one, state_two, total = get_state(state, quarter)
        weight = tail[...].astype(f32)
        d_one = dk_one[:, lanes] + weight * (dot_nt(values, state_one) + total)
        d_two = dk_two[:, lanes] + weight * dot_nt(values, state_two)
        halo_k = jnp.concatenate([empty, halo[quarter, 0].astype(f32)], axis=0)
        halo_v = jnp.concatenate([empty, halo[quarter, 1].astype(f32)], axis=0)
        d_qkv_out[1, :, lanes] = (
            maps_back(keys.astype(f32), d_one, d_two) + dk_near[:, lanes] + halo_k
        ).astype(bf16)
        d_qkv_out[2, :, lanes] = (
            dv[:, lanes] + weight * (dot(key_one, state_one) + dot(key_two, state_two)) + halo_v
        ).astype(bf16)
    d_qkv_out[0] = dq[...]
    total = None
    for kind in range(3):
        weight = jnp.concatenate([own[layer, kind], other[kind]], axis=1)
        product = dot_nt(d_qkv_out[kind], weight)
        total = product if total is None else total + product
    part_out[...] = total.astype(bf16)


JOB_REFS = {"up": 3, "down": 3, "out": 2, "qkv": 2}


def job_rows(job, units):
    return {"up": D, "down": units, "out": LANES, "qkv": 3 * LANES}[job]


def fill_grads(jobs, refs, own, far):
    at = 0
    for job in jobs:
        mine, refs = refs[: JOB_REFS[job]], refs[JOB_REFS[job] :]
        if job == "up":
            normed, grad_own, grad_far = mine
            own[at : at + D] = dot_tn(normed[...], grad_own[...]).astype(bf16)
            far[at : at + D] = dot_tn(normed[...], grad_far[...]).astype(bf16)
            at += D
        elif job == "down":
            act_own, act_far, grad = mine
            units = act_own.shape[1]
            own[at : at + units] = dot_tn(act_own[...], grad[...]).astype(bf16)
            far[at : at + units] = dot_tn(act_far[...], grad[...]).astype(bf16)
            at += units
        elif job == "out":
            mixed, grad = mine
            found = dot_tn(mixed[...], grad[...]).astype(bf16)
            own[at : at + LANES] = found[:LANES]
            far[at : at + LANES] = found[LANES:]
            at += LANES
        else:
            normed, d_qkv = mine
            for kind in range(3):
                found = dot_tn(normed[...], d_qkv[kind]).astype(bf16)
                for block in range(D // LANES):
                    lanes = slice(block * LANES, (block + 1) * LANES)
                    own[at : at + LANES, lanes] = found[lanes, :LANES]
                    far[at : at + LANES, lanes] = found[lanes, LANES:]
                at += LANES


def grads_kernel(jobs, place, *refs):
    fill_grads(jobs, refs[:-2], refs[-2], refs[-1])


def shard_bit(place, bit):
    return lax.rem(lax.div(place[2], 1 << bit), 2)


def halve_kernel(bit, place, first, second, keep_out, send_out):
    total = first[...].astype(f32) + second[...].astype(f32)
    rows = total.shape[0] // 2
    low = shard_bit(place, bit) == 0
    keep_out[...] = jnp.where(low, total[:rows], total[rows:])
    send_out[...] = jnp.where(low, total[rows:], total[:rows]).astype(bf16)


def add_kernel(first, second, out):
    out[...] = (first[...].astype(f32) + second[...].astype(f32)).astype(bf16)


def join_kernel(bit, place, mine, got, out):
    low = shard_bit(place, bit) == 0
    rows = mine.shape[0]
    out[:rows] = jnp.where(low, mine[...], got[...])
    out[rows:] = jnp.where(low, got[...], mine[...])


def fold_kernel(ways, got, out, small_out):
    rows = got.shape[0] // ways
    total = sum(got[k * rows : (k + 1) * rows].astype(f32) for k in range(ways))
    small_out[...] = total[rows - SMALL :, :LANES]
    total = total[: rows - SMALL].astype(bf16)
    for k in range(ways):
        out[k * (rows - SMALL) : (k + 1) * (rows - SMALL)] = total


def end_kernel(place, base, part_a, part_b, hidden, gains, *refs):
    smalls, (mine_out, theirs_out, own_out, far_out) = refs[: 4 * LAYERS - 1], refs[4 * LAYERS - 1 :]
    gain_refs, blend_refs = smalls[: 2 * LAYERS - 1], smalls[2 * LAYERS - 1 :]
    back, gain = norm_back(hidden[...], gains[0:1], part_a[...].astype(f32) + part_b[...].astype(f32))
    shard_rows((base[...] + back).astype(bf16), place, mine_out, theirs_out)
    gain_rows = jnp.concatenate([gain] + [ref[...] for ref in gain_refs], axis=0)
    blend_rows = jnp.concatenate([ref[...] for ref in blend_refs], axis=0)
    extras = []
    for to in range(2):
        features = jnp.where(
            place[1] == 0,
            gain_rows[:, to * LANES : (to + 1) * LANES],
            gain_rows[:, (2 + to) * LANES : (3 + to) * LANES],
        )
        blends = jnp.where(place[0] == to, blend_rows[:, :LANES], blend_rows[:, LANES:])
        extras.append(jnp.concatenate([features, blends, jnp.zeros((SMALL - 5 * LAYERS, LANES), f32)], axis=0))
    own_out[...] = jnp.where(place[0] == 0, extras[0], extras[1])
    far_out[...] = jnp.where(place[0] == 0, extras[1], extras[0])


def last_kernel(ways, own, far, small_own, small_far, out):
    total = (own[...].astype(f32) + far[...].astype(f32)).astype(bf16)
    small = small_own[...] + small_far[...]
    small = jnp.concatenate([small, jnp.zeros((SMALL, D - LANES), f32)], axis=1).astype(bf16)
    rows = total.shape[0] // ways
    for k in range(ways):
        at = k * (rows + SMALL)
        out[at : at + rows] = total[k * rows : (k + 1) * rows]
        out[at + rows : at + rows + SMALL] = small


def in_order(place, mine, other):
    low = shard_bit(place, 0) == 0
    first, second = jnp.where(low, mine[...], other[...]), jnp.where(low, other[...], mine[...])
    return jnp.concatenate([first, second], axis=0)


def finish_kernel(groups, place, last, *refs):
    refs, (up_out, down_out, out_out, qkv_out) = refs[:-4], refs[-4:]
    outs = {"up": up_out, "down": down_out, "out": out_out}
    qkv = {0: last[...]}
    for group, (layers, jobs) in enumerate(groups):
        whole = in_order(place, refs[2 * group], refs[2 * group + 1])
        at = 0
        for layer, job in zip(layers, jobs):
            rows = whole[at : at + job_rows(job, up_out.shape[2])]
            at += rows.shape[0]
            if job == "qkv":
                qkv[layer] = rows
            else:
                outs[job][layer] = rows.astype(f32)
    for layer in range(LAYERS):
        for kind in range(3):
            for block in range(D // LANES):
                lanes = slice(block * LANES, (block + 1) * LANES)
                qkv_out[layer, kind, lanes] = qkv[layer][kind * LANES : (kind + 1) * LANES, lanes].astype(f32)


def call(body, outs, operands, scalars=0, scratch=(), scalar_outs=0, bulk=(), bulk_outs=()):
    specs = [SM] * scalars + [VM] * (len(operands) - scalars)
    out_specs = [VM] * (len(outs) - scalar_outs) + [SM] * scalar_outs
    for index in bulk:
        specs[index] = pl.BlockSpec()
    for index in bulk_outs:
        out_specs[index] = pl.BlockSpec()
    return pl.pallas_call(
        body,
        out_shape=tuple(jax.ShapeDtypeStruct(shape, kind) for shape, kind in outs),
        in_specs=specs,
        out_specs=tuple(out_specs),
        scratch_shapes=scratch,
        compiler_params=pltpu.CompilerParams(vmem_limit_bytes=24 * 2**20),
    )(*operands)


def after(value, *others):
    return lax.optimization_barrier((value, *others))[0] if others else value


def half_swap(value):
    count = lax.axis_size("mlp")
    return lax.ppermute(value, "mlp", [(i, i ^ 1) for i in range(count)])


def part_swap(value):
    count = lax.axis_size("mlp")
    return lax.ppermute(value, "mlp", [(i, i ^ 2) for i in range(count)])


def chunk_move(value, target):
    shards, parts = lax.axis_size("seq"), lax.axis_size("mlp")
    pairs = []
    for chunk in range(2 * shards):
        goal = target(chunk)
        if goal is None or not 0 <= goal < 2 * shards:
            continue
        for part in range(2):
            pairs.append(((chunk // 2) * parts + chunk % 2 + 2 * part, (goal // 2) * parts + goal % 2 + 2 * part))
    return lax.ppermute(value, AXES, pairs)


def scan(value, flags, chunks, reverse, others=lambda: ()):
    places, _ = flag_places(chunks)
    found, arrived = None, None
    for stage, (size, ways, last) in enumerate(scan_plan(chunks)):
        got = []
        for step in range(1, ways):
            if last:

                def target(chunk, step=step):
                    move = -step if reverse else step
                    return chunk + move * size if 0 <= (chunk // size) % ways + move < ways else None

            else:

                def target(chunk, step=step):
                    member = (chunk // size) % ways
                    return chunk + ((member ^ step) - member) * size

            got.append(chunk_move(value, target))
        at = places[reverse, stage]
        if last:
            return (found, tuple(got), at), arrived, value
        arrived = arrived or tuple(got)
        operands = (flags, after(value, *others()), *got) + (() if found is None else (found,))
        value, found = call(
            functools.partial(combine_kernel, at, ways, found is not None),
            ((value.shape, bf16), (value.shape, f32)),
            operands,
            1,
        )


def shard_swap(value, bit):
    count = lax.axis_size("seq")
    return lax.ppermute(value, "seq", [(i, i ^ (1 << bit)) for i in range(count)])


def by_place(flag, mine, other):
    return jnp.where(flag == 0, mine, other), jnp.where(flag == 0, other, mine)


def per_device(inputs, lengths, valid, norm_attn, w_qkv, blend, w_out, norm_ffn, w_up, w_down, grad_out):
    shards, parts = lax.axis_size("seq"), lax.axis_size("mlp")
    shard, part = lax.axis_index("seq"), lax.axis_index("mlp")
    half = part % 2
    side = shard % 2
    rows = inputs.shape[0] // 2
    chunks = 2 * shards
    units = w_up.shape[2]
    place = jnp.stack([half, part // 2, shard]).astype(jnp.int32)

    wide = 2 * LANES
    hidden_like = ((rows, D), f32)
    low_like = ((rows, D), bf16)
    heads_like = ((rows, wide), f32)
    heads_low = ((rows, wide), bf16)
    qkv_like = ((3, rows, wide), bf16)
    state_like = ((2, STATE, LANES), bf16)
    halo_like = ((2, 2, HALO, LANES), bf16)
    ffn_like = ((rows, units), f32)
    ffn_low = ((rows, units), bf16)
    shard_like = ((rows, LANES), bf16)
    gain_like = ((1, D), f32)

    piece_like = ((rows + 3 * SMALL, LANES), bf16)
    mine, theirs = call(
        pack_kernel,
        (piece_like, piece_like),
        (place, blend, inputs, norm_attn, norm_ffn),
        2,
        bulk=(2, 3, 4),
    )
    got = half_swap(theirs)
    pieces = (mine, got, part_swap(mine), part_swap(got))
    far_qkv, far_out, far_up, far_down = [
        [half_swap(after(w[layer], theirs)) for layer in range(LAYERS)] for w in (w_qkv, w_out, w_up, w_down)
    ]
    grad_mine, grad_theirs = call(pack_grad_kernel, (shard_like, shard_like), (place, after(grad_out, theirs)), 1)
    grad_got = half_swap(grad_theirs)
    grad_pieces = (grad_mine, grad_got, part_swap(grad_mine), part_swap(grad_got))

    before = lax.ppermute(
        after(valid, theirs)[2 * rows - LANES :].reshape(1, LANES), "seq", [(source, source + 1) for source in range(shards - 1)]
    )
    _, flag_count = flag_places(chunks)
    causal, causal_t, band, carried, tail, flags = call(
        functools.partial(setup_kernel, chunks),
        (
            ((rows, rows), bf16),
            ((rows, rows), bf16),
            ((rows, LANES), f32),
            ((rows, LANES), f32),
            ((rows, LANES), bf16),
            ((flag_count,), f32),
        ),
        (place, lengths, valid.reshape(1, 2 * rows), before),
        2,
        scalar_outs=1,
    )

    saved = []
    base, adds = None, None
    for layer in range(LAYERS):
        outs = (hidden_like, low_like, qkv_like, state_like, halo_like)
        if layer == 0:
            hidden, normed, qkv, state, halo, gains, blends = call(
                functools.partial(qkv_kernel, True, layer),
                outs + (((SMALL, D), f32), ((SMALL, wide), f32)),
                (place, *pieces, w_qkv, far_qkv[layer], tail),
                1,
            )
        else:
            hidden, normed, qkv, state, halo = call(
                functools.partial(qkv_kernel, False, layer),
                outs,
                (place, base, *adds, gains, w_qkv, far_qkv[layer], tail),
                1,
            )
        halo = chunk_move(halo, lambda c: c + 1)
        one, two, sums = call(far_kernel, (heads_like,) * 3, (qkv, causal))
        (found, parts_got, at), arrived, _ = scan(state, flags, chunks, False, lambda: (one,))
        (near,) = call(near_kernel, (heads_like,), (place, qkv, halo, band), 1)
        mixed, far_one, far_two, root, prefix, state, piece = call(
            functools.partial(mix_kernel, layer, at, len(parts_got)),
            (heads_low, heads_like, heads_like, heads_like, heads_like, state_like, low_like),
            (place, flags, qkv, near, one, two, sums, carried, blends, w_out, far_out[layer], found, *parts_got),
            2,
        )
        weights = (w_up, w_down, far_up[layer], far_down[layer])
        middle, normed_ffn, pre_own, pre_far, act_own, act_far, piece_ffn = call(
            functools.partial(ffn_kernel, layer),
            (hidden_like, low_like, ffn_like, ffn_like, ffn_low, ffn_low, low_like),
            (hidden, piece, part_swap(piece), gains, *weights),
        )
        saved.append(
            (hidden, normed, qkv, state, halo, mixed, far_one, far_two, root, prefix, middle, normed_ffn,
             weights, pre_own, pre_far, act_own, act_far)
        )
        base, adds = middle, (piece_ffn, part_swap(piece_ffn))
    out_mine, out_theirs = call(output_kernel, (shard_like, shard_like), (place, base, *adds), 1)
    output = jnp.concatenate(by_place(half, out_mine, half_swap(out_theirs)))

    base, adds = None, None
    d_gain_attn, d_gain_ffn, d_blends = [None] * LAYERS, [None] * LAYERS, [None] * LAYERS
    d_qkvs = [None] * LAYERS
    bits = (shards - 1).bit_length()

    def first_step(jobs, operands):
        height = sum(job_rows(job, units) for job in jobs)
        like = ((height, D), bf16)
        return call(functools.partial(grads_kernel, jobs), (like, like), (place, *operands), 1, bulk_outs=(0,))

    def group_steps(own, far):
        height = own.shape[0]
        got = half_swap(far)
        others = yield
        if bits > 3:
            (total,) = call(add_kernel, ((own.shape, bf16),), (own, after(got, *others)))
            total = lax.psum(total, "seq").reshape(2, height // 2, D)
            total = jnp.where(shard % 2 == 0, total, total[::-1])
            for _ in range(2 * bits):
                yield total
            yield total[0], total[1]
        keep = own
        for bit in range(bits):
            height //= 2
            keep, send = call(
                functools.partial(halve_kernel, bit),
                (((height, D), f32), ((height, D), bf16)),
                (place, keep, after(got, *others)),
                1,
                bulk=(1,) if bit == 0 else (),
            )
            got = shard_swap(send, bit)
            others = yield send
        (value,) = call(add_kernel, (((height, D), bf16),), (keep, after(got, *others)))
        for bit in reversed(range(bits)):
            got = shard_swap(value, bit)
            if bit == 0:
                break
            others = yield value
            height *= 2
            (value,) = call(
                functools.partial(join_kernel, bit), (((height, D), bf16),), (place, value, after(got, *others)), 1
            )
        yield value
        yield (value, got)

    groups = []

    def start_group(layers, jobs, operands):
        own, far = first_step(jobs, operands)
        steps = group_steps(own, far)
        next(steps)
        groups.append((layers, jobs, steps))
        return far

    for layer in reversed(range(LAYERS)):
        (hidden, normed, qkv, state, halo, mixed, far_one, far_two, root, prefix, middle, normed_ffn,
         weights, pre_own, pre_far, act_own, act_far) = saved[layer]
        outs = (hidden_like, low_like, ffn_low, ffn_low, low_like)
        if base is None:
            resid, grad_rows, d_up_own, d_up_far, piece = call(
                functools.partial(ffn_back_kernel, True, layer),
                outs,
                (place, *grad_pieces, *weights, pre_own, pre_far),
                1,
            )
        else:
            resid, grad_rows, d_up_own, d_up_far, piece, d_gain_attn[layer + 1] = call(
                functools.partial(ffn_back_kernel, False, layer),
                outs + (gain_like,),
                (base, *adds, saved[layer + 1][0], gains, *weights, pre_own, pre_far),
            )
        (resid, out_rows, d_mixed, d_gain_ffn[layer], num_one, num_two, d_zeta, state_back, blend_far) = call(
            functools.partial(mix_back_kernel, layer),
            (hidden_like, low_like, heads_low, gain_like, heads_low, heads_low, heads_like, state_like,
             ((2, wide), f32)),
            (place, resid, piece, part_swap(piece), middle, gains, w_out, far_out[layer], qkv, far_one, far_two,
             root, carried, blends),
            1,
        )
        before_near = ()
        if layer == 0:
            made = start_group(
                (0, 1),
                ("up", "qkv"),
                (after(normed_ffn, state_back), d_up_own, d_up_far, saved[1][1], d_qkvs[1]),
            )
            made = start_group((0, 0), ("down", "out"), (after(act_own, made), act_far, grad_rows, mixed, out_rows))
            before_near = (made,)
        ext = HALO + rows + HALO
        dq_near, dk_near, dv_near, halo_back, blend_near = call(
            functools.partial(near_back_kernel, layer),
            (heads_like, heads_like, heads_like, halo_like, ((1, wide), f32)),
            (place, qkv, halo, band, after(d_mixed, *before_near), blends),
            1,
            scratch=(pltpu.VMEM((ext, LANES), f32), pltpu.VMEM((ext, LANES), f32)),
        )
        halo_back = chunk_move(halo_back, lambda c: c - 1)
        before_scan = [dq_near]
        if layer == 0:
            before_scan.append(groups[0][2].send((dq_near,)))
            before_scan.append(groups[1][2].send((before_scan[-1],)))
        (found, parts_got, at), arrived, value = scan(state_back, flags, chunks, True, lambda: before_scan)
        ready = [value]
        if layer > 0:
            made = start_group(
                (layer,) * 3,
                ("up", "down", "out"),
                (after(normed_ffn, value), d_up_own, d_up_far, act_own, act_far, grad_rows, mixed, out_rows),
            )
            ready.append(made)
        else:
            ready.append(groups[2][2].send((value,)))
        dq, dk_one, dk_two, dv = call(
            far_back_kernel,
            (heads_low, heads_like, heads_like, heads_like),
            (place, qkv, causal, causal_t, carried, state, prefix, after(num_one, *ready), num_two, d_zeta, dq_near,
             dv_near),
            1,
        )
        if layer > 0:
            dq = after(dq, groups[0][2].send((dq,)))
        else:
            made = groups[0][2].send((dq,))
            dq = after(dq, made)
        d_qkvs[layer], piece = call(
            functools.partial(qkv_back_kernel, layer, at, len(parts_got)),
            (qkv_like, low_like),
            (place, flags, qkv, dq, dk_one, dk_two, dk_near, dv, tail, halo_back, w_qkv, far_qkv[layer], found,
             *parts_got),
            2,
            scratch=(pltpu.VMEM((2, STATE, LANES), bf16),),
        )
        base, adds = resid, (piece, part_swap(piece))
        d_blends[layer] = (blend_near, blend_far)

    last_like = ((3 * LANES, D), bf16)
    own, far = call(functools.partial(grads_kernel, ("qkv",)), (last_like, last_like), (place, saved[0][1], d_qkvs[0]), 1)
    smalls = d_gain_attn[1:] + d_gain_ffn + [ref for pair in d_blends for ref in pair]
    small_like = ((SMALL, LANES), f32)
    mine, theirs, small_own, small_far = call(
        end_kernel,
        (shard_like, shard_like, small_like, small_like),
        (place, base, *adds, saved[0][0], gains, *smalls),
        1,
    )
    far, small_far = half_swap(far), half_swap(small_far)
    if bits > 3:
        last = lax.psum(own.astype(f32) + far.astype(f32), "seq").astype(bf16)
        small = lax.psum(small_own + small_far, "seq")
    else:
        height = 3 * LANES + shards * SMALL
        (made,) = call(
            functools.partial(last_kernel, shards), (((height, D), bf16),), (own, far, small_own, small_far)
        )
        got = lax.all_to_all(made, "seq", 0, 0, tiled=True)
    if bits > 3:
        made = last
    for turn in range(2 * bits - 1):
        if turn == 2 and bits <= 3:
            last, small = call(
                functools.partial(fold_kernel, shards), (last_like, small_like), (after(got, made),)
            )
            last, made = lax.all_to_all(last, "seq", 0, 0, tiled=True), last
        for _, _, steps in groups[(0 if turn < 2 * bits - 3 else 1) :]:
            made = steps.send((made,))
    d_inputs = jnp.concatenate(by_place(half, mine, half_swap(theirs)))
    sums = [part for _, _, steps in groups for part in next(steps)]
    d_up, d_down, d_out, d_qkv = call(
        functools.partial(finish_kernel, [group[:2] for group in groups]),
        (
            ((LAYERS, D, units), f32),
            ((LAYERS, units, D), f32),
            ((LAYERS, LANES, D), f32),
            ((LAYERS, 3, D, LANES), f32),
        ),
        (place, last, *sums),
        1,
    )
    count = 2 * LAYERS + 3 * LAYERS
    d_norm_attn = small[:LAYERS]
    d_norm_ffn = small[LAYERS : 2 * LAYERS]
    d_blend = jnp.sum(small[2 * LAYERS : count].reshape(LAYERS, 3, 2, HD), axis=3)
    return (output, d_inputs, d_norm_attn, d_qkv, d_blend, d_out, d_norm_ffn, d_up, d_down)


def solution(mesh):
    placed = (
        P("seq", "mlp"),
        P(),
        P("seq"),
        P(None, "mlp"),
        P(None, None, None, "mlp"),
        P(None, None, "mlp"),
        P(None, "mlp", None),
        P(None, "mlp"),
        P(None, None, "mlp"),
        P(None, "mlp", None),
        P("seq", "mlp"),
    )
    return jax.shard_map(
        per_device,
        mesh=mesh,
        in_specs=placed,
        out_specs=(
            P("seq", "mlp"),
            P("seq", "mlp"),
            P(None, "mlp"),
            P(None, None, None, "mlp"),
            P(None, None, "mlp"),
            P(None, "mlp", None),
            P(None, "mlp"),
            P(None, None, "mlp"),
            P(None, "mlp", None),
        ),
        check_vma=False,
    )
```

```python
import functools
import math

import jax
import jax.numpy as jnp
from jax import lax
from jax.experimental import pallas as pl
from jax.experimental.pallas import tpu as pltpu
from jax.sharding import PartitionSpec as P

HD = 64
D = 512
BAND = 30
LAYERS = 2
HALO = 32
TILE = 64
LANES = 128
STATE = 144
SMALL = 16
AXES = ("seq", "mlp")

epsilon = 1e-05
masked_score = -1e30
score_scale = 1.0 / math.sqrt(HD)
far_scale = 1.0 / math.sqrt(HD)
f32 = jnp.float32
bf16 = jnp.bfloat16

VM = pl.BlockSpec(memory_space=pltpu.VMEM)
SM = pl.BlockSpec(memory_space=pltpu.SMEM)


def dot(x, y):
    return jnp.dot(x, y, preferred_element_type=f32)


def dot_nt(x, y):
    return lax.dot_general(x, y, (((1,), (1,)), ((), ())), preferred_element_type=f32)


def dot_tn(x, y):
    return lax.dot_general(x, y, (((0,), (0,)), ((), ())), preferred_element_type=f32)


def low_lanes(rows):
    return lax.broadcasted_iota(jnp.int32, (rows, LANES), 1) < HD


def split_heads(x):
    low = low_lanes(x.shape[0])
    zero = jnp.zeros_like(x)
    return jnp.concatenate([jnp.where(low, x, zero), jnp.where(low, zero, x)], axis=0)


def merge_heads(y):
    rows = y.shape[0] // 2
    return jnp.where(low_lanes(rows), y[:rows], y[rows:])


def head_sum(x):
    row = lax.broadcasted_iota(jnp.int32, (LANES, LANES), 0) < HD
    ones = jnp.where(row == low_lanes(LANES), 1.0, 0.0).astype(bf16)
    high = x.astype(bf16)
    rest = (x - high.astype(f32)).astype(bf16)
    return dot(high, ones) + dot(rest, ones)


def kernel_maps(x):
    return (
        jnp.where(x > 0, x + 1.0, jnp.exp(jnp.minimum(x, 0.0))).astype(bf16),
        jnp.tanh(x).astype(bf16),
    )


def maps_back(x, d_one, d_two):
    tanh = jnp.tanh(x)
    return jnp.where(x > 0, 1.0, jnp.exp(jnp.minimum(x, 0.0))) * d_one + (1.0 - tanh * tanh) * d_two


def put_state(ref, quarter, one, two, total):
    row = lax.broadcasted_iota(jnp.int32, (STATE - 2 * HD, LANES), 0)
    low = low_lanes(HD)
    ref[quarter, 0:HD, :] = jnp.where(low, one[:HD], one[HD:]).astype(bf16)
    ref[quarter, HD : 2 * HD, :] = jnp.where(low, two[:HD], two[HD:]).astype(bf16)
    ref[quarter, 2 * HD : STATE, :] = jnp.where(row == 0, total, 0.0).astype(bf16)


def get_state(ref, quarter):
    one = split_heads(ref[quarter, 0:HD, :])
    two = split_heads(ref[quarter, HD : 2 * HD, :])
    total = ref[quarter, 2 * HD : STATE, :].astype(f32)[0:1]
    return one, two, total


def norm_scale(hidden):
    return lax.rsqrt(jnp.sum(hidden * hidden, axis=1, keepdims=True) * (1.0 / D) + epsilon)


def norm_back(hidden, gain, grad):
    scale = norm_scale(hidden)
    gained = grad * gain
    inner = jnp.sum(gained * hidden, axis=1, keepdims=True) * (1.0 / D)
    back = scale * gained - hidden * (scale * scale * scale * inner)
    return back, jnp.sum(grad * hidden * scale, axis=0, keepdims=True)


def extend(halo, rows):
    return jnp.concatenate([halo, rows, jnp.zeros((HALO, LANES), bf16)], axis=0)


def three_parts(value):
    high = value.astype(bf16)
    rest = value - high.astype(f32)
    middle = rest.astype(bf16)
    low = (rest - middle.astype(f32)).astype(bf16)
    return jnp.concatenate([high, middle, low], axis=0)


def pack_kernel(place, blend, inputs, norm_attn, norm_ffn, mine_out, theirs_out):
    rows = inputs.shape[0] // 2
    low = low_lanes(1)
    small = [norm_attn[...], norm_ffn[...]]
    for layer in range(LAYERS):
        for kind in range(3):
            small.append(jnp.where(low, blend[layer, kind, 0], blend[layer, kind, 1]))
    small.append(jnp.zeros((SMALL - 5 * LAYERS, LANES), f32))
    small = three_parts(jnp.concatenate(small, axis=0))
    first, second = inputs[:rows], inputs[rows:]
    mine_out[:rows] = jnp.where(place[0] == 0, first, second)
    theirs_out[:rows] = jnp.where(place[0] == 0, second, first)
    mine_out[rows:] = small
    theirs_out[rows:] = small


def pack_grad_kernel(place, grads, mine_out, theirs_out):
    rows = grads.shape[0] // 2
    first, second = grads[:rows], grads[rows:]
    mine_out[...] = jnp.where(place[0] == 0, first, second)
    theirs_out[...] = jnp.where(place[0] == 0, second, first)


def quarters(place):
    half, part = place[0], place[1]
    return 2 * part + half, 2 * part + 1 - half, 2 * (1 - part) + half, 2 * (1 - part) + 1 - half


def quarter_lanes(quarter):
    return pl.ds(pl.multiple_of(quarter * LANES, LANES), LANES)


def item_ends(lengths):
    ends = []
    for k in range(lengths.shape[0]):
        ends.append(lengths[k] if k == 0 else ends[-1] + lengths[k])
    return ends


def item_start(lengths, ends, positions):
    start = jnp.zeros_like(positions)
    for k, end in enumerate(ends):
        start = start + jnp.where(end <= positions, lengths[k], 0)
    return start


def scan_plan(chunks):
    stages, size = [], 1
    while size < chunks:
        ways = min(4, chunks // size)
        stages.append((size, ways, size * ways >= chunks))
        size *= ways
    return stages


def flag_places(chunks):
    at, places = 0, {}
    for reverse in (False, True):
        for stage, (_, ways, _) in enumerate(scan_plan(chunks)):
            places[reverse, stage] = at
            at += 2 * ways
    return places, at


def setup_kernel(chunks, place, lengths, valid, causal_out, causal_t_out, carried_out, tail_out, flags_out):
    rows = causal_out.shape[0]
    chunk = place[2] * 2 + place[0]
    first_row = chunk * rows
    ends = item_ends(lengths)

    def start_of(positions):
        return item_start(lengths, ends, positions)

    lane = lax.broadcasted_iota(jnp.int32, (1, rows), 1)
    starts_row = start_of(first_row + lane)
    starts = start_of(first_row + lax.broadcasted_iota(jnp.int32, (rows, LANES), 0))
    both = jnp.concatenate([starts, starts], axis=1)
    words = valid[...]
    own_words = jnp.where(place[0] == 0, words[:, :rows], words[:, rows:])
    row_at = lax.broadcasted_iota(jnp.int32, (rows, rows), 0)
    lane_at = lax.broadcasted_iota(jnp.int32, (rows, rows), 1)
    own_column = jnp.sum(jnp.where(row_at == lane_at, own_words, 0), axis=1, keepdims=True)
    same = both == starts_row
    causal_out[...] = jnp.where((lane_at <= row_at) & same & (own_words == 1), 1.0, 0.0).astype(bf16)
    causal_t_out[...] = jnp.where((row_at <= lane_at) & same & (own_column == 1), 1.0, 0.0).astype(bf16)
    carried_out[...] = jnp.where(starts < first_row, 1.0, 0.0)
    last_start = start_of(first_row + rows - 1)
    tail_out[...] = jnp.where((starts == last_start) & (own_column == 1), 1.0, 0.0).astype(bf16)
    places, _ = flag_places(chunks)
    for reverse in (False, True):
        edge = start_of(first_row + (rows - 1 if reverse else 0))
        for stage, (size, ways, last) in enumerate(scan_plan(chunks)):
            member = lax.rem(lax.div(chunk, size), ways)
            base = chunk - member * size - lax.rem(chunk, size)
            group = base if reverse else base + ways * size - 1
            group = start_of(group * rows + (0 if reverse else rows - 1))
            for step in range(ways):
                if last:
                    other = member + step if reverse else member - step
                else:
                    other = jnp.bitwise_xor(member, step)
                block = base + other * size + (0 if reverse else size - 1)
                start = start_of(block * rows + (0 if reverse else rows - 1))
                ahead = (other > member) if reverse else (other < member)
                ahead = ahead & (other >= 0) & (other < ways)
                at = places[reverse, stage] + 2 * step
                flags_out[at] = jnp.where(ahead & (start == edge), 1.0, 0.0)
                flags_out[at + 1] = jnp.where(start == group, 1.0, 0.0)


def band_kernel(place, lengths, valid, before, band_out):
    rows = band_out.shape[0]
    first_row = (place[2] * 2 + place[0]) * rows
    ends = item_ends(lengths)

    def start_of(positions):
        return item_start(lengths, ends, positions)

    words = valid[...]
    own_words = jnp.where(place[0] == 0, words[:, :rows], words[:, rows:])
    last_words = jnp.where(place[0] == 0, before[...], words[:, rows - LANES : rows])
    starts = start_of(first_row + lax.broadcasted_iota(jnp.int32, (rows, LANES), 0))
    all_words = jnp.concatenate([last_words, own_words, jnp.zeros((1, LANES), jnp.int32)], axis=1)
    tile_row = lax.broadcasted_iota(jnp.int32, (TILE, LANES), 0)
    tile_lane = lax.broadcasted_iota(jnp.int32, (TILE, LANES), 1)
    gap = tile_row + HALO - tile_lane
    for tile in range(rows // TILE):
        key_starts = start_of(first_row + tile * TILE - HALO + lax.broadcasted_iota(jnp.int32, (1, LANES), 1))
        offset = LANES - HALO + tile * TILE
        key_words = all_words[:, offset : offset + LANES]
        at = slice(tile * TILE, (tile + 1) * TILE)
        allowed = (gap >= 0) & (gap <= BAND) & (starts[at] == key_starts) & ((key_words == 1) | (gap == 0))
        band_out[at] = jnp.where(allowed, 0.0, masked_score)


def combine_kernel(at, ways, has_found, flags, *refs):
    got, refs = refs[:ways], refs[ways:]
    total = sum(flags[at + 2 * step + 1] * got[step][...].astype(f32) for step in range(ways))
    refs[-2][...] = total.astype(bf16)
    found = sum(flags[at + 2 * step] * got[step][...].astype(f32) for step in range(1, ways))
    refs[-1][...] = found + refs[0][...] if has_found else found


def last_combine(at, flags, found, got, out):
    value = found[...]
    for step, part in enumerate(got):
        value = value + flags[at + 2 * (step + 1)] * part[...].astype(f32)
    out[...] = value.astype(bf16)


def qkv_kernel(first, layer, place, *refs):
    if first:
        refs, outs = refs[:7], refs[7:]
        pieces, (own, other, tail) = refs[:4], refs[4:]
        hidden_out, normed_out, qkv_out, state_out, halo_out, gains, blends_out = outs
        rows = hidden_out.shape[0]
        for index, (piece, quarter) in enumerate(zip(pieces, quarters(place))):
            hidden_out[:, quarter_lanes(quarter)] = piece[:rows].astype(f32)
            parts = piece[rows:].astype(f32)
            small = parts[:SMALL] + parts[SMALL : 2 * SMALL] + parts[2 * SMALL :]
            gains[:, quarter_lanes(quarter)] = small
            if index < 2:
                blends_out[:, index * LANES : (index + 1) * LANES] = small
        hidden = hidden_out[...]
    else:
        base, part_a, part_b, gains, own, other, tail, hidden_out, normed_out, qkv_out, state_out, halo_out = refs
        hidden = base[...] + (part_a[...].astype(f32) + part_b[...].astype(f32))
        hidden_out[...] = hidden
    rows = hidden.shape[0]
    normed = (hidden * norm_scale(hidden) * gains[layer : layer + 1]).astype(bf16)
    normed_out[...] = normed
    found = []
    for kind in range(3):
        weight = jnp.concatenate([own[layer, kind], other[kind]], axis=1)
        found.append(dot(normed, weight).astype(bf16))
        qkv_out[kind] = found[kind]
    for pair in range(2):
        quarter = place[0] if pair == 0 else 1 - place[0]
        lanes = slice(pair * LANES, (pair + 1) * LANES)
        keys, values = found[1][:, lanes], found[2][:, lanes]
        one, two = kernel_maps(keys.astype(f32))
        one, two = one * tail[...], two * tail[...]
        put_state(
            state_out,
            quarter,
            dot_tn(one, values),
            dot_tn(two, values),
            jnp.sum(one.astype(f32), axis=0, keepdims=True),
        )
        halo_out[quarter, 0] = keys[rows - HALO :]
        halo_out[quarter, 1] = values[rows - HALO :]


def far_kernel(qkv, causal, one_out, two_out, sums_out):
    masks = jnp.concatenate([causal[...], causal[...]], axis=0)
    for pair in range(2):
        lanes = slice(pair * LANES, (pair + 1) * LANES)
        queries, keys, values = qkv[0, :, lanes], qkv[1, :, lanes], qkv[2, :, lanes]
        maps_q, maps_k = kernel_maps(queries.astype(f32)), kernel_maps(keys.astype(f32))
        for query, key, out in ((maps_q[0], maps_k[0], one_out), (maps_q[1], maps_k[1], two_out)):
            attn = dot_nt(split_heads(query), key).astype(bf16) * masks
            out[:, lanes] = merge_heads(dot(attn, values))
        sums_out[:, lanes] = dot(causal[...], maps_k[0])


def near_kernel(place, qkv, halo, band, near_out):
    rows = qkv.shape[1]
    for pair in range(2):
        quarter = place[0] if pair == 0 else 1 - place[0]
        lanes = slice(pair * LANES, (pair + 1) * LANES)
        queries, keys, values = qkv[0, :, lanes], qkv[1, :, lanes], qkv[2, :, lanes]
        ext_keys = extend(halo[quarter, 0], keys)
        ext_values = extend(halo[quarter, 1], values)
        for tile in range(rows // TILE):
            at = slice(tile * TILE, (tile + 1) * TILE)
            window = slice(tile * TILE, tile * TILE + LANES)
            allowed = jnp.concatenate([band[at], band[at]], axis=0)
            scores = dot_nt(split_heads(queries[at]), ext_keys[window]) * score_scale + allowed
            weights = jnp.exp(scores - jnp.max(scores, axis=1, keepdims=True))
            weights = weights / jnp.sum(weights, axis=1, keepdims=True)
            near_out[at, lanes] = merge_heads(dot(weights.astype(bf16), ext_values[window]))


def mix_kernel(layer, at, count, place, flags, qkv, near, one, two, sums, carried, blends, own, other, found, *refs):
    got = refs[:count]
    mixed_out, far_one_out, far_two_out, root_out, prefix_out, state, part_out = refs[count:]
    last_combine(at, flags, found, got, state)
    mixed = []
    row = 2 * LAYERS + 3 * layer
    for pair in range(2):
        quarter = place[0] if pair == 0 else 1 - place[0]
        lanes = slice(pair * LANES, (pair + 1) * LANES)
        query_one, query_two = kernel_maps(qkv[0, :, lanes].astype(f32))
        state_one, state_two, total = get_state(state, quarter)
        num_one = one[:, lanes] + carried[...] * dot(query_one, state_one)
        num_two = two[:, lanes] + carried[...] * dot(query_two, state_two)
        prefix = sums[:, lanes] + carried[...] * total
        zeta = head_sum(query_one.astype(f32) * prefix)
        root = lax.rsqrt(zeta + 1.0)
        far_one = num_one * root * far_scale
        far_two = num_two * root
        far_one_out[:, lanes] = far_one
        far_two_out[:, lanes] = far_two
        root_out[:, lanes] = root
        prefix_out[:, lanes] = prefix
        mixed.append(
            (
                blends[row : row + 1, lanes] * near[:, lanes]
                + blends[row + 1 : row + 2, lanes] * far_one
                + blends[row + 2 : row + 3, lanes] * far_two
            ).astype(bf16)
        )
        mixed_out[:, lanes] = mixed[pair]
    weight = jnp.concatenate([own[layer], other[...]], axis=0)
    part_out[...] = dot(jnp.concatenate(mixed, axis=1), weight).astype(bf16)


def ffn_kernel(
    layer, base, part_a, part_b, gains, up_own, down_own, up_far, down_far,
    middle_out, normed_out, pre_own_out, pre_far_out, act_own_out, act_far_out, part_out,
):
    middle = base[...] + (part_a[...].astype(f32) + part_b[...].astype(f32))
    middle_out[...] = middle
    gain = gains[LAYERS + layer : LAYERS + layer + 1]
    normed = (middle * norm_scale(middle) * gain).astype(bf16)
    normed_out[...] = normed
    weights = (
        (up_own[layer], down_own[layer], pre_own_out, act_own_out),
        (up_far[...], down_far[...], pre_far_out, act_far_out),
    )
    total = None
    for up, down, pre_out, act_out in weights:
        pre = dot(normed, up)
        pre_out[...] = pre
        inner = jnp.tanh(math.sqrt(2.0 / math.pi) * (pre + 0.044715 * pre * pre * pre))
        act = (0.5 * pre * (1.0 + inner)).astype(bf16)
        act_out[...] = act
        product = dot(act, down)
        total = product if total is None else total + product
    part_out[...] = total.astype(bf16)


def shard_rows(whole, place, mine_out, theirs_out):
    first = [whole[:, m * LANES : (m + 1) * LANES] for m in range(4)]
    even, odd = [jnp.where(place[1] == 0, first[h], first[2 + h]) for h in range(2)]
    mine_out[...] = jnp.where(place[0] == 0, even, odd)
    theirs_out[...] = jnp.where(place[0] == 0, odd, even)


def output_kernel(place, base, part_a, part_b, mine_out, theirs_out):
    whole = base[...] + (part_a[...].astype(f32) + part_b[...].astype(f32))
    shard_rows(whole.astype(bf16), place, mine_out, theirs_out)


def gelu_slope(pre):
    c = math.sqrt(2.0 / math.pi)
    inner = jnp.tanh(c * (pre + 0.044715 * pre * pre * pre))
    return 0.5 * (1.0 + inner) + 0.5 * pre * (1.0 - inner * inner) * (c * (1.0 + 3 * 0.044715 * pre * pre))


def ffn_back_kernel(first, layer, *refs):
    if first:
        place, *refs = refs
        pieces, refs = refs[:4], refs[4:]
        weights, outs = refs[:6], refs[6:]
        resid_out, rows_out, d_up_own_out, d_up_far_out, part_out = outs
        for piece, quarter in zip(pieces, quarters(place)):
            resid_out[:, quarter_lanes(quarter)] = piece[...].astype(f32)
        resid = resid_out[...]
    else:
        base, part_a, part_b, hidden, gains, *refs = refs
        weights, outs = refs[:6], refs[6:]
        resid_out, rows_out, d_up_own_out, d_up_far_out, part_out, gain_out = outs
        back, gain_out[...] = norm_back(
            hidden[...], gains[layer + 1 : layer + 2], part_a[...].astype(f32) + part_b[...].astype(f32)
        )
        resid = base[...] + back
        resid_out[...] = resid
    up_own, down_own, up_far, down_far, pre_own, pre_far = weights
    rows = resid.astype(bf16)
    rows_out[...] = rows
    total = None
    for up, down, pre, out in (
        (up_own[layer], down_own[layer], pre_own, d_up_own_out),
        (up_far[...], down_far[...], pre_far, d_up_far_out),
    ):
        d_up = (gelu_slope(pre[...]) * dot_nt(rows, down)).astype(bf16)
        out[...] = d_up
        product = dot_nt(d_up, up)
        total = product if total is None else total + product
    part_out[...] = total.astype(bf16)


def mix_back_kernel(
    layer, place, base, part_a, part_b, middle, gains, own, other, qkv, far_one, far_two, root, carried, blends,
    resid_out, rows_out, mixed_out, gain_out, num_one_out, num_two_out, zeta_out, state_out, blend_out,
):
    back, gain_out[...] = norm_back(
        middle[...],
        gains[LAYERS + layer : LAYERS + layer + 1],
        part_a[...].astype(f32) + part_b[...].astype(f32),
    )
    resid = base[...] + back
    resid_out[...] = resid
    blend = blends[2 * LAYERS + 3 * layer : 2 * LAYERS + 3 * layer + 3]
    rows = resid.astype(bf16)
    rows_out[...] = rows
    weight = jnp.concatenate([own[layer], other[...]], axis=0)
    d_mixed = dot_nt(rows, weight).astype(bf16)
    mixed_out[...] = d_mixed
    for pair in range(2):
        quarter = place[0] if pair == 0 else 1 - place[0]
        lanes = slice(pair * LANES, (pair + 1) * LANES)
        grad = d_mixed[:, lanes].astype(f32)
        scale = root[:, lanes]
        dot_one = grad * far_one[:, lanes]
        dot_two = grad * far_two[:, lanes]
        blend_one, blend_two = blend[1:2, lanes], blend[2:3, lanes]
        blend_out[0:1, lanes] = jnp.sum(dot_one, axis=0, keepdims=True)
        blend_out[1:2, lanes] = jnp.sum(dot_two, axis=0, keepdims=True)
        num_one = (grad * (blend_one * far_scale) * scale).astype(bf16)
        num_two = (grad * blend_two * scale).astype(bf16)
        d_zeta = head_sum(blend_one * dot_one + blend_two * dot_two) * (-0.5 * scale * scale)
        num_one_out[:, lanes] = num_one
        num_two_out[:, lanes] = num_two
        zeta_out[:, lanes] = d_zeta
        query_one, query_two = kernel_maps(qkv[0, :, lanes].astype(f32))
        reach = carried[...].astype(bf16)
        put_state(
            state_out,
            quarter,
            dot_tn(query_one * reach, num_one),
            dot_tn(query_two * reach, num_two),
            jnp.sum(carried[...] * d_zeta * query_one.astype(f32), axis=0, keepdims=True),
        )


def near_back_kernel(
    layer, place, qkv, halo, band, d_mixed, blends, dq_out, dk_out, dv_out, halo_out, blend_out, near_k, near_v
):
    rows = qkv.shape[1]
    row_low = lax.broadcasted_iota(jnp.int32, (2 * TILE, 1), 0) < TILE
    row = 2 * LAYERS + 3 * layer
    for pair in range(2):
        quarter = place[0] if pair == 0 else 1 - place[0]
        lanes = slice(pair * LANES, (pair + 1) * LANES)
        queries, keys, values = qkv[0, :, lanes], qkv[1, :, lanes], qkv[2, :, lanes]
        grads = d_mixed[:, lanes]
        blend = blends[row : row + 1, lanes]
        ext_keys = extend(halo[quarter, 0], keys)
        ext_values = extend(halo[quarter, 1], values)
        near_k[...] = jnp.zeros_like(near_k)
        near_v[...] = jnp.zeros_like(near_v)
        blend_rows = jnp.where(row_low, blend[:, :1], blend[:, HD : HD + 1])
        sums = None
        for tile in range(rows // TILE):
            at = slice(tile * TILE, (tile + 1) * TILE)
            window = slice(tile * TILE, tile * TILE + LANES)
            allowed = jnp.concatenate([band[at], band[at]], axis=0)
            query_split, grad_split = split_heads(queries[at]), split_heads(grads[at])
            scores = dot_nt(query_split, ext_keys[window]) * score_scale + allowed
            probs = jnp.exp(scores - jnp.max(scores, axis=1, keepdims=True))
            probs = probs / jnp.sum(probs, axis=1, keepdims=True)
            d_probs = dot_nt(grad_split, ext_values[window])
            inner = jnp.sum(probs * d_probs, axis=1, keepdims=True)
            sums = inner if sums is None else sums + inner
            d_scores = (probs * (d_probs - inner) * blend_rows).astype(bf16)
            dq_out[at, lanes] = score_scale * merge_heads(dot(d_scores, ext_keys[window]))
            near_k[window] += dot_tn(d_scores, query_split)
            near_v[window] += dot_tn(probs.astype(bf16), grad_split)
        sum_low = jnp.sum(sums[:TILE], axis=0, keepdims=True)
        sum_high = jnp.sum(sums[TILE:], axis=0, keepdims=True)
        blend_out[0:1, lanes] = jnp.where(low_lanes(1), sum_low, sum_high) * (1.0 / HD)
        dk_out[:, lanes] = score_scale * near_k[HALO : HALO + rows]
        dv_out[:, lanes] = blend * near_v[HALO : HALO + rows]
        halo_out[quarter, 0] = (score_scale * near_k[0:HALO]).astype(bf16)
        halo_out[quarter, 1] = (blend * near_v[0:HALO]).astype(bf16)


def far_back_kernel(
    place, qkv, causal, causal_t, carried, state, prefix, num_one, num_two, d_zeta, dq_near, dv_near,
    dq_out, dk_one_out, dk_two_out, dv_out,
):
    masks = jnp.concatenate([causal[...], causal[...]], axis=0)
    masks_t = jnp.concatenate([causal_t[...], causal_t[...]], axis=1)
    for pair in range(2):
        quarter = place[0] if pair == 0 else 1 - place[0]
        lanes = slice(pair * LANES, (pair + 1) * LANES)
        queries, keys, values = qkv[0, :, lanes], qkv[1, :, lanes], qkv[2, :, lanes]
        state_one, state_two, unused_total = get_state(state, quarter)
        query_one, query_two = kernel_maps(queries.astype(f32))
        key_one, key_two = kernel_maps(keys.astype(f32))
        d_values = dv_near[:, lanes]
        d_queries = []
        for query, key, num, square, out in (
            (query_one, key_one, num_one[:, lanes], state_one, dk_one_out),
            (query_two, key_two, num_two[:, lanes], state_two, dk_two_out),
        ):
            query_split, num_split = split_heads(query), split_heads(num)
            attn_t = dot_nt(key, query_split).astype(bf16) * masks_t
            grad = dot_nt(num_split, values).astype(bf16) * masks
            grad_t = dot_nt(values, num_split).astype(bf16) * masks_t
            d_values = d_values + dot(attn_t, num_split)
            d_queries.append(merge_heads(dot(grad, key)) + carried[...] * dot_nt(num, square))
            out[:, lanes] = dot(grad_t, query_split)
        zeta = d_zeta[:, lanes]
        d_queries[0] += zeta * prefix[:, lanes]
        dk_one_out[:, lanes] += dot(causal_t[...], (zeta * query_one.astype(f32)).astype(bf16))
        back = maps_back(queries.astype(f32), d_queries[0], d_queries[1])
        dq_out[:, lanes] = (back + dq_near[:, lanes]).astype(bf16)
        dv_out[:, lanes] = d_values


def qkv_back_kernel(
    layer, at, count, place, flags, qkv, dq, dk_one, dk_two, dk_near, dv, tail, halo, own, other, found, *refs
):
    got = refs[:count]
    d_qkv_out, part_out, state = refs[count:]
    last_combine(at, flags, found, got, state)
    rows = qkv.shape[1]
    empty = jnp.zeros((rows - HALO, LANES), f32)
    for pair in range(2):
        quarter = place[0] if pair == 0 else 1 - place[0]
        lanes = slice(pair * LANES, (pair + 1) * LANES)
        keys, values = qkv[1, :, lanes], qkv[2, :, lanes]
        key_one, key_two = kernel_maps(keys.astype(f32))
        state_one, state_two, total = get_state(state, quarter)
        weight = tail[...].astype(f32)
        d_one = dk_one[:, lanes] + weight * (dot_nt(values, state_one) + total)
        d_two = dk_two[:, lanes] + weight * dot_nt(values, state_two)
        halo_k = jnp.concatenate([empty, halo[quarter, 0].astype(f32)], axis=0)
        halo_v = jnp.concatenate([empty, halo[quarter, 1].astype(f32)], axis=0)
        d_qkv_out[1, :, lanes] = (
            maps_back(keys.astype(f32), d_one, d_two) + dk_near[:, lanes] + halo_k
        ).astype(bf16)
        d_qkv_out[2, :, lanes] = (
            dv[:, lanes] + weight * (dot(key_one, state_one) + dot(key_two, state_two)) + halo_v
        ).astype(bf16)
    d_qkv_out[0] = dq[...]
    total = None
    for kind in range(3):
        weight = jnp.concatenate([own[layer, kind], other[kind]], axis=1)
        product = dot_nt(d_qkv_out[kind], weight)
        total = product if total is None else total + product
    part_out[...] = total.astype(bf16)


JOB_REFS = {"up": 3, "down": 3, "out": 2, "qkv": 2}


def job_rows(job, units):
    return {"up": D, "down": units, "out": LANES, "qkv": 3 * LANES}[job]


def fill_grads(jobs, refs, own, far):
    at = 0
    for job in jobs:
        mine, refs = refs[: JOB_REFS[job]], refs[JOB_REFS[job] :]
        if job == "up":
            normed, grad_own, grad_far = mine
            own[at : at + D] = dot_tn(normed[...], grad_own[...]).astype(bf16)
            far[at : at + D] = dot_tn(normed[...], grad_far[...]).astype(bf16)
            at += D
        elif job == "down":
            act_own, act_far, grad = mine
            units = act_own.shape[1]
            own[at : at + units] = dot_tn(act_own[...], grad[...]).astype(bf16)
            far[at : at + units] = dot_tn(act_far[...], grad[...]).astype(bf16)
            at += units
        elif job == "out":
            mixed, grad = mine
            found = dot_tn(mixed[...], grad[...]).astype(bf16)
            own[at : at + LANES] = found[:LANES]
            far[at : at + LANES] = found[LANES:]
            at += LANES
        else:
            normed, d_qkv = mine
            for kind in range(3):
                found = dot_tn(normed[...], d_qkv[kind]).astype(bf16)
                for block in range(D // LANES):
                    lanes = slice(block * LANES, (block + 1) * LANES)
                    own[at : at + LANES, lanes] = found[lanes, :LANES]
                    far[at : at + LANES, lanes] = found[lanes, LANES:]
                at += LANES


def grads_kernel(jobs, place, *refs):
    fill_grads(jobs, refs[:-2], refs[-2], refs[-1])


def shard_bit(place, bit):
    return lax.rem(lax.div(place[2], 1 << bit), 2)


def give_half(bit, place, total, keep_out, send_out):
    rows = total.shape[0] // 2
    low = shard_bit(place, bit) == 0
    keep_out[...] = jnp.where(low, total[:rows], total[rows:])
    send_out[...] = jnp.where(low, total[rows:], total[:rows]).astype(bf16)


def halve_kernel(bit, rows, place, first, second, keep_out, send_out):
    at = slice(*rows)
    give_half(bit, place, first[at].astype(f32) + second[at].astype(f32), keep_out, send_out)


def add_kernel(first, second, out):
    out[...] = (first[...].astype(f32) + second[...].astype(f32)).astype(bf16)


def join_kernel(bit, place, mine, got, out):
    low = shard_bit(place, bit) == 0
    rows = mine.shape[0]
    out[:rows] = jnp.where(low, mine[...], got[...])
    out[rows:] = jnp.where(low, got[...], mine[...])


def end_kernel(place, base, part_a, part_b, hidden, gains, *refs):
    smalls, (mine_out, theirs_out, own_out, far_out) = refs[: 4 * LAYERS - 1], refs[4 * LAYERS - 1 :]
    gain_refs, blend_refs = smalls[: 2 * LAYERS - 1], smalls[2 * LAYERS - 1 :]
    back, gain = norm_back(hidden[...], gains[0:1], part_a[...].astype(f32) + part_b[...].astype(f32))
    shard_rows((base[...] + back).astype(bf16), place, mine_out, theirs_out)
    gain_rows = jnp.concatenate([gain] + [ref[...] for ref in gain_refs], axis=0)
    blend_rows = jnp.concatenate([ref[...] for ref in blend_refs], axis=0)
    extras = []
    for to in range(2):
        features = jnp.where(
            place[1] == 0,
            gain_rows[:, to * LANES : (to + 1) * LANES],
            gain_rows[:, (2 + to) * LANES : (3 + to) * LANES],
        )
        blends = jnp.where(place[0] == to, blend_rows[:, :LANES], blend_rows[:, LANES:])
        extras.append(jnp.concatenate([features, blends, jnp.zeros((SMALL - 5 * LAYERS, LANES), f32)], axis=0))
    own_out[...] = jnp.where(place[0] == 0, extras[0], extras[1])
    far_out[...] = jnp.where(place[0] == 0, extras[1], extras[0])


def last_kernel(bit, place, own, far, small_own, small_far, keep_out, send_out):
    small = jnp.concatenate([small_own[...] + small_far[...], jnp.zeros((SMALL, D - LANES), f32)], axis=1)
    small = jnp.concatenate([small, jnp.zeros((LANES - SMALL, D), f32)], axis=0)
    total = jnp.concatenate([own[...].astype(f32) + far[...].astype(f32), small], axis=0)
    give_half(bit, place, total, keep_out, send_out)


def in_order(bit, place, mine, other):
    low = shard_bit(place, bit) == 0
    first, second = jnp.where(low, mine[...], other[...]), jnp.where(low, other[...], mine[...])
    return jnp.concatenate([first, second], axis=0)


def finish_kernel(groups, place, *refs):
    refs, (up_out, down_out, out_out, qkv_out, small_out) = refs[:-5], refs[-5:]
    outs = {"up": up_out, "down": down_out, "out": out_out}
    qkv = {}
    for group, (layers, jobs, bit) in enumerate(groups):
        whole = in_order(bit, place, refs[2 * group], refs[2 * group + 1])
        at = 0
        for layer, job in zip(layers, jobs):
            rows = whole[at : at + job_rows(job, up_out.shape[2])]
            at += rows.shape[0]
            if job == "qkv":
                qkv[layer] = rows
            else:
                outs[job][layer] = rows.astype(f32)
    small_out[...] = whole[at : at + SMALL, :LANES].astype(f32)
    for layer in range(LAYERS):
        for kind in range(3):
            for block in range(D // LANES):
                lanes = slice(block * LANES, (block + 1) * LANES)
                qkv_out[layer, kind, lanes] = qkv[layer][kind * LANES : (kind + 1) * LANES, lanes].astype(f32)


def call(body, outs, operands, scalars=0, scratch=(), scalar_outs=0, bulk=(), bulk_outs=()):
    specs = [SM] * scalars + [VM] * (len(operands) - scalars)
    out_specs = [VM] * (len(outs) - scalar_outs) + [SM] * scalar_outs
    for index in bulk:
        specs[index] = pl.BlockSpec()
    for index in bulk_outs:
        out_specs[index] = pl.BlockSpec()
    return pl.pallas_call(
        body,
        out_shape=tuple(jax.ShapeDtypeStruct(shape, kind) for shape, kind in outs),
        in_specs=specs,
        out_specs=tuple(out_specs),
        scratch_shapes=scratch,
        compiler_params=pltpu.CompilerParams(vmem_limit_bytes=24 * 2**20),
    )(*operands)


def after(value, *others):
    return lax.optimization_barrier((value, *others))[0] if others else value


def half_swap(value):
    count = lax.axis_size("mlp")
    return lax.ppermute(value, "mlp", [(i, i ^ 1) for i in range(count)])


def part_swap(value):
    count = lax.axis_size("mlp")
    return lax.ppermute(value, "mlp", [(i, i ^ 2) for i in range(count)])


def chunk_move(value, target):
    shards, parts = lax.axis_size("seq"), lax.axis_size("mlp")
    pairs = []
    for chunk in range(2 * shards):
        goal = target(chunk)
        if goal is None or not 0 <= goal < 2 * shards:
            continue
        for part in range(2):
            pairs.append(((chunk // 2) * parts + chunk % 2 + 2 * part, (goal // 2) * parts + goal % 2 + 2 * part))
    return lax.ppermute(value, AXES, pairs)


def scan(value, flags, chunks, reverse, others=lambda: ()):
    places, _ = flag_places(chunks)
    found, arrived = None, None
    for stage, (size, ways, last) in enumerate(scan_plan(chunks)):
        got = []
        for step in range(1, ways):
            if last:

                def target(chunk, step=step):
                    move = -step if reverse else step
                    return chunk + move * size if 0 <= (chunk // size) % ways + move < ways else None

            else:

                def target(chunk, step=step):
                    member = (chunk // size) % ways
                    return chunk + ((member ^ step) - member) * size

            got.append(chunk_move(value, target))
        at = places[reverse, stage]
        if last:
            return (found, tuple(got), at), arrived, value
        arrived = arrived or tuple(got)
        operands = (flags, after(value, *others()), *got) + (() if found is None else (found,))
        value, found = call(
            functools.partial(combine_kernel, at, ways, found is not None),
            ((value.shape, bf16), (value.shape, f32)),
            operands,
            1,
        )


def shard_swap(value, bit):
    count = lax.axis_size("seq")
    return lax.ppermute(value, "seq", [(i, i ^ (1 << bit)) for i in range(count)])


def by_place(flag, mine, other):
    return jnp.where(flag == 0, mine, other), jnp.where(flag == 0, other, mine)


def per_device(inputs, lengths, valid, norm_attn, w_qkv, blend, w_out, norm_ffn, w_up, w_down, grad_out):
    shards, parts = lax.axis_size("seq"), lax.axis_size("mlp")
    shard, part = lax.axis_index("seq"), lax.axis_index("mlp")
    half = part % 2
    side = shard % 2
    rows = inputs.shape[0] // 2
    chunks = 2 * shards
    units = w_up.shape[2]
    place = jnp.stack([half, part // 2, shard]).astype(jnp.int32)

    wide = 2 * LANES
    hidden_like = ((rows, D), f32)
    low_like = ((rows, D), bf16)
    heads_like = ((rows, wide), f32)
    heads_low = ((rows, wide), bf16)
    qkv_like = ((3, rows, wide), bf16)
    state_like = ((2, STATE, LANES), bf16)
    halo_like = ((2, 2, HALO, LANES), bf16)
    ffn_like = ((rows, units), f32)
    ffn_low = ((rows, units), bf16)
    shard_like = ((rows, LANES), bf16)
    gain_like = ((1, D), f32)

    piece_like = ((rows + 3 * SMALL, LANES), bf16)
    mine, theirs = call(
        pack_kernel,
        (piece_like, piece_like),
        (place, blend, inputs, norm_attn, norm_ffn),
        2,
        bulk=(2, 3, 4),
    )
    got = half_swap(theirs)
    pieces = (mine, got, part_swap(mine), part_swap(got))
    far_qkv, far_out, far_up, far_down = [
        [half_swap(after(w[layer], theirs)) for layer in range(LAYERS)] for w in (w_qkv, w_out, w_up, w_down)
    ]
    grad_mine, grad_theirs = call(pack_grad_kernel, (shard_like, shard_like), (place, after(grad_out, theirs)), 1)
    grad_got = half_swap(grad_theirs)
    grad_pieces = (grad_mine, grad_got, part_swap(grad_mine), part_swap(grad_got))

    before = lax.ppermute(
        after(valid, pieces[3])[2 * rows - LANES :].reshape(1, LANES), "seq", [(source, source + 1) for source in range(shards - 1)]
    )
    _, flag_count = flag_places(chunks)
    causal, causal_t, carried, tail, flags = call(
        functools.partial(setup_kernel, chunks),
        (
            ((rows, rows), bf16),
            ((rows, rows), bf16),
            ((rows, LANES), f32),
            ((rows, LANES), bf16),
            ((flag_count,), f32),
        ),
        (place, lengths, valid.reshape(1, 2 * rows)),
        2,
        scalar_outs=1,
    )
    (band,) = call(
        band_kernel, (((rows, LANES), f32),), (place, lengths, valid.reshape(1, 2 * rows), before), 2
    )

    saved = []
    base, adds = None, None
    for layer in range(LAYERS):
        outs = (hidden_like, low_like, qkv_like, state_like, halo_like)
        if layer == 0:
            hidden, normed, qkv, state, halo, gains, blends = call(
                functools.partial(qkv_kernel, True, layer),
                outs + (((SMALL, D), f32), ((SMALL, wide), f32)),
                (place, *pieces, w_qkv, far_qkv[layer], tail),
                1,
            )
        else:
            hidden, normed, qkv, state, halo = call(
                functools.partial(qkv_kernel, False, layer),
                outs,
                (place, base, *adds, gains, w_qkv, far_qkv[layer], tail),
                1,
            )
        halo = chunk_move(halo, lambda c: c + 1)
        one, two, sums = call(far_kernel, (heads_like,) * 3, (qkv, causal))
        (found, parts_got, at), arrived, _ = scan(state, flags, chunks, False, lambda: (one,))
        if layer == 0:
            found = after(found, *grad_pieces)
        (near,) = call(near_kernel, (heads_like,), (place, qkv, halo, band), 1)
        mixed, far_one, far_two, root, prefix, state, piece = call(
            functools.partial(mix_kernel, layer, at, len(parts_got)),
            (heads_low, heads_like, heads_like, heads_like, heads_like, state_like, low_like),
            (place, flags, qkv, near, one, two, sums, carried, blends, w_out, far_out[layer], found, *parts_got),
            2,
        )
        weights = (w_up, w_down, far_up[layer], far_down[layer])
        middle, normed_ffn, pre_own, pre_far, act_own, act_far, piece_ffn = call(
            functools.partial(ffn_kernel, layer),
            (hidden_like, low_like, ffn_like, ffn_like, ffn_low, ffn_low, low_like),
            (hidden, piece, part_swap(piece), gains, *weights),
        )
        saved.append(
            (hidden, normed, qkv, state, halo, mixed, far_one, far_two, root, prefix, middle, normed_ffn,
             weights, pre_own, pre_far, act_own, act_far)
        )
        base, adds = middle, (piece_ffn, part_swap(piece_ffn))
    out_mine, out_theirs = call(output_kernel, (shard_like, shard_like), (place, base, *adds), 1)
    output = jnp.concatenate(by_place(half, out_mine, half_swap(out_theirs)))

    base, adds = None, None
    d_gain_attn, d_gain_ffn, d_blends = [None] * LAYERS, [None] * LAYERS, [None] * LAYERS
    d_qkvs = [None] * LAYERS
    bits = (shards - 1).bit_length()
    side_first, line_first = (0, 1, 2), (1, 2, 0)

    def first_step(jobs, operands):
        height = sum(job_rows(job, units) for job in jobs)
        like = ((height, D), bf16)
        return call(functools.partial(grads_kernel, jobs), (like, like), (place, *operands), 1, bulk_outs=(0,))

    def group_steps(order, rows, first, second):
        height = rows[1] - rows[0]
        others = yield
        if bits != 3:
            if len(first) > 1:
                small = jnp.pad(first[1] + second[1], ((0, LANES - SMALL), (0, D - LANES)))
                total = jnp.concatenate([first[0].astype(f32) + second[0].astype(f32), small])
            else:
                total = (first[0].astype(f32) + second[0].astype(f32))[slice(*rows)]
            total = lax.psum(total, "seq").astype(bf16).reshape(2, height // 2, D)
            total = jnp.where((shard >> order[0]) % 2 == 0, total, total[::-1])
            for _ in range(6):
                yield total
            yield total[0], total[1]
        for at, bit in enumerate(order):
            height //= 2
            if at == 0 and len(first) > 1:
                body, operands = functools.partial(last_kernel, bit), (first[0], second[0], first[1], second[1])
            elif at == 0:
                body, operands = functools.partial(halve_kernel, bit, rows), (first[0], second[0])
            else:
                body, operands = functools.partial(halve_kernel, bit, (0, 2 * height)), (keep, got)
            keep, send = call(
                body,
                (((height, D), f32), ((height, D), bf16)),
                (place, operands[0], after(operands[1], *others), *operands[2:]),
                1,
                bulk=(1,) if at == 0 else (),
            )
            got = shard_swap(send, bit)
            others = yield send
        (value,) = call(add_kernel, (((height, D), bf16),), (keep, after(got, *others)))
        for bit in reversed(order):
            got = shard_swap(value, bit)
            if bit == order[0]:
                break
            others = yield value
            height *= 2
            (value,) = call(
                functools.partial(join_kernel, bit), (((height, D), bf16),), (place, value, after(got, *others)), 1
            )
        yield value
        yield (value, got)

    groups = []

    def start_group(layers, jobs, order, rows, first, second):
        steps = group_steps(order, rows, first, second)
        next(steps)
        groups.append((layers, jobs, order[0], steps))

    def step(index, *others):
        return groups[index][3].send(others)

    for layer in reversed(range(LAYERS)):
        (hidden, normed, qkv, state, halo, mixed, far_one, far_two, root, prefix, middle, normed_ffn,
         weights, pre_own, pre_far, act_own, act_far) = saved[layer]
        outs = (hidden_like, low_like, ffn_low, ffn_low, low_like)
        if base is None:
            resid, grad_rows, d_up_own, d_up_far, piece = call(
                functools.partial(ffn_back_kernel, True, layer),
                outs,
                (place, *grad_pieces, *weights, pre_own, pre_far),
                1,
            )
        else:
            resid, grad_rows, d_up_own, d_up_far, piece, d_gain_attn[layer + 1] = call(
                functools.partial(ffn_back_kernel, False, layer),
                outs + (gain_like,),
                (base, *adds, saved[layer + 1][0], gains, *weights, pre_own, pre_far),
            )
        (resid, out_rows, d_mixed, d_gain_ffn[layer], num_one, num_two, d_zeta, state_back, blend_far) = call(
            functools.partial(mix_back_kernel, layer),
            (hidden_like, low_like, heads_low, gain_like, heads_low, heads_low, heads_like, state_like,
             ((2, wide), f32)),
            (place, resid, piece, part_swap(piece), middle, gains, w_out, far_out[layer], qkv, far_one, far_two,
             root, carried, blends),
            1,
        )
        ext = HALO + rows + HALO
        dq_near, dk_near, dv_near, halo_back, blend_near = call(
            functools.partial(near_back_kernel, layer),
            (heads_like, heads_like, heads_like, halo_like, ((1, wide), f32)),
            (place, qkv, halo, band, d_mixed, blends),
            1,
            scratch=(pltpu.VMEM((ext, LANES), f32), pltpu.VMEM((ext, LANES), f32)),
        )
        halo_back = chunk_move(halo_back, lambda c: c - 1)
        (found, parts_got, at), arrived, value = scan(state_back, flags, chunks, True, lambda: (dq_near,))
        if layer > 0:
            jobs = ("up", "down", "out")
            own, far = first_step(
                jobs, (after(normed_ffn, value), d_up_own, d_up_far, act_own, act_far, grad_rows, mixed, out_rows)
            )
            start_group((layer,) * 3, jobs, side_first, (0, own.shape[0]), (own,), (half_swap(far),))
            made = far
        else:
            made = step(0, value)
            jobs = ("up", "qkv", "down", "out")
            own, far = first_step(
                jobs,
                (after(normed_ffn, made), d_up_own, d_up_far, saved[1][1], d_qkvs[1], act_own, act_far, grad_rows,
                 mixed, out_rows),
            )
            cut = job_rows("up", units) + job_rows("qkv", units)
            got = half_swap(far)
            start_group((0, 1), jobs[:2], side_first, (0, cut), (own,), (got,))
            start_group((0, 0), jobs[2:], line_first, (cut, own.shape[0]), (own,), (got,))
            made = far
        ready = [made]
        dq, dk_one, dk_two, dv = call(
            far_back_kernel,
            (heads_low, heads_like, heads_like, heads_like),
            (place, qkv, causal, causal_t, carried, state, prefix, after(num_one, *ready), num_two, d_zeta, dq_near,
             dv_near),
            1,
        )
        d_qkvs[layer], piece = call(
            functools.partial(qkv_back_kernel, layer, at, len(parts_got)),
            (qkv_like, low_like),
            (place, flags, qkv, dq, dk_one, dk_two, dk_near, dv, tail, halo_back, w_qkv, far_qkv[layer], found,
             *parts_got),
            2,
            scratch=(pltpu.VMEM((2, STATE, LANES), bf16),),
        )
        base, adds = resid, (piece, part_swap(piece))
        if layer > 0:
            base = after(base, step(0, piece))
        d_blends[layer] = (blend_near, blend_far)

    last_like = ((3 * LANES, D), bf16)
    made = step(0, step(2, step(1, piece)))
    own, far = call(functools.partial(grads_kernel, ("qkv",)), (last_like, last_like), (place, after(saved[0][1], made), d_qkvs[0]), 1)
    smalls = d_gain_attn[1:] + d_gain_ffn + [ref for pair in d_blends for ref in pair]
    small_like = ((SMALL, LANES), f32)
    mine, theirs, small_own, small_far = call(
        end_kernel,
        (shard_like, shard_like, small_like, small_like),
        (place, after(base, far), *adds, saved[0][0], gains, *smalls),
        1,
    )
    start_group((0,), ("qkv",), line_first, (0, 4 * LANES), (own, small_own), (half_swap(far), half_swap(small_far)))
    made = step(3, mine)
    for index in (0, 1, 2, 3, 0, 1, 2, 3, 0, 1, 2, 3, 1, 2, 3, 1, 2, 3):
        made = step(index, made)
    d_inputs = jnp.concatenate(by_place(half, mine, half_swap(theirs)))
    sums = [part for group in groups for part in next(group[3])]
    d_up, d_down, d_out, d_qkv, small = call(
        functools.partial(finish_kernel, [group[:3] for group in groups]),
        (
            ((LAYERS, D, units), f32),
            ((LAYERS, units, D), f32),
            ((LAYERS, LANES, D), f32),
            ((LAYERS, 3, D, LANES), f32),
            small_like,
        ),
        (place, *sums),
        1,
    )
    count = 2 * LAYERS + 3 * LAYERS
    d_norm_attn = small[:LAYERS]
    d_norm_ffn = small[LAYERS : 2 * LAYERS]
    d_blend = jnp.sum(small[2 * LAYERS : count].reshape(LAYERS, 3, 2, HD), axis=3)
    return (output, d_inputs, d_norm_attn, d_qkv, d_blend, d_out, d_norm_ffn, d_up, d_down)


def solution(mesh):
    placed = (
        P("seq", "mlp"),
        P(),
        P("seq"),
        P(None, "mlp"),
        P(None, None, None, "mlp"),
        P(None, None, "mlp"),
        P(None, "mlp", None),
        P(None, "mlp"),
        P(None, None, "mlp"),
        P(None, "mlp", None),
        P("seq", "mlp"),
    )
    return jax.shard_map(
        per_device,
        mesh=mesh,
        in_specs=placed,
        out_specs=(
            P("seq", "mlp"),
            P("seq", "mlp"),
            P(None, "mlp"),
            P(None, None, None, "mlp"),
            P(None, None, "mlp"),
            P(None, "mlp", None),
            P(None, "mlp"),
            P(None, None, "mlp"),
            P(None, "mlp", None),
        ),
        check_vma=False,
    )
```

```python
import functools
import math

import jax
import jax.numpy as jnp
from jax import lax
from jax.experimental import pallas as pl
from jax.experimental.pallas import tpu as pltpu
from jax.sharding import PartitionSpec as P

HD = 64
D = 512
BAND = 30
LAYERS = 2
HALO = 32
TILE = 64
LANES = 128
STATE = 144
SMALL = 16
AXES = ("seq", "mlp")

epsilon = 1e-05
masked_score = -1e30
score_scale = 1.0 / math.sqrt(HD)
far_scale = 1.0 / math.sqrt(HD)
f32 = jnp.float32
bf16 = jnp.bfloat16

VM = pl.BlockSpec(memory_space=pltpu.VMEM)
SM = pl.BlockSpec(memory_space=pltpu.SMEM)


def dot(x, y):
    return jnp.dot(x, y, preferred_element_type=f32)


def dot_nt(x, y):
    return lax.dot_general(x, y, (((1,), (1,)), ((), ())), preferred_element_type=f32)


def dot_tn(x, y):
    return lax.dot_general(x, y, (((0,), (0,)), ((), ())), preferred_element_type=f32)


def low_lanes(rows):
    return lax.broadcasted_iota(jnp.int32, (rows, LANES), 1) < HD


def split_heads(x):
    low = low_lanes(x.shape[0])
    zero = jnp.zeros_like(x)
    return jnp.concatenate([jnp.where(low, x, zero), jnp.where(low, zero, x)], axis=0)


def merge_heads(y):
    rows = y.shape[0] // 2
    return jnp.where(low_lanes(rows), y[:rows], y[rows:])


def head_sum(x):
    row = lax.broadcasted_iota(jnp.int32, (LANES, LANES), 0) < HD
    ones = jnp.where(row == low_lanes(LANES), 1.0, 0.0).astype(bf16)
    high = x.astype(bf16)
    rest = (x - high.astype(f32)).astype(bf16)
    return dot(high, ones) + dot(rest, ones)


def kernel_maps(x):
    return (
        jnp.where(x > 0, x + 1.0, jnp.exp(jnp.minimum(x, 0.0))).astype(bf16),
        jnp.tanh(x).astype(bf16),
    )


def maps_back(x, d_one, d_two):
    tanh = jnp.tanh(x)
    return jnp.where(x > 0, 1.0, jnp.exp(jnp.minimum(x, 0.0))) * d_one + (1.0 - tanh * tanh) * d_two


def put_state(ref, quarter, one, two, total):
    row = lax.broadcasted_iota(jnp.int32, (STATE - 2 * HD, LANES), 0)
    low = low_lanes(HD)
    ref[quarter, 0:HD, :] = jnp.where(low, one[:HD], one[HD:]).astype(bf16)
    ref[quarter, HD : 2 * HD, :] = jnp.where(low, two[:HD], two[HD:]).astype(bf16)
    ref[quarter, 2 * HD : STATE, :] = jnp.where(row == 0, total, 0.0).astype(bf16)


def get_state(ref, quarter):
    one = split_heads(ref[quarter, 0:HD, :])
    two = split_heads(ref[quarter, HD : 2 * HD, :])
    total = ref[quarter, 2 * HD : STATE, :].astype(f32)[0:1]
    return one, two, total


def norm_scale(hidden):
    return lax.rsqrt(jnp.sum(hidden * hidden, axis=1, keepdims=True) * (1.0 / D) + epsilon)


def norm_back(hidden, gain, grad):
    scale = norm_scale(hidden)
    gained = grad * gain
    inner = jnp.sum(gained * hidden, axis=1, keepdims=True) * (1.0 / D)
    back = scale * gained - hidden * (scale * scale * scale * inner)
    return back, jnp.sum(grad * hidden * scale, axis=0, keepdims=True)


def halo_bias(halo):
    ones = jnp.ones((LANES - HALO, LANES), bf16)
    flags = jnp.concatenate([halo[4], ones], axis=0)
    flags = dot_nt(jnp.ones((2 * TILE, LANES), bf16), flags)
    return jnp.where(flags > 0.5 * LANES, 0.0, masked_score)


def extend(halo, rows):
    return jnp.concatenate([halo, rows, jnp.zeros((HALO, LANES), bf16)], axis=0)


def three_parts(value):
    high = value.astype(bf16)
    rest = value - high.astype(f32)
    middle = rest.astype(bf16)
    low = (rest - middle.astype(f32)).astype(bf16)
    return jnp.concatenate([high, middle, low], axis=0)


def pack_kernel(place, inputs, norm_attn, norm_ffn, mine_out, theirs_out, rows_in, attn_in, ffn_in, sems):
    copies = [
        pltpu.make_async_copy(source, target, sems.at[k])
        for k, (source, target) in enumerate(((inputs, rows_in), (norm_attn, attn_in), (norm_ffn, ffn_in)))
    ]
    for copy in copies:
        copy.start()
    for copy in copies:
        copy.wait()
    rows = rows_in.shape[0] // 2
    small = [attn_in[...], ffn_in[...], jnp.zeros((SMALL - 2 * LAYERS, LANES), f32)]
    small = three_parts(jnp.concatenate(small, axis=0))
    first, second = rows_in[:rows], rows_in[rows:]
    mine_out[:rows] = jnp.where(place[0] == 0, first, second)
    theirs_out[:rows] = jnp.where(place[0] == 0, second, first)
    mine_out[rows:] = small
    theirs_out[rows:] = small


def pack_blend_kernel(blend, out):
    low = low_lanes(1)
    rows = []
    for layer in range(LAYERS):
        for kind in range(3):
            rows.append(jnp.where(low, blend[layer, kind, 0], blend[layer, kind, 1]))
    rows.append(jnp.zeros((SMALL - 3 * LAYERS, LANES), f32))
    out[...] = jnp.concatenate(rows, axis=0)


def pack_grad_kernel(place, grads, mine_out, theirs_out):
    rows = grads.shape[0] // 2
    first, second = grads[:rows], grads[rows:]
    mine_out[...] = jnp.where(place[0] == 0, first, second)
    theirs_out[...] = jnp.where(place[0] == 0, second, first)


def quarters(place):
    half, part = place[0], place[1]
    return 2 * part + half, 2 * part + 1 - half, 2 * (1 - part) + half, 2 * (1 - part) + 1 - half


def quarter_lanes(quarter):
    return pl.ds(pl.multiple_of(quarter * LANES, LANES), LANES)


def item_ends(lengths):
    ends = []
    for k in range(lengths.shape[0]):
        ends.append(lengths[k] if k == 0 else ends[-1] + lengths[k])
    return ends


def item_start(lengths, ends, positions):
    start = jnp.zeros_like(positions)
    for k, end in enumerate(ends):
        start = start + jnp.where(end <= positions, lengths[k], 0)
    return start


def scan_plan(chunks):
    stages, size = [], 1
    while size < chunks:
        ways = min(4, chunks // size)
        stages.append((size, ways, size * ways >= chunks))
        size *= ways
    return stages


def flag_places(chunks):
    at, places = 0, {}
    for reverse in (False, True):
        for stage, (_, ways, _) in enumerate(scan_plan(chunks)):
            places[reverse, stage] = at
            at += 2 * ways
    return places, at


def setup_kernel(
    chunks, place, lengths, valid, causal_out, causal_t_out, band_out, carried_out, tail_out, edge_out, flags_out
):
    rows = causal_out.shape[0]
    chunk = place[2] * 2 + place[0]
    first_row = chunk * rows
    ends = item_ends(lengths)

    def start_of(positions):
        return item_start(lengths, ends, positions)

    lane = lax.broadcasted_iota(jnp.int32, (1, rows), 1)
    starts_row = start_of(first_row + lane)
    starts = start_of(first_row + lax.broadcasted_iota(jnp.int32, (rows, LANES), 0))
    both = jnp.concatenate([starts, starts], axis=1)
    words = valid[...]
    own_words = jnp.where(place[0] == 0, words[:, :rows], words[:, rows:])
    row_at = lax.broadcasted_iota(jnp.int32, (rows, rows), 0)
    lane_at = lax.broadcasted_iota(jnp.int32, (rows, rows), 1)
    own_column = jnp.sum(jnp.where(row_at == lane_at, own_words, 0), axis=1, keepdims=True)
    same = both == starts_row
    causal_out[...] = jnp.where((lane_at <= row_at) & same & (own_words == 1), 1.0, 0.0).astype(bf16)
    causal_t_out[...] = jnp.where((row_at <= lane_at) & same & (own_column == 1), 1.0, 0.0).astype(bf16)
    carried_out[...] = jnp.where(starts < first_row, 1.0, 0.0)
    last_start = start_of(first_row + rows - 1)
    edge_out[...] = jnp.where(jnp.broadcast_to(own_column, (rows, LANES))[rows - HALO :] == 1, 1.0, 0.0).astype(bf16)
    tail_out[...] = jnp.where((starts == last_start) & (own_column == 1), 1.0, 0.0).astype(bf16)
    all_words = jnp.concatenate([jnp.ones((1, LANES), jnp.int32), own_words, jnp.zeros((1, LANES), jnp.int32)], axis=1)
    tile_row = lax.broadcasted_iota(jnp.int32, (TILE, LANES), 0)
    tile_lane = lax.broadcasted_iota(jnp.int32, (TILE, LANES), 1)
    gap = tile_row + HALO - tile_lane
    for tile in range(rows // TILE):
        key_starts = start_of(first_row + tile * TILE - HALO + lax.broadcasted_iota(jnp.int32, (1, LANES), 1))
        offset = LANES - HALO + tile * TILE
        key_words = all_words[:, offset : offset + LANES]
        at = slice(tile * TILE, (tile + 1) * TILE)
        allowed = (gap >= 0) & (gap <= BAND) & (starts[at] == key_starts) & ((key_words == 1) | (gap == 0))
        band_out[at] = jnp.where(allowed, 0.0, masked_score)

    places, _ = flag_places(chunks)
    for reverse in (False, True):
        edge = start_of(first_row + (rows - 1 if reverse else 0))
        for stage, (size, ways, last) in enumerate(scan_plan(chunks)):
            member = lax.rem(lax.div(chunk, size), ways)
            base = chunk - member * size - lax.rem(chunk, size)
            group = base if reverse else base + ways * size - 1
            group = start_of(group * rows + (0 if reverse else rows - 1))
            for step in range(ways):
                if last:
                    other = member + step if reverse else member - step
                else:
                    other = jnp.bitwise_xor(member, step)
                block = base + other * size + (0 if reverse else size - 1)
                start = start_of(block * rows + (0 if reverse else rows - 1))
                ahead = (other > member) if reverse else (other < member)
                ahead = ahead & (other >= 0) & (other < ways)
                at = places[reverse, stage] + 2 * step
                flags_out[at] = jnp.where(ahead & (start == edge), 1.0, 0.0)
                flags_out[at + 1] = jnp.where(start == group, 1.0, 0.0)


def combine_kernel(at, ways, has_found, flags, *refs):
    got, refs = refs[:ways], refs[ways:]
    total = sum(flags[at + 2 * step + 1] * got[step][...].astype(f32) for step in range(ways))
    refs[-2][...] = total.astype(bf16)
    found = sum(flags[at + 2 * step] * got[step][...].astype(f32) for step in range(1, ways))
    refs[-1][...] = found + refs[0][...] if has_found else found


def last_combine(at, flags, found, got, out):
    value = found[...]
    for step, part in enumerate(got):
        value = value + flags[at + 2 * (step + 1)] * part[...].astype(f32)
    out[...] = value.astype(bf16)


def qkv_kernel(first, layer, place, *refs):
    if first:
        refs, outs = refs[:8], refs[8:]
        pieces, (own, other, tail, edge) = refs[:4], refs[4:]
        hidden_out, normed_out, qkv_out, state_out, halo_out, gains = outs
        rows = hidden_out.shape[0]
        for piece, quarter in zip(pieces, quarters(place)):
            hidden_out[:, quarter_lanes(quarter)] = piece[:rows].astype(f32)
            parts = piece[rows:].astype(f32)
            small = parts[:SMALL] + parts[SMALL : 2 * SMALL] + parts[2 * SMALL :]
            gains[:, quarter_lanes(quarter)] = small
        hidden = hidden_out[...]
    else:
        base, part_a, part_b, gains, own, other, tail, edge, *outs = refs
        hidden_out, normed_out, qkv_out, state_out, halo_out = outs
        hidden = base[...] + (part_a[...].astype(f32) + part_b[...].astype(f32))
        hidden_out[...] = hidden
    rows = hidden.shape[0]
    normed = (hidden * norm_scale(hidden) * gains[layer : layer + 1]).astype(bf16)
    normed_out[...] = normed
    found = []
    for kind in range(3):
        weight = jnp.concatenate([own[layer, kind], other[kind]], axis=1)
        found.append(dot(normed, weight).astype(bf16))
        qkv_out[kind] = found[kind]
    for pair in range(2):
        quarter = place[0] if pair == 0 else 1 - place[0]
        lanes = slice(pair * LANES, (pair + 1) * LANES)
        keys, values = found[1][:, lanes], found[2][:, lanes]
        one, two = kernel_maps(keys.astype(f32))
        one, two = one * tail[...], two * tail[...]
        put_state(
            state_out,
            quarter,
            dot_tn(one, values),
            dot_tn(two, values),
            jnp.sum(one.astype(f32), axis=0, keepdims=True),
        )
        halo_out[2 * quarter] = keys[rows - HALO :]
        halo_out[2 * quarter + 1] = values[rows - HALO :]
    halo_out[4] = edge[...]


def far_kernel(qkv, causal, one_out, two_out, sums_out):
    masks = jnp.concatenate([causal[...], causal[...]], axis=0)
    for pair in range(2):
        lanes = slice(pair * LANES, (pair + 1) * LANES)
        queries, keys, values = qkv[0, :, lanes], qkv[1, :, lanes], qkv[2, :, lanes]
        maps_q, maps_k = kernel_maps(queries.astype(f32)), kernel_maps(keys.astype(f32))
        for query, key, out in ((maps_q[0], maps_k[0], one_out), (maps_q[1], maps_k[1], two_out)):
            attn = dot_nt(split_heads(query), key).astype(bf16) * masks
            out[:, lanes] = merge_heads(dot(attn, values))
        sums_out[:, lanes] = dot(causal[...], maps_k[0])


def near_kernel(place, qkv, halo, band, near_out):
    rows = qkv.shape[1]
    bias = halo_bias(halo)
    for pair in range(2):
        quarter = place[0] if pair == 0 else 1 - place[0]
        lanes = slice(pair * LANES, (pair + 1) * LANES)
        queries, keys, values = qkv[0, :, lanes], qkv[1, :, lanes], qkv[2, :, lanes]
        ext_keys = extend(halo[2 * quarter], keys)
        ext_values = extend(halo[2 * quarter + 1], values)
        for tile in range(rows // TILE):
            at = slice(tile * TILE, (tile + 1) * TILE)
            window = slice(tile * TILE, tile * TILE + LANES)
            allowed = jnp.concatenate([band[at], band[at]], axis=0)
            allowed = allowed + bias if tile == 0 else allowed
            scores = dot_nt(split_heads(queries[at]), ext_keys[window]) * score_scale + allowed
            weights = jnp.exp(scores - jnp.max(scores, axis=1, keepdims=True))
            weights = weights / jnp.sum(weights, axis=1, keepdims=True)
            near_out[at, lanes] = merge_heads(dot(weights.astype(bf16), ext_values[window]))


def mix_kernel(layer, at, count, place, flags, qkv, near, one, two, sums, carried, blends, own, other, found, *refs):
    got = refs[:count]
    mixed_out, far_one_out, far_two_out, root_out, prefix_out, state, part_out = refs[count:]
    last_combine(at, flags, found, got, state)
    mixed = []
    row = 3 * layer
    for pair in range(2):
        quarter = place[0] if pair == 0 else 1 - place[0]
        lanes = slice(pair * LANES, (pair + 1) * LANES)
        query_one, query_two = kernel_maps(qkv[0, :, lanes].astype(f32))
        state_one, state_two, total = get_state(state, quarter)
        num_one = one[:, lanes] + carried[...] * dot(query_one, state_one)
        num_two = two[:, lanes] + carried[...] * dot(query_two, state_two)
        prefix = sums[:, lanes] + carried[...] * total
        zeta = head_sum(query_one.astype(f32) * prefix)
        root = lax.rsqrt(zeta + 1.0)
        far_one = num_one * root * far_scale
        far_two = num_two * root
        far_one_out[:, lanes] = far_one
        far_two_out[:, lanes] = far_two
        root_out[:, lanes] = root
        prefix_out[:, lanes] = prefix
        mixed.append(
            (
                blends[row : row + 1, lanes] * near[:, lanes]
                + blends[row + 1 : row + 2, lanes] * far_one
                + blends[row + 2 : row + 3, lanes] * far_two
            ).astype(bf16)
        )
        mixed_out[:, lanes] = mixed[pair]
    weight = jnp.concatenate([own[layer], other[...]], axis=0)
    part_out[...] = dot(jnp.concatenate(mixed, axis=1), weight).astype(bf16)


def ffn_kernel(
    layer, base, part_a, part_b, gains, up_own, down_own, up_far, down_far,
    middle_out, normed_out, pre_own_out, pre_far_out, act_own_out, act_far_out, part_out,
):
    middle = base[...] + (part_a[...].astype(f32) + part_b[...].astype(f32))
    middle_out[...] = middle
    gain = gains[LAYERS + layer : LAYERS + layer + 1]
    normed = (middle * norm_scale(middle) * gain).astype(bf16)
    normed_out[...] = normed
    weights = (
        (up_own[layer], down_own[layer], pre_own_out, act_own_out),
        (up_far[...], down_far[...], pre_far_out, act_far_out),
    )
    total = None
    for up, down, pre_out, act_out in weights:
        pre = dot(normed, up)
        pre_out[...] = pre
        inner = jnp.tanh(math.sqrt(2.0 / math.pi) * (pre + 0.044715 * pre * pre * pre))
        act = (0.5 * pre * (1.0 + inner)).astype(bf16)
        act_out[...] = act
        product = dot(act, down)
        total = product if total is None else total + product
    part_out[...] = total.astype(bf16)


def shard_rows(whole, place, mine_out, theirs_out):
    first = [whole[:, m * LANES : (m + 1) * LANES] for m in range(4)]
    even, odd = [jnp.where(place[1] == 0, first[h], first[2 + h]) for h in range(2)]
    mine_out[...] = jnp.where(place[0] == 0, even, odd)
    theirs_out[...] = jnp.where(place[0] == 0, odd, even)


def output_kernel(place, base, part_a, part_b, mine_out, theirs_out):
    whole = base[...] + (part_a[...].astype(f32) + part_b[...].astype(f32))
    shard_rows(whole.astype(bf16), place, mine_out, theirs_out)


def gelu_slope(pre):
    c = math.sqrt(2.0 / math.pi)
    inner = jnp.tanh(c * (pre + 0.044715 * pre * pre * pre))
    return 0.5 * (1.0 + inner) + 0.5 * pre * (1.0 - inner * inner) * (c * (1.0 + 3 * 0.044715 * pre * pre))


def ffn_back_kernel(first, layer, *refs):
    if first:
        place, *refs = refs
        pieces, refs = refs[:4], refs[4:]
        weights, outs = refs[:6], refs[6:]
        resid_out, rows_out, d_up_own_out, d_up_far_out, part_out = outs
        for piece, quarter in zip(pieces, quarters(place)):
            resid_out[:, quarter_lanes(quarter)] = piece[...].astype(f32)
        resid = resid_out[...]
    else:
        base, part_a, part_b, hidden, gains, *refs = refs
        weights, outs = refs[:6], refs[6:]
        resid_out, rows_out, d_up_own_out, d_up_far_out, part_out, gain_out = outs
        back, gain_out[...] = norm_back(
            hidden[...], gains[layer + 1 : layer + 2], part_a[...].astype(f32) + part_b[...].astype(f32)
        )
        resid = base[...] + back
        resid_out[...] = resid
    up_own, down_own, up_far, down_far, pre_own, pre_far = weights
    rows = resid.astype(bf16)
    rows_out[...] = rows
    total = None
    for up, down, pre, out in (
        (up_own[layer], down_own[layer], pre_own, d_up_own_out),
        (up_far[...], down_far[...], pre_far, d_up_far_out),
    ):
        d_up = (gelu_slope(pre[...]) * dot_nt(rows, down)).astype(bf16)
        out[...] = d_up
        product = dot_nt(d_up, up)
        total = product if total is None else total + product
    part_out[...] = total.astype(bf16)


def mix_back_kernel(
    layer, place, base, part_a, part_b, middle, gains, own, other, qkv, far_one, far_two, root, carried, blends,
    resid_out, rows_out, mixed_out, gain_out, num_one_out, num_two_out, zeta_out, state_out, blend_out,
):
    back, gain_out[...] = norm_back(
        middle[...],
        gains[LAYERS + layer : LAYERS + layer + 1],
        part_a[...].astype(f32) + part_b[...].astype(f32),
    )
    resid = base[...] + back
    resid_out[...] = resid
    blend = blends[3 * layer : 3 * layer + 3]
    rows = resid.astype(bf16)
    rows_out[...] = rows
    weight = jnp.concatenate([own[layer], other[...]], axis=0)
    d_mixed = dot_nt(rows, weight).astype(bf16)
    mixed_out[...] = d_mixed
    for pair in range(2):
        quarter = place[0] if pair == 0 else 1 - place[0]
        lanes = slice(pair * LANES, (pair + 1) * LANES)
        grad = d_mixed[:, lanes].astype(f32)
        scale = root[:, lanes]
        dot_one = grad * far_one[:, lanes]
        dot_two = grad * far_two[:, lanes]
        blend_one, blend_two = blend[1:2, lanes], blend[2:3, lanes]
        blend_out[0:1, lanes] = jnp.sum(dot_one, axis=0, keepdims=True)
        blend_out[1:2, lanes] = jnp.sum(dot_two, axis=0, keepdims=True)
        num_one = (grad * (blend_one * far_scale) * scale).astype(bf16)
        num_two = (grad * blend_two * scale).astype(bf16)
        d_zeta = head_sum(blend_one * dot_one + blend_two * dot_two) * (-0.5 * scale * scale)
        num_one_out[:, lanes] = num_one
        num_two_out[:, lanes] = num_two
        zeta_out[:, lanes] = d_zeta
        query_one, query_two = kernel_maps(qkv[0, :, lanes].astype(f32))
        reach = carried[...].astype(bf16)
        put_state(
            state_out,
            quarter,
            dot_tn(query_one * reach, num_one),
            dot_tn(query_two * reach, num_two),
            jnp.sum(carried[...] * d_zeta * query_one.astype(f32), axis=0, keepdims=True),
        )


def near_back_kernel(
    layer, place, qkv, halo, band, d_mixed, blends, dq_out, dk_out, dv_out, halo_out, blend_out, near_k, near_v
):
    rows = qkv.shape[1]
    row_low = lax.broadcasted_iota(jnp.int32, (2 * TILE, 1), 0) < TILE
    bias = halo_bias(halo)
    row = 3 * layer
    for pair in range(2):
        quarter = place[0] if pair == 0 else 1 - place[0]
        lanes = slice(pair * LANES, (pair + 1) * LANES)
        queries, keys, values = qkv[0, :, lanes], qkv[1, :, lanes], qkv[2, :, lanes]
        grads = d_mixed[:, lanes]
        blend = blends[row : row + 1, lanes]
        ext_keys = extend(halo[2 * quarter], keys)
        ext_values = extend(halo[2 * quarter + 1], values)
        near_k[...] = jnp.zeros_like(near_k)
        near_v[...] = jnp.zeros_like(near_v)
        blend_rows = jnp.where(row_low, blend[:, :1], blend[:, HD : HD + 1])
        sums = None
        for tile in range(rows // TILE):
            at = slice(tile * TILE, (tile + 1) * TILE)
            window = slice(tile * TILE, tile * TILE + LANES)
            allowed = jnp.concatenate([band[at], band[at]], axis=0)
            allowed = allowed + bias if tile == 0 else allowed
            query_split, grad_split = split_heads(queries[at]), split_heads(grads[at])
            scores = dot_nt(query_split, ext_keys[window]) * score_scale + allowed
            probs = jnp.exp(scores - jnp.max(scores, axis=1, keepdims=True))
            probs = probs / jnp.sum(probs, axis=1, keepdims=True)
            d_probs = dot_nt(grad_split, ext_values[window])
            inner = jnp.sum(probs * d_probs, axis=1, keepdims=True)
            sums = inner if sums is None else sums + inner
            d_scores = (probs * (d_probs - inner) * blend_rows).astype(bf16)
            dq_out[at, lanes] = score_scale * merge_heads(dot(d_scores, ext_keys[window]))
            near_k[window] += dot_tn(d_scores, query_split)
            near_v[window] += dot_tn(probs.astype(bf16), grad_split)
        sum_low = jnp.sum(sums[:TILE], axis=0, keepdims=True)
        sum_high = jnp.sum(sums[TILE:], axis=0, keepdims=True)
        blend_out[0:1, lanes] = jnp.where(low_lanes(1), sum_low, sum_high) * (1.0 / HD)
        dk_out[:, lanes] = score_scale * near_k[HALO : HALO + rows]
        dv_out[:, lanes] = blend * near_v[HALO : HALO + rows]
        halo_out[quarter, 0] = (score_scale * near_k[0:HALO]).astype(bf16)
        halo_out[quarter, 1] = (blend * near_v[0:HALO]).astype(bf16)


def far_back_kernel(
    place, qkv, causal, causal_t, carried, state, prefix, num_one, num_two, d_zeta, dq_near, dv_near,
    dq_out, dk_one_out, dk_two_out, dv_out,
):
    masks = jnp.concatenate([causal[...], causal[...]], axis=0)
    masks_t = jnp.concatenate([causal_t[...], causal_t[...]], axis=1)
    for pair in range(2):
        quarter = place[0] if pair == 0 else 1 - place[0]
        lanes = slice(pair * LANES, (pair + 1) * LANES)
        queries, keys, values = qkv[0, :, lanes], qkv[1, :, lanes], qkv[2, :, lanes]
        state_one, state_two, unused_total = get_state(state, quarter)
        query_one, query_two = kernel_maps(queries.astype(f32))
        key_one, key_two = kernel_maps(keys.astype(f32))
        d_values = dv_near[:, lanes]
        d_queries = []
        for query, key, num, square, out in (
            (query_one, key_one, num_one[:, lanes], state_one, dk_one_out),
            (query_two, key_two, num_two[:, lanes], state_two, dk_two_out),
        ):
            query_split, num_split = split_heads(query), split_heads(num)
            attn_t = dot_nt(key, query_split).astype(bf16) * masks_t
            grad = dot_nt(num_split, values).astype(bf16) * masks
            grad_t = dot_nt(values, num_split).astype(bf16) * masks_t
            d_values = d_values + dot(attn_t, num_split)
            d_queries.append(merge_heads(dot(grad, key)) + carried[...] * dot_nt(num, square))
            out[:, lanes] = dot(grad_t, query_split)
        zeta = d_zeta[:, lanes]
        d_queries[0] += zeta * prefix[:, lanes]
        dk_one_out[:, lanes] += dot(causal_t[...], (zeta * query_one.astype(f32)).astype(bf16))
        back = maps_back(queries.astype(f32), d_queries[0], d_queries[1])
        dq_out[:, lanes] = (back + dq_near[:, lanes]).astype(bf16)
        dv_out[:, lanes] = d_values


def qkv_back_kernel(
    layer, at, count, place, flags, qkv, dq, dk_one, dk_two, dk_near, dv, tail, halo, own, other, found, *refs
):
    got = refs[:count]
    d_qkv_out, part_out, state = refs[count:]
    last_combine(at, flags, found, got, state)
    rows = qkv.shape[1]
    empty = jnp.zeros((rows - HALO, LANES), f32)
    for pair in range(2):
        quarter = place[0] if pair == 0 else 1 - place[0]
        lanes = slice(pair * LANES, (pair + 1) * LANES)
        keys, values = qkv[1, :, lanes], qkv[2, :, lanes]
        key_one, key_two = kernel_maps(keys.astype(f32))
        state_one, state_two, total = get_state(state, quarter)
        weight = tail[...].astype(f32)
        d_one = dk_one[:, lanes] + weight * (dot_nt(values, state_one) + total)
        d_two = dk_two[:, lanes] + weight * dot_nt(values, state_two)
        halo_k = jnp.concatenate([empty, halo[quarter, 0].astype(f32)], axis=0)
        halo_v = jnp.concatenate([empty, halo[quarter, 1].astype(f32)], axis=0)
        d_qkv_out[1, :, lanes] = (
            maps_back(keys.astype(f32), d_one, d_two) + dk_near[:, lanes] + halo_k
        ).astype(bf16)
        d_qkv_out[2, :, lanes] = (
            dv[:, lanes] + weight * (dot(key_one, state_one) + dot(key_two, state_two)) + halo_v
        ).astype(bf16)
    d_qkv_out[0] = dq[...]
    total = None
    for kind in range(3):
        weight = jnp.concatenate([own[layer, kind], other[kind]], axis=1)
        product = dot_nt(d_qkv_out[kind], weight)
        total = product if total is None else total + product
    part_out[...] = total.astype(bf16)


JOB_REFS = {"up": 3, "down": 3, "out": 2, "qkv": 2}


def job_rows(job, units):
    return {"up": D, "down": units, "out": LANES, "qkv": 3 * LANES}[job]


def fill_grads(jobs, refs, own, far):
    at = 0
    for job in jobs:
        mine, refs = refs[: JOB_REFS[job]], refs[JOB_REFS[job] :]
        if job == "up":
            normed, grad_own, grad_far = mine
            own[at : at + D] = dot_tn(normed[...], grad_own[...]).astype(bf16)
            far[at : at + D] = dot_tn(normed[...], grad_far[...]).astype(bf16)
            at += D
        elif job == "down":
            act_own, act_far, grad = mine
            units = act_own.shape[1]
            own[at : at + units] = dot_tn(act_own[...], grad[...]).astype(bf16)
            far[at : at + units] = dot_tn(act_far[...], grad[...]).astype(bf16)
            at += units
        elif job == "out":
            mixed, grad = mine
            found = dot_tn(mixed[...], grad[...]).astype(bf16)
            own[at : at + LANES] = found[:LANES]
            far[at : at + LANES] = found[LANES:]
            at += LANES
        else:
            normed, d_qkv = mine
            for kind in range(3):
                found = dot_tn(normed[...], d_qkv[kind]).astype(bf16)
                for block in range(D // LANES):
                    lanes = slice(block * LANES, (block + 1) * LANES)
                    own[at : at + LANES, lanes] = found[lanes, :LANES]
                    far[at : at + LANES, lanes] = found[lanes, LANES:]
                at += LANES


def grads_kernel(jobs, place, *refs):
    fill_grads(jobs, refs[:-2], refs[-2], refs[-1])


def shard_bit(place, bit):
    return lax.rem(lax.div(place[2], 1 << bit), 2)


def give_half(bit, place, total, keep_out, send_out):
    rows = total.shape[0] // 2
    low = shard_bit(place, bit) == 0
    keep_out[...] = jnp.where(low, total[:rows], total[rows:])
    send_out[...] = jnp.where(low, total[rows:], total[:rows]).astype(bf16)


def halve_kernel(bit, rows, place, first, second, keep_out, send_out):
    at = slice(*rows)
    give_half(bit, place, first[at].astype(f32) + second[at].astype(f32), keep_out, send_out)


def add_kernel(first, second, out):
    out[...] = (first[...].astype(f32) + second[...].astype(f32)).astype(bf16)


def join_kernel(bit, place, mine, got, out):
    low = shard_bit(place, bit) == 0
    rows = mine.shape[0]
    out[:rows] = jnp.where(low, mine[...], got[...])
    out[rows:] = jnp.where(low, got[...], mine[...])


def end_kernel(place, base, part_a, part_b, hidden, gains, *refs):
    smalls, (mine_out, theirs_out, own_out, far_out) = refs[: 4 * LAYERS - 1], refs[4 * LAYERS - 1 :]
    gain_refs, blend_refs = smalls[: 2 * LAYERS - 1], smalls[2 * LAYERS - 1 :]
    back, gain = norm_back(hidden[...], gains[0:1], part_a[...].astype(f32) + part_b[...].astype(f32))
    shard_rows((base[...] + back).astype(bf16), place, mine_out, theirs_out)
    gain_rows = jnp.concatenate([gain] + [ref[...] for ref in gain_refs], axis=0)
    blend_rows = jnp.concatenate([ref[...] for ref in blend_refs], axis=0)
    extras = []
    for to in range(2):
        features = jnp.where(
            place[1] == 0,
            gain_rows[:, to * LANES : (to + 1) * LANES],
            gain_rows[:, (2 + to) * LANES : (3 + to) * LANES],
        )
        blends = jnp.where(place[0] == to, blend_rows[:, :LANES], blend_rows[:, LANES:])
        extras.append(jnp.concatenate([features, blends, jnp.zeros((SMALL - 5 * LAYERS, LANES), f32)], axis=0))
    own_out[...] = jnp.where(place[0] == 0, extras[0], extras[1])
    far_out[...] = jnp.where(place[0] == 0, extras[1], extras[0])


def last_kernel(bit, place, own, far, small_own, small_far, keep_out, send_out):
    small = jnp.concatenate([small_own[...] + small_far[...], jnp.zeros((SMALL, D - LANES), f32)], axis=1)
    small = jnp.concatenate([small, jnp.zeros((LANES - SMALL, D), f32)], axis=0)
    total = jnp.concatenate([own[...].astype(f32) + far[...].astype(f32), small], axis=0)
    give_half(bit, place, total, keep_out, send_out)


def in_order(bit, place, mine, other):
    low = shard_bit(place, bit) == 0
    first, second = jnp.where(low, mine[...], other[...]), jnp.where(low, other[...], mine[...])
    return jnp.concatenate([first, second], axis=0)


def finish_wide_kernel(groups, place, *refs):
    refs, (up_out, down_out, out_out, above_out) = refs[:-4], refs[-4:]
    outs = {"up": up_out, "down": down_out, "out": out_out}
    for group, (layers, jobs, bit) in enumerate(groups):
        whole = in_order(bit, place, refs[2 * group], refs[2 * group + 1])
        at = 0
        for layer, job in zip(layers, jobs):
            rows = whole[at : at + job_rows(job, up_out.shape[2])]
            at += rows.shape[0]
            if job == "qkv":
                above_out[...] = rows
            else:
                outs[job][layer] = rows.astype(f32)


def finish_qkv_kernel(bit, place, mine, other, above, qkv_out, attn_out, ffn_out, blend_out):
    whole = in_order(bit, place, mine, other)
    at = 3 * LANES
    for layer, rows in enumerate((whole, above)):
        for kind in range(3):
            for block in range(D // LANES):
                lanes = slice(block * LANES, (block + 1) * LANES)
                qkv_out[layer, kind, lanes] = rows[kind * LANES : (kind + 1) * LANES, lanes].astype(f32)
    small = whole[at : at + SMALL, :LANES].astype(f32)
    attn_out[...] = small[:LAYERS]
    ffn_out[...] = small[LAYERS : 2 * LAYERS]
    blends = small[2 * LAYERS : 5 * LAYERS]
    low = low_lanes(3 * LAYERS)
    lane = lax.broadcasted_iota(jnp.int32, (3 * LAYERS, LANES), 1)
    first = jnp.sum(jnp.where(low, blends, 0.0), axis=1, keepdims=True)
    second = jnp.sum(jnp.where(low, 0.0, blends), axis=1, keepdims=True)
    blend_out[...] = jnp.where(lane == 0, first, second)


def call(body, outs, operands, scalars=0, scratch=(), scalar_outs=0, bulk=(), bulk_outs=()):
    specs = [SM] * scalars + [VM] * (len(operands) - scalars)
    out_specs = [VM] * (len(outs) - scalar_outs) + [SM] * scalar_outs
    for index in bulk:
        specs[index] = pl.BlockSpec()
    for index in bulk_outs:
        out_specs[index] = pl.BlockSpec()
    return pl.pallas_call(
        body,
        out_shape=tuple(jax.ShapeDtypeStruct(shape, kind) for shape, kind in outs),
        in_specs=specs,
        out_specs=tuple(out_specs),
        scratch_shapes=scratch,
        compiler_params=pltpu.CompilerParams(vmem_limit_bytes=24 * 2**20),
    )(*operands)


def after(value, *others):
    return lax.optimization_barrier((value, *others))[0] if others else value


def half_swap(value):
    count = lax.axis_size("mlp")
    return lax.ppermute(value, "mlp", [(i, i ^ 1) for i in range(count)])


def part_swap(value):
    count = lax.axis_size("mlp")
    return lax.ppermute(value, "mlp", [(i, i ^ 2) for i in range(count)])


def both_swap(value):
    count = lax.axis_size("mlp")
    return lax.ppermute(value, "mlp", [(i, i ^ 3) for i in range(count)])


def chunk_move(value, target):
    shards, parts = lax.axis_size("seq"), lax.axis_size("mlp")
    pairs = []
    for chunk in range(2 * shards):
        goal = target(chunk)
        if goal is None or not 0 <= goal < 2 * shards:
            continue
        for part in range(2):
            pairs.append(((chunk // 2) * parts + chunk % 2 + 2 * part, (goal // 2) * parts + goal % 2 + 2 * part))
    return lax.ppermute(value, AXES, pairs)


def scan(value, flags, chunks, reverse, others=lambda: ()):
    places, _ = flag_places(chunks)
    found, arrived = None, None
    for stage, (size, ways, last) in enumerate(scan_plan(chunks)):
        got = []
        for step in range(1, ways):
            if last:

                def target(chunk, step=step):
                    move = -step if reverse else step
                    return chunk + move * size if 0 <= (chunk // size) % ways + move < ways else None

            else:

                def target(chunk, step=step):
                    member = (chunk // size) % ways
                    return chunk + ((member ^ step) - member) * size

            got.append(chunk_move(value, target))
        at = places[reverse, stage]
        if last:
            return (found, tuple(got), at), arrived, value
        arrived = arrived or tuple(got)
        operands = (flags, after(value, *others()), *got) + (() if found is None else (found,))
        value, found = call(
            functools.partial(combine_kernel, at, ways, found is not None),
            ((value.shape, bf16), (value.shape, f32)),
            operands,
            1,
        )


def shard_swap(value, bit):
    count = lax.axis_size("seq")
    return lax.ppermute(value, "seq", [(i, i ^ (1 << bit)) for i in range(count)])


def by_place(flag, mine, other):
    return jnp.where(flag == 0, mine, other), jnp.where(flag == 0, other, mine)


def per_device(inputs, lengths, valid, norm_attn, w_qkv, blend, w_out, norm_ffn, w_up, w_down, grad_out):
    shards, parts = lax.axis_size("seq"), lax.axis_size("mlp")
    shard, part = lax.axis_index("seq"), lax.axis_index("mlp")
    half = part % 2
    side = shard % 2
    rows = inputs.shape[0] // 2
    chunks = 2 * shards
    units = w_up.shape[2]
    place = jnp.stack([half, part // 2, shard]).astype(jnp.int32)

    wide = 2 * LANES
    hidden_like = ((rows, D), f32)
    low_like = ((rows, D), bf16)
    heads_like = ((rows, wide), f32)
    heads_low = ((rows, wide), bf16)
    qkv_like = ((3, rows, wide), bf16)
    state_like = ((2, STATE, LANES), bf16)
    halo_like = ((2, 2, HALO, LANES), bf16)
    ffn_like = ((rows, units), f32)
    ffn_low = ((rows, units), bf16)
    shard_like = ((rows, LANES), bf16)
    gain_like = ((1, D), f32)

    piece_like = ((rows + 3 * SMALL, LANES), bf16)
    (blend_rows,) = call(pack_blend_kernel, (((SMALL, LANES), f32),), (blend,), 1)
    mine, theirs = pl.pallas_call(
        pack_kernel,
        out_shape=tuple(jax.ShapeDtypeStruct(*piece_like) for _ in range(2)),
        in_specs=[SM] + [pl.BlockSpec(memory_space=pl.ANY)] * 3,
        out_specs=(VM, VM),
        scratch_shapes=(
            pltpu.VMEM(inputs.shape, bf16),
            pltpu.VMEM(norm_attn.shape, f32),
            pltpu.VMEM(norm_ffn.shape, f32),
            pltpu.SemaphoreType.DMA((3,)),
        ),
        compiler_params=pltpu.CompilerParams(vmem_limit_bytes=24 * 2**20),
    )(place, inputs, norm_attn, norm_ffn)
    got = half_swap(theirs)
    pieces = (mine, got, part_swap(mine), both_swap(theirs))
    far_qkv, far_out, far_up, far_down = [
        [
            half_swap(after(w[layer], theirs)) for layer in range(LAYERS)
        ]
        for w in (w_qkv, w_out, w_up, w_down)
    ]
    grad_mine, grad_theirs = call(pack_grad_kernel, (shard_like, shard_like), (place, after(grad_out, theirs)), 1)
    grad_pieces = (grad_mine, half_swap(grad_theirs), part_swap(grad_mine), both_swap(grad_theirs))

    _, flag_count = flag_places(chunks)
    causal, causal_t, band, carried, tail, edge, flags = call(
        functools.partial(setup_kernel, chunks),
        (
            ((rows, rows), bf16),
            ((rows, rows), bf16),
            ((rows, LANES), f32),
            ((rows, LANES), f32),
            ((rows, LANES), bf16),
            ((HALO, LANES), bf16),
            ((flag_count,), f32),
        ),
        (place, lengths, valid.reshape(1, 2 * rows)),
        2,
        scalar_outs=1,
    )
    blends = jnp.concatenate([blend_rows, half_swap(blend_rows)], axis=1)

    saved = []
    base, adds = None, None
    for layer in range(LAYERS):
        outs = (hidden_like, low_like, qkv_like, state_like, ((5, HALO, LANES), bf16))
        if layer == 0:
            hidden, normed, qkv, state, halo, gains = call(
                functools.partial(qkv_kernel, True, layer),
                outs + (((SMALL, D), f32),),
                (place, *pieces, w_qkv, far_qkv[layer], tail, edge),
                1,
            )
        else:
            hidden, normed, qkv, state, halo = call(
                functools.partial(qkv_kernel, False, layer),
                outs,
                (place, base, *adds, gains, w_qkv, far_qkv[layer], tail, edge),
                1,
            )
        halo = chunk_move(halo, lambda c: c + 1)
        one, two, sums = call(far_kernel, (heads_like,) * 3, (qkv, causal))
        (found, parts_got, at), arrived, _ = scan(state, flags, chunks, False, lambda: (one,))
        if layer == 0:
            found = after(found, *grad_pieces)
        (near,) = call(near_kernel, (heads_like,), (place, qkv, halo, band), 1)
        mixed, far_one, far_two, root, prefix, state, piece = call(
            functools.partial(mix_kernel, layer, at, len(parts_got)),
            (heads_low, heads_like, heads_like, heads_like, heads_like, state_like, low_like),
            (place, flags, qkv, near, one, two, sums, carried, blends, w_out, far_out[layer], found, *parts_got),
            2,
        )
        weights = (w_up, w_down, far_up[layer], far_down[layer])
        middle, normed_ffn, pre_own, pre_far, act_own, act_far, piece_ffn = call(
            functools.partial(ffn_kernel, layer),
            (hidden_like, low_like, ffn_like, ffn_like, ffn_low, ffn_low, low_like),
            (hidden, piece, part_swap(piece), gains, *weights),
        )
        saved.append(
            (hidden, normed, qkv, state, halo, mixed, far_one, far_two, root, prefix, middle, normed_ffn,
             weights, pre_own, pre_far, act_own, act_far)
        )
        base, adds = middle, (piece_ffn, part_swap(piece_ffn) if layer + 1 < LAYERS else None)
    last_base, last_piece = base, adds[0]
    base, adds = None, None
    d_gain_attn, d_gain_ffn, d_blends = [None] * LAYERS, [None] * LAYERS, [None] * LAYERS
    d_qkvs = [None] * LAYERS
    bits = (shards - 1).bit_length()
    side_first, line_first = (0, 1, 2), (1, 2, 0)

    def first_step(jobs, operands):
        height = sum(job_rows(job, units) for job in jobs)
        like = ((height, D), bf16)
        return call(functools.partial(grads_kernel, jobs), (like, like), (place, *operands), 1, bulk_outs=(0,))

    def group_steps(order, rows, first, second):
        height = rows[1] - rows[0]
        others = yield
        if bits != 3:
            if len(first) > 1:
                small = jnp.pad(first[1] + second[1], ((0, LANES - SMALL), (0, D - LANES)))
                total = jnp.concatenate([first[0].astype(f32) + second[0].astype(f32), small])
            else:
                total = (first[0].astype(f32) + second[0].astype(f32))[slice(*rows)]
            total = lax.psum(total, "seq").astype(bf16).reshape(2, height // 2, D)
            total = jnp.where((shard >> order[0]) % 2 == 0, total, total[::-1])
            for _ in range(6):
                yield total
            yield total[0], total[1]
        for at, bit in enumerate(order):
            height //= 2
            if at == 0 and len(first) > 1:
                body, operands = functools.partial(last_kernel, bit), (first[0], second[0], first[1], second[1])
            elif at == 0:
                body, operands = functools.partial(halve_kernel, bit, rows), (first[0], second[0])
            else:
                body, operands = functools.partial(halve_kernel, bit, (0, 2 * height)), (keep, got)
            keep, send = call(
                body,
                (((height, D), f32), ((height, D), bf16)),
                (place, operands[0], after(operands[1], *others), *operands[2:]),
                1,
                bulk=(1,) if at == 0 else (),
            )
            got = shard_swap(send, bit)
            others = yield send
        (value,) = call(add_kernel, (((height, D), bf16),), (keep, after(got, *others)))
        for bit in reversed(order):
            got = shard_swap(value, bit)
            if bit == order[0]:
                break
            others = yield value
            height *= 2
            (value,) = call(
                functools.partial(join_kernel, bit), (((height, D), bf16),), (place, value, after(got, *others)), 1
            )
        yield value
        yield (value, got)

    groups, taken = [], {}

    def start_group(layers, jobs, order, rows, first, second):
        steps = group_steps(order, rows, first, second)
        next(steps)
        groups.append((layers, jobs, order[0], steps))

    def step(index, *others):
        taken[index] = taken.get(index, 0) + 1
        return groups[index][3].send(others)

    for layer in reversed(range(LAYERS)):
        (hidden, normed, qkv, state, halo, mixed, far_one, far_two, root, prefix, middle, normed_ffn,
         weights, pre_own, pre_far, act_own, act_far) = saved[layer]
        outs = (hidden_like, low_like, ffn_low, ffn_low, low_like)
        if base is None:
            resid, grad_rows, d_up_own, d_up_far, piece = call(
                functools.partial(ffn_back_kernel, True, layer),
                outs,
                (place, *grad_pieces, *weights, pre_own, pre_far),
                1,
            )
        else:
            resid, grad_rows, d_up_own, d_up_far, piece, d_gain_attn[layer + 1] = call(
                functools.partial(ffn_back_kernel, False, layer),
                outs + (gain_like,),
                (base, *adds, saved[layer + 1][0], gains, *weights, pre_own, pre_far),
            )
        def upper_grads(*others):
            jobs = ("up", "down", "out")
            own, far = first_step(
                jobs, (after(normed_ffn, *others), d_up_own, d_up_far, act_own, act_far, grad_rows, mixed, out_rows)
            )
            start_group((layer,) * 3, jobs, side_first, (0, own.shape[0]), (own,), (half_swap(far),))
            return far

        def lower_grads(*others):
            jobs = ("up", "qkv", "down", "out")
            operands = (
                after(normed_ffn, *others), d_up_own, d_up_far, saved[1][1], d_qkvs[1], act_own, act_far, grad_rows,
                mixed, out_rows,
            )
            own, far = first_step(jobs, operands)
            cut = job_rows("up", units) + job_rows("qkv", units)
            got = half_swap(far)
            start_group((0, 1), jobs[:2], side_first, (0, cut), (own,), (got,))
            start_group((0,) * len(jobs[2:]), jobs[2:], line_first, (cut, own.shape[0]), (own,), (got,))
            return far

        (resid, out_rows, d_mixed, d_gain_ffn[layer], num_one, num_two, d_zeta, state_back, blend_far) = call(
            functools.partial(mix_back_kernel, layer),
            (hidden_like, low_like, heads_low, gain_like, heads_low, heads_low, heads_like, state_like,
             ((2, wide), f32)),
            (place, resid, piece, part_swap(piece), middle, gains, w_out, far_out[layer], qkv, far_one, far_two,
             root, carried, blends),
            1,
        )
        ext = HALO + rows + HALO
        dq_near, dk_near, dv_near, halo_back, blend_near = call(
            functools.partial(near_back_kernel, layer),
            (heads_like, heads_like, heads_like, halo_like, ((1, wide), f32)),
            (place, qkv, halo, band, d_mixed, blends),
            1,
            scratch=(pltpu.VMEM((ext, LANES), f32), pltpu.VMEM((ext, LANES), f32)),
        )
        halo_back = chunk_move(halo_back, lambda c: c - 1)
        (found, parts_got, at), arrived, value = scan(state_back, flags, chunks, True, lambda: (dq_near,))
        ready = [value]
        if layer > 0:
            ready.append(upper_grads(value))
        else:
            ready.append(step(0, *ready))
            ready.append(lower_grads(*ready))
        dq, dk_one, dk_two, dv = call(
            far_back_kernel,
            (heads_low, heads_like, heads_like, heads_like),
            (place, qkv, causal, causal_t, carried, state, prefix, after(num_one, *ready), num_two, d_zeta, dq_near,
             dv_near),
            1,
        )
        d_qkvs[layer], piece = call(
            functools.partial(qkv_back_kernel, layer, at, len(parts_got)),
            (qkv_like, low_like),
            (place, flags, qkv, dq, dk_one, dk_two, dk_near, dv, tail, halo_back, w_qkv, far_qkv[layer], found,
             *parts_got),
            2,
            scratch=(pltpu.VMEM((2, STATE, LANES), bf16),),
        )
        base, adds = resid, (piece, part_swap(piece))
        if layer > 0:
            base = after(base, step(0, piece))
        d_blends[layer] = (blend_near, blend_far)

    made = step(0, step(2, step(1, piece)))
    jobs = ("qkv",)
    height = job_rows("qkv", units)
    last_like = ((height, D), bf16)
    own, far = call(
        functools.partial(grads_kernel, jobs),
        (last_like, last_like),
        (place, after(saved[0][1], made), d_qkvs[0]),
        1,
    )
    smalls = d_gain_attn[1:] + d_gain_ffn + [ref for pair in d_blends for ref in pair]
    small_like = ((SMALL, LANES), f32)
    mine, theirs, small_own, small_far = call(
        end_kernel,
        (shard_like, shard_like, small_like, small_like),
        (place, after(base, far), *adds, saved[0][0], gains, *smalls),
        1,
    )
    start_group((0,), jobs, line_first, (0, height + LANES), (own, small_own), (half_swap(far), half_swap(small_far)))
    made = step(3, mine)
    for turn in range(6):
        for index in range(4):
            if taken[index] < 6:
                made = step(index, made)
        if turn == 1:
            last_piece = after(last_piece, made)
            out_mine, out_theirs = call(
                output_kernel, (shard_like, shard_like), (place, last_base, last_piece, part_swap(last_piece)), 1
            )
            output = jnp.concatenate(by_place(half, out_mine, half_swap(out_theirs)))
    d_inputs = jnp.concatenate(by_place(half, mine, half_swap(theirs)))
    sums = [part for group in groups for part in next(group[3])]
    d_up, d_down, d_out, above = call(
        functools.partial(finish_wide_kernel, [group[:3] for group in groups[:3]]),
        (
            ((LAYERS, D, units), f32),
            ((LAYERS, units, D), f32),
            ((LAYERS, LANES, D), f32),
            ((3 * LANES, D), bf16),
        ),
        (place, *sums[:6]),
        1,
    )
    d_qkv, d_norm_attn, d_norm_ffn, d_blend = call(
        functools.partial(finish_qkv_kernel, line_first[0]),
        (
            ((LAYERS, 3, D, LANES), f32),
            ((LAYERS, LANES), f32),
            ((LAYERS, LANES), f32),
            ((3 * LAYERS, LANES), f32),
        ),
        (place, *sums[6:], above),
        1,
    )
    d_blend = d_blend[:, :2].reshape(LAYERS, 3, 2)
    return (output, d_inputs, d_norm_attn, d_qkv, d_blend, d_out, d_norm_ffn, d_up, d_down)


def solution(mesh):
    placed = (
        P("seq", "mlp"),
        P(),
        P("seq"),
        P(None, "mlp"),
        P(None, None, None, "mlp"),
        P(None, None, "mlp"),
        P(None, "mlp", None),
        P(None, "mlp"),
        P(None, None, "mlp"),
        P(None, "mlp", None),
        P("seq", "mlp"),
    )
    return jax.shard_map(
        per_device,
        mesh=mesh,
        in_specs=placed,
        out_specs=(
            P("seq", "mlp"),
            P("seq", "mlp"),
            P(None, "mlp"),
            P(None, None, None, "mlp"),
            P(None, None, "mlp"),
            P(None, "mlp", None),
            P(None, "mlp"),
            P(None, None, "mlp"),
            P(None, "mlp", None),
        ),
        check_vma=False,
    )
```

```python
import functools
import math

import jax
import jax.numpy as jnp
from jax import lax
from jax.experimental import pallas as pl
from jax.experimental.pallas import tpu as pltpu
from jax.sharding import PartitionSpec as P

HD = 64
D = 512
BAND = 30
LAYERS = 2
HALO = 32
TILE = 64
LANES = 128
STATE = 144
SMALL = 16
AXES = ("seq", "mlp")

epsilon = 1e-05
masked_score = -1e30
score_scale = 1.0 / math.sqrt(HD)
far_scale = 1.0 / math.sqrt(HD)
f32 = jnp.float32
bf16 = jnp.bfloat16

VM = pl.BlockSpec(memory_space=pltpu.VMEM)
SM = pl.BlockSpec(memory_space=pltpu.SMEM)


def dot(x, y):
    return jnp.dot(x, y, preferred_element_type=f32)


def dot_nt(x, y):
    return lax.dot_general(x, y, (((1,), (1,)), ((), ())), preferred_element_type=f32)


def dot_tn(x, y):
    return lax.dot_general(x, y, (((0,), (0,)), ((), ())), preferred_element_type=f32)


def low_lanes(rows):
    return lax.broadcasted_iota(jnp.int32, (rows, LANES), 1) < HD


def split_heads(x):
    low = low_lanes(x.shape[0])
    zero = jnp.zeros_like(x)
    return jnp.concatenate([jnp.where(low, x, zero), jnp.where(low, zero, x)], axis=0)


def merge_heads(y):
    rows = y.shape[0] // 2
    return jnp.where(low_lanes(rows), y[:rows], y[rows:])


def head_sum(x):
    row = lax.broadcasted_iota(jnp.int32, (LANES, LANES), 0) < HD
    ones = jnp.where(row == low_lanes(LANES), 1.0, 0.0).astype(bf16)
    high = x.astype(bf16)
    rest = (x - high.astype(f32)).astype(bf16)
    return dot(high, ones) + dot(rest, ones)


def kernel_maps(x):
    return (
        jnp.where(x > 0, x + 1.0, jnp.exp(jnp.minimum(x, 0.0))).astype(bf16),
        jnp.tanh(x).astype(bf16),
    )


def maps_back(x, d_one, d_two):
    tanh = jnp.tanh(x)
    return jnp.where(x > 0, 1.0, jnp.exp(jnp.minimum(x, 0.0))) * d_one + (1.0 - tanh * tanh) * d_two


def put_state(ref, quarter, one, two, total):
    row = lax.broadcasted_iota(jnp.int32, (STATE - 2 * HD, LANES), 0)
    low = low_lanes(HD)
    ref[quarter, 0:HD, :] = jnp.where(low, one[:HD], one[HD:]).astype(bf16)
    ref[quarter, HD : 2 * HD, :] = jnp.where(low, two[:HD], two[HD:]).astype(bf16)
    ref[quarter, 2 * HD : STATE, :] = jnp.where(row == 0, total, 0.0).astype(bf16)


def get_state(ref, quarter):
    one = split_heads(ref[quarter, 0:HD, :])
    two = split_heads(ref[quarter, HD : 2 * HD, :])
    total = ref[quarter, 2 * HD : STATE, :].astype(f32)[0:1]
    return one, two, total


def norm_scale(hidden):
    return lax.rsqrt(jnp.sum(hidden * hidden, axis=1, keepdims=True) * (1.0 / D) + epsilon)


def norm_back(hidden, gain, grad):
    scale = norm_scale(hidden)
    gained = grad * gain
    inner = jnp.sum(gained * hidden, axis=1, keepdims=True) * (1.0 / D)
    back = scale * gained - hidden * (scale * scale * scale * inner)
    return back, jnp.sum(grad * hidden * scale, axis=0, keepdims=True)


def halo_bias(halo):
    ones = jnp.ones((LANES - HALO, LANES), bf16)
    flags = jnp.concatenate([halo[4], ones], axis=0)
    flags = dot_nt(jnp.ones((2 * TILE, LANES), bf16), flags)
    return jnp.where(flags > 0.5 * LANES, 0.0, masked_score)


def extend(halo, rows):
    return jnp.concatenate([halo, rows, jnp.zeros((HALO, LANES), bf16)], axis=0)


def three_parts(value):
    high = value.astype(bf16)
    rest = value - high.astype(f32)
    middle = rest.astype(bf16)
    low = (rest - middle.astype(f32)).astype(bf16)
    return jnp.concatenate([high, middle, low], axis=0)


def pack_kernel(place, inputs, norm_attn, norm_ffn, mine_out, theirs_out, rows_in, attn_in, ffn_in, sems):
    copies = [
        pltpu.make_async_copy(source, target, sems.at[k])
        for k, (source, target) in enumerate(((inputs, rows_in), (norm_attn, attn_in), (norm_ffn, ffn_in)))
    ]
    for copy in copies:
        copy.start()
    for copy in copies:
        copy.wait()
    rows = rows_in.shape[0] // 2
    small = [attn_in[...], ffn_in[...], jnp.zeros((SMALL - 2 * LAYERS, LANES), f32)]
    small = three_parts(jnp.concatenate(small, axis=0))
    first, second = rows_in[:rows], rows_in[rows:]
    mine_out[:rows] = jnp.where(place[0] == 0, first, second)
    theirs_out[:rows] = jnp.where(place[0] == 0, second, first)
    mine_out[rows:] = small
    theirs_out[rows:] = small


def pack_blend_kernel(blend, out):
    low = low_lanes(1)
    rows = []
    for layer in range(LAYERS):
        for kind in range(3):
            rows.append(jnp.where(low, blend[layer, kind, 0], blend[layer, kind, 1]))
    rows.append(jnp.zeros((SMALL - 3 * LAYERS, LANES), f32))
    out[...] = jnp.concatenate(rows, axis=0)


def pack_grad_kernel(place, grads, mine_out, theirs_out):
    rows = grads.shape[0] // 2
    first, second = grads[:rows], grads[rows:]
    mine_out[...] = jnp.where(place[0] == 0, first, second)
    theirs_out[...] = jnp.where(place[0] == 0, second, first)


def quarters(place):
    half, part = place[0], place[1]
    return 2 * part + half, 2 * part + 1 - half, 2 * (1 - part) + half, 2 * (1 - part) + 1 - half


def quarter_lanes(quarter):
    return pl.ds(pl.multiple_of(quarter * LANES, LANES), LANES)


def item_ends(lengths):
    ends = []
    for k in range(lengths.shape[0]):
        ends.append(lengths[k] if k == 0 else ends[-1] + lengths[k])
    return ends


def item_start(lengths, ends, positions):
    start = jnp.zeros_like(positions)
    for k, end in enumerate(ends):
        start = start + jnp.where(end <= positions, lengths[k], 0)
    return start


def scan_plan(chunks):
    stages, size = [], 1
    while size < chunks:
        ways = min(4, chunks // size)
        stages.append((size, ways, size * ways >= chunks))
        size *= ways
    return stages


def flag_places(chunks):
    at, places = 0, {}
    for reverse in (False, True):
        for stage, (_, ways, _) in enumerate(scan_plan(chunks)):
            places[reverse, stage] = at
            at += 2 * ways
    return places, at


def setup_kernel(
    chunks, place, lengths, valid, causal_out, causal_t_out, band_out, carried_out, tail_out, edge_out, flags_out
):
    rows = causal_out.shape[0]
    chunk = place[2] * 2 + place[0]
    first_row = chunk * rows
    ends = item_ends(lengths)

    def start_of(positions):
        return item_start(lengths, ends, positions)

    lane = lax.broadcasted_iota(jnp.int32, (1, rows), 1)
    starts_row = start_of(first_row + lane)
    starts = start_of(first_row + lax.broadcasted_iota(jnp.int32, (rows, LANES), 0))
    both = jnp.concatenate([starts, starts], axis=1)
    words = valid[...]
    own_words = jnp.where(place[0] == 0, words[:, :rows], words[:, rows:])
    row_at = lax.broadcasted_iota(jnp.int32, (rows, rows), 0)
    lane_at = lax.broadcasted_iota(jnp.int32, (rows, rows), 1)
    own_column = jnp.sum(jnp.where(row_at == lane_at, own_words, 0), axis=1, keepdims=True)
    same = both == starts_row
    causal_out[...] = jnp.where((lane_at <= row_at) & same & (own_words == 1), 1.0, 0.0).astype(bf16)
    causal_t_out[...] = jnp.where((row_at <= lane_at) & same & (own_column == 1), 1.0, 0.0).astype(bf16)
    carried_out[...] = jnp.where(starts < first_row, 1.0, 0.0)
    last_start = start_of(first_row + rows - 1)
    edge_out[...] = jnp.where(jnp.broadcast_to(own_column, (rows, LANES))[rows - HALO :] == 1, 1.0, 0.0).astype(bf16)
    tail_out[...] = jnp.where((starts == last_start) & (own_column == 1), 1.0, 0.0).astype(bf16)
    all_words = jnp.concatenate([jnp.ones((1, LANES), jnp.int32), own_words, jnp.zeros((1, LANES), jnp.int32)], axis=1)
    tile_row = lax.broadcasted_iota(jnp.int32, (TILE, LANES), 0)
    tile_lane = lax.broadcasted_iota(jnp.int32, (TILE, LANES), 1)
    gap = tile_row + HALO - tile_lane
    for tile in range(rows // TILE):
        key_starts = start_of(first_row + tile * TILE - HALO + lax.broadcasted_iota(jnp.int32, (1, LANES), 1))
        offset = LANES - HALO + tile * TILE
        key_words = all_words[:, offset : offset + LANES]
        at = slice(tile * TILE, (tile + 1) * TILE)
        allowed = (gap >= 0) & (gap <= BAND) & (starts[at] == key_starts) & ((key_words == 1) | (gap == 0))
        band_out[at] = jnp.where(allowed, 0.0, masked_score)

    places, _ = flag_places(chunks)
    for reverse in (False, True):
        edge = start_of(first_row + (rows - 1 if reverse else 0))
        for stage, (size, ways, last) in enumerate(scan_plan(chunks)):
            member = lax.rem(lax.div(chunk, size), ways)
            base = chunk - member * size - lax.rem(chunk, size)
            group = base if reverse else base + ways * size - 1
            group = start_of(group * rows + (0 if reverse else rows - 1))
            for step in range(ways):
                if last:
                    other = member + step if reverse else member - step
                else:
                    other = jnp.bitwise_xor(member, step)
                block = base + other * size + (0 if reverse else size - 1)
                start = start_of(block * rows + (0 if reverse else rows - 1))
                ahead = (other > member) if reverse else (other < member)
                ahead = ahead & (other >= 0) & (other < ways)
                at = places[reverse, stage] + 2 * step
                flags_out[at] = jnp.where(ahead & (start == edge), 1.0, 0.0)
                flags_out[at + 1] = jnp.where(start == group, 1.0, 0.0)


def combine_kernel(at, ways, has_found, flags, *refs):
    got, refs = refs[:ways], refs[ways:]
    total = sum(flags[at + 2 * step + 1] * got[step][...].astype(f32) for step in range(ways))
    refs[-2][...] = total.astype(bf16)
    found = sum(flags[at + 2 * step] * got[step][...].astype(f32) for step in range(1, ways))
    refs[-1][...] = found + refs[0][...] if has_found else found


def last_combine(at, flags, found, got, out):
    value = found[...]
    for step, part in enumerate(got):
        value = value + flags[at + 2 * (step + 1)] * part[...].astype(f32)
    out[...] = value.astype(bf16)


def qkv_kernel(first, layer, place, *refs):
    if first:
        refs, outs = refs[:8], refs[8:]
        pieces, (own, other, tail, edge) = refs[:4], refs[4:]
        hidden_out, normed_out, qkv_out, state_out, halo_out, gains = outs
        rows = hidden_out.shape[0]
        for piece, quarter in zip(pieces, quarters(place)):
            hidden_out[:, quarter_lanes(quarter)] = piece[:rows].astype(f32)
            parts = piece[rows:].astype(f32)
            small = parts[:SMALL] + parts[SMALL : 2 * SMALL] + parts[2 * SMALL :]
            gains[:, quarter_lanes(quarter)] = small
        hidden = hidden_out[...]
    else:
        base, part_a, part_b, gains, own, other, tail, edge, *outs = refs
        hidden_out, normed_out, qkv_out, state_out, halo_out = outs
        hidden = base[...] + (part_a[...].astype(f32) + part_b[...].astype(f32))
        hidden_out[...] = hidden
    rows = hidden.shape[0]
    normed = (hidden * norm_scale(hidden) * gains[layer : layer + 1]).astype(bf16)
    normed_out[...] = normed
    found = []
    for kind in range(3):
        weight = jnp.concatenate([own[layer, kind], other[kind]], axis=1)
        found.append(dot(normed, weight).astype(bf16))
        qkv_out[kind] = found[kind]
    for pair in range(2):
        quarter = place[0] if pair == 0 else 1 - place[0]
        lanes = slice(pair * LANES, (pair + 1) * LANES)
        keys, values = found[1][:, lanes], found[2][:, lanes]
        one, two = kernel_maps(keys.astype(f32))
        one, two = one * tail[...], two * tail[...]
        put_state(
            state_out,
            quarter,
            dot_tn(one, values),
            dot_tn(two, values),
            jnp.sum(one.astype(f32), axis=0, keepdims=True),
        )
        halo_out[2 * quarter] = keys[rows - HALO :]
        halo_out[2 * quarter + 1] = values[rows - HALO :]
    halo_out[4] = edge[...]


def far_kernel(qkv, causal, one_out, two_out, sums_out):
    masks = jnp.concatenate([causal[...], causal[...]], axis=0)
    for pair in range(2):
        lanes = slice(pair * LANES, (pair + 1) * LANES)
        queries, keys, values = qkv[0, :, lanes], qkv[1, :, lanes], qkv[2, :, lanes]
        maps_q, maps_k = kernel_maps(queries.astype(f32)), kernel_maps(keys.astype(f32))
        for query, key, out in ((maps_q[0], maps_k[0], one_out), (maps_q[1], maps_k[1], two_out)):
            attn = dot_nt(split_heads(query), key).astype(bf16) * masks
            out[:, lanes] = merge_heads(dot(attn, values))
        sums_out[:, lanes] = dot(causal[...], maps_k[0])


def near_kernel(place, qkv, halo, band, near_out):
    rows = qkv.shape[1]
    bias = halo_bias(halo)
    for pair in range(2):
        quarter = place[0] if pair == 0 else 1 - place[0]
        lanes = slice(pair * LANES, (pair + 1) * LANES)
        queries, keys, values = qkv[0, :, lanes], qkv[1, :, lanes], qkv[2, :, lanes]
        ext_keys = extend(halo[2 * quarter], keys)
        ext_values = extend(halo[2 * quarter + 1], values)
        for tile in range(rows // TILE):
            at = slice(tile * TILE, (tile + 1) * TILE)
            window = slice(tile * TILE, tile * TILE + LANES)
            allowed = jnp.concatenate([band[at], band[at]], axis=0)
            allowed = allowed + bias if tile == 0 else allowed
            scores = dot_nt(split_heads(queries[at]), ext_keys[window]) * score_scale + allowed
            weights = jnp.exp(scores - jnp.max(scores, axis=1, keepdims=True))
            weights = weights / jnp.sum(weights, axis=1, keepdims=True)
            near_out[at, lanes] = merge_heads(dot(weights.astype(bf16), ext_values[window]))


def mix_kernel(layer, at, count, place, flags, qkv, near, one, two, sums, carried, blends, own, other, found, *refs):
    got = refs[:count]
    mixed_out, far_one_out, far_two_out, root_out, prefix_out, state, part_out = refs[count:]
    last_combine(at, flags, found, got, state)
    mixed = []
    row = 3 * layer
    for pair in range(2):
        quarter = place[0] if pair == 0 else 1 - place[0]
        lanes = slice(pair * LANES, (pair + 1) * LANES)
        query_one, query_two = kernel_maps(qkv[0, :, lanes].astype(f32))
        state_one, state_two, total = get_state(state, quarter)
        num_one = one[:, lanes] + carried[...] * dot(query_one, state_one)
        num_two = two[:, lanes] + carried[...] * dot(query_two, state_two)
        prefix = sums[:, lanes] + carried[...] * total
        zeta = head_sum(query_one.astype(f32) * prefix)
        root = lax.rsqrt(zeta + 1.0)
        far_one = num_one * root * far_scale
        far_two = num_two * root
        far_one_out[:, lanes] = far_one
        far_two_out[:, lanes] = far_two
        root_out[:, lanes] = root
        prefix_out[:, lanes] = prefix
        mixed.append(
            (
                blends[row : row + 1, lanes] * near[:, lanes]
                + blends[row + 1 : row + 2, lanes] * far_one
                + blends[row + 2 : row + 3, lanes] * far_two
            ).astype(bf16)
        )
        mixed_out[:, lanes] = mixed[pair]
    weight = jnp.concatenate([own[layer], other[...]], axis=0)
    part_out[...] = dot(jnp.concatenate(mixed, axis=1), weight).astype(bf16)


def ffn_kernel(
    layer, base, part_a, part_b, gains, up_own, down_own, up_far, down_far,
    middle_out, normed_out, pre_own_out, pre_far_out, act_own_out, act_far_out, part_out,
):
    middle = base[...] + (part_a[...].astype(f32) + part_b[...].astype(f32))
    middle_out[...] = middle
    gain = gains[LAYERS + layer : LAYERS + layer + 1]
    normed = (middle * norm_scale(middle) * gain).astype(bf16)
    normed_out[...] = normed
    weights = (
        (up_own[layer], down_own[layer], pre_own_out, act_own_out),
        (up_far[...], down_far[...], pre_far_out, act_far_out),
    )
    total = None
    for up, down, pre_out, act_out in weights:
        pre = dot(normed, up)
        pre_out[...] = pre
        inner = jnp.tanh(math.sqrt(2.0 / math.pi) * (pre + 0.044715 * pre * pre * pre))
        act = (0.5 * pre * (1.0 + inner)).astype(bf16)
        act_out[...] = act
        product = dot(act, down)
        total = product if total is None else total + product
    part_out[...] = total.astype(bf16)


def shard_rows(whole, place, mine_out, theirs_out):
    first = [whole[:, m * LANES : (m + 1) * LANES] for m in range(4)]
    even, odd = [jnp.where(place[1] == 0, first[h], first[2 + h]) for h in range(2)]
    mine_out[...] = jnp.where(place[0] == 0, even, odd)
    theirs_out[...] = jnp.where(place[0] == 0, odd, even)


def output_kernel(place, base, part_a, part_b, mine_out, theirs_out):
    whole = base[...] + (part_a[...].astype(f32) + part_b[...].astype(f32))
    shard_rows(whole.astype(bf16), place, mine_out, theirs_out)


def gelu_slope(pre):
    c = math.sqrt(2.0 / math.pi)
    inner = jnp.tanh(c * (pre + 0.044715 * pre * pre * pre))
    return 0.5 * (1.0 + inner) + 0.5 * pre * (1.0 - inner * inner) * (c * (1.0 + 3 * 0.044715 * pre * pre))


def ffn_back_kernel(first, layer, *refs):
    if first:
        place, *refs = refs
        pieces, refs = refs[:4], refs[4:]
        weights, outs = refs[:6], refs[6:]
        resid_out, rows_out, d_up_own_out, d_up_far_out, part_out = outs
        for piece, quarter in zip(pieces, quarters(place)):
            resid_out[:, quarter_lanes(quarter)] = piece[...].astype(f32)
        resid = resid_out[...]
    else:
        base, part_a, part_b, hidden, gains, *refs = refs
        weights, outs = refs[:6], refs[6:]
        resid_out, rows_out, d_up_own_out, d_up_far_out, part_out, gain_out = outs
        back, gain_out[...] = norm_back(
            hidden[...], gains[layer + 1 : layer + 2], part_a[...].astype(f32) + part_b[...].astype(f32)
        )
        resid = base[...] + back
        resid_out[...] = resid
    up_own, down_own, up_far, down_far, pre_own, pre_far = weights
    rows = resid.astype(bf16)
    rows_out[...] = rows
    total = None
    for up, down, pre, out in (
        (up_own[layer], down_own[layer], pre_own, d_up_own_out),
        (up_far[...], down_far[...], pre_far, d_up_far_out),
    ):
        d_up = (gelu_slope(pre[...]) * dot_nt(rows, down)).astype(bf16)
        out[...] = d_up
        product = dot_nt(d_up, up)
        total = product if total is None else total + product
    part_out[...] = total.astype(bf16)


def mix_back_kernel(
    layer, place, base, part_a, part_b, middle, gains, own, other, qkv, far_one, far_two, root, carried, blends,
    resid_out, rows_out, mixed_out, gain_out, num_one_out, num_two_out, zeta_out, state_out, blend_out,
):
    back, gain_out[...] = norm_back(
        middle[...],
        gains[LAYERS + layer : LAYERS + layer + 1],
        part_a[...].astype(f32) + part_b[...].astype(f32),
    )
    resid = base[...] + back
    resid_out[...] = resid
    blend = blends[3 * layer : 3 * layer + 3]
    rows = resid.astype(bf16)
    rows_out[...] = rows
    weight = jnp.concatenate([own[layer], other[...]], axis=0)
    d_mixed = dot_nt(rows, weight).astype(bf16)
    mixed_out[...] = d_mixed
    for pair in range(2):
        quarter = place[0] if pair == 0 else 1 - place[0]
        lanes = slice(pair * LANES, (pair + 1) * LANES)
        grad = d_mixed[:, lanes].astype(f32)
        scale = root[:, lanes]
        dot_one = grad * far_one[:, lanes]
        dot_two = grad * far_two[:, lanes]
        blend_one, blend_two = blend[1:2, lanes], blend[2:3, lanes]
        blend_out[0:1, lanes] = jnp.sum(dot_one, axis=0, keepdims=True)
        blend_out[1:2, lanes] = jnp.sum(dot_two, axis=0, keepdims=True)
        num_one = (grad * (blend_one * far_scale) * scale).astype(bf16)
        num_two = (grad * blend_two * scale).astype(bf16)
        d_zeta = head_sum(blend_one * dot_one + blend_two * dot_two) * (-0.5 * scale * scale)
        num_one_out[:, lanes] = num_one
        num_two_out[:, lanes] = num_two
        zeta_out[:, lanes] = d_zeta
        query_one, query_two = kernel_maps(qkv[0, :, lanes].astype(f32))
        reach = carried[...].astype(bf16)
        put_state(
            state_out,
            quarter,
            dot_tn(query_one * reach, num_one),
            dot_tn(query_two * reach, num_two),
            jnp.sum(carried[...] * d_zeta * query_one.astype(f32), axis=0, keepdims=True),
        )


def near_back_kernel(
    layer, place, qkv, halo, band, d_mixed, blends, dq_out, dk_out, dv_out, halo_out, blend_out, near_k, near_v
):
    rows = qkv.shape[1]
    row_low = lax.broadcasted_iota(jnp.int32, (2 * TILE, 1), 0) < TILE
    bias = halo_bias(halo)
    row = 3 * layer
    for pair in range(2):
        quarter = place[0] if pair == 0 else 1 - place[0]
        lanes = slice(pair * LANES, (pair + 1) * LANES)
        queries, keys, values = qkv[0, :, lanes], qkv[1, :, lanes], qkv[2, :, lanes]
        grads = d_mixed[:, lanes]
        blend = blends[row : row + 1, lanes]
        ext_keys = extend(halo[2 * quarter], keys)
        ext_values = extend(halo[2 * quarter + 1], values)
        near_k[...] = jnp.zeros_like(near_k)
        near_v[...] = jnp.zeros_like(near_v)
        blend_rows = jnp.where(row_low, blend[:, :1], blend[:, HD : HD + 1])
        sums = None
        for tile in range(rows // TILE):
            at = slice(tile * TILE, (tile + 1) * TILE)
            window = slice(tile * TILE, tile * TILE + LANES)
            allowed = jnp.concatenate([band[at], band[at]], axis=0)
            allowed = allowed + bias if tile == 0 else allowed
            query_split, grad_split = split_heads(queries[at]), split_heads(grads[at])
            scores = dot_nt(query_split, ext_keys[window]) * score_scale + allowed
            probs = jnp.exp(scores - jnp.max(scores, axis=1, keepdims=True))
            probs = probs / jnp.sum(probs, axis=1, keepdims=True)
            d_probs = dot_nt(grad_split, ext_values[window])
            inner = jnp.sum(probs * d_probs, axis=1, keepdims=True)
            sums = inner if sums is None else sums + inner
            d_scores = (probs * (d_probs - inner) * blend_rows).astype(bf16)
            dq_out[at, lanes] = score_scale * merge_heads(dot(d_scores, ext_keys[window]))
            near_k[window] += dot_tn(d_scores, query_split)
            near_v[window] += dot_tn(probs.astype(bf16), grad_split)
        sum_low = jnp.sum(sums[:TILE], axis=0, keepdims=True)
        sum_high = jnp.sum(sums[TILE:], axis=0, keepdims=True)
        blend_out[0:1, lanes] = jnp.where(low_lanes(1), sum_low, sum_high) * (1.0 / HD)
        dk_out[:, lanes] = score_scale * near_k[HALO : HALO + rows]
        dv_out[:, lanes] = blend * near_v[HALO : HALO + rows]
        halo_out[quarter, 0] = (score_scale * near_k[0:HALO]).astype(bf16)
        halo_out[quarter, 1] = (blend * near_v[0:HALO]).astype(bf16)


def far_back_kernel(
    place, qkv, causal, causal_t, carried, state, prefix, num_one, num_two, d_zeta, dq_near, dv_near,
    dq_out, dk_one_out, dk_two_out, dv_out,
):
    masks = jnp.concatenate([causal[...], causal[...]], axis=0)
    masks_t = jnp.concatenate([causal_t[...], causal_t[...]], axis=1)
    for pair in range(2):
        quarter = place[0] if pair == 0 else 1 - place[0]
        lanes = slice(pair * LANES, (pair + 1) * LANES)
        queries, keys, values = qkv[0, :, lanes], qkv[1, :, lanes], qkv[2, :, lanes]
        state_one, state_two, unused_total = get_state(state, quarter)
        query_one, query_two = kernel_maps(queries.astype(f32))
        key_one, key_two = kernel_maps(keys.astype(f32))
        d_values = dv_near[:, lanes]
        d_queries = []
        for query, key, num, square, out in (
            (query_one, key_one, num_one[:, lanes], state_one, dk_one_out),
            (query_two, key_two, num_two[:, lanes], state_two, dk_two_out),
        ):
            query_split, num_split = split_heads(query), split_heads(num)
            attn_t = dot_nt(key, query_split).astype(bf16) * masks_t
            grad = dot_nt(num_split, values).astype(bf16) * masks
            grad_t = dot_nt(values, num_split).astype(bf16) * masks_t
            d_values = d_values + dot(attn_t, num_split)
            d_queries.append(merge_heads(dot(grad, key)) + carried[...] * dot_nt(num, square))
            out[:, lanes] = dot(grad_t, query_split)
        zeta = d_zeta[:, lanes]
        d_queries[0] += zeta * prefix[:, lanes]
        dk_one_out[:, lanes] += dot(causal_t[...], (zeta * query_one.astype(f32)).astype(bf16))
        back = maps_back(queries.astype(f32), d_queries[0], d_queries[1])
        dq_out[:, lanes] = (back + dq_near[:, lanes]).astype(bf16)
        dv_out[:, lanes] = d_values


def qkv_back_kernel(
    layer, at, count, place, flags, qkv, dq, dk_one, dk_two, dk_near, dv, tail, halo, own, other, found, *refs
):
    got = refs[:count]
    d_qkv_out, part_out, state = refs[count:]
    last_combine(at, flags, found, got, state)
    rows = qkv.shape[1]
    empty = jnp.zeros((rows - HALO, LANES), f32)
    for pair in range(2):
        quarter = place[0] if pair == 0 else 1 - place[0]
        lanes = slice(pair * LANES, (pair + 1) * LANES)
        keys, values = qkv[1, :, lanes], qkv[2, :, lanes]
        key_one, key_two = kernel_maps(keys.astype(f32))
        state_one, state_two, total = get_state(state, quarter)
        weight = tail[...].astype(f32)
        d_one = dk_one[:, lanes] + weight * (dot_nt(values, state_one) + total)
        d_two = dk_two[:, lanes] + weight * dot_nt(values, state_two)
        halo_k = jnp.concatenate([empty, halo[quarter, 0].astype(f32)], axis=0)
        halo_v = jnp.concatenate([empty, halo[quarter, 1].astype(f32)], axis=0)
        d_qkv_out[1, :, lanes] = (
            maps_back(keys.astype(f32), d_one, d_two) + dk_near[:, lanes] + halo_k
        ).astype(bf16)
        d_qkv_out[2, :, lanes] = (
            dv[:, lanes] + weight * (dot(key_one, state_one) + dot(key_two, state_two)) + halo_v
        ).astype(bf16)
    d_qkv_out[0] = dq[...]
    total = None
    for kind in range(3):
        weight = jnp.concatenate([own[layer, kind], other[kind]], axis=1)
        product = dot_nt(d_qkv_out[kind], weight)
        total = product if total is None else total + product
    part_out[...] = total.astype(bf16)


JOB_REFS = {"up": 3, "down": 3, "out": 2, "qkv": 2}


def job_rows(job, units):
    return {"up": D, "down": units, "out": LANES, "qkv": 3 * LANES}[job]


def fill_grads(jobs, refs, own, far):
    at = 0
    for job in jobs:
        mine, refs = refs[: JOB_REFS[job]], refs[JOB_REFS[job] :]
        if job == "up":
            normed, grad_own, grad_far = mine
            own[at : at + D] = dot_tn(normed[...], grad_own[...]).astype(bf16)
            far[at : at + D] = dot_tn(normed[...], grad_far[...]).astype(bf16)
            at += D
        elif job == "down":
            act_own, act_far, grad = mine
            units = act_own.shape[1]
            own[at : at + units] = dot_tn(act_own[...], grad[...]).astype(bf16)
            far[at : at + units] = dot_tn(act_far[...], grad[...]).astype(bf16)
            at += units
        elif job == "out":
            mixed, grad = mine
            found = dot_tn(mixed[...], grad[...]).astype(bf16)
            own[at : at + LANES] = found[:LANES]
            far[at : at + LANES] = found[LANES:]
            at += LANES
        else:
            normed, d_qkv = mine
            for kind in range(3):
                found = dot_tn(normed[...], d_qkv[kind]).astype(bf16)
                for block in range(D // LANES):
                    lanes = slice(block * LANES, (block + 1) * LANES)
                    own[at : at + LANES, lanes] = found[lanes, :LANES]
                    far[at : at + LANES, lanes] = found[lanes, LANES:]
                at += LANES


def grads_kernel(jobs, place, *refs):
    fill_grads(jobs, refs[:-2], refs[-2], refs[-1])


def shard_bit(place, bit):
    return lax.rem(lax.div(place[2], 1 << bit), 2)


def give_half(bit, place, total, keep_out, send_out):
    rows = total.shape[0] // 2
    low = shard_bit(place, bit) == 0
    keep_out[...] = jnp.where(low, total[:rows], total[rows:])
    send_out[...] = jnp.where(low, total[rows:], total[:rows]).astype(bf16)


def halve_kernel(bit, rows, place, first, second, keep_out, send_out):
    at = slice(*rows)
    give_half(bit, place, first[at].astype(f32) + second[at].astype(f32), keep_out, send_out)


def add_kernel(first, second, out):
    out[...] = (first[...].astype(f32) + second[...].astype(f32)).astype(bf16)


def join_kernel(bit, place, mine, got, out):
    low = shard_bit(place, bit) == 0
    rows = mine.shape[0]
    out[:rows] = jnp.where(low, mine[...], got[...])
    out[rows:] = jnp.where(low, got[...], mine[...])


def end_kernel(place, base, part_a, part_b, hidden, gains, *refs):
    smalls, (mine_out, theirs_out, own_out, far_out) = refs[: 4 * LAYERS - 1], refs[4 * LAYERS - 1 :]
    gain_refs, blend_refs = smalls[: 2 * LAYERS - 1], smalls[2 * LAYERS - 1 :]
    back, gain = norm_back(hidden[...], gains[0:1], part_a[...].astype(f32) + part_b[...].astype(f32))
    shard_rows((base[...] + back).astype(bf16), place, mine_out, theirs_out)
    gain_rows = jnp.concatenate([gain] + [ref[...] for ref in gain_refs], axis=0)
    blend_rows = jnp.concatenate([ref[...] for ref in blend_refs], axis=0)
    extras = []
    for to in range(2):
        features = jnp.where(
            place[1] == 0,
            gain_rows[:, to * LANES : (to + 1) * LANES],
            gain_rows[:, (2 + to) * LANES : (3 + to) * LANES],
        )
        blends = jnp.where(place[0] == to, blend_rows[:, :LANES], blend_rows[:, LANES:])
        extras.append(jnp.concatenate([features, blends, jnp.zeros((SMALL - 5 * LAYERS, LANES), f32)], axis=0))
    own_out[...] = jnp.where(place[0] == 0, extras[0], extras[1])
    far_out[...] = jnp.where(place[0] == 0, extras[1], extras[0])


def last_kernel(bit, place, own, far, small_own, small_far, keep_out, send_out):
    small = jnp.concatenate([small_own[...] + small_far[...], jnp.zeros((SMALL, D - LANES), f32)], axis=1)
    small = jnp.concatenate([small, jnp.zeros((LANES - SMALL, D), f32)], axis=0)
    total = jnp.concatenate([own[...].astype(f32) + far[...].astype(f32), small], axis=0)
    give_half(bit, place, total, keep_out, send_out)


def in_order(bit, place, mine, other):
    low = shard_bit(place, bit) == 0
    first, second = jnp.where(low, mine[...], other[...]), jnp.where(low, other[...], mine[...])
    return jnp.concatenate([first, second], axis=0)


def finish_wide_kernel(groups, place, *refs):
    refs, (up_out, down_out, out_out, above_out) = refs[:-4], refs[-4:]
    outs = {"up": up_out, "down": down_out, "out": out_out}
    for group, (layers, jobs, bit) in enumerate(groups):
        whole = in_order(bit, place, refs[2 * group], refs[2 * group + 1])
        at = 0
        for layer, job in zip(layers, jobs):
            rows = whole[at : at + job_rows(job, up_out.shape[2])]
            at += rows.shape[0]
            if job == "qkv":
                above_out[...] = rows
            else:
                outs[job][layer] = rows.astype(f32)


def finish_qkv_kernel(bit, place, mine, other, above, qkv_out, attn_out, ffn_out, blend_out):
    whole = in_order(bit, place, mine, other)
    at = 3 * LANES
    for layer, rows in enumerate((whole, above)):
        for kind in range(3):
            for block in range(D // LANES):
                lanes = slice(block * LANES, (block + 1) * LANES)
                qkv_out[layer, kind, lanes] = rows[kind * LANES : (kind + 1) * LANES, lanes].astype(f32)
    small = whole[at : at + SMALL, :LANES].astype(f32)
    attn_out[...] = small[:LAYERS]
    ffn_out[...] = small[LAYERS : 2 * LAYERS]
    blends = small[2 * LAYERS : 5 * LAYERS]
    low = low_lanes(3 * LAYERS)
    lane = lax.broadcasted_iota(jnp.int32, (3 * LAYERS, LANES), 1)
    first = jnp.sum(jnp.where(low, blends, 0.0), axis=1, keepdims=True)
    second = jnp.sum(jnp.where(low, 0.0, blends), axis=1, keepdims=True)
    blend_out[...] = jnp.where(lane == 0, first, second)


def call(body, outs, operands, scalars=0, scratch=(), scalar_outs=0, bulk=(), bulk_outs=(), flops=None):
    specs = [SM] * scalars + [VM] * (len(operands) - scalars)
    out_specs = [VM] * (len(outs) - scalar_outs) + [SM] * scalar_outs
    for index in bulk:
        specs[index] = pl.BlockSpec()
    for index in bulk_outs:
        out_specs[index] = pl.BlockSpec()
    cost = flops and pl.CostEstimate(flops=flops, bytes_accessed=0, transcendentals=0)
    return pl.pallas_call(
        body,
        out_shape=tuple(jax.ShapeDtypeStruct(shape, kind) for shape, kind in outs),
        in_specs=specs,
        out_specs=tuple(out_specs),
        scratch_shapes=scratch,
        cost_estimate=cost,
        compiler_params=pltpu.CompilerParams(vmem_limit_bytes=24 * 2**20),
    )(*operands)


def after(value, *others):
    return lax.optimization_barrier((value, *others))[0] if others else value


def half_swap(value):
    count = lax.axis_size("mlp")
    return lax.ppermute(value, "mlp", [(i, i ^ 1) for i in range(count)])


def part_swap(value):
    count = lax.axis_size("mlp")
    return lax.ppermute(value, "mlp", [(i, i ^ 2) for i in range(count)])


def both_swap(value):
    count = lax.axis_size("mlp")
    return lax.ppermute(value, "mlp", [(i, i ^ 3) for i in range(count)])


def chunk_move(value, target):
    shards, parts = lax.axis_size("seq"), lax.axis_size("mlp")
    pairs = []
    for chunk in range(2 * shards):
        goal = target(chunk)
        if goal is None or not 0 <= goal < 2 * shards:
            continue
        for part in range(2):
            pairs.append(((chunk // 2) * parts + chunk % 2 + 2 * part, (goal // 2) * parts + goal % 2 + 2 * part))
    return lax.ppermute(value, AXES, pairs)


def scan(value, flags, chunks, reverse, others=lambda: ()):
    places, _ = flag_places(chunks)
    found, arrived = None, None
    for stage, (size, ways, last) in enumerate(scan_plan(chunks)):
        got = []
        for step in range(1, ways):
            if last:

                def target(chunk, step=step):
                    move = -step if reverse else step
                    return chunk + move * size if 0 <= (chunk // size) % ways + move < ways else None

            else:

                def target(chunk, step=step):
                    member = (chunk // size) % ways
                    return chunk + ((member ^ step) - member) * size

            got.append(chunk_move(value, target))
        at = places[reverse, stage]
        if last:
            return (found, tuple(got), at), arrived, value
        arrived = arrived or tuple(got)
        operands = (flags, after(value, *others()), *got) + (() if found is None else (found,))
        value, found = call(
            functools.partial(combine_kernel, at, ways, found is not None),
            ((value.shape, bf16), (value.shape, f32)),
            operands,
            1,
        )


def shard_swap(value, bit):
    count = lax.axis_size("seq")
    return lax.ppermute(value, "seq", [(i, i ^ (1 << bit)) for i in range(count)])


def by_place(flag, mine, other):
    return jnp.where(flag == 0, mine, other), jnp.where(flag == 0, other, mine)


def per_device(inputs, lengths, valid, norm_attn, w_qkv, blend, w_out, norm_ffn, w_up, w_down, grad_out):
    shards, parts = lax.axis_size("seq"), lax.axis_size("mlp")
    shard, part = lax.axis_index("seq"), lax.axis_index("mlp")
    half = part % 2
    side = shard % 2
    rows = inputs.shape[0] // 2
    chunks = 2 * shards
    units = w_up.shape[2]
    place = jnp.stack([half, part // 2, shard]).astype(jnp.int32)

    wide = 2 * LANES
    hidden_like = ((rows, D), f32)
    low_like = ((rows, D), bf16)
    heads_like = ((rows, wide), f32)
    heads_low = ((rows, wide), bf16)
    qkv_like = ((3, rows, wide), bf16)
    state_like = ((2, STATE, LANES), bf16)
    halo_like = ((2, 2, HALO, LANES), bf16)
    ffn_like = ((rows, units), f32)
    ffn_low = ((rows, units), bf16)
    shard_like = ((rows, LANES), bf16)
    gain_like = ((1, D), f32)

    piece_like = ((rows + 3 * SMALL, LANES), bf16)
    (blend_rows,) = call(pack_blend_kernel, (((SMALL, LANES), f32),), (blend,), 1)
    mine, theirs = pl.pallas_call(
        pack_kernel,
        out_shape=tuple(jax.ShapeDtypeStruct(*piece_like) for _ in range(2)),
        in_specs=[SM] + [pl.BlockSpec(memory_space=pl.ANY)] * 3,
        out_specs=(VM, VM),
        scratch_shapes=(
            pltpu.VMEM(inputs.shape, bf16),
            pltpu.VMEM(norm_attn.shape, f32),
            pltpu.VMEM(norm_ffn.shape, f32),
            pltpu.SemaphoreType.DMA((3,)),
        ),
        compiler_params=pltpu.CompilerParams(vmem_limit_bytes=24 * 2**20),
    )(place, inputs, norm_attn, norm_ffn)
    got = half_swap(theirs)
    pieces = (mine, got, part_swap(mine), both_swap(theirs))
    far_qkv, far_out, far_up, far_down = [
        [
            half_swap(after(w[layer], theirs)) for layer in range(LAYERS)
        ]
        for w in (w_qkv, w_out, w_up, w_down)
    ]

    _, flag_count = flag_places(chunks)
    causal, causal_t, band, carried, tail, edge, flags = call(
        functools.partial(setup_kernel, chunks),
        (
            ((rows, rows), bf16),
            ((rows, rows), bf16),
            ((rows, LANES), f32),
            ((rows, LANES), f32),
            ((rows, LANES), bf16),
            ((HALO, LANES), bf16),
            ((flag_count,), f32),
        ),
        (place, lengths, valid.reshape(1, 2 * rows)),
        2,
        scalar_outs=1,
    )
    blends = jnp.concatenate([blend_rows, half_swap(blend_rows)], axis=1)

    saved = []
    base, adds = None, None
    for layer in range(LAYERS):
        outs = (hidden_like, low_like, qkv_like, state_like, ((5, HALO, LANES), bf16))
        if layer == 0:
            hidden, normed, qkv, state, halo, gains = call(
                functools.partial(qkv_kernel, True, layer),
                outs + (((SMALL, D), f32),),
                (place, *pieces, w_qkv, far_qkv[layer], tail, edge),
                1,
            )
        else:
            hidden, normed, qkv, state, halo = call(
                functools.partial(qkv_kernel, False, layer),
                outs,
                (place, base, *adds, gains, w_qkv, far_qkv[layer], tail, edge),
                1,
            )
        halo = chunk_move(halo, lambda c: c + 1)
        one, two, sums = call(far_kernel, (heads_like,) * 3, (qkv, causal), flops=10**9)
        (found, parts_got, at), arrived, _ = scan(state, flags, chunks, False, lambda: (one,))
        if layer == 0:
            grad_mine, grad_theirs = call(pack_grad_kernel, (shard_like, shard_like), (place, after(grad_out, normed)), 1)
            grad_pieces = (grad_mine, half_swap(grad_theirs), part_swap(grad_mine), both_swap(grad_theirs))
            found = after(found, *grad_pieces)
        (near,) = call(near_kernel, (heads_like,), (place, qkv, halo, band), 1)
        mixed, far_one, far_two, root, prefix, state, piece = call(
            functools.partial(mix_kernel, layer, at, len(parts_got)),
            (heads_low, heads_like, heads_like, heads_like, heads_like, state_like, low_like),
            (place, flags, qkv, near, one, two, sums, carried, blends, w_out, far_out[layer], found, *parts_got),
            2,
        )
        weights = (w_up, w_down, far_up[layer], far_down[layer])
        middle, normed_ffn, pre_own, pre_far, act_own, act_far, piece_ffn = call(
            functools.partial(ffn_kernel, layer),
            (hidden_like, low_like, ffn_like, ffn_like, ffn_low, ffn_low, low_like),
            (hidden, piece, part_swap(piece), gains, *weights),
        )
        saved.append(
            (hidden, normed, qkv, state, halo, mixed, far_one, far_two, root, prefix, middle, normed_ffn,
             weights, pre_own, pre_far, act_own, act_far)
        )
        base, adds = middle, (piece_ffn, part_swap(piece_ffn) if layer + 1 < LAYERS else None)
    last_base, last_piece = base, adds[0]
    base, adds = None, None
    d_gain_attn, d_gain_ffn, d_blends = [None] * LAYERS, [None] * LAYERS, [None] * LAYERS
    d_qkvs = [None] * LAYERS
    bits = (shards - 1).bit_length()
    side_first, line_first = (0, 1, 2), (1, 2, 0)

    def first_step(jobs, operands):
        height = sum(job_rows(job, units) for job in jobs)
        like = ((height, D), bf16)
        return call(functools.partial(grads_kernel, jobs), (like, like), (place, *operands), 1, bulk_outs=(0,))

    def group_steps(order, rows, first, second):
        height = rows[1] - rows[0]
        others = yield
        if bits != 3:
            if len(first) > 1:
                small = jnp.pad(first[1] + second[1], ((0, LANES - SMALL), (0, D - LANES)))
                total = jnp.concatenate([first[0].astype(f32) + second[0].astype(f32), small])
            else:
                total = (first[0].astype(f32) + second[0].astype(f32))[slice(*rows)]
            total = lax.psum(total, "seq").astype(bf16).reshape(2, height // 2, D)
            total = jnp.where((shard >> order[0]) % 2 == 0, total, total[::-1])
            for _ in range(6):
                yield total
            yield total[0], total[1]
        for at, bit in enumerate(order):
            height //= 2
            if at == 0 and len(first) > 1:
                body, operands = functools.partial(last_kernel, bit), (first[0], second[0], first[1], second[1])
            elif at == 0:
                body, operands = functools.partial(halve_kernel, bit, rows), (first[0], second[0])
            else:
                body, operands = functools.partial(halve_kernel, bit, (0, 2 * height)), (keep, got)
            keep, send = call(
                body,
                (((height, D), f32), ((height, D), bf16)),
                (place, operands[0], after(operands[1], *others), *operands[2:]),
                1,
                bulk=(1,) if at == 0 else (),
            )
            got = shard_swap(send, bit)
            others = yield send
        (value,) = call(add_kernel, (((height, D), bf16),), (keep, after(got, *others)))
        for bit in reversed(order):
            got = shard_swap(value, bit)
            if bit == order[0]:
                break
            others = yield value
            height *= 2
            (value,) = call(
                functools.partial(join_kernel, bit), (((height, D), bf16),), (place, value, after(got, *others)), 1
            )
        yield value
        yield (value, got)

    groups, taken = [], {}

    def start_group(layers, jobs, order, rows, first, second):
        steps = group_steps(order, rows, first, second)
        next(steps)
        groups.append((layers, jobs, order[0], steps))

    def step(index, *others):
        taken[index] = taken.get(index, 0) + 1
        return groups[index][3].send(others)

    for layer in reversed(range(LAYERS)):
        (hidden, normed, qkv, state, halo, mixed, far_one, far_two, root, prefix, middle, normed_ffn,
         weights, pre_own, pre_far, act_own, act_far) = saved[layer]
        outs = (hidden_like, low_like, ffn_low, ffn_low, low_like)
        if base is None:
            resid, grad_rows, d_up_own, d_up_far, piece = call(
                functools.partial(ffn_back_kernel, True, layer),
                outs,
                (place, *grad_pieces, *weights, pre_own, pre_far),
                1,
            )
        else:
            resid, grad_rows, d_up_own, d_up_far, piece, d_gain_attn[layer + 1] = call(
                functools.partial(ffn_back_kernel, False, layer),
                outs + (gain_like,),
                (base, *adds, saved[layer + 1][0], gains, *weights, pre_own, pre_far),
            )
        def upper_grads(*others):
            jobs = ("up", "down", "out")
            own, far = first_step(
                jobs, (after(normed_ffn, *others), d_up_own, d_up_far, act_own, act_far, grad_rows, mixed, out_rows)
            )
            start_group((layer,) * 3, jobs, side_first, (0, own.shape[0]), (own,), (half_swap(far),))
            return far

        def lower_grads(*others):
            jobs = ("up", "qkv", "down", "out")
            operands = (
                after(normed_ffn, *others), d_up_own, d_up_far, saved[1][1], d_qkvs[1], act_own, act_far, grad_rows,
                mixed, out_rows,
            )
            own, far = first_step(jobs, operands)
            cut = job_rows("up", units) + job_rows("qkv", units)
            got = half_swap(far)
            start_group((0, 1), jobs[:2], side_first, (0, cut), (own,), (got,))
            start_group((0,) * len(jobs[2:]), jobs[2:], line_first, (cut, own.shape[0]), (own,), (got,))
            return far

        (resid, out_rows, d_mixed, d_gain_ffn[layer], num_one, num_two, d_zeta, state_back, blend_far) = call(
            functools.partial(mix_back_kernel, layer),
            (hidden_like, low_like, heads_low, gain_like, heads_low, heads_low, heads_like, state_like,
             ((2, wide), f32)),
            (place, resid, piece, part_swap(piece), middle, gains, w_out, far_out[layer], qkv, far_one, far_two,
             root, carried, blends),
            1,
        )
        ext = HALO + rows + HALO
        dq_near, dk_near, dv_near, halo_back, blend_near = call(
            functools.partial(near_back_kernel, layer),
            (heads_like, heads_like, heads_like, halo_like, ((1, wide), f32)),
            (place, qkv, halo, band, d_mixed, blends),
            1,
            scratch=(pltpu.VMEM((ext, LANES), f32), pltpu.VMEM((ext, LANES), f32)),
        )
        halo_back = chunk_move(halo_back, lambda c: c - 1)
        (found, parts_got, at), arrived, value = scan(state_back, flags, chunks, True, lambda: (dq_near,))
        ready = [value]
        if layer > 0:
            ready.append(upper_grads(value))
        else:
            ready.append(step(0, *ready))
            ready.append(lower_grads(*ready))
        dq, dk_one, dk_two, dv = call(
            far_back_kernel,
            (heads_low, heads_like, heads_like, heads_like),
            (place, qkv, causal, causal_t, carried, state, prefix, after(num_one, *ready), num_two, d_zeta, dq_near,
             dv_near),
            1,
        )
        d_qkvs[layer], piece = call(
            functools.partial(qkv_back_kernel, layer, at, len(parts_got)),
            (qkv_like, low_like),
            (place, flags, qkv, dq, dk_one, dk_two, dk_near, dv, tail, halo_back, w_qkv, far_qkv[layer], found,
             *parts_got),
            2,
            scratch=(pltpu.VMEM((2, STATE, LANES), bf16),),
        )
        base, adds = resid, (piece, part_swap(piece))
        if layer > 0:
            base = after(base, step(0, piece))
        d_blends[layer] = (blend_near, blend_far)

    made = step(0, step(2, step(1, piece)))
    jobs = ("qkv",)
    height = job_rows("qkv", units)
    last_like = ((height, D), bf16)
    own, far = call(
        functools.partial(grads_kernel, jobs),
        (last_like, last_like),
        (place, after(saved[0][1], made), d_qkvs[0]),
        1,
    )
    smalls = d_gain_attn[1:] + d_gain_ffn + [ref for pair in d_blends for ref in pair]
    small_like = ((SMALL, LANES), f32)
    mine, theirs, small_own, small_far = call(
        end_kernel,
        (shard_like, shard_like, small_like, small_like),
        (place, after(base, far), *adds, saved[0][0], gains, *smalls),
        1,
    )
    start_group((0,), jobs, line_first, (0, height + LANES), (own, small_own), (half_swap(far), half_swap(small_far)))
    made = step(3, mine)
    for turn in range(6):
        for index in range(4):
            if taken[index] < 6:
                made = step(index, made)
        if turn == 1:
            last_piece = after(last_piece, made)
            out_mine, out_theirs = call(
                output_kernel, (shard_like, shard_like), (place, last_base, last_piece, part_swap(last_piece)), 1
            )
            output = jnp.concatenate(by_place(half, out_mine, half_swap(out_theirs)))
    d_inputs = jnp.concatenate(by_place(half, mine, half_swap(theirs)))
    sums = [part for group in groups for part in next(group[3])]
    d_up, d_down, d_out, above = call(
        functools.partial(finish_wide_kernel, [group[:3] for group in groups[:3]]),
        (
            ((LAYERS, D, units), f32),
            ((LAYERS, units, D), f32),
            ((LAYERS, LANES, D), f32),
            ((3 * LANES, D), bf16),
        ),
        (place, *sums[:6]),
        1,
    )
    d_qkv, d_norm_attn, d_norm_ffn, d_blend = call(
        functools.partial(finish_qkv_kernel, line_first[0]),
        (
            ((LAYERS, 3, D, LANES), f32),
            ((LAYERS, LANES), f32),
            ((LAYERS, LANES), f32),
            ((3 * LAYERS, LANES), f32),
        ),
        (place, *sums[6:], above),
        1,
    )
    d_blend = d_blend[:, :2].reshape(LAYERS, 3, 2)
    return (output, d_inputs, d_norm_attn, d_qkv, d_blend, d_out, d_norm_ffn, d_up, d_down)


def solution(mesh):
    placed = (
        P("seq", "mlp"),
        P(),
        P("seq"),
        P(None, "mlp"),
        P(None, None, None, "mlp"),
        P(None, None, "mlp"),
        P(None, "mlp", None),
        P(None, "mlp"),
        P(None, None, "mlp"),
        P(None, "mlp", None),
        P("seq", "mlp"),
    )
    return jax.shard_map(
        per_device,
        mesh=mesh,
        in_specs=placed,
        out_specs=(
            P("seq", "mlp"),
            P("seq", "mlp"),
            P(None, "mlp"),
            P(None, None, None, "mlp"),
            P(None, None, "mlp"),
            P(None, "mlp", None),
            P(None, "mlp"),
            P(None, None, "mlp"),
            P(None, "mlp", None),
        ),
        check_vma=False,
    )
```

```python
import functools
import math

import jax
import jax.numpy as jnp
from jax import lax
from jax.experimental import pallas as pl
from jax.experimental.pallas import tpu as pltpu
from jax.sharding import PartitionSpec as P

HD = 64
D = 512
BAND = 30
LAYERS = 2
HALO = 32
TILE = 64
LANES = 128
STATE = 144
SMALL = 16
AXES = ("seq", "mlp")

epsilon = 1e-05
masked_score = -1e30
score_scale = 1.0 / math.sqrt(HD)
far_scale = 1.0 / math.sqrt(HD)
f32 = jnp.float32
bf16 = jnp.bfloat16

VM = pl.BlockSpec(memory_space=pltpu.VMEM)
SM = pl.BlockSpec(memory_space=pltpu.SMEM)


def dot(x, y):
    return jnp.dot(x, y, preferred_element_type=f32)


def dot_nt(x, y):
    return lax.dot_general(x, y, (((1,), (1,)), ((), ())), preferred_element_type=f32)


def dot_tn(x, y):
    return lax.dot_general(x, y, (((0,), (0,)), ((), ())), preferred_element_type=f32)


def low_lanes(rows):
    return lax.broadcasted_iota(jnp.int32, (rows, LANES), 1) < HD


def split_heads(x):
    low = low_lanes(x.shape[0])
    zero = jnp.zeros_like(x)
    return jnp.concatenate([jnp.where(low, x, zero), jnp.where(low, zero, x)], axis=0)


def merge_heads(y):
    rows = y.shape[0] // 2
    return jnp.where(low_lanes(rows), y[:rows], y[rows:])


def head_sum(x):
    row = lax.broadcasted_iota(jnp.int32, (LANES, LANES), 0) < HD
    ones = jnp.where(row == low_lanes(LANES), 1.0, 0.0).astype(bf16)
    high = x.astype(bf16)
    rest = (x - high.astype(f32)).astype(bf16)
    return dot(high, ones) + dot(rest, ones)


def kernel_maps(x):
    return (
        jnp.where(x > 0, x + 1.0, jnp.exp(jnp.minimum(x, 0.0))).astype(bf16),
        jnp.tanh(x).astype(bf16),
    )


def maps_back(x, d_one, d_two):
    tanh = jnp.tanh(x)
    return jnp.where(x > 0, 1.0, jnp.exp(jnp.minimum(x, 0.0))) * d_one + (1.0 - tanh * tanh) * d_two


def put_state(ref, quarter, one, two, total):
    row = lax.broadcasted_iota(jnp.int32, (STATE - 2 * HD, LANES), 0)
    low = low_lanes(HD)
    ref[quarter, 0:HD, :] = jnp.where(low, one[:HD], one[HD:]).astype(bf16)
    ref[quarter, HD : 2 * HD, :] = jnp.where(low, two[:HD], two[HD:]).astype(bf16)
    ref[quarter, 2 * HD : STATE, :] = jnp.where(row == 0, total, 0.0).astype(bf16)


def get_state(ref, quarter):
    one = split_heads(ref[quarter, 0:HD, :])
    two = split_heads(ref[quarter, HD : 2 * HD, :])
    total = ref[quarter, 2 * HD : STATE, :].astype(f32)[0:1]
    return one, two, total


def norm_scale(hidden):
    return lax.rsqrt(jnp.sum(hidden * hidden, axis=1, keepdims=True) * (1.0 / D) + epsilon)


def norm_back(hidden, gain, grad):
    scale = norm_scale(hidden)
    gained = grad * gain
    inner = jnp.sum(gained * hidden, axis=1, keepdims=True) * (1.0 / D)
    back = scale * gained - hidden * (scale * scale * scale * inner)
    return back, jnp.sum(grad * hidden * scale, axis=0, keepdims=True)


def halo_bias(halo):
    ones = jnp.ones((LANES - HALO, LANES), bf16)
    flags = jnp.concatenate([halo[4], ones], axis=0)
    flags = dot_nt(jnp.ones((2 * TILE, LANES), bf16), flags)
    return jnp.where(flags > 0.5 * LANES, 0.0, masked_score)


def extend(halo, rows):
    return jnp.concatenate([halo, rows, jnp.zeros((HALO, LANES), bf16)], axis=0)


def three_parts(value):
    high = value.astype(bf16)
    rest = value - high.astype(f32)
    middle = rest.astype(bf16)
    low = (rest - middle.astype(f32)).astype(bf16)
    return jnp.concatenate([high, middle, low], axis=0)


def pack_kernel(place, inputs, norm_attn, norm_ffn, mine_out, theirs_out, rows_in, attn_in, ffn_in, sems):
    copies = [
        pltpu.make_async_copy(source, target, sems.at[k])
        for k, (source, target) in enumerate(((inputs, rows_in), (norm_attn, attn_in), (norm_ffn, ffn_in)))
    ]
    for copy in copies:
        copy.start()
    for copy in copies:
        copy.wait()
    rows = rows_in.shape[0] // 2
    small = [attn_in[...], ffn_in[...], jnp.zeros((SMALL - 2 * LAYERS, LANES), f32)]
    small = three_parts(jnp.concatenate(small, axis=0))
    first, second = rows_in[:rows], rows_in[rows:]
    mine_out[:rows] = jnp.where(place[0] == 0, first, second)
    theirs_out[:rows] = jnp.where(place[0] == 0, second, first)
    mine_out[rows:] = small
    theirs_out[rows:] = small


def pack_blend_kernel(blend, out):
    low = low_lanes(1)
    rows = []
    for layer in range(LAYERS):
        for kind in range(3):
            rows.append(jnp.where(low, blend[layer, kind, 0], blend[layer, kind, 1]))
    rows.append(jnp.zeros((SMALL - 3 * LAYERS, LANES), f32))
    out[...] = jnp.concatenate(rows, axis=0)


def pack_grad_kernel(place, grads, mine_out, theirs_out):
    rows = grads.shape[0] // 2
    first, second = grads[:rows], grads[rows:]
    mine_out[...] = jnp.where(place[0] == 0, first, second)
    theirs_out[...] = jnp.where(place[0] == 0, second, first)


def quarters(place):
    half, part = place[0], place[1]
    return 2 * part + half, 2 * part + 1 - half, 2 * (1 - part) + half, 2 * (1 - part) + 1 - half


def quarter_lanes(quarter):
    return pl.ds(pl.multiple_of(quarter * LANES, LANES), LANES)


def item_ends(lengths):
    ends = []
    for k in range(lengths.shape[0]):
        ends.append(lengths[k] if k == 0 else ends[-1] + lengths[k])
    return ends


def item_start(lengths, ends, positions):
    start = jnp.zeros_like(positions)
    for k, end in enumerate(ends):
        start = start + jnp.where(end <= positions, lengths[k], 0)
    return start


def scan_plan(chunks):
    stages, size = [], 1
    while size < chunks:
        ways = min(4, chunks // size)
        stages.append((size, ways, size * ways >= chunks))
        size *= ways
    return stages


def flag_places(chunks):
    at, places = 0, {}
    for reverse in (False, True):
        for stage, (_, ways, _) in enumerate(scan_plan(chunks)):
            places[reverse, stage] = at
            at += 2 * ways
    return places, at


def setup_kernel(
    chunks, place, lengths, valid, causal_out, causal_t_out, band_out, carried_out, tail_out, edge_out, flags_out
):
    rows = causal_out.shape[0]
    chunk = place[2] * 2 + place[0]
    first_row = chunk * rows
    ends = item_ends(lengths)

    def start_of(positions):
        return item_start(lengths, ends, positions)

    lane = lax.broadcasted_iota(jnp.int32, (1, rows), 1)
    starts_row = start_of(first_row + lane)
    starts = start_of(first_row + lax.broadcasted_iota(jnp.int32, (rows, LANES), 0))
    both = jnp.concatenate([starts, starts], axis=1)
    words = valid[...]
    own_words = jnp.where(place[0] == 0, words[:, :rows], words[:, rows:])
    row_at = lax.broadcasted_iota(jnp.int32, (rows, rows), 0)
    lane_at = lax.broadcasted_iota(jnp.int32, (rows, rows), 1)
    own_column = jnp.sum(jnp.where(row_at == lane_at, own_words, 0), axis=1, keepdims=True)
    same = both == starts_row
    causal_out[...] = jnp.where((lane_at <= row_at) & same & (own_words == 1), 1.0, 0.0).astype(bf16)
    causal_t_out[...] = jnp.where((row_at <= lane_at) & same & (own_column == 1), 1.0, 0.0).astype(bf16)
    carried_out[...] = jnp.where(starts < first_row, 1.0, 0.0)
    last_start = start_of(first_row + rows - 1)
    edge_out[...] = jnp.where(jnp.broadcast_to(own_column, (rows, LANES))[rows - HALO :] == 1, 1.0, 0.0).astype(bf16)
    tail_out[...] = jnp.where((starts == last_start) & (own_column == 1), 1.0, 0.0).astype(bf16)
    all_words = jnp.concatenate([jnp.ones((1, LANES), jnp.int32), own_words, jnp.zeros((1, LANES), jnp.int32)], axis=1)
    tile_row = lax.broadcasted_iota(jnp.int32, (TILE, LANES), 0)
    tile_lane = lax.broadcasted_iota(jnp.int32, (TILE, LANES), 1)
    gap = tile_row + HALO - tile_lane
    for tile in range(rows // TILE):
        key_starts = start_of(first_row + tile * TILE - HALO + lax.broadcasted_iota(jnp.int32, (1, LANES), 1))
        offset = LANES - HALO + tile * TILE
        key_words = all_words[:, offset : offset + LANES]
        at = slice(tile * TILE, (tile + 1) * TILE)
        allowed = (gap >= 0) & (gap <= BAND) & (starts[at] == key_starts) & ((key_words == 1) | (gap == 0))
        band_out[at] = jnp.where(allowed, 0.0, masked_score)

    places, _ = flag_places(chunks)
    for reverse in (False, True):
        edge = start_of(first_row + (rows - 1 if reverse else 0))
        for stage, (size, ways, last) in enumerate(scan_plan(chunks)):
            member = lax.rem(lax.div(chunk, size), ways)
            base = chunk - member * size - lax.rem(chunk, size)
            group = base if reverse else base + ways * size - 1
            group = start_of(group * rows + (0 if reverse else rows - 1))
            for step in range(ways):
                if last:
                    other = member + step if reverse else member - step
                else:
                    other = jnp.bitwise_xor(member, step)
                block = base + other * size + (0 if reverse else size - 1)
                start = start_of(block * rows + (0 if reverse else rows - 1))
                ahead = (other > member) if reverse else (other < member)
                ahead = ahead & (other >= 0) & (other < ways)
                at = places[reverse, stage] + 2 * step
                flags_out[at] = jnp.where(ahead & (start == edge), 1.0, 0.0)
                flags_out[at + 1] = jnp.where(start == group, 1.0, 0.0)


def combine_kernel(at, ways, has_found, flags, *refs):
    got, refs = refs[:ways], refs[ways:]
    total = sum(flags[at + 2 * step + 1] * got[step][...].astype(f32) for step in range(ways))
    refs[-2][...] = total.astype(bf16)
    found = sum(flags[at + 2 * step] * got[step][...].astype(f32) for step in range(1, ways))
    refs[-1][...] = found + refs[0][...] if has_found else found


def last_combine(at, flags, found, got, out):
    value = found[...]
    for step, part in enumerate(got):
        value = value + flags[at + 2 * (step + 1)] * part[...].astype(f32)
    out[...] = value.astype(bf16)


def qkv_kernel(first, layer, place, *refs):
    if first:
        refs, outs = refs[:8], refs[8:]
        pieces, (own, other, tail, edge) = refs[:4], refs[4:]
        hidden_out, normed_out, qkv_out, state_out, halo_out, gains = outs
        rows = hidden_out.shape[0]
        for piece, quarter in zip(pieces, quarters(place)):
            hidden_out[:, quarter_lanes(quarter)] = piece[:rows].astype(f32)
            parts = piece[rows:].astype(f32)
            small = parts[:SMALL] + parts[SMALL : 2 * SMALL] + parts[2 * SMALL :]
            gains[:, quarter_lanes(quarter)] = small
        hidden = hidden_out[...]
    else:
        base, part_a, part_b, gains, own, other, tail, edge, *outs = refs
        hidden_out, normed_out, qkv_out, state_out, halo_out = outs
        hidden = base[...] + (part_a[...].astype(f32) + part_b[...].astype(f32))
        hidden_out[...] = hidden
    rows = hidden.shape[0]
    normed = (hidden * norm_scale(hidden) * gains[layer : layer + 1]).astype(bf16)
    normed_out[...] = normed
    found = []
    for kind in range(3):
        weight = jnp.concatenate([own[layer, kind], other[kind]], axis=1)
        found.append(dot(normed, weight).astype(bf16))
        qkv_out[kind] = found[kind]
    for pair in range(2):
        quarter = place[0] if pair == 0 else 1 - place[0]
        lanes = slice(pair * LANES, (pair + 1) * LANES)
        keys, values = found[1][:, lanes], found[2][:, lanes]
        one, two = kernel_maps(keys.astype(f32))
        one, two = one * tail[...], two * tail[...]
        put_state(
            state_out,
            quarter,
            dot_tn(one, values),
            dot_tn(two, values),
            jnp.sum(one.astype(f32), axis=0, keepdims=True),
        )
        halo_out[2 * quarter] = keys[rows - HALO :]
        halo_out[2 * quarter + 1] = values[rows - HALO :]
    halo_out[4] = edge[...]


def far_kernel(qkv, causal, one_out, two_out, sums_out):
    masks = jnp.concatenate([causal[...], causal[...]], axis=0)
    for pair in range(2):
        lanes = slice(pair * LANES, (pair + 1) * LANES)
        queries, keys, values = qkv[0, :, lanes], qkv[1, :, lanes], qkv[2, :, lanes]
        maps_q, maps_k = kernel_maps(queries.astype(f32)), kernel_maps(keys.astype(f32))
        for query, key, out in ((maps_q[0], maps_k[0], one_out), (maps_q[1], maps_k[1], two_out)):
            attn = dot_nt(split_heads(query), key).astype(bf16) * masks
            out[:, lanes] = merge_heads(dot(attn, values))
        sums_out[:, lanes] = dot(causal[...], maps_k[0])


def near_kernel(place, qkv, halo, band, near_out):
    rows = qkv.shape[1]
    bias = halo_bias(halo)
    for pair in range(2):
        quarter = place[0] if pair == 0 else 1 - place[0]
        lanes = slice(pair * LANES, (pair + 1) * LANES)
        queries, keys, values = qkv[0, :, lanes], qkv[1, :, lanes], qkv[2, :, lanes]
        ext_keys = extend(halo[2 * quarter], keys)
        ext_values = extend(halo[2 * quarter + 1], values)
        for tile in range(rows // TILE):
            at = slice(tile * TILE, (tile + 1) * TILE)
            window = slice(tile * TILE, tile * TILE + LANES)
            allowed = jnp.concatenate([band[at], band[at]], axis=0)
            allowed = allowed + bias if tile == 0 else allowed
            scores = dot_nt(split_heads(queries[at]), ext_keys[window]) * score_scale + allowed
            weights = jnp.exp(scores - jnp.max(scores, axis=1, keepdims=True))
            weights = weights / jnp.sum(weights, axis=1, keepdims=True)
            near_out[at, lanes] = merge_heads(dot(weights.astype(bf16), ext_values[window]))


def mix_kernel(layer, at, count, place, flags, qkv, near, one, two, sums, carried, blends, own, other, found, *refs):
    got = refs[:count]
    mixed_out, far_one_out, far_two_out, root_out, prefix_out, state, part_out = refs[count:]
    last_combine(at, flags, found, got, state)
    mixed = []
    row = 3 * layer
    for pair in range(2):
        quarter = place[0] if pair == 0 else 1 - place[0]
        lanes = slice(pair * LANES, (pair + 1) * LANES)
        query_one, query_two = kernel_maps(qkv[0, :, lanes].astype(f32))
        state_one, state_two, total = get_state(state, quarter)
        num_one = one[:, lanes] + carried[...] * dot(query_one, state_one)
        num_two = two[:, lanes] + carried[...] * dot(query_two, state_two)
        prefix = sums[:, lanes] + carried[...] * total
        zeta = head_sum(query_one.astype(f32) * prefix)
        root = lax.rsqrt(zeta + 1.0)
        far_one = num_one * root * far_scale
        far_two = num_two * root
        far_one_out[:, lanes] = far_one
        far_two_out[:, lanes] = far_two
        root_out[:, lanes] = root
        prefix_out[:, lanes] = prefix
        mixed.append(
            (
                blends[row : row + 1, lanes] * near[:, lanes]
                + blends[row + 1 : row + 2, lanes] * far_one
                + blends[row + 2 : row + 3, lanes] * far_two
            ).astype(bf16)
        )
        mixed_out[:, lanes] = mixed[pair]
    weight = jnp.concatenate([own[layer], other[...]], axis=0)
    part_out[...] = dot(jnp.concatenate(mixed, axis=1), weight).astype(bf16)


def ffn_kernel(
    layer, base, part_a, part_b, gains, up_own, down_own, up_far, down_far,
    middle_out, normed_out, pre_own_out, pre_far_out, act_own_out, act_far_out, part_out,
):
    middle = base[...] + (part_a[...].astype(f32) + part_b[...].astype(f32))
    middle_out[...] = middle
    gain = gains[LAYERS + layer : LAYERS + layer + 1]
    normed = (middle * norm_scale(middle) * gain).astype(bf16)
    normed_out[...] = normed
    weights = (
        (up_own[layer], down_own[layer], pre_own_out, act_own_out),
        (up_far[...], down_far[...], pre_far_out, act_far_out),
    )
    total = None
    for up, down, pre_out, act_out in weights:
        pre = dot(normed, up)
        pre_out[...] = pre
        inner = jnp.tanh(math.sqrt(2.0 / math.pi) * (pre + 0.044715 * pre * pre * pre))
        act = (0.5 * pre * (1.0 + inner)).astype(bf16)
        act_out[...] = act
        product = dot(act, down)
        total = product if total is None else total + product
    part_out[...] = total.astype(bf16)


def shard_rows(whole, place, mine_out, theirs_out):
    first = [whole[:, m * LANES : (m + 1) * LANES] for m in range(4)]
    even, odd = [jnp.where(place[1] == 0, first[h], first[2 + h]) for h in range(2)]
    mine_out[...] = jnp.where(place[0] == 0, even, odd)
    theirs_out[...] = jnp.where(place[0] == 0, odd, even)


def output_kernel(place, base, part_a, part_b, mine_out, theirs_out):
    whole = base[...] + (part_a[...].astype(f32) + part_b[...].astype(f32))
    shard_rows(whole.astype(bf16), place, mine_out, theirs_out)


def gelu_slope(pre):
    c = math.sqrt(2.0 / math.pi)
    inner = jnp.tanh(c * (pre + 0.044715 * pre * pre * pre))
    return 0.5 * (1.0 + inner) + 0.5 * pre * (1.0 - inner * inner) * (c * (1.0 + 3 * 0.044715 * pre * pre))


def ffn_back_kernel(first, layer, *refs):
    if first:
        place, *refs = refs
        pieces, refs = refs[:4], refs[4:]
        weights, outs = refs[:6], refs[6:]
        resid_out, rows_out, d_up_own_out, d_up_far_out, part_out = outs
        for piece, quarter in zip(pieces, quarters(place)):
            resid_out[:, quarter_lanes(quarter)] = piece[...].astype(f32)
        resid = resid_out[...]
    else:
        base, part_a, part_b, hidden, gains, *refs = refs
        weights, outs = refs[:6], refs[6:]
        resid_out, rows_out, d_up_own_out, d_up_far_out, part_out, gain_out = outs
        back, gain_out[...] = norm_back(
            hidden[...], gains[layer + 1 : layer + 2], part_a[...].astype(f32) + part_b[...].astype(f32)
        )
        resid = base[...] + back
        resid_out[...] = resid
    up_own, down_own, up_far, down_far, pre_own, pre_far = weights
    rows = resid.astype(bf16)
    rows_out[...] = rows
    total = None
    for up, down, pre, out in (
        (up_own[layer], down_own[layer], pre_own, d_up_own_out),
        (up_far[...], down_far[...], pre_far, d_up_far_out),
    ):
        d_up = (gelu_slope(pre[...]) * dot_nt(rows, down)).astype(bf16)
        out[...] = d_up
        product = dot_nt(d_up, up)
        total = product if total is None else total + product
    part_out[...] = total.astype(bf16)


def mix_back_kernel(
    layer, place, base, part_a, part_b, middle, gains, own, other, qkv, far_one, far_two, root, carried, blends,
    resid_out, rows_out, mixed_out, gain_out, num_one_out, num_two_out, zeta_out, state_out, blend_out,
):
    back, gain_out[...] = norm_back(
        middle[...],
        gains[LAYERS + layer : LAYERS + layer + 1],
        part_a[...].astype(f32) + part_b[...].astype(f32),
    )
    resid = base[...] + back
    resid_out[...] = resid
    blend = blends[3 * layer : 3 * layer + 3]
    rows = resid.astype(bf16)
    rows_out[...] = rows
    weight = jnp.concatenate([own[layer], other[...]], axis=0)
    d_mixed = dot_nt(rows, weight).astype(bf16)
    mixed_out[...] = d_mixed
    for pair in range(2):
        quarter = place[0] if pair == 0 else 1 - place[0]
        lanes = slice(pair * LANES, (pair + 1) * LANES)
        grad = d_mixed[:, lanes].astype(f32)
        scale = root[:, lanes]
        dot_one = grad * far_one[:, lanes]
        dot_two = grad * far_two[:, lanes]
        blend_one, blend_two = blend[1:2, lanes], blend[2:3, lanes]
        blend_out[0:1, lanes] = jnp.sum(dot_one, axis=0, keepdims=True)
        blend_out[1:2, lanes] = jnp.sum(dot_two, axis=0, keepdims=True)
        num_one = (grad * (blend_one * far_scale) * scale).astype(bf16)
        num_two = (grad * blend_two * scale).astype(bf16)
        d_zeta = head_sum(blend_one * dot_one + blend_two * dot_two) * (-0.5 * scale * scale)
        num_one_out[:, lanes] = num_one
        num_two_out[:, lanes] = num_two
        zeta_out[:, lanes] = d_zeta
        query_one, query_two = kernel_maps(qkv[0, :, lanes].astype(f32))
        reach = carried[...].astype(bf16)
        put_state(
            state_out,
            quarter,
            dot_tn(query_one * reach, num_one),
            dot_tn(query_two * reach, num_two),
            jnp.sum(carried[...] * d_zeta * query_one.astype(f32), axis=0, keepdims=True),
        )


def near_back_kernel(
    layer, place, qkv, halo, band, d_mixed, blends, dq_out, dk_out, dv_out, halo_out, blend_out, near_k, near_v
):
    rows = qkv.shape[1]
    row_low = lax.broadcasted_iota(jnp.int32, (2 * TILE, 1), 0) < TILE
    bias = halo_bias(halo)
    row = 3 * layer
    for pair in range(2):
        quarter = place[0] if pair == 0 else 1 - place[0]
        lanes = slice(pair * LANES, (pair + 1) * LANES)
        queries, keys, values = qkv[0, :, lanes], qkv[1, :, lanes], qkv[2, :, lanes]
        grads = d_mixed[:, lanes]
        blend = blends[row : row + 1, lanes]
        ext_keys = extend(halo[2 * quarter], keys)
        ext_values = extend(halo[2 * quarter + 1], values)
        near_k[...] = jnp.zeros_like(near_k)
        near_v[...] = jnp.zeros_like(near_v)
        blend_rows = jnp.where(row_low, blend[:, :1], blend[:, HD : HD + 1])
        sums = None
        for tile in range(rows // TILE):
            at = slice(tile * TILE, (tile + 1) * TILE)
            window = slice(tile * TILE, tile * TILE + LANES)
            allowed = jnp.concatenate([band[at], band[at]], axis=0)
            allowed = allowed + bias if tile == 0 else allowed
            query_split, grad_split = split_heads(queries[at]), split_heads(grads[at])
            scores = dot_nt(query_split, ext_keys[window]) * score_scale + allowed
            probs = jnp.exp(scores - jnp.max(scores, axis=1, keepdims=True))
            probs = probs / jnp.sum(probs, axis=1, keepdims=True)
            d_probs = dot_nt(grad_split, ext_values[window])
            inner = jnp.sum(probs * d_probs, axis=1, keepdims=True)
            sums = inner if sums is None else sums + inner
            d_scores = (probs * (d_probs - inner) * blend_rows).astype(bf16)
            dq_out[at, lanes] = score_scale * merge_heads(dot(d_scores, ext_keys[window]))
            near_k[window] += dot_tn(d_scores, query_split)
            near_v[window] += dot_tn(probs.astype(bf16), grad_split)
        sum_low = jnp.sum(sums[:TILE], axis=0, keepdims=True)
        sum_high = jnp.sum(sums[TILE:], axis=0, keepdims=True)
        blend_out[0:1, lanes] = jnp.where(low_lanes(1), sum_low, sum_high) * (1.0 / HD)
        dk_out[:, lanes] = score_scale * near_k[HALO : HALO + rows]
        dv_out[:, lanes] = blend * near_v[HALO : HALO + rows]
        halo_out[quarter, 0] = (score_scale * near_k[0:HALO]).astype(bf16)
        halo_out[quarter, 1] = (blend * near_v[0:HALO]).astype(bf16)


def far_back_kernel(
    place, qkv, causal, causal_t, carried, state, prefix, num_one, num_two, d_zeta, dq_near, dv_near,
    dq_out, dk_one_out, dk_two_out, dv_out,
):
    masks = jnp.concatenate([causal[...], causal[...]], axis=0)
    masks_t = jnp.concatenate([causal_t[...], causal_t[...]], axis=1)
    for pair in range(2):
        quarter = place[0] if pair == 0 else 1 - place[0]
        lanes = slice(pair * LANES, (pair + 1) * LANES)
        queries, keys, values = qkv[0, :, lanes], qkv[1, :, lanes], qkv[2, :, lanes]
        state_one, state_two, unused_total = get_state(state, quarter)
        query_one, query_two = kernel_maps(queries.astype(f32))
        key_one, key_two = kernel_maps(keys.astype(f32))
        d_values = dv_near[:, lanes]
        d_queries = []
        for query, key, num, square, out in (
            (query_one, key_one, num_one[:, lanes], state_one, dk_one_out),
            (query_two, key_two, num_two[:, lanes], state_two, dk_two_out),
        ):
            query_split, num_split = split_heads(query), split_heads(num)
            attn_t = dot_nt(key, query_split).astype(bf16) * masks_t
            grad = dot_nt(num_split, values).astype(bf16) * masks
            grad_t = dot_nt(values, num_split).astype(bf16) * masks_t
            d_values = d_values + dot(attn_t, num_split)
            d_queries.append(merge_heads(dot(grad, key)) + carried[...] * dot_nt(num, square))
            out[:, lanes] = dot(grad_t, query_split)
        zeta = d_zeta[:, lanes]
        d_queries[0] += zeta * prefix[:, lanes]
        dk_one_out[:, lanes] += dot(causal_t[...], (zeta * query_one.astype(f32)).astype(bf16))
        back = maps_back(queries.astype(f32), d_queries[0], d_queries[1])
        dq_out[:, lanes] = (back + dq_near[:, lanes]).astype(bf16)
        dv_out[:, lanes] = d_values


def qkv_back_kernel(
    layer, at, count, place, flags, qkv, dq, dk_one, dk_two, dk_near, dv, tail, halo, own, other, found, *refs
):
    got = refs[:count]
    d_qkv_out, part_out, state = refs[count:]
    last_combine(at, flags, found, got, state)
    rows = qkv.shape[1]
    empty = jnp.zeros((rows - HALO, LANES), f32)
    for pair in range(2):
        quarter = place[0] if pair == 0 else 1 - place[0]
        lanes = slice(pair * LANES, (pair + 1) * LANES)
        keys, values = qkv[1, :, lanes], qkv[2, :, lanes]
        key_one, key_two = kernel_maps(keys.astype(f32))
        state_one, state_two, total = get_state(state, quarter)
        weight = tail[...].astype(f32)
        d_one = dk_one[:, lanes] + weight * (dot_nt(values, state_one) + total)
        d_two = dk_two[:, lanes] + weight * dot_nt(values, state_two)
        halo_k = jnp.concatenate([empty, halo[quarter, 0].astype(f32)], axis=0)
        halo_v = jnp.concatenate([empty, halo[quarter, 1].astype(f32)], axis=0)
        d_qkv_out[1, :, lanes] = (
            maps_back(keys.astype(f32), d_one, d_two) + dk_near[:, lanes] + halo_k
        ).astype(bf16)
        d_qkv_out[2, :, lanes] = (
            dv[:, lanes] + weight * (dot(key_one, state_one) + dot(key_two, state_two)) + halo_v
        ).astype(bf16)
    d_qkv_out[0] = dq[...]
    total = None
    for kind in range(3):
        weight = jnp.concatenate([own[layer, kind], other[kind]], axis=1)
        product = dot_nt(d_qkv_out[kind], weight)
        total = product if total is None else total + product
    part_out[...] = total.astype(bf16)


JOB_REFS = {"up": 3, "down": 3, "out": 2, "qkv": 2}


def job_rows(job, units):
    return {"up": D, "down": units, "out": LANES, "qkv": 3 * LANES}[job]


def fill_grads(jobs, refs, own, far):
    at = 0
    for job in jobs:
        mine, refs = refs[: JOB_REFS[job]], refs[JOB_REFS[job] :]
        if job == "up":
            normed, grad_own, grad_far = mine
            own[at : at + D] = dot_tn(normed[...], grad_own[...]).astype(bf16)
            far[at : at + D] = dot_tn(normed[...], grad_far[...]).astype(bf16)
            at += D
        elif job == "down":
            act_own, act_far, grad = mine
            units = act_own.shape[1]
            own[at : at + units] = dot_tn(act_own[...], grad[...]).astype(bf16)
            far[at : at + units] = dot_tn(act_far[...], grad[...]).astype(bf16)
            at += units
        elif job == "out":
            mixed, grad = mine
            found = dot_tn(mixed[...], grad[...]).astype(bf16)
            own[at : at + LANES] = found[:LANES]
            far[at : at + LANES] = found[LANES:]
            at += LANES
        else:
            normed, d_qkv = mine
            for kind in range(3):
                found = dot_tn(normed[...], d_qkv[kind]).astype(bf16)
                for block in range(D // LANES):
                    lanes = slice(block * LANES, (block + 1) * LANES)
                    own[at : at + LANES, lanes] = found[lanes, :LANES]
                    far[at : at + LANES, lanes] = found[lanes, LANES:]
                at += LANES


def grads_kernel(jobs, place, *refs):
    fill_grads(jobs, refs[:-2], refs[-2], refs[-1])


def shard_bit(place, bit):
    return lax.rem(lax.div(place[2], 1 << bit), 2)


def give_half(bit, place, total, keep_out, send_out):
    rows = total.shape[0] // 2
    low = shard_bit(place, bit) == 0
    keep_out[...] = jnp.where(low, total[:rows], total[rows:])
    send_out[...] = jnp.where(low, total[rows:], total[:rows]).astype(bf16)


def halve_kernel(bit, rows, place, first, second, keep_out, send_out):
    at = slice(*rows)
    give_half(bit, place, first[at].astype(f32) + second[at].astype(f32), keep_out, send_out)


def add_kernel(first, second, out):
    out[...] = (first[...].astype(f32) + second[...].astype(f32)).astype(bf16)


def join_kernel(bit, place, mine, got, out):
    low = shard_bit(place, bit) == 0
    rows = mine.shape[0]
    out[:rows] = jnp.where(low, mine[...], got[...])
    out[rows:] = jnp.where(low, got[...], mine[...])


def end_kernel(place, base, part_a, part_b, hidden, gains, *refs):
    smalls, (mine_out, theirs_out, own_out, far_out) = refs[: 4 * LAYERS - 1], refs[4 * LAYERS - 1 :]
    gain_refs, blend_refs = smalls[: 2 * LAYERS - 1], smalls[2 * LAYERS - 1 :]
    back, gain = norm_back(hidden[...], gains[0:1], part_a[...].astype(f32) + part_b[...].astype(f32))
    shard_rows((base[...] + back).astype(bf16), place, mine_out, theirs_out)
    gain_rows = jnp.concatenate([gain] + [ref[...] for ref in gain_refs], axis=0)
    blend_rows = jnp.concatenate([ref[...] for ref in blend_refs], axis=0)
    extras = []
    for to in range(2):
        features = jnp.where(
            place[1] == 0,
            gain_rows[:, to * LANES : (to + 1) * LANES],
            gain_rows[:, (2 + to) * LANES : (3 + to) * LANES],
        )
        blends = jnp.where(place[0] == to, blend_rows[:, :LANES], blend_rows[:, LANES:])
        extras.append(jnp.concatenate([features, blends, jnp.zeros((SMALL - 5 * LAYERS, LANES), f32)], axis=0))
    own_out[...] = jnp.where(place[0] == 0, extras[0], extras[1])
    far_out[...] = jnp.where(place[0] == 0, extras[1], extras[0])


def last_kernel(bit, place, own, far, small_own, small_far, keep_out, send_out):
    small = jnp.concatenate([small_own[...] + small_far[...], jnp.zeros((SMALL, D - LANES), f32)], axis=1)
    small = jnp.concatenate([small, jnp.zeros((LANES - SMALL, D), f32)], axis=0)
    total = jnp.concatenate([own[...].astype(f32) + far[...].astype(f32), small], axis=0)
    give_half(bit, place, total, keep_out, send_out)


def in_order(bit, place, mine, other):
    low = shard_bit(place, bit) == 0
    first, second = jnp.where(low, mine[...], other[...]), jnp.where(low, other[...], mine[...])
    return jnp.concatenate([first, second], axis=0)


def finish_wide_kernel(groups, place, *refs):
    refs, (up_out, down_out, out_out, above_out) = refs[:-4], refs[-4:]
    outs = {"up": up_out, "down": down_out, "out": out_out}
    for group, (layers, jobs, bit) in enumerate(groups):
        whole = in_order(bit, place, refs[2 * group], refs[2 * group + 1])
        at = 0
        for layer, job in zip(layers, jobs):
            rows = whole[at : at + job_rows(job, up_out.shape[2])]
            at += rows.shape[0]
            if job == "qkv":
                above_out[...] = rows
            else:
                outs[job][layer] = rows.astype(f32)


def finish_qkv_kernel(bit, place, mine, other, above, qkv_out, attn_out, ffn_out, blend_out):
    whole = in_order(bit, place, mine, other)
    at = 3 * LANES
    for layer, rows in enumerate((whole, above)):
        for kind in range(3):
            for block in range(D // LANES):
                lanes = slice(block * LANES, (block + 1) * LANES)
                qkv_out[layer, kind, lanes] = rows[kind * LANES : (kind + 1) * LANES, lanes].astype(f32)
    small = whole[at : at + SMALL, :LANES].astype(f32)
    attn_out[...] = small[:LAYERS]
    ffn_out[...] = small[LAYERS : 2 * LAYERS]
    blends = small[2 * LAYERS : 5 * LAYERS]
    low = low_lanes(3 * LAYERS)
    lane = lax.broadcasted_iota(jnp.int32, (3 * LAYERS, LANES), 1)
    first = jnp.sum(jnp.where(low, blends, 0.0), axis=1, keepdims=True)
    second = jnp.sum(jnp.where(low, 0.0, blends), axis=1, keepdims=True)
    blend_out[...] = jnp.where(lane == 0, first, second)


def call(body, outs, operands, scalars=0, scratch=(), scalar_outs=0, bulk=(), bulk_outs=(), flops=None):
    specs = [SM] * scalars + [VM] * (len(operands) - scalars)
    out_specs = [VM] * (len(outs) - scalar_outs) + [SM] * scalar_outs
    for index in bulk:
        specs[index] = pl.BlockSpec()
    for index in bulk_outs:
        out_specs[index] = pl.BlockSpec()
    cost = flops and pl.CostEstimate(flops=flops, bytes_accessed=0, transcendentals=0)
    return pl.pallas_call(
        body,
        out_shape=tuple(jax.ShapeDtypeStruct(shape, kind) for shape, kind in outs),
        in_specs=specs,
        out_specs=tuple(out_specs),
        scratch_shapes=scratch,
        cost_estimate=cost,
        compiler_params=pltpu.CompilerParams(vmem_limit_bytes=24 * 2**20),
    )(*operands)


def after(value, *others):
    return lax.optimization_barrier((value, *others))[0] if others else value


def half_swap(value):
    count = lax.axis_size("mlp")
    return lax.ppermute(value, "mlp", [(i, i ^ 1) for i in range(count)])


def part_swap(value):
    count = lax.axis_size("mlp")
    return lax.ppermute(value, "mlp", [(i, i ^ 2) for i in range(count)])


def both_swap(value):
    count = lax.axis_size("mlp")
    return lax.ppermute(value, "mlp", [(i, i ^ 3) for i in range(count)])


def chunk_move(value, target):
    shards, parts = lax.axis_size("seq"), lax.axis_size("mlp")
    pairs = []
    for chunk in range(2 * shards):
        goal = target(chunk)
        if goal is None or not 0 <= goal < 2 * shards:
            continue
        for part in range(2):
            pairs.append(((chunk // 2) * parts + chunk % 2 + 2 * part, (goal // 2) * parts + goal % 2 + 2 * part))
    return lax.ppermute(value, AXES, pairs)


def scan(value, flags, chunks, reverse, others=lambda: ()):
    places, _ = flag_places(chunks)
    found, arrived = None, None
    for stage, (size, ways, last) in enumerate(scan_plan(chunks)):
        got = []
        for step in range(1, ways):
            if last:

                def target(chunk, step=step):
                    move = -step if reverse else step
                    return chunk + move * size if 0 <= (chunk // size) % ways + move < ways else None

            else:

                def target(chunk, step=step):
                    member = (chunk // size) % ways
                    return chunk + ((member ^ step) - member) * size

            got.append(chunk_move(value, target))
        at = places[reverse, stage]
        if last:
            return (found, tuple(got), at), arrived, value
        arrived = arrived or tuple(got)
        operands = (flags, after(value, *others()), *got) + (() if found is None else (found,))
        value, found = call(
            functools.partial(combine_kernel, at, ways, found is not None),
            ((value.shape, bf16), (value.shape, f32)),
            operands,
            1,
        )


def shard_swap(value, bit):
    count = lax.axis_size("seq")
    return lax.ppermute(value, "seq", [(i, i ^ (1 << bit)) for i in range(count)])


def by_place(flag, mine, other):
    return jnp.where(flag == 0, mine, other), jnp.where(flag == 0, other, mine)


def per_device(inputs, lengths, valid, norm_attn, w_qkv, blend, w_out, norm_ffn, w_up, w_down, grad_out):
    shards, parts = lax.axis_size("seq"), lax.axis_size("mlp")
    shard, part = lax.axis_index("seq"), lax.axis_index("mlp")
    half = part % 2
    side = shard % 2
    rows = inputs.shape[0] // 2
    chunks = 2 * shards
    units = w_up.shape[2]
    place = jnp.stack([half, part // 2, shard]).astype(jnp.int32)

    wide = 2 * LANES
    hidden_like = ((rows, D), f32)
    low_like = ((rows, D), bf16)
    heads_like = ((rows, wide), f32)
    heads_low = ((rows, wide), bf16)
    qkv_like = ((3, rows, wide), bf16)
    state_like = ((2, STATE, LANES), bf16)
    halo_like = ((2, 2, HALO, LANES), bf16)
    ffn_like = ((rows, units), f32)
    ffn_low = ((rows, units), bf16)
    shard_like = ((rows, LANES), bf16)
    gain_like = ((1, D), f32)

    piece_like = ((rows + 3 * SMALL, LANES), bf16)
    (blend_rows,) = call(pack_blend_kernel, (((SMALL, LANES), f32),), (blend,), 1)
    mine, theirs = pl.pallas_call(
        pack_kernel,
        out_shape=tuple(jax.ShapeDtypeStruct(*piece_like) for _ in range(2)),
        in_specs=[SM] + [pl.BlockSpec(memory_space=pl.ANY)] * 3,
        out_specs=(VM, VM),
        scratch_shapes=(
            pltpu.VMEM(inputs.shape, bf16),
            pltpu.VMEM(norm_attn.shape, f32),
            pltpu.VMEM(norm_ffn.shape, f32),
            pltpu.SemaphoreType.DMA((3,)),
        ),
        compiler_params=pltpu.CompilerParams(vmem_limit_bytes=24 * 2**20),
    )(place, inputs, norm_attn, norm_ffn)
    got = half_swap(theirs)
    pieces = (mine, got, part_swap(mine), both_swap(theirs))
    far_qkv, far_out, far_up, far_down = [
        [
            half_swap(after(w[layer], theirs)) for layer in range(LAYERS)
        ]
        for w in (w_qkv, w_out, w_up, w_down)
    ]

    _, flag_count = flag_places(chunks)
    causal, causal_t, band, carried, tail, edge, flags = call(
        functools.partial(setup_kernel, chunks),
        (
            ((rows, rows), bf16),
            ((rows, rows), bf16),
            ((rows, LANES), f32),
            ((rows, LANES), f32),
            ((rows, LANES), bf16),
            ((HALO, LANES), bf16),
            ((flag_count,), f32),
        ),
        (place, lengths, valid.reshape(1, 2 * rows)),
        2,
        scalar_outs=1,
    )
    blends = jnp.concatenate([blend_rows, half_swap(blend_rows)], axis=1)

    saved = []
    base, adds = None, None
    for layer in range(LAYERS):
        outs = (hidden_like, low_like, qkv_like, state_like, ((5, HALO, LANES), bf16))
        if layer == 0:
            hidden, normed, qkv, state, halo, gains = call(
                functools.partial(qkv_kernel, True, layer),
                outs + (((SMALL, D), f32),),
                (place, *pieces, w_qkv, far_qkv[layer], tail, edge),
                1,
            )
        else:
            hidden, normed, qkv, state, halo = call(
                functools.partial(qkv_kernel, False, layer),
                outs,
                (place, base, *adds, gains, w_qkv, far_qkv[layer], tail, edge),
                1,
            )
        halo = chunk_move(halo, lambda c: c + 1)
        one, two, sums = call(far_kernel, (heads_like,) * 3, (qkv, causal), flops=10**9)
        (found, parts_got, at), arrived, _ = scan(state, flags, chunks, False, lambda: (one,))
        if layer == 0:
            grad_mine, grad_theirs = call(pack_grad_kernel, (shard_like, shard_like), (place, after(grad_out, normed)), 1)
            grad_pieces = (grad_mine, half_swap(grad_theirs), part_swap(grad_mine), both_swap(grad_theirs))
            found = after(found, *grad_pieces)
        (near,) = call(near_kernel, (heads_like,), (place, qkv, halo, band), 1)
        mixed, far_one, far_two, root, prefix, state, piece = call(
            functools.partial(mix_kernel, layer, at, len(parts_got)),
            (heads_low, heads_like, heads_like, heads_like, heads_like, state_like, low_like),
            (place, flags, qkv, near, one, two, sums, carried, blends, w_out, far_out[layer], found, *parts_got),
            2,
        )
        weights = (w_up, w_down, far_up[layer], far_down[layer])
        middle, normed_ffn, pre_own, pre_far, act_own, act_far, piece_ffn = call(
            functools.partial(ffn_kernel, layer),
            (hidden_like, low_like, ffn_like, ffn_like, ffn_low, ffn_low, low_like),
            (hidden, piece, part_swap(piece), gains, *weights),
        )
        saved.append(
            (hidden, normed, qkv, state, halo, mixed, far_one, far_two, root, prefix, middle, normed_ffn,
             weights, pre_own, pre_far, act_own, act_far)
        )
        base, adds = middle, (piece_ffn, part_swap(piece_ffn) if layer + 1 < LAYERS else None)
    last_base, last_piece = base, adds[0]
    base, adds = None, None
    d_gain_attn, d_gain_ffn, d_blends = [None] * LAYERS, [None] * LAYERS, [None] * LAYERS
    d_qkvs = [None] * LAYERS
    bits = (shards - 1).bit_length()
    side_first, line_first, last_order = (0, 1, 2), (1, 2, 0), (1, 0, 2)

    def first_step(jobs, operands):
        height = sum(job_rows(job, units) for job in jobs)
        like = ((height, D), bf16)
        return call(functools.partial(grads_kernel, jobs), (like, like), (place, *operands), 1, bulk_outs=(0,))

    def group_steps(order, rows, first, second):
        height = rows[1] - rows[0]
        others = yield
        if bits != 3:
            if len(first) > 1:
                small = jnp.pad(first[1] + second[1], ((0, LANES - SMALL), (0, D - LANES)))
                total = jnp.concatenate([first[0].astype(f32) + second[0].astype(f32), small])
            else:
                total = (first[0].astype(f32) + second[0].astype(f32))[slice(*rows)]
            total = lax.psum(total, "seq").astype(bf16).reshape(2, height // 2, D)
            total = jnp.where((shard >> order[0]) % 2 == 0, total, total[::-1])
            for _ in range(6):
                yield total
            yield total[0], total[1]
        for at, bit in enumerate(order):
            height //= 2
            if at == 0 and len(first) > 1:
                body, operands = functools.partial(last_kernel, bit), (first[0], second[0], first[1], second[1])
            elif at == 0:
                body, operands = functools.partial(halve_kernel, bit, rows), (first[0], second[0])
            else:
                body, operands = functools.partial(halve_kernel, bit, (0, 2 * height)), (keep, got)
            keep, send = call(
                body,
                (((height, D), f32), ((height, D), bf16)),
                (place, operands[0], after(operands[1], *others), *operands[2:]),
                1,
                bulk=(1,) if at == 0 else (),
            )
            got = shard_swap(send, bit)
            others = yield send
        (value,) = call(add_kernel, (((height, D), bf16),), (keep, after(got, *others)))
        for bit in reversed(order):
            got = shard_swap(value, bit)
            if bit == order[0]:
                break
            others = yield value
            height *= 2
            (value,) = call(
                functools.partial(join_kernel, bit), (((height, D), bf16),), (place, value, after(got, *others)), 1
            )
        yield value
        yield (value, got)

    groups, taken = [], {}

    def start_group(layers, jobs, order, rows, first, second):
        steps = group_steps(order, rows, first, second)
        next(steps)
        groups.append((layers, jobs, order[0], steps))

    def step(index, *others):
        taken[index] = taken.get(index, 0) + 1
        return groups[index][3].send(others)

    for layer in reversed(range(LAYERS)):
        (hidden, normed, qkv, state, halo, mixed, far_one, far_two, root, prefix, middle, normed_ffn,
         weights, pre_own, pre_far, act_own, act_far) = saved[layer]
        outs = (hidden_like, low_like, ffn_low, ffn_low, low_like)
        if base is None:
            resid, grad_rows, d_up_own, d_up_far, piece = call(
                functools.partial(ffn_back_kernel, True, layer),
                outs,
                (place, *grad_pieces, *weights, pre_own, pre_far),
                1,
            )
        else:
            resid, grad_rows, d_up_own, d_up_far, piece, d_gain_attn[layer + 1] = call(
                functools.partial(ffn_back_kernel, False, layer),
                outs + (gain_like,),
                (base, *adds, saved[layer + 1][0], gains, *weights, pre_own, pre_far),
            )
        def upper_grads(*others):
            jobs = ("up", "down", "out")
            own, far = first_step(
                jobs, (after(normed_ffn, *others), d_up_own, d_up_far, act_own, act_far, grad_rows, mixed, out_rows)
            )
            start_group((layer,) * 3, jobs, side_first, (0, own.shape[0]), (own,), (half_swap(far),))
            return far

        def lower_grads(*others):
            jobs = ("up", "qkv", "down", "out")
            operands = (
                after(normed_ffn, *others), d_up_own, d_up_far, saved[1][1], d_qkvs[1], act_own, act_far, grad_rows,
                mixed, out_rows,
            )
            own, far = first_step(jobs, operands)
            cut = job_rows("up", units) + job_rows("qkv", units)
            got = half_swap(far)
            start_group((0, 1), jobs[:2], side_first, (0, cut), (own,), (got,))
            start_group((0,) * len(jobs[2:]), jobs[2:], line_first, (cut, own.shape[0]), (own,), (got,))
            return far

        (resid, out_rows, d_mixed, d_gain_ffn[layer], num_one, num_two, d_zeta, state_back, blend_far) = call(
            functools.partial(mix_back_kernel, layer),
            (hidden_like, low_like, heads_low, gain_like, heads_low, heads_low, heads_like, state_like,
             ((2, wide), f32)),
            (place, resid, piece, part_swap(piece), middle, gains, w_out, far_out[layer], qkv, far_one, far_two,
             root, carried, blends),
            1,
        )
        ext = HALO + rows + HALO
        dq_near, dk_near, dv_near, halo_back, blend_near = call(
            functools.partial(near_back_kernel, layer),
            (heads_like, heads_like, heads_like, halo_like, ((1, wide), f32)),
            (place, qkv, halo, band, d_mixed, blends),
            1,
            scratch=(pltpu.VMEM((ext, LANES), f32), pltpu.VMEM((ext, LANES), f32)),
        )
        halo_back = chunk_move(halo_back, lambda c: c - 1)
        (found, parts_got, at), arrived, value = scan(state_back, flags, chunks, True, lambda: (dq_near,))
        ready = [value]
        if layer > 0:
            ready.append(upper_grads(value))
        else:
            ready.append(step(0, *ready))
            ready.append(lower_grads(*ready))
        dq, dk_one, dk_two, dv = call(
            far_back_kernel,
            (heads_low, heads_like, heads_like, heads_like),
            (place, qkv, causal, causal_t, carried, state, prefix, after(num_one, *ready), num_two, d_zeta, dq_near,
             dv_near),
            1,
        )
        d_qkvs[layer], piece = call(
            functools.partial(qkv_back_kernel, layer, at, len(parts_got)),
            (qkv_like, low_like),
            (place, flags, qkv, dq, dk_one, dk_two, dk_near, dv, tail, halo_back, w_qkv, far_qkv[layer], found,
             *parts_got),
            2,
            scratch=(pltpu.VMEM((2, STATE, LANES), bf16),),
        )
        base, adds = resid, (piece, part_swap(piece))
        if layer > 0:
            base = after(base, step(0, piece))
        d_blends[layer] = (blend_near, blend_far)

    made = step(0, step(2, step(1, piece)))
    jobs = ("qkv",)
    height = job_rows("qkv", units)
    last_like = ((height, D), bf16)
    own, far = call(
        functools.partial(grads_kernel, jobs),
        (last_like, last_like),
        (place, after(saved[0][1], made), d_qkvs[0]),
        1,
    )
    smalls = d_gain_attn[1:] + d_gain_ffn + [ref for pair in d_blends for ref in pair]
    small_like = ((SMALL, LANES), f32)
    mine, theirs, small_own, small_far = call(
        end_kernel,
        (shard_like, shard_like, small_like, small_like),
        (place, after(base, far), *adds, saved[0][0], gains, *smalls),
        1,
    )
    start_group((0,), jobs, last_order, (0, height + LANES), (own, small_own), (half_swap(far), half_swap(small_far)))
    made = step(3, mine)
    for turn in range(6):
        for index in range(4):
            if taken[index] < 6:
                made = step(index, made)
        if turn == 1:
            last_piece = after(last_piece, made)
            out_mine, out_theirs = call(
                output_kernel, (shard_like, shard_like), (place, last_base, last_piece, part_swap(last_piece)), 1
            )
            output = jnp.concatenate(by_place(half, out_mine, half_swap(out_theirs)))
    d_inputs = jnp.concatenate(by_place(half, mine, half_swap(theirs)))
    sums = [part for group in groups for part in next(group[3])]
    d_up, d_down, d_out, above = call(
        functools.partial(finish_wide_kernel, [group[:3] for group in groups[:3]]),
        (
            ((LAYERS, D, units), f32),
            ((LAYERS, units, D), f32),
            ((LAYERS, LANES, D), f32),
            ((3 * LANES, D), bf16),
        ),
        (place, *sums[:6]),
        1,
    )
    d_qkv, d_norm_attn, d_norm_ffn, d_blend = call(
        functools.partial(finish_qkv_kernel, line_first[0]),
        (
            ((LAYERS, 3, D, LANES), f32),
            ((LAYERS, LANES), f32),
            ((LAYERS, LANES), f32),
            ((3 * LAYERS, LANES), f32),
        ),
        (place, *sums[6:], above),
        1,
    )
    d_blend = d_blend[:, :2].reshape(LAYERS, 3, 2)
    return (output, d_inputs, d_norm_attn, d_qkv, d_blend, d_out, d_norm_ffn, d_up, d_down)


def solution(mesh):
    placed = (
        P("seq", "mlp"),
        P(),
        P("seq"),
        P(None, "mlp"),
        P(None, None, None, "mlp"),
        P(None, None, "mlp"),
        P(None, "mlp", None),
        P(None, "mlp"),
        P(None, None, "mlp"),
        P(None, "mlp", None),
        P("seq", "mlp"),
    )
    return jax.shard_map(
        per_device,
        mesh=mesh,
        in_specs=placed,
        out_specs=(
            P("seq", "mlp"),
            P("seq", "mlp"),
            P(None, "mlp"),
            P(None, None, None, "mlp"),
            P(None, None, "mlp"),
            P(None, "mlp", None),
            P(None, "mlp"),
            P(None, None, "mlp"),
            P(None, "mlp", None),
        ),
        check_vma=False,
    )
```
